32 devices in a mesh: order: 4 (over y, x), lat: 8 (over z, core).
Axes of the slice: x: 2, y: 2, z: 4, core: 2. Of those that a mesh axis runs over, the one named last changes fastest.
Arguments:
- fourier: bfloat16 [128, 64, 2048], P('order', None, 'lat'), may hold values from -6 to 6
- quad_weights: float32 [2048], P('lat'), may hold values from 0.5 to 1.5
- leaf_basis: bfloat16 [128, 64, 2048], P('order', None, 'lat'), may hold values from -0.375 to 0.375
- level_factors: bfloat16 [128, 3, 2, 8, 64, 64], P('order', None, None, 'lat'), may hold values from -0.5 to 0.5
- sparsity: int32 [128, 3, 8], P('order', None, 'lat'), may hold values 0 or 1
- root_basis: bfloat16 [128, 64, 2048], P(None, None, 'lat'), may hold values from -0.75 to 0.75
- order_of_slot: int32 [128], replicated, may hold values from 0 to 127, each once
Outputs:
- spectra: bfloat16 [32, 2, 2048, 128], P('order', None, 'lat')
The draws below stay inside these ranges and needn't reach their ends.
Inputs may be any that keep to these rules, and one draw needn't show every extreme that they name: `order_of_slot`: every window index appears in exactly one slot.
All inputs are finite; a program needn't handle non-finite values. No bound on the sum of `sparsity` on one device may be relied on, other than what follows from the above.
Results may differ from the reference program's by a relative error of at most 0.0081.
Values may be sent and summed in bfloat16 or wider, within the bound.
No kernel may reach another device: no remote copies, remote signals or barrier semaphores. Data moves between devices by JAX's collectives and lax.ppermute only.
A program may use at most 64 MiB of HBM per device.

```python
import jax
import jax.numpy as jnp
from jax import lax

DEGREES = 2048
LATS = 2048
FIELDS = 32
RANK = 64
ORDERS = 128
LEVELS = 3
STRIDE = 16
COLS = 64
LAT_DEV = 256
DEG_DEV = 256
N_LAT = 8


def with_ends(values, key, smallest, top_value):
    spot = [jax.random.randint(jax.random.fold_in(key, axis), (), 0, length) for axis, length in enumerate(values.shape)]
    widest = values.shape.index(max(values.shape))
    neighbour = spot[:widest] + [(spot[widest] + 1) % values.shape[widest]] + spot[widest + 1:]
    return values.at[tuple(spot)].set(smallest).at[tuple(neighbour)].set(top_value)


def block_scale(own_key, dims, pieces, smallest, largest):
    def one(position, parts):
        steps = jax.random.uniform(jax.random.fold_in(jax.random.fold_in(own_key, 6), position), (parts,), jnp.float32, smallest / len(pieces), largest / len(pieces))
        return jnp.repeat(jnp.exp(steps), dims[position] // parts).reshape((-1,) + (1,) * (len(dims) - position - 1))

    gain = one(*pieces[0])
    for cut in pieces[1:]:
        gain = gain * one(*cut)
    return gain


def centred(own_key, extent, spread, limit, cuts=(), held_as=jnp.bfloat16):
    result = spread * jax.random.normal(own_key, extent, jnp.float32)
    if cuts:
        result = result * block_scale(own_key, extent, cuts, -0.22, 0.18)
    return jnp.clip(result, -limit, limit).astype(held_as)


def setup_inputs(seed: int = 0) -> dict:
    streams_of = jax.random.split(jax.random.key(seed), 8)
    fourier = centred(streams_of[0], (ORDERS, COLS, LATS), 1.0, 6.0, ((0, 4), (2, 8)))
    quad_weights = jnp.clip(0.5 + 1.0 * jax.random.uniform(streams_of[1], (LATS,), jnp.float32) ** block_scale(streams_of[1], (LATS,), ((0, 8),), -0.2, 0.2), 0.5, 1.5)
    leaf_basis = centred(streams_of[2], (ORDERS, RANK, LATS), (LATS // N_LAT) ** -0.5, 0.375, ((0, 4), (2, 8)))
    level_factors = centred(streams_of[3], (ORDERS, LEVELS, 2, N_LAT, RANK, RANK), (2 * RANK) ** -0.5, 0.5, ((0, 4), (3, 8)))
    sparsity = with_ends((jax.random.randint(streams_of[4], (ORDERS, LEVELS, N_LAT), 0, 4) < 3).astype(jnp.int32), jax.random.fold_in(streams_of[4], 1), 0, 1)
    root_basis = centred(streams_of[5], (ORDERS, RANK, DEGREES), RANK ** -0.5, 0.75, ((2, 8),))
    order_of_slot = jax.random.permutation(streams_of[6], ORDERS).astype(jnp.int32)
    return dict(fourier=fourier, quad_weights=quad_weights, leaf_basis=leaf_basis, level_factors=level_factors, sparsity=sparsity, root_basis=root_basis, order_of_slot=order_of_slot)


def reference(fourier, quad_weights, leaf_basis, level_factors, sparsity, root_basis, order_of_slot):
    blocks = jnp.arange(N_LAT, dtype=jnp.int32)

    def one_order(order_items):
        fourier_one, basis_one, factor_one, mask_one, root_one = order_items
        weighted = (fourier_one.astype(jnp.float32) * quad_weights[None, :]).astype(jnp.bfloat16)
        weighted = weighted.reshape(COLS, N_LAT, LAT_DEV).astype(jnp.float32)
        basis_blocks = basis_one.reshape(RANK, N_LAT, LAT_DEV).astype(jnp.float32)
        rank_state = jnp.einsum("rbj,cbj->brc", basis_blocks, weighted).astype(jnp.bfloat16)
        for depth_bit in range(LEVELS):
            partner = jnp.take(rank_state, blocks ^ (1 << depth_bit), axis=0)
            own_term = jnp.einsum("bst,btc->bsc", factor_one[depth_bit, 0].astype(jnp.float32), rank_state.astype(jnp.float32))
            cross_term = jnp.einsum("bst,btc->bsc", factor_one[depth_bit, 1].astype(jnp.float32), partner.astype(jnp.float32))
            present = mask_one[depth_bit].astype(jnp.float32)[:, None, None]
            rank_state = (own_term + present * cross_term).astype(jnp.bfloat16)
        root_blocks = root_one.reshape(RANK, N_LAT, DEG_DEV).astype(jnp.float32)
        coefficient = jnp.einsum("rbl,brc->blc", root_blocks, rank_state.astype(jnp.float32)).astype(jnp.bfloat16)
        return coefficient.reshape(DEGREES, COLS)

    coeffs = lax.map(one_order, (fourier, leaf_basis, level_factors, sparsity, root_basis))
    natural = jnp.zeros_like(coeffs).at[order_of_slot].set(coeffs)
    degree = jnp.arange(DEGREES, dtype=jnp.int32)
    window = STRIDE * jnp.arange(ORDERS, dtype=jnp.int32)
    alive_mask = degree[None, :, None] >= window[:, None, None]
    masked = jnp.where(alive_mask, natural, jnp.zeros((), natural.dtype))
    return masked.reshape(ORDERS, DEGREES, FIELDS, 2).transpose(2, 3, 1, 0)
```

```python
import functools

import jax
import jax.numpy as jnp
from jax import lax
from jax.experimental import pallas as pl
from jax.experimental.pallas import tpu as pltpu
from jax.sharding import PartitionSpec as P

DEGREES = 2048
F32, BF16 = jnp.float32, jnp.bfloat16
MIB = 1 << 20


def contract(lhs, rhs, dims):
    return lax.dot_general(lhs, rhs, (dims, ((), ())), preferred_element_type=F32)


def lane_half(shape, rank):
    return lax.broadcasted_iota(jnp.int32, shape, len(shape) - 1) < rank


def leaf_kernel(fourier_ref, weight_ref, leaf_ref, state_ref):
    slots, columns, lats = fourier_ref.shape
    rank = leaf_ref.shape[1]
    weight = weight_ref[...]
    for pair in range(slots // 2):
        both = pl.ds(2 * pair, 2)
        weighted = (fourier_ref[both].astype(F32) * weight[None]).astype(BF16)
        product = contract(
            weighted.reshape(2 * columns, lats), leaf_ref[both].reshape(2 * rank, lats), ((1,), (1,))
        )
        mine = lane_half((columns, 2 * rank), rank)
        state_ref[pair] = jnp.where(mine, product[:columns], product[columns:]).astype(BF16)


def factor_kernel(factor_ref, present_ref, weight_ref):
    slots, _, rank, _ = factor_ref.shape
    empty = jnp.zeros((rank, rank), BF16)
    for pair in range(slots // 2):
        for half in range(2):
            first, second = factor_ref[2 * pair, half], factor_ref[2 * pair + 1, half]
            if half:
                first = (first.astype(F32) * present_ref[2 * pair].astype(F32)).astype(BF16)
                second = (second.astype(F32) * present_ref[2 * pair + 1].astype(F32)).astype(BF16)
            lanes = pl.ds(half * 2 * rank, 2 * rank)
            weight_ref[pair, :rank, lanes] = jnp.concatenate([first, empty], axis=1)
            weight_ref[pair, rank:, lanes] = jnp.concatenate([empty, second], axis=1)


def level_kernel(state_ref, partner_ref, weight_ref, out_ref):
    pairs = state_ref.shape[0]
    for pair in range(pairs):
        both = jnp.concatenate([state_ref[pair], partner_ref[pair]], axis=1)
        result = contract(both, weight_ref[pair], ((1,), (1,))).astype(BF16)
        if len(out_ref.shape) == 3:
            out_ref[pair] = result
        else:
            group = out_ref.shape[2]
            for owner in range(out_ref.shape[0]):
                out_ref[owner, pair] = result[owner * group : (owner + 1) * group]


def root_kernel(group, degree_first, state_ref, root_ref, order_ref, out_ref, rows_ref):
    owner = pl.program_id(0)
    columns = out_ref.shape[0] * 2
    rank, degrees = root_ref.shape[1:]
    slots = order_ref.shape[1]
    group_rows = group * columns
    steps = state_ref.shape[1] // group_rows
    shape = (group_rows, 2 * rank)
    row_pair = lax.broadcasted_iota(jnp.int32, shape, 0) // columns
    row_half = lax.broadcasted_iota(jnp.int32, shape, 1) // rank
    for step in range(steps):
        state = state_ref[0, step * group_rows : (step + 1) * group_rows]
        parts = []
        for half in range(2):
            parts.append(
                jnp.concatenate(
                    [
                        jnp.where((row_pair == pair) & (row_half == half), state, jnp.zeros((), BF16))
                        for pair in range(group)
                    ],
                    axis=1,
                )
            )
        left = jnp.concatenate(parts, axis=0)
        right = root_ref[pl.ds(step * group * 2, group * 2)].reshape(group * 2 * rank, degrees)
        begin = pl.multiple_of((owner * steps + step) * 2 * group_rows, 2 * group_rows)
        product = contract(left, right, ((1,), (0,)))
        for tile in range(degrees // 128):
            rows_ref[tile, pl.ds(begin, 2 * group_rows), :] = product[:, tile * 128 : (tile + 1) * 128]

    @pl.when(owner == pl.num_programs(0) - 1)
    def _():
        window = lax.broadcasted_iota(jnp.int32, (slots, slots), 0)
        place = (window == order_ref[...]).astype(F32).astype(BF16)
        degree = degree_first() + lax.broadcasted_iota(jnp.int32, (degrees, slots), 0)
        alive = degree >= DEGREES // slots * lax.broadcasted_iota(jnp.int32, (degrees, slots), 1)
        for column in range(columns):
            for tile in range(degrees // 128):
                span = slice(tile * 128, (tile + 1) * 128)
                one = rows_ref[tile, pl.ds(column, slots, stride=columns), :].astype(BF16)
                natural = contract(one.T, place, ((1,), (1,)))
                out_ref[column // 2, column % 2, span] = jnp.where(alive[span], natural, 0.0).astype(BF16)


def params(mib):
    return pltpu.CompilerParams(vmem_limit_bytes=mib * MIB)


def cost(flops, size):
    return pl.CostEstimate(flops=flops, bytes_accessed=size, transcendentals=0)


def leaf_states(fourier, quad_weights, leaf_basis):
    slots, columns, lats = fourier.shape
    rank = leaf_basis.shape[1]
    steps = 4
    return pl.pallas_call(
        leaf_kernel,
        grid=(steps,),
        in_specs=[
            pl.BlockSpec((slots // steps, columns, lats), lambda i: (i, 0, 0)),
            pl.BlockSpec((1, lats), lambda i: (0, 0)),
            pl.BlockSpec((slots // steps, rank, lats), lambda i: (i, 0, 0)),
        ],
        out_specs=pl.BlockSpec((slots // steps // 2, columns, 2 * rank), lambda i: (i, 0, 0)),
        out_shape=jax.ShapeDtypeStruct((slots // 2, columns, 2 * rank), BF16),
        compiler_params=params(16),
        cost_estimate=cost(2 * slots * columns * rank * lats, 4 * slots * columns * lats),
        name="leaf",
    )(fourier, quad_weights.reshape(1, lats), leaf_basis)


def level_weights(level_factors, sparsity, level):
    slots, _, _, _, rank, _ = level_factors.shape
    present = sparsity[:, level, 0]
    return pl.pallas_call(
        factor_kernel,
        grid=(1,),
        in_specs=[
            pl.BlockSpec((slots, None, 2, None, rank, rank), lambda i: (0, level, 0, 0, 0, 0)),
            pl.BlockSpec(memory_space=pltpu.SMEM),
        ],
        out_specs=pl.BlockSpec((slots // 2, 2 * rank, 4 * rank), lambda i: (0, 0, 0)),
        out_shape=jax.ShapeDtypeStruct((slots // 2, 2 * rank, 4 * rank), BF16),
        compiler_params=params(16),
        cost_estimate=cost(slots * rank * rank * 4, slots * rank * rank * 16),
        name=f"factors{level}",
    )(level_factors, present)


def next_states(state, partner, weights, owners):
    pairs, columns, lanes = state.shape
    shape = (pairs, columns, lanes)
    if owners:
        shape = (owners, pairs, columns // owners, lanes)
    return pl.pallas_call(
        level_kernel,
        out_shape=jax.ShapeDtypeStruct(shape, BF16),
        compiler_params=params(16),
        cost_estimate=cost(4 * pairs * columns * lanes * lanes, 6 * pairs * columns * lanes),
        name="level",
    )(state, partner, weights)


def spectra_of(states, root_basis, order_rows, group):
    owners, state_rows, lanes = states.shape
    slots, rank, degrees = root_basis.shape
    here = slots // owners
    columns = state_rows * 2 // here
    degree_first = lambda: lax.axis_index("lat") * degrees
    return pl.pallas_call(
        functools.partial(root_kernel, group, degree_first),
        grid=(owners,),
        in_specs=[
            pl.BlockSpec((1, state_rows, lanes), lambda i: (i, 0, 0)),
            pl.BlockSpec((here, rank, degrees), lambda i: (i, 0, 0)),
            pl.BlockSpec((1, slots), lambda i: (0, 0)),
        ],
        out_specs=pl.BlockSpec((columns // 2, 2, degrees, slots), lambda i: (0, 0, 0, 0)),
        out_shape=jax.ShapeDtypeStruct((columns // 2, 2, degrees, slots), BF16),
        scratch_shapes=[pltpu.VMEM((degrees // 128, slots * columns, 128), F32)],
        compiler_params=params(32),
        cost_estimate=cost(2 * slots * rank * degrees * columns, 2 * slots * rank * degrees),
        name="root",
    )(states, root_basis, order_rows)


def per_device(
    fourier, quad_weights, leaf_basis, level_factors, sparsity, root_basis, order_of_slot
):
    slots, columns, _ = fourier.shape
    owners = lax.axis_size("order")
    own_columns = columns // owners
    levels = level_factors.shape[1]
    blocks = lax.axis_size("lat")
    state = leaf_states(fourier, quad_weights, leaf_basis)
    for level in range(levels):
        partner = lax.ppermute(state, "lat", [(i, i ^ 1 << level) for i in range(blocks)])
        weights = level_weights(level_factors, sparsity, level)
        by_owner = level == levels - 1 and own_columns % 16 == 0
        state = next_states(state, partner, weights, owners if by_owner else 0)
    pairs, lanes = slots // 2, state.shape[-1]
    if state.ndim == 3:
        state = state.reshape(pairs, owners, own_columns, lanes).transpose(1, 0, 2, 3)
    sent = state.reshape(owners, pairs * own_columns, lanes)
    arrived = lax.all_to_all(sent, "order", split_axis=0, concat_axis=0, tiled=True)
    group = max(2, 16 // own_columns)
    order_rows = order_of_slot.reshape(owners, pairs // group, group, 2).transpose(0, 1, 3, 2).reshape(1, -1)
    return spectra_of(arrived, root_basis, order_rows, group)


def solution(mesh):
    return jax.shard_map(
        per_device,
        mesh=mesh,
        in_specs=(
            P("order", None, "lat"),
            P("lat"),
            P("order", None, "lat"),
            P("order", None, None, "lat", None, None),
            P("order", None, "lat"),
            P(None, None, "lat"),
            P(),
        ),
        out_specs=P("order", None, "lat", None),
        check_vma=False,
    )
```

```python
import functools

import jax
import jax.numpy as jnp
from jax import lax
from jax.experimental import pallas as pl
from jax.experimental.pallas import tpu as pltpu
from jax.sharding import PartitionSpec as P

DEGREES = 2048
CHUNKS = 2
F32, BF16 = jnp.float32, jnp.bfloat16
MIB = 1 << 20
IN_HBM = pl.BlockSpec(memory_space=pltpu.HBM)
IN_SMEM = pl.BlockSpec(memory_space=pltpu.SMEM)


def contract(lhs, rhs, dims):
    return lax.dot_general(lhs, rhs, (dims, ((), ())), preferred_element_type=F32)


def call(kernel, name, out_shape, in_specs, flops, size, scratch=(), mib=16):
    return pl.pallas_call(
        kernel,
        out_shape=out_shape,
        in_specs=in_specs,
        scratch_shapes=list(scratch),
        compiler_params=pltpu.CompilerParams(vmem_limit_bytes=mib * MIB),
        cost_estimate=pl.CostEstimate(flops=flops, bytes_accessed=size, transcendentals=0),
        name=name,
    )


def whole_blocks(count):
    return [pl.BlockSpec()] * count


def leaf_kernel(first, pieces, fourier_hbm, weight_hbm, leaf_hbm, state_ref, fourier_ref, weight_ref, leaf_ref, sems):
    slots, columns, lats = fourier_ref.shape
    rank = leaf_ref.shape[1]
    per = slots // pieces
    copies = [pltpu.make_async_copy(weight_hbm, weight_ref, sems.at[0])]
    for piece in range(pieces):
        here, there = pl.ds(piece * per, per), pl.ds(first + piece * per, per)
        copies.append(pltpu.make_async_copy(fourier_hbm.at[there], fourier_ref.at[here], sems.at[1 + 2 * piece]))
        copies.append(pltpu.make_async_copy(leaf_hbm.at[there], leaf_ref.at[here], sems.at[2 + 2 * piece]))
    for copy in copies:
        copy.start()
    copies[0].wait()
    weight = weight_ref[...]
    mine = lax.broadcasted_iota(jnp.int32, (columns, 2 * rank), 1) < rank
    for pair in range(slots // 2):
        if 2 * pair % per == 0:
            copies[1 + 2 * (2 * pair // per)].wait()
            copies[2 + 2 * (2 * pair // per)].wait()
        both = pl.ds(2 * pair, 2)
        weighted = (fourier_ref[both].astype(F32) * weight[None]).astype(BF16)
        product = contract(
            weighted.reshape(2 * columns, lats), leaf_ref[both].reshape(2 * rank, lats), ((1,), (1,))
        )
        state_ref[pair] = jnp.where(mine, product[:columns], product[columns:]).astype(BF16)


def leaf_states(fourier, quad_weights, leaf_basis, first, slots):
    _, columns, lats = fourier.shape
    rank = leaf_basis.shape[1]
    pieces = 2
    return call(
        functools.partial(leaf_kernel, first, pieces),
        "leaf",
        jax.ShapeDtypeStruct((slots // 2, columns, 2 * rank), BF16),
        [IN_HBM] * 3,
        2 * slots * columns * rank * lats,
        4 * slots * columns * lats,
        [
            pltpu.VMEM((slots, columns, lats), BF16),
            pltpu.VMEM((1, lats), F32),
            pltpu.VMEM((slots, rank, lats), BF16),
            pltpu.SemaphoreType.DMA((1 + 2 * pieces,)),
        ],
    )(fourier, quad_weights.reshape(1, lats), leaf_basis)


def factor_kernel(level, first, factor_hbm, present_ref, weight_ref, factor_ref, sem):
    slots, _, rank, _ = factor_ref.shape
    copy = pltpu.make_async_copy(factor_hbm.at[pl.ds(first, slots), level, :, 0], factor_ref, sem)
    copy.start()
    copy.wait()
    empty = jnp.zeros((rank, rank), BF16)
    for pair in range(slots // 2):
        for half in range(2):
            blocks = []
            for slot in (2 * pair, 2 * pair + 1):
                block = factor_ref[slot, half]
                if half:
                    block = (block.astype(F32) * present_ref[level, first + slot].astype(F32)).astype(BF16)
                blocks.append(block)
            lanes = pl.ds(half * 2 * rank, 2 * rank)
            weight_ref[pair, :rank, lanes] = jnp.concatenate([blocks[0], empty], axis=1)
            weight_ref[pair, rank:, lanes] = jnp.concatenate([empty, blocks[1]], axis=1)


def level_weights(level_factors, present, level, first, slots):
    rank = level_factors.shape[-1]
    return call(
        functools.partial(factor_kernel, level, first),
        f"factors{level}",
        jax.ShapeDtypeStruct((slots // 2, 2 * rank, 4 * rank), BF16),
        [IN_HBM, IN_SMEM],
        slots * rank * rank * 4,
        slots * rank * rank * 16,
        [pltpu.VMEM((slots, 2, rank, rank), BF16), pltpu.SemaphoreType.DMA],
    )(level_factors, present)


def level_of(pair, state_ref, partner_ref, weight_ref):
    both = jnp.concatenate([state_ref[pair], partner_ref[pair]], axis=1)
    return contract(both, weight_ref[pair], ((1,), (1,))).astype(BF16)


def level_kernel(state_ref, partner_ref, weight_ref, out_ref):
    for pair in range(state_ref.shape[0]):
        out_ref[pair] = level_of(pair, state_ref, partner_ref, weight_ref)


def last_level_kernel(axis, state_ref, partner_ref, weight_ref, *refs):
    out_refs, groups_ref = refs[:-1], refs[-1]
    me = lax.axis_index(axis)
    group = groups_ref.shape[2]
    for pair in range(state_ref.shape[0]):
        result = level_of(pair, state_ref, partner_ref, weight_ref)
        for owner in range(len(out_refs)):
            groups_ref[pair, owner] = result[owner * group : (owner + 1) * group]
    for k, out_ref in enumerate(out_refs):
        owner = me ^ k
        for pair in range(state_ref.shape[0]):
            out_ref[pl.ds(pair * group, group)] = groups_ref[pair, owner]


def next_states(state, partner, weights):
    pairs, columns, lanes = state.shape
    return call(
        level_kernel,
        "level",
        jax.ShapeDtypeStruct(state.shape, BF16),
        whole_blocks(3),
        4 * pairs * columns * lanes * lanes,
        6 * pairs * columns * lanes,
    )(state, partner, weights)


def last_states(state, partner, weights, owners):
    pairs, columns, lanes = state.shape
    group = columns // owners
    if group % 16:
        state = next_states(state, partner, weights)
        me = lax.axis_index("order")
        parts = [lax.dynamic_slice_in_dim(state, (me ^ k) * group, group, 1) for k in range(owners)]
        return [part.reshape(pairs * group, lanes) for part in parts]
    return call(
        functools.partial(last_level_kernel, "order"),
        "last_level",
        [jax.ShapeDtypeStruct((pairs * group, lanes), BF16)] * owners,
        whole_blocks(3),
        4 * pairs * columns * lanes * lanes,
        6 * pairs * columns * lanes,
        [pltpu.VMEM((pairs, owners, group, lanes), BF16)],
    )(state, partner, weights)


def near_kernel(here, group, root_hbm, order_ref, root_ref, place_ref, rows_ref, sems):
    chunks, owners, size = root_ref.shape[:3]
    slots = rows_ref.shape[1]
    me = lax.axis_index("order")
    copies = []
    for chunk in range(chunks):
        for k in range(owners):
            first = (me ^ k) * here + chunk * size
            copies.append(
                pltpu.make_async_copy(
                    root_hbm.at[pl.ds(first, size)], root_ref.at[chunk, k], sems.at[chunk * owners + k]
                )
            )
            copies[-1].start()
    lane = lax.broadcasted_iota(jnp.int32, (1, slots), 1)
    for chunk in range(chunks):
        for k in range(owners):
            first = (me ^ k) * here + chunk * size
            for slot in range(size):
                pair, half = slot // 2, slot % 2
                row = k * size + (pair // group * 2 + half) * group + pair % group
                rows_ref[pl.ds(row, 1), :] = (lane == order_ref[first + slot]).astype(F32)
        place_ref[chunk] = rows_ref[...].astype(BF16)
    for copy in copies:
        copy.wait()


def near_roots(root_basis, order_of_slot, owners, group):
    slots, rank, degrees = root_basis.shape
    here = slots // owners
    size = here // CHUNKS
    return call(
        functools.partial(near_kernel, here, group),
        "near_roots",
        [
            jax.ShapeDtypeStruct((CHUNKS, owners, size, rank, degrees), BF16),
            jax.ShapeDtypeStruct((CHUNKS, owners * size, slots), BF16),
        ],
        [IN_HBM, IN_SMEM],
        slots * slots,
        4 * slots * rank * degrees,
        [pltpu.VMEM((owners * size, slots), F32), pltpu.SemaphoreType.DMA((CHUNKS * owners,))],
    )(root_basis, order_of_slot)


def root_kernel(group, chunk, *refs):
    owners = len(refs) - (5 if chunk else 4)
    state_refs, root_ref, place_ref = refs[:owners], refs[owners], refs[owners + 1]
    out_ref, rows_ref = refs[-2:]
    fields, parts, degrees, slots = out_ref.shape
    columns = fields * parts
    rank = root_ref.shape[3]
    group_rows = group * columns
    steps = state_refs[0].shape[0] // group_rows
    shape = (group_rows, 2 * rank)
    row_pair = lax.broadcasted_iota(jnp.int32, shape, 0) // columns
    row_half = lax.broadcasted_iota(jnp.int32, shape, 1) // rank
    masks = [[(row_pair == pair) & (row_half == half) for pair in range(group)] for half in range(2)]
    empty = jnp.zeros(shape, BF16)
    for k in range(owners):
        for step in range(steps):
            state = state_refs[k][pl.ds(step * group_rows, group_rows)]
            left = jnp.concatenate(
                [jnp.concatenate([jnp.where(m, state, empty) for m in line], axis=1) for line in masks], axis=0
            )
            right = root_ref[chunk, k, pl.ds(step * group * 2, group * 2)].reshape(group * 2 * rank, degrees)
            product = contract(left, right, ((1,), (0,)))
            begin = (k * steps + step) * 2 * group_rows
            for tile in range(degrees // 128):
                rows_ref[tile, pl.ds(begin, 2 * group_rows), :] = product[:, tile * 128 : (tile + 1) * 128]
    place = place_ref[chunk]
    last = chunk == CHUNKS - 1
    if last:
        degree = lax.axis_index("lat") * degrees + lax.broadcasted_iota(jnp.int32, (degrees, slots), 0)
        alive = degree >= DEGREES // slots * lax.broadcasted_iota(jnp.int32, (degrees, slots), 1)
    for column in range(columns):
        for tile in range(degrees // 128):
            span = slice(tile * 128, (tile + 1) * 128)
            one = rows_ref[tile, pl.ds(column, place.shape[0], stride=columns), :].astype(BF16)
            natural = contract(one.T, place, ((1,), (0,)))
            where = (column // 2, column % 2, span)
            if chunk:
                natural = natural + refs[owners + 2][where].astype(F32)
            if last:
                natural = jnp.where(alive[span], natural, 0.0)
            out_ref[where] = natural.astype(BF16)


def spectra_of(states, roots, places, so_far, chunk, group):
    owners = len(states)
    state_rows, lanes = states[0].shape
    _, _, size, rank, degrees = roots.shape
    slots = places.shape[2]
    columns = state_rows * 2 // size
    inputs = [*states, roots, places] + ([so_far] if chunk else [])
    return call(
        functools.partial(root_kernel, group, chunk),
        "root",
        jax.ShapeDtypeStruct((columns // 2, 2, degrees, slots), BF16),
        whole_blocks(len(inputs)),
        2 * slots * rank * degrees * columns,
        2 * slots * rank * degrees,
        [pltpu.VMEM((degrees // 128, owners * size * columns, 128), F32)],
        mib=24,
    )(*inputs)


def per_device(
    fourier, quad_weights, leaf_basis, level_factors, sparsity, root_basis, order_of_slot
):
    slots, columns, _ = fourier.shape
    owners = lax.axis_size("order")
    blocks = lax.axis_size("lat")
    levels = level_factors.shape[1]
    group = max(2, 16 * owners // columns)
    size = slots // CHUNKS
    present = sparsity[:, :, 0].T

    def swap(array, axis, bits):
        return lax.ppermute(array, axis, [(i, i ^ bits) for i in range(lax.axis_size(axis))])

    states = [leaf_states(fourier, quad_weights, leaf_basis, c * size, size) for c in range(CHUNKS)]
    for level in range(levels):
        for c in range(CHUNKS):
            partner = swap(states[c], "lat", 1 << level)
            weights = level_weights(level_factors, present, level, c * size, size)
            if level < levels - 1:
                states[c] = next_states(states[c], partner, weights)
            else:
                states[c] = last_states(states[c], partner, weights, owners)
    roots, places = near_roots(root_basis, order_of_slot, owners, group)
    spectra = None
    for c in range(CHUNKS):
        arrived = [swap(part, "order", k) if k else part for k, part in enumerate(states[c])]
        spectra = spectra_of(arrived, roots, places, spectra, c, group)
    return spectra


def solution(mesh):
    return jax.shard_map(
        per_device,
        mesh=mesh,
        in_specs=(
            P("order", None, "lat"),
            P("lat"),
            P("order", None, "lat"),
            P("order", None, None, "lat", None, None),
            P("order", None, "lat"),
            P(None, None, "lat"),
            P(),
        ),
        out_specs=P("order", None, "lat", None),
        check_vma=False,
    )
```

```python
import functools

import jax
import jax.numpy as jnp
from jax import lax
from jax.experimental import pallas as pl
from jax.experimental.pallas import tpu as pltpu
from jax.sharding import PartitionSpec as P

DEGREES = 2048
CHUNKS = 2
F32, BF16 = jnp.float32, jnp.bfloat16
MIB = 1 << 20
IN_HBM = pl.BlockSpec(memory_space=pltpu.HBM)
IN_SMEM = pl.BlockSpec(memory_space=pltpu.SMEM)
ANYWHERE = pl.BlockSpec(memory_space=pl.ANY)


def contract(lhs, rhs, dims):
    return lax.dot_general(lhs, rhs, (dims, ((), ())), preferred_element_type=F32)


def in_hbm(array):
    return pltpu.with_memory_space_constraint(array, pltpu.HBM)


def call(kernel, name, out_shape, in_specs, flops, size, scratch=(), mib=16, **more):
    return pl.pallas_call(
        kernel,
        out_shape=out_shape,
        in_specs=in_specs,
        scratch_shapes=list(scratch),
        compiler_params=pltpu.CompilerParams(vmem_limit_bytes=mib * MIB),
        cost_estimate=pl.CostEstimate(flops=flops // 1000, bytes_accessed=size // 1000, transcendentals=0),
        name=name,
        **more,
    )


def whole_blocks(count):
    return [pl.BlockSpec()] * count


def leaf_kernel(pieces, fourier_hbm, weight_hbm, leaf_hbm, state_ref, fourier_ref, weight_ref, leaf_ref, sems):
    slots, columns, lats = fourier_ref.shape
    rank = leaf_ref.shape[1]
    per = slots // pieces
    copies = [pltpu.make_async_copy(weight_hbm, weight_ref, sems.at[0])]
    for piece in range(pieces):
        part = pl.ds(piece * per, per)
        copies.append(pltpu.make_async_copy(fourier_hbm.at[part], fourier_ref.at[part], sems.at[1 + 2 * piece]))
        copies.append(pltpu.make_async_copy(leaf_hbm.at[part], leaf_ref.at[part], sems.at[2 + 2 * piece]))
    for copy in copies:
        copy.start()
    copies[0].wait()
    weight = weight_ref[...]
    mine = lax.broadcasted_iota(jnp.int32, (columns, 2 * rank), 1) < rank
    for pair in range(slots // 2):
        if 2 * pair % per == 0:
            copies[1 + 2 * (2 * pair // per)].wait()
            copies[2 + 2 * (2 * pair // per)].wait()
        both = pl.ds(2 * pair, 2)
        weighted = (fourier_ref[both].astype(F32) * weight[None]).astype(BF16)
        product = contract(
            weighted.reshape(2 * columns, lats), leaf_ref[both].reshape(2 * rank, lats), ((1,), (1,))
        )
        state_ref[pair] = jnp.where(mine, product[:columns], product[columns:]).astype(BF16)


def leaf_states(fourier, quad_weights, leaf_basis):
    slots, columns, lats = fourier.shape
    rank = leaf_basis.shape[1]
    pieces = 4
    return call(
        functools.partial(leaf_kernel, pieces),
        "leaf",
        jax.ShapeDtypeStruct((slots // 2, columns, 2 * rank), BF16),
        [IN_HBM] * 3,
        2 * slots * columns * rank * lats,
        4 * slots * columns * lats,
        [
            pltpu.VMEM((slots, columns, lats), BF16),
            pltpu.VMEM((1, lats), F32),
            pltpu.VMEM((slots, rank, lats), BF16),
            pltpu.SemaphoreType.DMA((1 + 2 * pieces,)),
        ],
    )(fourier, quad_weights, leaf_basis)


def factor_kernel(levels, factor_hbm, present_ref, after, *refs):
    del after
    weight_refs, (factor_ref, sems) = refs[: len(levels)], refs[len(levels) :]
    _, slots, _, rank, _ = factor_ref.shape
    copies = [
        pltpu.make_async_copy(factor_hbm.at[:, level, :, 0], factor_ref.at[i], sems.at[i])
        for i, level in enumerate(levels)
    ]
    for copy in copies:
        copy.start()
    empty = jnp.zeros((rank, rank), BF16)
    for i, level in enumerate(levels):
        copies[i].wait()
        for pair in range(slots // 2):
            for half in range(2):
                blocks = []
                for slot in (2 * pair, 2 * pair + 1):
                    block = factor_ref[i, slot, half]
                    if half:
                        block = (block.astype(F32) * present_ref[level, slot].astype(F32)).astype(BF16)
                    blocks.append(block)
                lanes = pl.ds(half * 2 * rank, 2 * rank)
                weight_refs[i][pair, :rank, lanes] = jnp.concatenate([blocks[0], empty], axis=1)
                weight_refs[i][pair, rank:, lanes] = jnp.concatenate([empty, blocks[1]], axis=1)


def level_weights(level_factors, present, levels, after):
    slots, _, _, _, rank, _ = level_factors.shape
    count = len(levels)
    return call(
        functools.partial(factor_kernel, levels),
        "factors",
        [jax.ShapeDtypeStruct((slots // 2, 2 * rank, 4 * rank), BF16)] * count,
        [IN_HBM, IN_SMEM, ANYWHERE],
        slots * rank * rank * 4 * count,
        slots * rank * rank * 16 * count,
        [pltpu.VMEM((count, slots, 2, rank, rank), BF16), pltpu.SemaphoreType.DMA((count,))],
        mib=24,
    )(level_factors, present, after)


def level_of(state, partner, weight):
    return contract(jnp.concatenate([state, partner], axis=1), weight, ((1,), (1,))).astype(BF16)


def level_kernel(first, first_weight, state_ref, partner_ref, weight_ref, out_ref):
    for pair in range(out_ref.shape[0]):
        out_ref[pair] = level_of(
            state_ref[first + pair], partner_ref[first + pair], weight_ref[first_weight + pair]
        )


def last_level_kernel(chunks, axis, after, *refs):
    del after
    state_refs, partner_refs, weight_ref = refs[:chunks], refs[chunks : 2 * chunks], refs[2 * chunks]
    out_refs, groups_ref = refs[2 * chunks + 1 : -1], refs[-1]
    me = lax.axis_index(axis)
    pairs, owners, group, _ = groups_ref.shape
    pair = 0
    for state_ref, partner_ref in zip(state_refs, partner_refs):
        for i in range(state_ref.shape[0]):
            result = level_of(state_ref[i], partner_ref[i], weight_ref[pair])
            for owner in range(owners):
                groups_ref[pair, owner] = result[owner * group : (owner + 1) * group]
            pair += 1
    for k, out_ref in enumerate(out_refs):
        for pair in range(pairs):
            out_ref[pl.ds(pair * group, group)] = groups_ref[pair, me ^ k]


def next_states(state, partner, weights, first, first_weight, pairs):
    _, columns, lanes = state.shape
    return call(
        functools.partial(level_kernel, first, first_weight),
        "level",
        jax.ShapeDtypeStruct((pairs, columns, lanes), BF16),
        whole_blocks(3),
        4 * pairs * columns * lanes * lanes,
        6 * pairs * columns * lanes,
    )(state, partner, weights)


def last_states(states, partners, weights, owners, after):
    _, columns, lanes = states[0].shape
    pairs = sum(state.shape[0] for state in states)
    group = columns // owners
    if group % 16:
        state = jnp.concatenate(states)
        state = next_states(state, jnp.concatenate(partners), weights, 0, 0, pairs)
        me = lax.axis_index("order")
        parts = [lax.dynamic_slice_in_dim(state, (me ^ k) * group, group, 1) for k in range(owners)]
        return [part.reshape(pairs * group, lanes) for part in parts]
    return call(
        functools.partial(last_level_kernel, len(states), "order"),
        "last_level",
        [jax.ShapeDtypeStruct((pairs * group, lanes), BF16)] * owners,
        [ANYWHERE] + whole_blocks(2 * len(states) + 1),
        4 * pairs * columns * lanes * lanes,
        6 * pairs * columns * lanes,
        [pltpu.VMEM((pairs, owners, group, lanes), BF16)],
    )(after, *states, *partners, weights)


def near_kernel(group, root_hbm, order_ref, after, root_ref, place_ref, alive_ref, rows_ref, sems):
    del after
    owners, here, _, degrees = root_ref.shape
    slots = rows_ref.shape[1]
    me = lax.axis_index("order")
    copies = []
    for k in range(owners):
        copies.append(pltpu.make_async_copy(root_hbm.at[pl.ds((me ^ k) * here, here)], root_ref.at[k], sems.at[k]))
        copies[-1].start()
    lane = lax.broadcasted_iota(jnp.int32, (1, slots), 1)
    for k in range(owners):
        for slot in range(here):
            pair, half = slot // 2, slot % 2
            row = (pair // group * 2 + half) * group + pair % group
            rows_ref[pl.ds(row, 1), :] = (lane == order_ref[(me ^ k) * here + slot]).astype(F32)
        place_ref[k] = rows_ref[...].astype(BF16)
    degree = lax.axis_index("lat") * degrees + lax.broadcasted_iota(jnp.int32, (degrees, slots), 0)
    window = DEGREES // slots * lax.broadcasted_iota(jnp.int32, (degrees, slots), 1)
    alive_ref[...] = (degree >= window).astype(F32).astype(BF16)
    for copy in copies:
        copy.wait()


def near_roots(root_basis, order_of_slot, owners, group, after):
    slots, rank, degrees = root_basis.shape
    here = slots // owners
    return call(
        functools.partial(near_kernel, group),
        "near_roots",
        [
            jax.ShapeDtypeStruct((owners, here, rank, degrees), BF16),
            jax.ShapeDtypeStruct((owners, here, slots), BF16),
            jax.ShapeDtypeStruct((degrees, slots), BF16),
        ],
        [IN_HBM, IN_SMEM, ANYWHERE],
        slots * slots,
        4 * slots * rank * degrees,
        [pltpu.VMEM((here, slots), F32), pltpu.SemaphoreType.DMA((owners,))],
    )(root_basis, order_of_slot, after)


def root_kernel(group, first, last, *refs):
    refs = list(refs)
    so_far_ref = refs.pop(0) if last else None
    root_ref, place_ref, alive_ref = refs[:3]
    count = len(refs) - (7 if last else 5)
    state_refs = refs[3 : 3 + count]
    out_ref, rows_ref = refs[3 + count : 5 + count]
    natural_ref = refs[5 + count] if last else out_ref
    fields, parts, degrees, slots = out_ref.shape
    columns = fields * parts
    rank = root_ref.shape[2]
    group_rows = group * columns
    here = place_ref.shape[1]
    steps = state_refs[0].shape[0] // group_rows
    shape = (group_rows, 2 * rank)
    row_pair = lax.broadcasted_iota(jnp.int32, shape, 0) // columns
    row_half = lax.broadcasted_iota(jnp.int32, shape, 1) // rank
    masks = [[(row_pair == pair) & (row_half == half) for pair in range(group)] for half in range(2)]
    empty = jnp.zeros(shape, BF16)
    for i, state_ref in enumerate(state_refs):
        for step in range(steps):
            state = state_ref[pl.ds(step * group_rows, group_rows)]
            left = jnp.concatenate(
                [jnp.concatenate([jnp.where(m, state, empty) for m in line], axis=1) for line in masks], axis=0
            )
            right = root_ref[first + i, pl.ds(step * group * 2, group * 2)].reshape(group * 2 * rank, degrees)
            product = contract(left, right, ((1,), (0,)))
            begin = (i * steps + step) * 2 * group_rows
            for tile in range(degrees // 128):
                rows_ref[tile, pl.ds(begin, 2 * group_rows), :] = product[:, tile * 128 : (tile + 1) * 128]
    place = place_ref[pl.ds(first, count)].reshape(count * here, slots)
    copies = []
    for column in range(columns):
        for tile in range(degrees // 128):
            span = slice(tile * 128, (tile + 1) * 128)
            one = rows_ref[tile, pl.ds(column, count * here, stride=columns), :].astype(BF16)
            natural = contract(one.T, place, ((1,), (0,))).astype(BF16)
            where = (column // 2, column % 2, span)
            if last:
                natural = natural + so_far_ref[where]
                natural = jnp.where(alive_ref[span] != 0, natural, jnp.zeros((), BF16))
            natural_ref[where] = natural
        if last and column % 2:
            field = column // 2
            copies.append(pltpu.make_async_copy(natural_ref.at[field], out_ref.at[field], refs[-1].at[field]))
            copies[-1].start()
    for copy in copies:
        copy.wait()


def spectra_of(states, roots, places, alive, so_far, first, group):
    state_rows, lanes = states[0].shape
    owners, here, rank, degrees = roots.shape
    slots = places.shape[2]
    columns = state_rows * 2 // here
    last = so_far is not None
    shape = (columns // 2, 2, degrees, slots)
    inputs = ([so_far] if last else []) + [roots, places, alive, *states]
    scratch = [pltpu.VMEM((degrees // 128, len(states) * here * columns, 128), F32)]
    more = {}
    if last:
        scratch += [pltpu.VMEM(shape, BF16), pltpu.SemaphoreType.DMA((columns // 2,))]
        more["out_specs"] = IN_HBM
    return call(
        functools.partial(root_kernel, group, first, last),
        "root",
        jax.ShapeDtypeStruct(shape, BF16),
        whole_blocks(len(inputs)),
        2 * len(states) * here * rank * degrees * columns,
        2 * len(states) * here * rank * degrees,
        scratch,
        mib=24,
        **more,
    )(*inputs)


def per_device(
    fourier, quad_weights, leaf_basis, level_factors, sparsity, root_basis, order_of_slot
):
    slots, columns, lats = fourier.shape
    owners = lax.axis_size("order")
    levels = level_factors.shape[1]
    group = max(2, 16 * owners // columns)
    present = sparsity[:, :, 0].T
    fourier, leaf_basis, level_factors, root_basis = map(in_hbm, (fourier, leaf_basis, level_factors, root_basis))
    quad_weights = in_hbm(quad_weights.reshape(1, lats))

    def swap(array, axis, bits):
        return lax.ppermute(array, axis, [(i, i ^ bits) for i in range(lax.axis_size(axis))])

    size = slots // 2 // CHUNKS
    state = leaf_states(fourier, quad_weights, leaf_basis)
    partner = swap(state, "lat", 1)
    weights = level_weights(level_factors, present, (0,), state)
    states = [next_states(state, partner, weights[0], c * size, c * size, size) for c in range(CHUNKS)]
    weights += level_weights(level_factors, present, tuple(range(1, levels)), states[-1])
    for level in range(1, levels):
        partners = [swap(state, "lat", 1 << level) for state in states]
        if level < levels - 1:
            states = [
                next_states(*both, weights[level], 0, c * size, size) for c, both in enumerate(zip(states, partners))
            ]
    roots, places, alive = near_roots(root_basis, order_of_slot, owners, group, states[-1])
    sent = last_states(states, partners, weights[-1], owners, alive)
    arrived = [swap(part, "order", k) if k else part for k, part in enumerate(sent)]
    half = owners // 2
    spectra = spectra_of(arrived[:half], roots, places, alive, None, 0, group)
    return spectra_of(arrived[half:], roots, places, alive, spectra, half, group)


def solution(mesh):
    return jax.shard_map(
        per_device,
        mesh=mesh,
        in_specs=(
            P("order", None, "lat"),
            P("lat"),
            P("order", None, "lat"),
            P("order", None, None, "lat", None, None),
            P("order", None, "lat"),
            P(None, None, "lat"),
            P(),
        ),
        out_specs=P("order", None, "lat", None),
        check_vma=False,
    )
```

```python
import functools

import jax
import jax.numpy as jnp
from jax import lax
from jax.experimental import pallas as pl
from jax.experimental.pallas import tpu as pltpu
from jax.sharding import PartitionSpec as P

DEGREES = 2048
CHUNKS = 2
F32, BF16 = jnp.float32, jnp.bfloat16
MIB = 1 << 20
IN_HBM = pl.BlockSpec(memory_space=pltpu.HBM)
IN_SMEM = pl.BlockSpec(memory_space=pltpu.SMEM)
ANYWHERE = pl.BlockSpec(memory_space=pl.ANY)


def contract(lhs, rhs, dims):
    return lax.dot_general(lhs, rhs, (dims, ((), ())), preferred_element_type=F32)


def in_hbm(array):
    return pltpu.with_memory_space_constraint(array, pltpu.HBM)


def call(kernel, name, out_shape, in_specs, flops, size, scratch=(), mib=16, **more):
    return pl.pallas_call(
        kernel,
        out_shape=out_shape,
        in_specs=in_specs,
        scratch_shapes=list(scratch),
        compiler_params=pltpu.CompilerParams(vmem_limit_bytes=mib * MIB),
        cost_estimate=pl.CostEstimate(flops=flops // 1000, bytes_accessed=size // 1000, transcendentals=0),
        name=name,
        **more,
    )


def whole_blocks(count):
    return [pl.BlockSpec()] * count


def leaf_kernel(
    pieces, fourier_hbm, weight_hbm, leaf_hbm, factor_hbm, state_ref, factor_ref, fourier_ref, weight_ref, leaf_ref, sems
):
    slots, columns, lats = fourier_ref.shape
    rank = leaf_ref.shape[1]
    per = slots // pieces
    copies = [pltpu.make_async_copy(weight_hbm, weight_ref, sems.at[0])]
    for piece in range(pieces):
        part = pl.ds(piece * per, per)
        copies.append(pltpu.make_async_copy(fourier_hbm.at[part], fourier_ref.at[part], sems.at[1 + 2 * piece]))
        copies.append(pltpu.make_async_copy(leaf_hbm.at[part], leaf_ref.at[part], sems.at[2 + 2 * piece]))
    copies.append(pltpu.make_async_copy(factor_hbm.at[:, 0, :, 0], factor_ref, sems.at[1 + 2 * pieces]))
    for copy in copies:
        copy.start()
    copies[0].wait()
    weight = weight_ref[...]
    mine = lax.broadcasted_iota(jnp.int32, (rank, 2 * columns), 1) < columns
    for pair in range(slots // 2):
        if 2 * pair % per == 0:
            copies[1 + 2 * (2 * pair // per)].wait()
            copies[2 + 2 * (2 * pair // per)].wait()
        both = pl.ds(2 * pair, 2)
        weighted = (fourier_ref[both].astype(F32) * weight[None]).astype(BF16)
        product = contract(
            leaf_ref[both].reshape(2 * rank, lats), weighted.reshape(2 * columns, lats), ((1,), (1,))
        )
        state_ref[pair] = jnp.where(mine, product[:rank], product[rank:]).astype(BF16)
    copies[-1].wait()


def leaf_states(fourier, quad_weights, leaf_basis, level_factors):
    slots, columns, lats = fourier.shape
    rank = leaf_basis.shape[1]
    pieces = 8
    return call(
        functools.partial(leaf_kernel, pieces),
        "leaf",
        [
            jax.ShapeDtypeStruct((slots // 2, rank, 2 * columns), BF16),
            jax.ShapeDtypeStruct((slots, 2, rank, rank), BF16),
        ],
        [IN_HBM] * 4,
        2 * slots * columns * rank * lats,
        4 * slots * columns * lats,
        [
            pltpu.VMEM((slots, columns, lats), BF16),
            pltpu.VMEM((1, lats), F32),
            pltpu.VMEM((slots, rank, lats), BF16),
            pltpu.SemaphoreType.DMA((2 + 2 * pieces,)),
        ],
    )(fourier, quad_weights, leaf_basis, level_factors)


def factor_kernel(level, factor_ref, present_ref, after, weight_ref):
    del after
    slots, rank = factor_ref.shape[0], factor_ref.shape[-1]
    empty = jnp.zeros((rank, rank), BF16)
    for pair in range(slots // 2):
        for half in range(2):
            first, second = (factor_ref[slot, half] for slot in (2 * pair, 2 * pair + 1))
            if half:
                first = jnp.where(present_ref[level, 2 * pair] != 0, first, empty)
                second = jnp.where(present_ref[level, 2 * pair + 1] != 0, second, empty)
            lanes = pl.ds(half * 2 * rank, 2 * rank)
            weight_ref[pair, :rank, lanes] = jnp.concatenate([first, empty], axis=1)
            weight_ref[pair, rank:, lanes] = jnp.concatenate([empty, second], axis=1)


def last_weights(factors, present, level, after):
    slots, _, rank, _ = factors.shape
    return call(
        functools.partial(factor_kernel, level),
        "factors",
        jax.ShapeDtypeStruct((slots // 2, 2 * rank, 4 * rank), BF16),
        [pl.BlockSpec(), IN_SMEM, ANYWHERE],
        slots * rank * rank * 4,
        slots * rank * rank * 16,
    )(factors, present, after)


def level_kernel(level, first, first_slot, turn, factor_ref, present_ref, after, state_ref, partner_ref, out_ref):
    del after
    rank = factor_ref.shape[-1]
    pairs, rows, lanes = out_ref.shape
    mine = lax.broadcasted_iota(jnp.int32, (rows, lanes), 1) < lanes // 2
    for pair in range(pairs):
        slot = first_slot + 2 * pair
        terms = []
        for half, ref in enumerate((state_ref, partner_ref)):
            factor = factor_ref[pl.ds(slot, 2), half].reshape(2 * rank, rank)
            state = ref[first + pair]
            if turn:
                terms.append(contract(state, factor, ((0,), (1,))))
            else:
                terms.append(contract(factor, state, ((1,), (0,))))
        own, cross = terms
        both = [
            own[side * rows : (side + 1) * rows]
            + present_ref[level, slot + side].astype(F32) * cross[side * rows : (side + 1) * rows]
            for side in range(2)
        ]
        out_ref[pair] = jnp.where(mine, *both).astype(BF16)


def next_states(factors, present, level, after, state, partner, first, first_slot, pairs, turn):
    rank = factors.shape[-1]
    columns = state.shape[2] // 2
    shape = (pairs, columns, 2 * rank) if turn else (pairs, rank, 2 * columns)
    return call(
        functools.partial(level_kernel, level, first, first_slot, turn),
        "level",
        jax.ShapeDtypeStruct(shape, BF16),
        [pl.BlockSpec(), IN_SMEM, ANYWHERE] + whole_blocks(2),
        16 * pairs * columns * rank * rank,
        12 * pairs * columns * rank,
    )(factors, present, after, state, partner)


def last_level_kernel(first, axis, state_ref, partner_ref, weight_ref, *refs):
    out_refs, groups_ref = refs[:-1], refs[-1]
    me = lax.axis_index(axis)
    pairs, owners, group, _ = groups_ref.shape
    for pair in range(pairs):
        both = jnp.concatenate([state_ref[pair], partner_ref[pair]], axis=1)
        result = contract(both, weight_ref[first + pair], ((1,), (1,))).astype(BF16)
        if len(out_refs) == 1:
            out_refs[0][pair] = result
            continue
        for owner in range(owners):
            groups_ref[pair, owner] = result[owner * group : (owner + 1) * group]
    if len(out_refs) > 1:
        for k, out_ref in enumerate(out_refs):
            for pair in range(pairs):
                out_ref[pl.ds(pair * group, group)] = groups_ref[pair, me ^ k]


def last_states(state, partner, weights, first, owners):
    pairs, columns, lanes = state.shape
    group = columns // owners
    aligned = group % 16 == 0
    out_shape = [jax.ShapeDtypeStruct((pairs * group, lanes), BF16)] * owners
    if not aligned:
        out_shape = [jax.ShapeDtypeStruct(state.shape, BF16)]
    parts = call(
        functools.partial(last_level_kernel, first, "order"),
        "last_level",
        out_shape,
        whole_blocks(3),
        4 * pairs * columns * lanes * lanes,
        6 * pairs * columns * lanes,
        [pltpu.VMEM((pairs, owners, group, lanes), BF16)],
    )(state, partner, weights)
    if aligned:
        return parts
    me = lax.axis_index("order")
    parts = [lax.dynamic_slice_in_dim(parts[0], (me ^ k) * group, group, 1) for k in range(owners)]
    return [part.reshape(pairs * group, lanes) for part in parts]


def near_kernel(group, root_hbm, factor_hbm, order_ref, after, *refs):
    del after
    alive_ref, rows_ref, sems = refs[-3:]
    levels = factor_hbm.shape[1]
    factor_refs, refs = refs[: levels - 1], refs[levels - 1 : -3]
    chunks = len(refs) // 2
    root_refs, place_refs = refs[:chunks], refs[chunks:]
    degrees, slots = alive_ref.shape
    owners = root_refs[0].shape[0]
    me = lax.axis_index("order")
    copies = []
    for level in range(1, levels):
        copies.append(
            pltpu.make_async_copy(factor_hbm.at[:, level, :, 0], factor_refs[level - 1], sems.at[chunks * owners + level - 1])
        )
        copies[-1].start()
    begin = 0
    for c, root_ref in enumerate(root_refs):
        size = root_ref.shape[1]
        for k in range(owners):
            there = pl.ds((me ^ k) * (slots // owners) + begin, size)
            copies.append(pltpu.make_async_copy(root_hbm.at[there], root_ref.at[k], sems.at[c * owners + k]))
            copies[-1].start()
        begin += size
    lane = lax.broadcasted_iota(jnp.int32, (1, slots), 1)
    begin = 0
    for root_ref, place_ref in zip(root_refs, place_refs):
        size = root_ref.shape[1]
        for k in range(owners):
            for slot in range(size):
                pair, half = slot // 2, slot % 2
                row = k * size + (pair // group * 2 + half) * group + pair % group
                window = order_ref[(me ^ k) * (slots // owners) + begin + slot]
                rows_ref[pl.ds(row, 1), :] = (lane == window).astype(F32)
        place_ref[...] = rows_ref[: owners * size].astype(BF16)
        begin += size
    degree = lax.axis_index("lat") * degrees + lax.broadcasted_iota(jnp.int32, (degrees, slots), 0)
    window = DEGREES // slots * lax.broadcasted_iota(jnp.int32, (degrees, slots), 1)
    alive_ref[...] = (degree >= window).astype(F32).astype(BF16)
    for copy in copies:
        copy.wait()


def near_roots(root_basis, level_factors, order_of_slot, owners, sizes, group, after):
    slots, rank, degrees = root_basis.shape
    here, levels = level_factors.shape[:2]
    outs = call(
        functools.partial(near_kernel, group),
        "near_roots",
        [jax.ShapeDtypeStruct((here, 2, rank, rank), BF16)] * (levels - 1)
        + [jax.ShapeDtypeStruct((owners, size, rank, degrees), BF16) for size in sizes]
        + [jax.ShapeDtypeStruct((owners * size, slots), BF16) for size in sizes]
        + [jax.ShapeDtypeStruct((degrees, slots), BF16)],
        [IN_HBM, IN_HBM, IN_SMEM, ANYWHERE],
        slots * slots,
        4 * slots * rank * degrees,
        [pltpu.VMEM((owners * max(sizes), slots), F32), pltpu.SemaphoreType.DMA((len(sizes) * owners + levels - 1,))],
    )(root_basis, level_factors, order_of_slot, after)
    factors, outs = outs[: levels - 1], outs[levels - 1 :]
    return factors, outs[: len(sizes)], outs[len(sizes) : -1], outs[-1]


def root_kernel(group, more, last, *refs):
    refs = list(refs)
    so_far_ref = refs.pop(0) if more else None
    root_ref, place_ref, alive_ref = refs[:3]
    count = len(refs) - (7 if last else 5)
    state_refs = refs[3 : 3 + count]
    out_ref, rows_ref = refs[3 + count : 5 + count]
    natural_ref = refs[5 + count] if last else out_ref
    fields, parts, degrees, slots = out_ref.shape
    columns = fields * parts
    rank = root_ref.shape[2]
    group_rows = group * columns
    here = root_ref.shape[1]
    steps = state_refs[0].shape[0] // group_rows
    shape = (group_rows, 2 * rank)
    row_pair = lax.broadcasted_iota(jnp.int32, shape, 0) // columns
    row_half = lax.broadcasted_iota(jnp.int32, shape, 1) // rank
    masks = [[(row_pair == pair) & (row_half == half) for pair in range(group)] for half in range(2)]
    empty = jnp.zeros(shape, BF16)
    for i, state_ref in enumerate(state_refs):
        for step in range(steps):
            state = state_ref[pl.ds(step * group_rows, group_rows)]
            left = jnp.concatenate(
                [jnp.concatenate([jnp.where(m, state, empty) for m in line], axis=1) for line in masks], axis=0
            )
            right = root_ref[i, pl.ds(step * group * 2, group * 2)].reshape(group * 2 * rank, degrees)
            product = contract(left, right, ((1,), (0,)))
            begin = (i * steps + step) * 2 * group_rows
            for tile in range(degrees // 128):
                rows_ref[tile, pl.ds(begin, 2 * group_rows), :] = product[:, tile * 128 : (tile + 1) * 128]
    place = place_ref[...]
    copies = []
    for column in range(columns):
        for tile in range(degrees // 128):
            span = slice(tile * 128, (tile + 1) * 128)
            one = rows_ref[tile, pl.ds(column, count * here, stride=columns), :].astype(BF16)
            natural = contract(one.T, place, ((1,), (0,))).astype(BF16)
            where = (column // 2, column % 2, span)
            if more:
                natural = natural + so_far_ref[where]
            if last:
                natural = jnp.where(alive_ref[span] != 0, natural, jnp.zeros((), BF16))
            natural_ref[where] = natural
        if last:
            where = (column // 2, column % 2)
            copies.append(pltpu.make_async_copy(natural_ref.at[where], out_ref.at[where], refs[-1].at[column]))
            copies[-1].start()
    for copy in copies:
        copy.wait()


def spectra_of(states, roots, place, alive, so_far, last, group):
    state_rows, lanes = states[0].shape
    owners, here, rank, degrees = roots.shape
    slots = place.shape[1]
    columns = state_rows * 2 // here
    more = so_far is not None
    shape = (columns // 2, 2, degrees, slots)
    inputs = ([so_far] if more else []) + [roots, place, alive, *states]
    scratch = [pltpu.VMEM((degrees // 128, owners * here * columns, 128), F32)]
    specs = {}
    if last:
        scratch += [pltpu.VMEM(shape, BF16), pltpu.SemaphoreType.DMA((columns,))]
        specs["out_specs"] = IN_HBM
    return call(
        functools.partial(root_kernel, group, more, last),
        "root",
        jax.ShapeDtypeStruct(shape, BF16),
        whole_blocks(len(inputs)),
        2 * owners * here * rank * degrees * columns,
        2 * owners * here * rank * degrees,
        scratch,
        mib=24,
        **specs,
    )(*inputs)


def per_device(
    fourier, quad_weights, leaf_basis, level_factors, sparsity, root_basis, order_of_slot
):
    slots, columns, lats = fourier.shape
    owners = lax.axis_size("order")
    levels = level_factors.shape[1]
    group = max(2, 16 * owners // columns)
    sizes = [slots // CHUNKS] * CHUNKS
    begins = [sum(sizes[:c]) for c in range(CHUNKS)]
    present = sparsity[:, :, 0].T
    fourier, leaf_basis, level_factors, root_basis = map(in_hbm, (fourier, leaf_basis, level_factors, root_basis))
    quad_weights = in_hbm(quad_weights.reshape(1, lats))

    def swap(array, axis, bits):
        return lax.ppermute(array, axis, [(i, i ^ bits) for i in range(lax.axis_size(axis))])

    def next_of(level, c, after, state, partner, first):
        turn = level == levels - 2
        return next_states(
            factors[level], present, level, after, state, partner, first, begins[c], sizes[c] // 2, turn
        )

    state, *factors = leaf_states(fourier, quad_weights, leaf_basis, level_factors)
    partner = swap(state, "lat", 1)
    states = []
    after = present
    for c in range(CHUNKS):
        states.append(next_of(0, c, after, state, partner, begins[c] // 2))
        if c == 0:
            others, roots, places, alive = near_roots(
                root_basis, level_factors, order_of_slot, owners, sizes, group, states[0]
            )
            after = alive
    factors += others
    for level in range(1, levels):
        partners = [swap(state, "lat", 1 << level) for state in states]
        if level < levels - 1:
            after = alive
            for c in range(CHUNKS):
                states[c] = next_of(level, c, after, states[c], partners[c], 0)
                if c == 0 and level == levels - 2:
                    after = weights = last_weights(factors[-1], present, levels - 1, states[0])
    spectra = None
    for c in range(CHUNKS):
        sent = last_states(states[c], partners[c], weights, begins[c] // 2, owners)
        arrived = [swap(part, "order", k) if k else part for k, part in enumerate(sent)]
        spectra = spectra_of(arrived, roots[c], places[c], alive, spectra, c == CHUNKS - 1, group)
    return spectra


def solution(mesh):
    return jax.shard_map(
        per_device,
        mesh=mesh,
        in_specs=(
            P("order", None, "lat"),
            P("lat"),
            P("order", None, "lat"),
            P("order", None, None, "lat", None, None),
            P("order", None, "lat"),
            P(None, None, "lat"),
            P(),
        ),
        out_specs=P("order", None, "lat", None),
        check_vma=False,
    )
```

```python
import functools

import jax
import jax.numpy as jnp
from jax import lax
from jax.experimental import pallas as pl
from jax.experimental.pallas import tpu as pltpu
from jax.sharding import PartitionSpec as P

DEGREES = 2048
F32, BF16 = jnp.float32, jnp.bfloat16
MIB = 1 << 20
IN_HBM = pl.BlockSpec(memory_space=pltpu.HBM)
IN_SMEM = pl.BlockSpec(memory_space=pltpu.SMEM)
ANYWHERE = pl.BlockSpec(memory_space=pl.ANY)


def contract(lhs, rhs, dims):
    return lax.dot_general(lhs, rhs, (dims, ((), ())), preferred_element_type=F32)


def in_hbm(array):
    return pltpu.with_memory_space_constraint(array, pltpu.HBM)


def call(kernel, name, out_shape, in_specs, flops, size, scratch=(), mib=16, **more):
    return pl.pallas_call(
        kernel,
        out_shape=out_shape,
        in_specs=in_specs,
        scratch_shapes=list(scratch),
        compiler_params=pltpu.CompilerParams(vmem_limit_bytes=mib * MIB),
        cost_estimate=pl.CostEstimate(flops=flops // 1000, bytes_accessed=size // 1000, transcendentals=0),
        name=name,
        **more,
    )


def whole_blocks(count):
    return [pl.BlockSpec()] * count


def leaf_kernel(pieces, fourier_hbm, weight_hbm, leaf_hbm, state_ref, fourier_ref, weight_ref, leaf_ref, sems):
    slots, columns, lats = fourier_ref.shape
    rank = leaf_ref.shape[1]
    per = slots // pieces
    copies = [pltpu.make_async_copy(weight_hbm, weight_ref, sems.at[0])]
    for piece in range(pieces):
        part = pl.ds(piece * per, per)
        copies.append(pltpu.make_async_copy(fourier_hbm.at[part], fourier_ref.at[part], sems.at[1 + 2 * piece]))
        copies.append(pltpu.make_async_copy(leaf_hbm.at[part], leaf_ref.at[part], sems.at[2 + 2 * piece]))
    for copy in copies:
        copy.start()
    copies[0].wait()
    weight = weight_ref[...]
    mine = lax.broadcasted_iota(jnp.int32, (columns, 2 * rank), 1) < rank
    for pair in range(slots // 2):
        if 2 * pair % per == 0:
            copies[1 + 2 * (2 * pair // per)].wait()
            copies[2 + 2 * (2 * pair // per)].wait()
        both = pl.ds(2 * pair, 2)
        weighted = (fourier_ref[both].astype(F32) * weight[None]).astype(BF16)
        product = contract(
            weighted.reshape(2 * columns, lats), leaf_ref[both].reshape(2 * rank, lats), ((1,), (1,))
        )
        state_ref[pair] = jnp.where(mine, product[:columns], product[columns:]).astype(BF16)


def leaf_states(fourier, quad_weights, leaf_basis):
    slots, columns, lats = fourier.shape
    rank = leaf_basis.shape[1]
    pieces = 8
    return call(
        functools.partial(leaf_kernel, pieces),
        "leaf",
        jax.ShapeDtypeStruct((slots // 2, columns, 2 * rank), BF16),
        [IN_HBM] * 3,
        2 * slots * columns * rank * lats,
        4 * slots * columns * lats,
        [
            pltpu.VMEM((slots, columns, lats), BF16),
            pltpu.VMEM((1, lats), F32),
            pltpu.VMEM((slots, rank, lats), BF16),
            pltpu.SemaphoreType.DMA((1 + 2 * pieces,)),
        ],
    )(fourier, quad_weights, leaf_basis)


def factor_kernel(levels, pieces, factor_hbm, present_hbm, after, *refs):
    del after
    weight_refs, (factor_ref, present_ref, sems) = refs[: len(levels)], refs[len(levels) :]
    present_copy = pltpu.make_async_copy(present_hbm, present_ref, sems.at[len(levels) * pieces])
    present_copy.start()
    _, slots, _, rank, _ = factor_ref.shape
    per = slots // pieces
    copies = {}
    for i, level in enumerate(levels):
        for piece in range(pieces):
            part = pl.ds(piece * per, per)
            copies[i, piece] = pltpu.make_async_copy(
                factor_hbm.at[part, level, :, 0], factor_ref.at[i, part], sems.at[i * pieces + piece]
            )
            copies[i, piece].start()
    empty = jnp.zeros((rank, rank), BF16)
    present_copy.wait()
    for i, level in enumerate(levels):
        for pair in range(slots // 2):
            if 2 * pair % per == 0:
                copies[i, 2 * pair // per].wait()
            for half in range(2):
                first, second = (factor_ref[i, slot, half] for slot in (2 * pair, 2 * pair + 1))
                if half:
                    first = jnp.where(present_ref[level, 0, 2 * pair] != 0, first, empty)
                    second = jnp.where(present_ref[level, 0, 2 * pair + 1] != 0, second, empty)
                lanes = pl.ds(half * 2 * rank, 2 * rank)
                weight_refs[i][pair, :rank, lanes] = jnp.concatenate([first, empty], axis=1)
                weight_refs[i][pair, rank:, lanes] = jnp.concatenate([empty, second], axis=1)


def level_weights(level_factors, present, levels, after):
    slots, _, _, _, rank, _ = level_factors.shape
    count, pieces = len(levels), 4
    return call(
        functools.partial(factor_kernel, levels, pieces),
        "factors",
        [jax.ShapeDtypeStruct((slots // 2, 2 * rank, 4 * rank), BF16)] * count,
        [IN_HBM, IN_HBM, ANYWHERE],
        slots * rank * rank * 4 * count,
        slots * rank * rank * 16 * count,
        [
            pltpu.VMEM((count, slots, 2, rank, rank), BF16),
            pltpu.SMEM(present.shape, jnp.int32),
            pltpu.SemaphoreType.DMA((count * pieces + 1,)),
        ],
        mib=24,
    )(level_factors, present, after)


def level_kernel(first, first_weight, after, state_ref, partner_ref, weight_ref, out_ref):
    del after
    for pair in range(out_ref.shape[0]):
        both = jnp.concatenate([state_ref[first + pair], partner_ref[first + pair]], axis=1)
        out_ref[pair] = contract(both, weight_ref[first_weight + pair], ((1,), (1,))).astype(BF16)


def next_states(name, after, state, partner, weights, first, first_weight, pairs):
    _, columns, lanes = state.shape
    return call(
        functools.partial(level_kernel, first, first_weight),
        name,
        jax.ShapeDtypeStruct((pairs, columns, lanes), BF16),
        [ANYWHERE] + whole_blocks(3),
        4 * pairs * columns * lanes * lanes,
        6 * pairs * columns * lanes,
    )(after, state, partner, weights)


def last_level_kernel(first, whole, axis, after, state_ref, partner_ref, weight_ref, *refs):
    del after
    out_refs, groups_ref = refs[:-1], refs[-1]
    me = lax.axis_index(axis)
    pairs, owners, group, _ = groups_ref.shape
    for pair in range(pairs):
        both = jnp.concatenate([state_ref[pair], partner_ref[pair]], axis=1)
        result = contract(both, weight_ref[first + pair], ((1,), (1,))).astype(BF16)
        for owner in range(owners):
            part = result[owner * group : (owner + 1) * group]
            if whole:
                out_refs[0][owner, pl.ds(pair * group, group)] = part
            else:
                groups_ref[pair, owner] = part
    if not whole:
        for k, out_ref in enumerate(out_refs):
            for pair in range(pairs):
                out_ref[pl.ds(pair * group, group)] = groups_ref[pair, me ^ k]


def last_states(after, state, partner, weights, first, owners, whole):
    pairs, columns, lanes = state.shape
    group = columns // owners
    rows = pairs * group
    if group % 16:
        state = next_states("level", after, state, partner, weights, 0, first, pairs)
        parts = state.reshape(pairs, owners, group, lanes).transpose(1, 0, 2, 3).reshape(owners, rows, lanes)
        if whole:
            return [parts]
        me = lax.axis_index("order")
        return [lax.dynamic_index_in_dim(parts, me ^ k, 0, False) for k in range(owners)]
    if whole:
        out_shape = [jax.ShapeDtypeStruct((owners, rows, lanes), BF16)]
    else:
        out_shape = [jax.ShapeDtypeStruct((rows, lanes), BF16)] * owners
    return call(
        functools.partial(last_level_kernel, first, whole, "order"),
        "last_whole" if whole else "last_parts",
        out_shape,
        [ANYWHERE] + whole_blocks(3),
        4 * pairs * columns * lanes * lanes,
        6 * pairs * columns * lanes,
        [pltpu.VMEM((pairs, owners, group, lanes), BF16)],
    )(after, state, partner, weights)


def place_kernel(sizes, owners, group, order_ref, after, *refs):
    del after
    place_refs, alive_ref, rows_ref = refs[:-2], refs[-2], refs[-1]
    degrees, slots = alive_ref.shape
    me = lax.axis_index("order")
    lane = lax.broadcasted_iota(jnp.int32, (1, slots), 1)
    begin = 0
    for c, (size, place_ref) in enumerate(zip(sizes, place_refs)):
        for k in range(owners):
            owner = me ^ k if c else k
            for slot in range(size):
                pair, half = slot // 2, slot % 2
                row = k * size + (pair // group * 2 + half) * group + pair % group
                window = order_ref[owner * (slots // owners) + begin + slot]
                rows_ref[pl.ds(row, 1), :] = (lane == window).astype(F32)
        place_ref[...] = rows_ref[: owners * size].astype(BF16)
        begin += size
    degree = lax.axis_index("lat") * degrees + lax.broadcasted_iota(jnp.int32, (degrees, slots), 0)
    window = DEGREES // slots * lax.broadcasted_iota(jnp.int32, (degrees, slots), 1)
    alive_ref[...] = (degree >= window).astype(F32).astype(BF16)


def places_of(order_of_slot, degrees, owners, sizes, group, after):
    slots = order_of_slot.shape[0]
    outs = call(
        functools.partial(place_kernel, sizes, owners, group),
        "places",
        [jax.ShapeDtypeStruct((owners * size, slots), BF16) for size in sizes]
        + [jax.ShapeDtypeStruct((degrees, slots), BF16)],
        [IN_SMEM, ANYWHERE],
        slots * slots,
        8 * slots * slots,
        [pltpu.VMEM((owners * max(sizes), slots), F32)],
    )(order_of_slot, after)
    return outs[:-1], outs[-1]


def root_kernel(group, begin, more, last, *refs):
    refs = list(refs)
    so_far_ref = refs.pop(0) if more else None
    root_ref, place_ref, alive_ref = refs[:3]
    if last:
        state_refs, out_ref, rows_ref, natural_ref = refs[3:-4], *refs[-4:-1]
    else:
        whole_ref, out_ref, rows_ref = refs[3:]
        state_refs, natural_ref = [whole_ref.at[i] for i in range(whole_ref.shape[0])], out_ref
    count = len(state_refs)
    fields, parts, degrees, slots = out_ref.shape
    columns = fields * parts
    rank = root_ref.shape[1]
    group_rows = group * columns
    here = place_ref.shape[0] // count
    held = root_ref.shape[0] // count
    me = lax.axis_index("order")
    steps = state_refs[0].shape[0] // group_rows
    shape = (group_rows, 2 * rank)
    row_pair = lax.broadcasted_iota(jnp.int32, shape, 0) // columns
    row_half = lax.broadcasted_iota(jnp.int32, shape, 1) // rank
    masks = [[(row_pair == pair) & (row_half == half) for pair in range(group)] for half in range(2)]
    empty = jnp.zeros(shape, BF16)
    for i, state_ref in enumerate(state_refs):
        for step in range(steps):
            state = state_ref[pl.ds(step * group_rows, group_rows)]
            left = jnp.concatenate(
                [jnp.concatenate([jnp.where(m, state, empty) for m in line], axis=1) for line in masks], axis=0
            )
            there = (me ^ i if last else i) * held + begin + step * group * 2
            right = root_ref[pl.ds(there, group * 2)].reshape(group * 2 * rank, degrees)
            product = contract(left, right, ((1,), (0,)))
            row = (i * steps + step) * 2 * group_rows
            for tile in range(degrees // 128):
                rows_ref[tile, pl.ds(row, 2 * group_rows), :] = product[:, tile * 128 : (tile + 1) * 128]
    place = place_ref[...]
    copies = []
    for column in range(columns):
        for tile in range(degrees // 128):
            span = slice(tile * 128, (tile + 1) * 128)
            one = rows_ref[tile, pl.ds(column, count * here, stride=columns), :].astype(BF16)
            natural = contract(one.T, place, ((1,), (0,))).astype(BF16)
            where = (column // 2, column % 2, span)
            if more:
                natural = natural + so_far_ref[where]
            if last:
                natural = jnp.where(alive_ref[span] != 0, natural, jnp.zeros((), BF16))
            natural_ref[where] = natural
        if last:
            where = (column // 2, column % 2)
            copies.append(pltpu.make_async_copy(natural_ref.at[where], out_ref.at[where], refs[-1].at[column]))
            copies[-1].start()
    for copy in copies:
        copy.wait()


def spectra_of(states, root_basis, place, alive, so_far, begin, last, group):
    state_rows = states[0].shape[-2]
    _, rank, degrees = root_basis.shape
    slots = place.shape[1]
    owners = lax.axis_size("order")
    here = place.shape[0] // owners
    columns = state_rows * 2 // here
    more = so_far is not None
    shape = (columns // 2, 2, degrees, slots)
    inputs = ([so_far] if more else []) + [root_basis, place, alive, *states]
    scratch = [pltpu.VMEM((degrees // 128, owners * here * columns, 128), F32)]
    specs = {}
    if last:
        scratch += [pltpu.VMEM(shape, BF16), pltpu.SemaphoreType.DMA((columns,))]
        specs["out_specs"] = IN_HBM
    return call(
        functools.partial(root_kernel, group, begin, more, last),
        "root",
        jax.ShapeDtypeStruct(shape, BF16),
        whole_blocks(len(inputs)),
        2 * owners * here * rank * degrees * columns,
        2 * owners * here * rank * degrees,
        scratch,
        mib=24,
        **specs,
    )(*inputs)


def per_device(
    fourier, quad_weights, leaf_basis, level_factors, sparsity, root_basis, order_of_slot
):
    slots, columns, lats = fourier.shape
    owners = lax.axis_size("order")
    levels = level_factors.shape[1]
    group = max(2, 16 * owners // columns)
    first = slots // (4 * group) * 2 * group
    sizes = [first, slots - first]
    begins = [0, first]
    present = in_hbm(sparsity.transpose(1, 2, 0))
    fourier, leaf_basis, level_factors = map(in_hbm, (fourier, leaf_basis, level_factors))
    quad_weights = in_hbm(quad_weights.reshape(1, lats))

    def swap(array, axis, bits):
        return lax.ppermute(array, axis, [(i, i ^ bits) for i in range(lax.axis_size(axis))])

    state = leaf_states(fourier, quad_weights, leaf_basis)
    partner = swap(state, "lat", 1)
    weights = level_weights(level_factors, present, (0,), state)
    states = [next_states("level0_0", state, state, partner, weights[0], 0, 0, sizes[0] // 2)]
    weights += level_weights(level_factors, present, (1,), states[0])
    at = begins[1] // 2
    states.append(next_states("level0_1", weights[1], state, partner, weights[0], at, at, sizes[1] // 2))
    weights += level_weights(level_factors, present, tuple(range(2, levels)), states[1])
    for level in range(1, levels):
        partners = [swap(state, "lat", 1 << level) for state in states]
        if level < levels - 1:
            for c in range(2):
                states[c] = next_states(
                    f"level{level}_{c}", states[c], states[c], partners[c], weights[level], 0, begins[c] // 2, sizes[c] // 2
                )
    places, alive = places_of(order_of_slot, root_basis.shape[2], owners, sizes, group, states[1])
    begin = begins[0] // 2
    (sent,) = last_states(alive, states[0], partners[0], weights[-1], begin, owners, True)
    arrived = [lax.all_to_all(sent, "order", split_axis=0, concat_axis=0, tiled=True)]
    spectra = spectra_of(arrived, root_basis, places[0], alive, None, begins[0], False, group)
    begin = begins[1] // 2
    sent = last_states(sent, states[1], partners[1], weights[-1], begin, owners, False)
    arrived = [swap(part, "order", k) if k else part for k, part in enumerate(sent)]
    return spectra_of(arrived, root_basis, places[1], alive, spectra, begins[1], True, group)


def solution(mesh):
    return jax.shard_map(
        per_device,
        mesh=mesh,
        in_specs=(
            P("order", None, "lat"),
            P("lat"),
            P("order", None, "lat"),
            P("order", None, None, "lat", None, None),
            P("order", None, "lat"),
            P(None, None, "lat"),
            P(),
        ),
        out_specs=P("order", None, "lat", None),
        check_vma=False,
    )
```

```python
import functools

import jax
import jax.numpy as jnp
from jax import lax
from jax.experimental import pallas as pl
from jax.experimental.pallas import tpu as pltpu
from jax.sharding import PartitionSpec as P

DEGREES = 2048
F32, BF16 = jnp.float32, jnp.bfloat16
MIB = 1 << 20
IN_HBM = pl.BlockSpec(memory_space=pltpu.HBM)
IN_SMEM = pl.BlockSpec(memory_space=pltpu.SMEM)
ANYWHERE = pl.BlockSpec(memory_space=pl.ANY)


def contract(lhs, rhs, dims):
    return lax.dot_general(lhs, rhs, (dims, ((), ())), preferred_element_type=F32)


def in_hbm(array):
    return pltpu.with_memory_space_constraint(array, pltpu.HBM)


def call(kernel, name, out_shape, in_specs, flops, size, scratch=(), mib=16, **more):
    return pl.pallas_call(
        kernel,
        out_shape=out_shape,
        in_specs=in_specs,
        scratch_shapes=list(scratch),
        compiler_params=pltpu.CompilerParams(vmem_limit_bytes=mib * MIB),
        cost_estimate=pl.CostEstimate(flops=flops // 1000, bytes_accessed=size // 1000, transcendentals=0),
        name=name,
        **more,
    )


def whole_blocks(count):
    return [pl.BlockSpec()] * count


def leaf_kernel(pieces, fourier_hbm, weight_hbm, leaf_hbm, state_ref, fourier_ref, weight_ref, leaf_ref, sems):
    slots, columns, lats = fourier_ref.shape
    rank = leaf_ref.shape[1]
    per = slots // pieces
    copies = [pltpu.make_async_copy(weight_hbm, weight_ref, sems.at[0])]
    for piece in range(pieces):
        part = pl.ds(piece * per, per)
        copies.append(pltpu.make_async_copy(fourier_hbm.at[part], fourier_ref.at[part], sems.at[1 + 2 * piece]))
        copies.append(pltpu.make_async_copy(leaf_hbm.at[part], leaf_ref.at[part], sems.at[2 + 2 * piece]))
    for copy in copies:
        copy.start()
    copies[0].wait()
    weight = weight_ref[...]
    mine = lax.broadcasted_iota(jnp.int32, (columns, 2 * rank), 1) < rank
    for pair in range(slots // 2):
        if 2 * pair % per == 0:
            copies[1 + 2 * (2 * pair // per)].wait()
            copies[2 + 2 * (2 * pair // per)].wait()
        both = pl.ds(2 * pair, 2)
        weighted = (fourier_ref[both].astype(F32) * weight[None]).astype(BF16)
        product = contract(
            weighted.reshape(2 * columns, lats), leaf_ref[both].reshape(2 * rank, lats), ((1,), (1,))
        )
        state_ref[pair] = jnp.where(mine, product[:columns], product[columns:]).astype(BF16)


def leaf_states(fourier, quad_weights, leaf_basis):
    slots, columns, lats = fourier.shape
    rank = leaf_basis.shape[1]
    pieces = 2
    return call(
        functools.partial(leaf_kernel, pieces),
        "leaf",
        jax.ShapeDtypeStruct((slots // 2, columns, 2 * rank), BF16),
        [IN_HBM] * 3,
        2 * slots * columns * rank * lats,
        4 * slots * columns * lats,
        [
            pltpu.VMEM((slots, columns, lats), BF16),
            pltpu.VMEM((1, lats), F32),
            pltpu.VMEM((slots, rank, lats), BF16),
            pltpu.SemaphoreType.DMA((1 + 2 * pieces,)),
        ],
    )(fourier, quad_weights, leaf_basis)


def factor_kernel(levels, pieces, factor_hbm, present_hbm, after, *refs):
    del after
    weight_refs, (factor_ref, present_ref, sems) = refs[: len(levels)], refs[len(levels) :]
    present_copy = pltpu.make_async_copy(present_hbm, present_ref, sems.at[len(levels) * pieces])
    present_copy.start()
    _, slots, _, rank, _ = factor_ref.shape
    per = slots // pieces
    copies = {}
    for i, level in enumerate(levels):
        for piece in range(pieces):
            part = pl.ds(piece * per, per)
            copies[i, piece] = pltpu.make_async_copy(
                factor_hbm.at[part, level, :, 0], factor_ref.at[i, part], sems.at[i * pieces + piece]
            )
            copies[i, piece].start()
    empty = jnp.zeros((rank, rank), BF16)
    present_copy.wait()
    for i, level in enumerate(levels):
        for pair in range(slots // 2):
            if 2 * pair % per == 0:
                copies[i, 2 * pair // per].wait()
            for half in range(2):
                first, second = (factor_ref[i, slot, half] for slot in (2 * pair, 2 * pair + 1))
                if half:
                    first = jnp.where(present_ref[level, 0, 2 * pair] != 0, first, empty)
                    second = jnp.where(present_ref[level, 0, 2 * pair + 1] != 0, second, empty)
                lanes = pl.ds(half * 2 * rank, 2 * rank)
                weight_refs[i][pair, :rank, lanes] = jnp.concatenate([first, empty], axis=1)
                weight_refs[i][pair, rank:, lanes] = jnp.concatenate([empty, second], axis=1)


def level_weights(level_factors, present, levels, after):
    slots, _, _, _, rank, _ = level_factors.shape
    count, pieces = len(levels), 2
    return call(
        functools.partial(factor_kernel, levels, pieces),
        "factors",
        [jax.ShapeDtypeStruct((slots // 2, 2 * rank, 4 * rank), BF16)] * count,
        [IN_HBM, IN_HBM, ANYWHERE],
        slots * rank * rank * 4 * count,
        slots * rank * rank * 16 * count,
        [
            pltpu.VMEM((count, slots, 2, rank, rank), BF16),
            pltpu.SMEM(present.shape, jnp.int32),
            pltpu.SemaphoreType.DMA((count * pieces + 1,)),
        ],
        mib=24,
    )(level_factors, present, after)


def level_kernel(first, first_weight, after, state_ref, partner_ref, weight_ref, out_ref):
    del after
    for pair in range(out_ref.shape[0]):
        both = jnp.concatenate([state_ref[first + pair], partner_ref[first + pair]], axis=1)
        out_ref[pair] = contract(both, weight_ref[first_weight + pair], ((1,), (1,))).astype(BF16)


def next_states(name, after, state, partner, weights, first, first_weight, pairs):
    _, columns, lanes = state.shape
    return call(
        functools.partial(level_kernel, first, first_weight),
        name,
        jax.ShapeDtypeStruct((pairs, columns, lanes), BF16),
        [ANYWHERE] + whole_blocks(3),
        4 * pairs * columns * lanes * lanes,
        6 * pairs * columns * lanes,
    )(after, state, partner, weights)


def last_level_kernel(chunks, axis, after, *refs):
    del after
    state_refs, partner_refs, weight_ref = refs[:chunks], refs[chunks : 2 * chunks], refs[2 * chunks]
    out_refs, groups_ref = refs[2 * chunks + 1 : -1], refs[-1]
    me = lax.axis_index(axis)
    pairs, owners, group, _ = groups_ref.shape
    pair = 0
    for state_ref, partner_ref in zip(state_refs, partner_refs):
        for i in range(state_ref.shape[0]):
            both = jnp.concatenate([state_ref[i], partner_ref[i]], axis=1)
            result = contract(both, weight_ref[pair], ((1,), (1,))).astype(BF16)
            for owner in range(owners):
                groups_ref[pair, owner] = result[owner * group : (owner + 1) * group]
            pair += 1
    for k, out_ref in enumerate(out_refs):
        for pair in range(pairs):
            out_ref[pl.ds(pair * group, group)] = groups_ref[pair, me ^ k]


def last_states(after, states, partners, weights, owners):
    _, columns, lanes = states[0].shape
    pairs = sum(state.shape[0] for state in states)
    group = columns // owners
    rows = pairs * group
    if group % 16:
        state, partner = jnp.concatenate(states), jnp.concatenate(partners)
        state = next_states("level", after, state, partner, weights, 0, 0, pairs)
        me = lax.axis_index("order")
        parts = [lax.dynamic_slice_in_dim(state, (me ^ k) * group, group, 1) for k in range(owners)]
        return [part.reshape(rows, lanes) for part in parts]
    return call(
        functools.partial(last_level_kernel, len(states), "order"),
        "last_level",
        [jax.ShapeDtypeStruct((rows, lanes), BF16)] * owners,
        [ANYWHERE] + whole_blocks(2 * len(states) + 1),
        4 * pairs * columns * lanes * lanes,
        6 * pairs * columns * lanes,
        [pltpu.VMEM((pairs, owners, group, lanes), BF16)],
    )(after, *states, *partners, weights)


def near_kernel(group, root_hbm, order_ref, after, root_ref, place_ref, alive_ref, rows_ref, sems):
    del after
    owners, here, _, degrees = root_ref.shape
    slots = rows_ref.shape[1]
    me = lax.axis_index("order")
    copies = []
    for k in range(owners):
        copies.append(pltpu.make_async_copy(root_hbm.at[pl.ds((me ^ k) * here, here)], root_ref.at[k], sems.at[k]))
        copies[-1].start()
    lane = lax.broadcasted_iota(jnp.int32, (1, slots), 1)
    for k in range(owners):
        for slot in range(here):
            pair, half = slot // 2, slot % 2
            row = (pair // group * 2 + half) * group + pair % group
            rows_ref[pl.ds(row, 1), :] = (lane == order_ref[(me ^ k) * here + slot]).astype(F32)
        place_ref[k] = rows_ref[...].astype(BF16)
    degree = lax.axis_index("lat") * degrees + lax.broadcasted_iota(jnp.int32, (degrees, slots), 0)
    window = DEGREES // slots * lax.broadcasted_iota(jnp.int32, (degrees, slots), 1)
    alive_ref[...] = (degree >= window).astype(F32).astype(BF16)
    for copy in copies:
        copy.wait()


def near_roots(root_basis, order_of_slot, owners, group, after):
    slots, rank, degrees = root_basis.shape
    here = slots // owners
    return call(
        functools.partial(near_kernel, group),
        "near_roots",
        [
            jax.ShapeDtypeStruct((owners, here, rank, degrees), BF16),
            jax.ShapeDtypeStruct((owners, here, slots), BF16),
            jax.ShapeDtypeStruct((degrees, slots), BF16),
        ],
        [IN_HBM, IN_SMEM, ANYWHERE],
        slots * slots,
        4 * slots * rank * degrees,
        [pltpu.VMEM((here, slots), F32), pltpu.SemaphoreType.DMA((owners,))],
    )(root_basis, order_of_slot, after)


def root_kernel(group, first, last, *refs):
    refs = list(refs)
    so_far_ref = refs.pop(0) if last else None
    root_ref, place_ref, alive_ref = refs[:3]
    count = len(refs) - (7 if last else 5)
    state_refs = refs[3 : 3 + count]
    out_ref, rows_ref = refs[3 + count : 5 + count]
    natural_ref = refs[5 + count] if last else out_ref
    fields, parts, degrees, slots = out_ref.shape
    columns = fields * parts
    rank = root_ref.shape[2]
    group_rows = group * columns
    here = place_ref.shape[1]
    steps = state_refs[0].shape[0] // group_rows
    shape = (group_rows, 2 * rank)
    row_pair = lax.broadcasted_iota(jnp.int32, shape, 0) // columns
    row_half = lax.broadcasted_iota(jnp.int32, shape, 1) // rank
    masks = [[(row_pair == pair) & (row_half == half) for pair in range(group)] for half in range(2)]
    empty = jnp.zeros(shape, BF16)
    for i, state_ref in enumerate(state_refs):
        for step in range(steps):
            state = state_ref[pl.ds(step * group_rows, group_rows)]
            left = jnp.concatenate(
                [jnp.concatenate([jnp.where(m, state, empty) for m in line], axis=1) for line in masks], axis=0
            )
            right = root_ref[first + i, pl.ds(step * group * 2, group * 2)].reshape(group * 2 * rank, degrees)
            product = contract(left, right, ((1,), (0,)))
            begin = (i * steps + step) * 2 * group_rows
            for tile in range(degrees // 128):
                rows_ref[tile, pl.ds(begin, 2 * group_rows), :] = product[:, tile * 128 : (tile + 1) * 128]
    place = place_ref[pl.ds(first, count)].reshape(count * here, slots)
    copies = []
    for column in range(columns):
        for tile in range(degrees // 128):
            span = slice(tile * 128, (tile + 1) * 128)
            one = rows_ref[tile, pl.ds(column, count * here, stride=columns), :].astype(BF16)
            natural = contract(one.T, place, ((1,), (0,))).astype(BF16)
            where = (column // 2, column % 2, span)
            if last:
                natural = natural + so_far_ref[where]
                natural = jnp.where(alive_ref[span] != 0, natural, jnp.zeros((), BF16))
            natural_ref[where] = natural
        if last:
            where = (column // 2, column % 2)
            copies.append(pltpu.make_async_copy(natural_ref.at[where], out_ref.at[where], refs[-1].at[column]))
            copies[-1].start()
    for copy in copies:
        copy.wait()


def spectra_of(states, roots, places, alive, so_far, first, group):
    state_rows, lanes = states[0].shape
    owners, here, rank, degrees = roots.shape
    slots = places.shape[2]
    columns = state_rows * 2 // here
    last = so_far is not None
    shape = (columns // 2, 2, degrees, slots)
    inputs = ([so_far] if last else []) + [roots, places, alive, *states]
    scratch = [pltpu.VMEM((degrees // 128, len(states) * here * columns, 128), F32)]
    more = {}
    if last:
        scratch += [pltpu.VMEM(shape, BF16), pltpu.SemaphoreType.DMA((columns,))]
        more["out_specs"] = IN_HBM
    return call(
        functools.partial(root_kernel, group, first, last),
        "root",
        jax.ShapeDtypeStruct(shape, BF16),
        whole_blocks(len(inputs)),
        2 * len(states) * here * rank * degrees * columns,
        2 * len(states) * here * rank * degrees,
        scratch,
        mib=24,
        **more,
    )(*inputs)


def per_device(
    fourier, quad_weights, leaf_basis, level_factors, sparsity, root_basis, order_of_slot
):
    slots, columns, lats = fourier.shape
    owners = lax.axis_size("order")
    levels = level_factors.shape[1]
    group = max(2, 16 * owners // columns)
    first = slots // 2
    sizes = [first, slots - first]
    begins = [0, first]
    present = in_hbm(sparsity.transpose(1, 2, 0))
    fourier, leaf_basis, level_factors, root_basis = map(in_hbm, (fourier, leaf_basis, level_factors, root_basis))
    quad_weights = in_hbm(quad_weights.reshape(1, lats))

    def swap(array, axis, bits):
        return lax.ppermute(array, axis, [(i, i ^ bits) for i in range(lax.axis_size(axis))])

    state = leaf_states(fourier, quad_weights, leaf_basis)
    partner = swap(state, "lat", 1)
    weights = level_weights(level_factors, present, (0,), state)
    states = [
        next_states(f"level0_{c}", state, state, partner, weights[0], begins[c] // 2, begins[c] // 2, sizes[c] // 2)
        for c in range(2)
    ]
    weights += level_weights(level_factors, present, tuple(range(1, levels)), states[1])
    for level in range(1, levels):
        partners = [swap(state, "lat", 1 << level) for state in states]
        if level < levels - 1:
            states = [
                next_states(
                    f"level{level}_{c}", states[c], states[c], partners[c], weights[level], 0, begins[c] // 2, sizes[c] // 2
                )
                for c in range(2)
            ]
    roots, places, alive = near_roots(root_basis, order_of_slot, owners, group, states[1])
    sent = last_states(alive, states, partners, weights[-1], owners)
    arrived = [swap(part, "order", k) if k else part for k, part in enumerate(sent)]
    early = 3 * owners // 4
    spectra = spectra_of(arrived[:early], roots, places, alive, None, 0, group)
    return spectra_of(arrived[early:], roots, places, alive, spectra, early, group)


def solution(mesh):
    return jax.shard_map(
        per_device,
        mesh=mesh,
        in_specs=(
            P("order", None, "lat"),
            P("lat"),
            P("order", None, "lat"),
            P("order", None, None, "lat", None, None),
            P("order", None, "lat"),
            P(None, None, "lat"),
            P(),
        ),
        out_specs=P("order", None, "lat", None),
        check_vma=False,
    )
```

```python
import functools

import jax
import jax.numpy as jnp
from jax import lax
from jax.experimental import pallas as pl
from jax.experimental.pallas import tpu as pltpu
from jax.sharding import PartitionSpec as P

DEGREES = 2048
F32, BF16 = jnp.float32, jnp.bfloat16
MIB = 1 << 20
IN_HBM = pl.BlockSpec(memory_space=pltpu.HBM)
IN_SMEM = pl.BlockSpec(memory_space=pltpu.SMEM)
ANYWHERE = pl.BlockSpec(memory_space=pl.ANY)


def contract(lhs, rhs, dims):
    return lax.dot_general(lhs, rhs, (dims, ((), ())), preferred_element_type=F32)


def in_hbm(array):
    return pltpu.with_memory_space_constraint(array, pltpu.HBM)


def call(kernel, name, out_shape, in_specs, flops, size, scratch=(), mib=16, **more):
    return pl.pallas_call(
        kernel,
        out_shape=out_shape,
        in_specs=in_specs,
        scratch_shapes=list(scratch),
        compiler_params=pltpu.CompilerParams(vmem_limit_bytes=mib * MIB),
        cost_estimate=pl.CostEstimate(flops=flops // 1000, bytes_accessed=size // 1000, transcendentals=0),
        name=name,
        **more,
    )


def whole_blocks(count):
    return [pl.BlockSpec()] * count


def leaf_kernel(
    pieces, group, fourier_hbm, weight_hbm, leaf_hbm, state_ref, fourier_ref, weight_ref, leaf_ref, sems
):
    side = lax.axis_index("order") & 1
    slots, columns, lats = fourier_ref.shape
    rank = leaf_ref.shape[1]
    per = slots // pieces
    copies = [pltpu.make_async_copy(weight_hbm, weight_ref, sems.at[0])]
    for piece in range(pieces):
        part = pl.ds(piece * per, per)
        copies.append(pltpu.make_async_copy(fourier_hbm.at[part], fourier_ref.at[part], sems.at[1 + 2 * piece]))
        copies.append(pltpu.make_async_copy(leaf_hbm.at[part], leaf_ref.at[part], sems.at[2 + 2 * piece]))
    for copy in copies:
        copy.start()
    copies[0].wait()
    weight = weight_ref[...]
    mine = lax.broadcasted_iota(jnp.int32, (columns, 2 * rank), 1) < rank
    for pair in range(slots // 2):
        if 2 * pair % per == 0:
            copies[1 + 2 * (2 * pair // per)].wait()
            copies[2 + 2 * (2 * pair // per)].wait()
        both = pl.ds(2 * pair, 2)
        weighted = (fourier_ref[both].astype(F32) * weight[None]).astype(BF16)
        product = contract(
            weighted.reshape(2 * columns, lats), leaf_ref[both].reshape(2 * rank, lats), ((1,), (1,))
        )
        state = jnp.where(mine, product[:columns], product[columns:]).astype(BF16)
        if group % 16:
            state_ref[pair] = state
            continue
        for owner in range(columns // group):
            rows = pl.ds(owner // 2 * group, group)
            state_ref[pair, owner % 2 ^ side, rows] = state[owner * group : (owner + 1) * group]


def leaf_states(fourier, quad_weights, leaf_basis, owners):
    slots, columns, lats = fourier.shape
    rank = leaf_basis.shape[1]
    pairs, half, lanes, group = slots // 2, columns // 2, 2 * rank, columns // owners
    pieces = 2
    state = call(
        functools.partial(leaf_kernel, pieces, group),
        "leaf",
        jax.ShapeDtypeStruct((pairs, columns, lanes) if group % 16 else (pairs, 2, half, lanes), BF16),
        [IN_HBM] * 3,
        2 * slots * columns * rank * lats,
        4 * slots * columns * lats,
        [
            pltpu.VMEM((slots, columns, lats), BF16),
            pltpu.VMEM((1, lats), F32),
            pltpu.VMEM((slots, rank, lats), BF16),
            pltpu.SemaphoreType.DMA((1 + 2 * pieces,)),
        ],
    )(fourier, quad_weights, leaf_basis)
    if group % 16:
        side = lax.axis_index("order") & 1
        state = state.reshape(pairs, owners // 2, 2, group, lanes)
        sides = [lax.dynamic_index_in_dim(state, side ^ i, 2, False).reshape(pairs, half, lanes) for i in range(2)]
        state = jnp.stack(sides, axis=1)
    return state


def factor_kernel(levels, pieces, factor_hbm, present_hbm, after, *refs):
    del after
    weight_refs, (factor_ref, present_ref, sems) = refs[: len(levels)], refs[len(levels) :]
    present_copy = pltpu.make_async_copy(present_hbm, present_ref, sems.at[len(levels) * pieces])
    present_copy.start()
    _, slots, _, rank, _ = factor_ref.shape
    per = slots // pieces
    copies = {}
    for i, level in enumerate(levels):
        for piece in range(pieces):
            part = pl.ds(piece * per, per)
            copies[i, piece] = pltpu.make_async_copy(
                factor_hbm.at[part, level, :, 0], factor_ref.at[i, part], sems.at[i * pieces + piece]
            )
            copies[i, piece].start()
    empty = jnp.zeros((rank, rank), BF16)
    present_copy.wait()
    for i, level in enumerate(levels):
        for pair in range(slots // 2):
            if 2 * pair % per == 0:
                copies[i, 2 * pair // per].wait()
            for half in range(2):
                first, second = (factor_ref[i, slot, half] for slot in (2 * pair, 2 * pair + 1))
                if half:
                    first = jnp.where(present_ref[level, 0, 2 * pair] != 0, first, empty)
                    second = jnp.where(present_ref[level, 0, 2 * pair + 1] != 0, second, empty)
                if len(weight_refs[i].shape) == 4:
                    weight_refs[i][pair, half] = jnp.concatenate([first, second], axis=1)
                    continue
                lanes = pl.ds(half * 2 * rank, 2 * rank)
                weight_refs[i][pair, :rank, lanes] = jnp.concatenate([first, empty], axis=1)
                weight_refs[i][pair, rank:, lanes] = jnp.concatenate([empty, second], axis=1)


def level_weights(level_factors, present, levels, after):
    slots, last, _, _, rank, _ = level_factors.shape
    count, pieces = len(levels), 2
    return call(
        functools.partial(factor_kernel, levels, pieces),
        "factors",
        [
            jax.ShapeDtypeStruct((slots // 2, *((2, rank, 2 * rank) if level == last - 1 else (2 * rank, 4 * rank))), BF16)
            for level in levels
        ],
        [IN_HBM, IN_HBM, ANYWHERE],
        slots * rank * rank * 4 * count,
        slots * rank * rank * 16 * count,
        [
            pltpu.VMEM((count, slots, 2, rank, rank), BF16),
            pltpu.SMEM(present.shape, jnp.int32),
            pltpu.SemaphoreType.DMA((count * pieces + 1,)),
        ],
        mib=24,
    )(level_factors, present, after)


def fetch_kernel(axis, both_hbm, after, other_ref, sem):
    del after
    copy = pltpu.make_async_copy(both_hbm.at[lax.axis_index(axis) & 1 ^ 1], other_ref, sem)
    copy.start()
    copy.wait()


def fetch_other(both, after):
    return call(
        functools.partial(fetch_kernel, "order"),
        "fetch_other",
        jax.ShapeDtypeStruct(both.shape[1:], BF16),
        [IN_HBM, ANYWHERE],
        1,
        both.size,
        [pltpu.SemaphoreType.DMA],
    )(in_hbm(both), after)


def level_kernel(side, state_ref, partner_ref, weight_ref, out_ref):
    for pair in range(out_ref.shape[0]):
        at = pair if side is None else (pair, side)
        both = jnp.concatenate([state_ref[at], partner_ref[at]], axis=1)
        out_ref[pair] = contract(both, weight_ref[pair], ((1,), (1,))).astype(BF16)


def next_states(name, state, partner, weights, side=None):
    pairs, rows, lanes = state.shape[0], *state.shape[-2:]
    return call(
        functools.partial(level_kernel, side),
        name,
        jax.ShapeDtypeStruct((pairs, rows, lanes), BF16),
        whole_blocks(3),
        4 * pairs * rows * lanes * lanes,
        6 * pairs * rows * lanes,
    )(state, partner, weights)


def last_level_kernel(axis, after, state_ref, partner_ref, packed_ref, *refs):
    del after
    out_refs, groups_ref = refs[:-1], refs[-1]
    me = lax.axis_index(axis) // 2
    pairs, owners, group, lanes = groups_ref.shape
    rank = packed_ref.shape[2]
    shape = (rank, lanes)
    first = lax.broadcasted_iota(jnp.int32, shape, 1) < rank
    empty = jnp.zeros(shape, BF16)
    for pair in range(pairs):
        packed = [packed_ref[pair, half] for half in range(2)]
        weight = jnp.concatenate(
            [
                jnp.concatenate([jnp.where(first, part, empty) for part in packed], axis=1),
                jnp.concatenate([jnp.where(first, empty, part) for part in packed], axis=1),
            ],
            axis=0,
        )
        both = jnp.concatenate([state_ref[pair], partner_ref[pair]], axis=1)
        result = contract(both, weight, ((1,), (1,))).astype(BF16)
        if len(out_refs) == 1:
            out_refs[0][pair] = result
            continue
        for owner in range(owners):
            groups_ref[pair, owner] = result[owner * group : (owner + 1) * group]
    if len(out_refs) > 1:
        for k, out_ref in enumerate(out_refs):
            for pair in range(pairs):
                out_ref[pl.ds(pair * group, group)] = groups_ref[pair, me ^ k]


def last_states(name, after, state, partner, packed, owners):
    pairs, columns, lanes = state.shape
    group = columns // owners
    rows = pairs * group
    by_owner = group % 16 == 0 and owners > 1
    parts = call(
        functools.partial(last_level_kernel, "order"),
        name,
        [jax.ShapeDtypeStruct((rows, lanes), BF16)] * owners if by_owner else [jax.ShapeDtypeStruct(state.shape, BF16)],
        [ANYWHERE] + whole_blocks(3),
        4 * pairs * columns * lanes * lanes,
        6 * pairs * columns * lanes,
        [pltpu.VMEM((pairs, owners, group, lanes), BF16)],
    )(after, state, partner, packed)
    if by_owner:
        return parts
    me = lax.axis_index("order") // 2
    parts = [lax.dynamic_slice_in_dim(parts[0], (me ^ k) * group, group, 1) for k in range(owners)]
    return [part.reshape(rows, lanes) for part in parts]


def near_kernel(group, root_hbm, order_ref, after, root_ref, place_ref, alive_ref, rows_ref, sems):
    del after
    owners, here, _, degrees = root_ref.shape
    slots = rows_ref.shape[1]
    me = lax.axis_index("order")
    copies = []
    for k in range(owners):
        copies.append(pltpu.make_async_copy(root_hbm.at[pl.ds((me ^ k) * here, here)], root_ref.at[k], sems.at[k]))
        copies[-1].start()
    lane = lax.broadcasted_iota(jnp.int32, (1, slots), 1)
    for k in range(owners):
        for slot in range(here):
            pair, half = slot // 2, slot % 2
            row = (pair // group * 2 + half) * group + pair % group
            rows_ref[pl.ds(row, 1), :] = (lane == order_ref[(me ^ k) * here + slot]).astype(F32)
        place_ref[k] = rows_ref[...].astype(BF16)
    degree = lax.axis_index("lat") * degrees + lax.broadcasted_iota(jnp.int32, (degrees, slots), 0)
    window = DEGREES // slots * lax.broadcasted_iota(jnp.int32, (degrees, slots), 1)
    alive_ref[...] = (degree >= window).astype(F32).astype(BF16)
    for copy in copies:
        copy.wait()


def near_roots(root_basis, order_of_slot, owners, group, after):
    slots, rank, degrees = root_basis.shape
    here = slots // owners
    return call(
        functools.partial(near_kernel, group),
        "near_roots",
        [
            jax.ShapeDtypeStruct((owners, here, rank, degrees), BF16),
            jax.ShapeDtypeStruct((owners, here, slots), BF16),
            jax.ShapeDtypeStruct((degrees, slots), BF16),
        ],
        [IN_HBM, IN_SMEM, ANYWHERE],
        slots * slots,
        4 * slots * rank * degrees,
        [pltpu.VMEM((here, slots), F32), pltpu.SemaphoreType.DMA((owners,))],
    )(root_basis, order_of_slot, after)


def root_kernel(group, first, last, *refs):
    refs = list(refs)
    so_far_ref = refs.pop(0) if last else None
    root_ref, place_ref, alive_ref = refs[:3]
    count = len(refs) - (7 if last else 5)
    state_refs = refs[3 : 3 + count]
    out_ref, rows_ref = refs[3 + count : 5 + count]
    natural_ref = refs[5 + count] if last else out_ref
    fields, parts, degrees, slots = out_ref.shape
    columns = fields * parts
    rank = root_ref.shape[2]
    group_rows = group * columns
    here = place_ref.shape[1]
    steps = state_refs[0].shape[0] // group_rows
    shape = (group_rows, 2 * rank)
    row_pair = lax.broadcasted_iota(jnp.int32, shape, 0) // columns
    row_half = lax.broadcasted_iota(jnp.int32, shape, 1) // rank
    masks = [[(row_pair == pair) & (row_half == half) for pair in range(group)] for half in range(2)]
    empty = jnp.zeros(shape, BF16)
    for i, state_ref in enumerate(state_refs):
        for step in range(steps):
            state = state_ref[pl.ds(step * group_rows, group_rows)]
            left = jnp.concatenate(
                [jnp.concatenate([jnp.where(m, state, empty) for m in line], axis=1) for line in masks], axis=0
            )
            right = root_ref[first + i, pl.ds(step * group * 2, group * 2)].reshape(group * 2 * rank, degrees)
            product = contract(left, right, ((1,), (0,)))
            begin = (i * steps + step) * 2 * group_rows
            for tile in range(degrees // 128):
                rows_ref[tile, pl.ds(begin, 2 * group_rows), :] = product[:, tile * 128 : (tile + 1) * 128]
    place = place_ref[pl.ds(first, count)].reshape(count * here, slots)
    copies = []
    for column in range(columns):
        for tile in range(degrees // 128):
            span = slice(tile * 128, (tile + 1) * 128)
            one = rows_ref[tile, pl.ds(column, count * here, stride=columns), :].astype(BF16)
            natural = contract(one.T, place, ((1,), (0,))).astype(BF16)
            where = (column // 2, column % 2, span)
            if last:
                natural = natural + so_far_ref[where]
                natural = jnp.where(alive_ref[span] != 0, natural, jnp.zeros((), BF16))
            natural_ref[where] = natural
        if last:
            where = (column // 2, column % 2)
            copies.append(pltpu.make_async_copy(natural_ref.at[where], out_ref.at[where], refs[-1].at[column]))
            copies[-1].start()
    for copy in copies:
        copy.wait()


def spectra_of(states, roots, places, alive, so_far, first, group):
    state_rows, lanes = states[0].shape
    owners, here, rank, degrees = roots.shape
    slots = places.shape[2]
    columns = state_rows * 2 // here
    last = so_far is not None
    shape = (columns // 2, 2, degrees, slots)
    inputs = ([so_far] if last else []) + [roots, places, alive, *states]
    scratch = [pltpu.VMEM((degrees // 128, len(states) * here * columns, 128), F32)]
    more = {}
    if last:
        scratch += [pltpu.VMEM(shape, BF16), pltpu.SemaphoreType.DMA((columns,))]
        more["out_specs"] = IN_HBM
    return call(
        functools.partial(root_kernel, group, first, last),
        "root",
        jax.ShapeDtypeStruct(shape, BF16),
        whole_blocks(len(inputs)),
        2 * len(states) * here * rank * degrees * columns,
        2 * len(states) * here * rank * degrees,
        scratch,
        mib=24,
        **more,
    )(*inputs)


def per_device(
    fourier, quad_weights, leaf_basis, level_factors, sparsity, root_basis, order_of_slot
):
    slots, columns, lats = fourier.shape
    owners = lax.axis_size("order")
    levels = level_factors.shape[1]
    group = max(2, 16 * owners // columns)
    present = in_hbm(sparsity.transpose(1, 2, 0))
    fourier, leaf_basis, level_factors, root_basis = map(in_hbm, (fourier, leaf_basis, level_factors, root_basis))
    quad_weights = in_hbm(quad_weights.reshape(1, lats))

    def swap(array, axis, bits):
        return lax.ppermute(array, axis, [(i, i ^ bits) for i in range(lax.axis_size(axis))])

    def swap_both(array, order_bits, lat_bits):
        blocks = lax.axis_size("lat")
        pairs = [
            (o * blocks + b, (o ^ order_bits) * blocks + (b ^ lat_bits)) for o in range(owners) for b in range(blocks)
        ]
        return lax.ppermute(array, ("order", "lat"), pairs)

    state = leaf_states(fourier, quad_weights, leaf_basis, owners)
    partner = swap(state, "lat", 1)
    weights = list(level_weights(level_factors, present, (0, levels - 1), state))
    packed = weights.pop()
    neighbours = [[i, i ^ 1] for i in range(0, owners, 2)]
    both_packed = lax.all_gather(packed, "order", axis_index_groups=neighbours)
    states = [next_states(f"level0_{c}", state, partner, weights[0], c) for c in range(2)]
    weights += level_weights(level_factors, present, tuple(range(1, levels - 1)), states[1])
    for level in range(1, levels - 1):
        partners = [swap(state, "lat", 1 << level) for state in states]
        states = [next_states(f"level{level}_{c}", states[c], partners[c], weights[level]) for c in range(2)]
    top = 1 << levels - 1
    partner = swap(states[0], "lat", top)
    other_partner = swap_both(states[1], 1, top)
    other = swap(states[1], "order", 1)
    roots, places, alive = near_roots(root_basis, order_of_slot, owners, group, states[1])
    other_packed = fetch_other(both_packed, alive)
    both = (
        last_states("last_own", other_packed, states[0], partner, packed, owners // 2),
        last_states("last_other", other_packed, other, other_partner, other_packed, owners // 2),
    )
    arrived = [swap(both[k % 2][k // 2], "order", k // 2 * 2) if k > 1 else both[k][0] for k in range(owners)]
    early = 3 * owners // 4
    spectra = spectra_of(arrived[:early], roots, places, alive, None, 0, group)
    return spectra_of(arrived[early:], roots, places, alive, spectra, early, group)


def solution(mesh):
    return jax.shard_map(
        per_device,
        mesh=mesh,
        in_specs=(
            P("order", None, "lat"),
            P("lat"),
            P("order", None, "lat"),
            P("order", None, None, "lat", None, None),
            P("order", None, "lat"),
            P(None, None, "lat"),
            P(),
        ),
        out_specs=P("order", None, "lat", None),
        check_vma=False,
    )
```

```python
import functools

import jax
import jax.numpy as jnp
from jax import lax
from jax.experimental import pallas as pl
from jax.experimental.pallas import tpu as pltpu
from jax.sharding import PartitionSpec as P

DEGREES = 2048
F32, BF16 = jnp.float32, jnp.bfloat16
MIB = 1 << 20
IN_HBM = pl.BlockSpec(memory_space=pltpu.HBM)
IN_SMEM = pl.BlockSpec(memory_space=pltpu.SMEM)
ANYWHERE = pl.BlockSpec(memory_space=pl.ANY)


def contract(lhs, rhs, dims):
    return lax.dot_general(lhs, rhs, (dims, ((), ())), preferred_element_type=F32)


def in_hbm(array):
    return pltpu.with_memory_space_constraint(array, pltpu.HBM)


def call(kernel, name, out_shape, in_specs, flops, size, scratch=(), mib=16, **more):
    return pl.pallas_call(
        kernel,
        out_shape=out_shape,
        in_specs=in_specs,
        scratch_shapes=list(scratch),
        compiler_params=pltpu.CompilerParams(vmem_limit_bytes=mib * MIB),
        cost_estimate=pl.CostEstimate(flops=flops // 1000, bytes_accessed=size // 1000, transcendentals=0),
        name=name,
        **more,
    )


def whole_blocks(count):
    return [pl.BlockSpec()] * count


def leaf_kernel(
    pieces, group, fourier_hbm, weight_hbm, leaf_hbm, state_ref, fourier_ref, weight_ref, leaf_ref, sems
):
    side = lax.axis_index("order") & 1
    slots, columns, lats = fourier_ref.shape
    rank = leaf_ref.shape[1]
    per = slots // pieces
    copies = [pltpu.make_async_copy(weight_hbm, weight_ref, sems.at[0])]
    for piece in range(pieces):
        part = pl.ds(piece * per, per)
        copies.append(pltpu.make_async_copy(fourier_hbm.at[part], fourier_ref.at[part], sems.at[1 + 2 * piece]))
        copies.append(pltpu.make_async_copy(leaf_hbm.at[part], leaf_ref.at[part], sems.at[2 + 2 * piece]))
    for copy in copies:
        copy.start()
    copies[0].wait()
    weight = weight_ref[...]
    mine = lax.broadcasted_iota(jnp.int32, (columns, 2 * rank), 1) < rank
    for pair in range(slots // 2):
        if 2 * pair % per == 0:
            copies[1 + 2 * (2 * pair // per)].wait()
            copies[2 + 2 * (2 * pair // per)].wait()
        both = pl.ds(2 * pair, 2)
        weighted = (fourier_ref[both].astype(F32) * weight[None]).astype(BF16)
        product = contract(
            weighted.reshape(2 * columns, lats), leaf_ref[both].reshape(2 * rank, lats), ((1,), (1,))
        )
        state = jnp.where(mine, product[:columns], product[columns:]).astype(BF16)
        if group % 16:
            state_ref[pair] = state
            continue
        for owner in range(columns // group):
            rows = pl.ds(owner // 2 * group, group)
            state_ref[pair, owner % 2 ^ side, rows] = state[owner * group : (owner + 1) * group]


def leaf_states(fourier, quad_weights, leaf_basis, owners):
    slots, columns, lats = fourier.shape
    rank = leaf_basis.shape[1]
    pairs, half, lanes, group = slots // 2, columns // 2, 2 * rank, columns // owners
    pieces = 2
    state = call(
        functools.partial(leaf_kernel, pieces, group),
        "leaf",
        jax.ShapeDtypeStruct((pairs, columns, lanes) if group % 16 else (pairs, 2, half, lanes), BF16),
        [IN_HBM] * 3,
        2 * slots * columns * rank * lats,
        4 * slots * columns * lats,
        [
            pltpu.VMEM((slots, columns, lats), BF16),
            pltpu.VMEM((1, lats), F32),
            pltpu.VMEM((slots, rank, lats), BF16),
            pltpu.SemaphoreType.DMA((1 + 2 * pieces,)),
        ],
    )(fourier, quad_weights, leaf_basis)
    if group % 16:
        side = lax.axis_index("order") & 1
        state = state.reshape(pairs, owners // 2, 2, group, lanes)
        sides = [lax.dynamic_index_in_dim(state, side ^ i, 2, False).reshape(pairs, half, lanes) for i in range(2)]
        state = jnp.stack(sides, axis=1)
    return state


def factor_kernel(levels, pieces, factor_hbm, present_hbm, after, *refs):
    del after
    weight_refs, (factor_ref, present_ref, sems) = refs[:-3], refs[-3:]
    present_copy = pltpu.make_async_copy(present_hbm, present_ref, sems.at[len(levels) * pieces])
    present_copy.start()
    _, slots, _, rank, _ = factor_ref.shape
    per = slots // pieces
    copies = {}
    for i, level in enumerate(levels):
        for piece in range(pieces):
            part = pl.ds(piece * per, per)
            copies[i, piece] = pltpu.make_async_copy(
                factor_hbm.at[part, level, :, 0], factor_ref.at[i, part], sems.at[i * pieces + piece]
            )
            copies[i, piece].start()
    empty = jnp.zeros((rank, rank), BF16)
    present_copy.wait()
    for i, level in enumerate(levels):
        for pair in range(slots // 2):
            if 2 * pair % per == 0:
                copies[i, 2 * pair // per].wait()
            for half in range(2):
                first, second = (factor_ref[i, slot, half] for slot in (2 * pair, 2 * pair + 1))
                if half:
                    first = jnp.where(present_ref[level, 0, 2 * pair] != 0, first, empty)
                    second = jnp.where(present_ref[level, 0, 2 * pair + 1] != 0, second, empty)
                if weight_refs[i].shape[1] == rank:
                    weight_refs[i + half][pair] = jnp.concatenate([first, second], axis=1)
                    continue
                lanes = pl.ds(half * 2 * rank, 2 * rank)
                weight_refs[i][pair, :rank, lanes] = jnp.concatenate([first, empty], axis=1)
                weight_refs[i][pair, rank:, lanes] = jnp.concatenate([empty, second], axis=1)


def level_weights(level_factors, present, levels, after):
    slots, last, _, _, rank, _ = level_factors.shape
    count, pieces = len(levels), 2
    return call(
        functools.partial(factor_kernel, levels, pieces),
        "factors",
        [
            jax.ShapeDtypeStruct((slots // 2, *((rank, 2 * rank) if level == last - 1 else (2 * rank, 4 * rank))), BF16)
            for level in levels
            for _ in range(1 + (level == last - 1))
        ],
        [IN_HBM, IN_HBM, ANYWHERE],
        slots * rank * rank * 4 * count,
        slots * rank * rank * 16 * count,
        [
            pltpu.VMEM((count, slots, 2, rank, rank), BF16),
            pltpu.SMEM(present.shape, jnp.int32),
            pltpu.SemaphoreType.DMA((count * pieces + 1,)),
        ],
        mib=24,
    )(level_factors, present, after)


def level_kernel(side, state_ref, partner_ref, weight_ref, out_ref):
    for pair in range(out_ref.shape[0]):
        at = pair if side is None else (pair, side)
        both = jnp.concatenate([state_ref[at], partner_ref[at]], axis=1)
        out_ref[pair] = contract(both, weight_ref[pair], ((1,), (1,))).astype(BF16)


def next_states(name, state, partner, weights, side=None):
    pairs, rows, lanes = state.shape[0], *state.shape[-2:]
    return call(
        functools.partial(level_kernel, side),
        name,
        jax.ShapeDtypeStruct((pairs, rows, lanes), BF16),
        whole_blocks(3),
        4 * pairs * rows * lanes * lanes,
        6 * pairs * rows * lanes,
    )(state, partner, weights)


def last_level_kernel(axis, after, state_ref, partner_ref, own_ref, cross_ref, *refs):
    del after
    out_refs, groups_ref = refs[:-1], refs[-1]
    me = lax.axis_index(axis) // 2
    pairs, owners, group, lanes = groups_ref.shape
    rank = own_ref.shape[1]
    shape = (rank, lanes)
    first = lax.broadcasted_iota(jnp.int32, shape, 1) < rank
    empty = jnp.zeros(shape, BF16)
    for pair in range(pairs):
        packed = [own_ref[pair], cross_ref[pair]]
        weight = jnp.concatenate(
            [
                jnp.concatenate([jnp.where(first, part, empty) for part in packed], axis=1),
                jnp.concatenate([jnp.where(first, empty, part) for part in packed], axis=1),
            ],
            axis=0,
        )
        both = jnp.concatenate([state_ref[pair], partner_ref[pair]], axis=1)
        result = contract(both, weight, ((1,), (1,))).astype(BF16)
        if len(out_refs) == 1:
            out_refs[0][pair] = result
            continue
        for owner in range(owners):
            groups_ref[pair, owner] = result[owner * group : (owner + 1) * group]
    if len(out_refs) > 1:
        for k, out_ref in enumerate(out_refs):
            for pair in range(pairs):
                out_ref[pl.ds(pair * group, group)] = groups_ref[pair, me ^ k]


def last_states(name, after, state, partner, packed, owners):
    pairs, columns, lanes = state.shape
    group = columns // owners
    rows = pairs * group
    by_owner = group % 16 == 0 and owners > 1
    parts = call(
        functools.partial(last_level_kernel, "order"),
        name,
        [jax.ShapeDtypeStruct((rows, lanes), BF16)] * owners if by_owner else [jax.ShapeDtypeStruct(state.shape, BF16)],
        [ANYWHERE] + whole_blocks(4),
        4 * pairs * columns * lanes * lanes,
        6 * pairs * columns * lanes,
        [pltpu.VMEM((pairs, owners, group, lanes), BF16)],
    )(after, state, partner, *packed)
    if by_owner:
        return parts
    me = lax.axis_index("order") // 2
    parts = [lax.dynamic_slice_in_dim(parts[0], (me ^ k) * group, group, 1) for k in range(owners)]
    return [part.reshape(rows, lanes) for part in parts]


def near_kernel(group, root_hbm, order_ref, after, root_ref, place_ref, alive_ref, rows_ref, sems):
    del after
    owners, here, _, degrees = root_ref.shape
    slots = rows_ref.shape[1]
    me = lax.axis_index("order")
    copies = []
    for k in range(owners):
        copies.append(pltpu.make_async_copy(root_hbm.at[pl.ds((me ^ k) * here, here)], root_ref.at[k], sems.at[k]))
        copies[-1].start()
    lane = lax.broadcasted_iota(jnp.int32, (1, slots), 1)
    for k in range(owners):
        for slot in range(here):
            pair, half = slot // 2, slot % 2
            row = (pair // group * 2 + half) * group + pair % group
            rows_ref[pl.ds(row, 1), :] = (lane == order_ref[(me ^ k) * here + slot]).astype(F32)
        place_ref[k] = rows_ref[...].astype(BF16)
    degree = lax.axis_index("lat") * degrees + lax.broadcasted_iota(jnp.int32, (degrees, slots), 0)
    window = DEGREES // slots * lax.broadcasted_iota(jnp.int32, (degrees, slots), 1)
    alive_ref[...] = (degree >= window).astype(F32).astype(BF16)
    for copy in copies:
        copy.wait()


def near_roots(root_basis, order_of_slot, owners, group, after):
    slots, rank, degrees = root_basis.shape
    here = slots // owners
    return call(
        functools.partial(near_kernel, group),
        "near_roots",
        [
            jax.ShapeDtypeStruct((owners, here, rank, degrees), BF16),
            jax.ShapeDtypeStruct((owners, here, slots), BF16),
            jax.ShapeDtypeStruct((degrees, slots), BF16),
        ],
        [IN_HBM, IN_SMEM, ANYWHERE],
        slots * slots,
        4 * slots * rank * degrees,
        [pltpu.VMEM((here, slots), F32), pltpu.SemaphoreType.DMA((owners,))],
    )(root_basis, order_of_slot, after)


def root_kernel(group, first, last, *refs):
    refs = list(refs)
    so_far_ref = refs.pop(0) if last else None
    root_ref, place_ref, alive_ref = refs[:3]
    count = len(refs) - (7 if last else 5)
    state_refs = refs[3 : 3 + count]
    out_ref, rows_ref = refs[3 + count : 5 + count]
    natural_ref = refs[5 + count] if last else out_ref
    fields, parts, degrees, slots = out_ref.shape
    columns = fields * parts
    rank = root_ref.shape[2]
    group_rows = group * columns
    here = place_ref.shape[1]
    steps = state_refs[0].shape[0] // group_rows
    shape = (group_rows, 2 * rank)
    row_pair = lax.broadcasted_iota(jnp.int32, shape, 0) // columns
    row_half = lax.broadcasted_iota(jnp.int32, shape, 1) // rank
    masks = [[(row_pair == pair) & (row_half == half) for pair in range(group)] for half in range(2)]
    empty = jnp.zeros(shape, BF16)
    for i, state_ref in enumerate(state_refs):
        for step in range(steps):
            state = state_ref[pl.ds(step * group_rows, group_rows)]
            left = jnp.concatenate(
                [jnp.concatenate([jnp.where(m, state, empty) for m in line], axis=1) for line in masks], axis=0
            )
            right = root_ref[first + i, pl.ds(step * group * 2, group * 2)].reshape(group * 2 * rank, degrees)
            product = contract(left, right, ((1,), (0,)))
            begin = (i * steps + step) * 2 * group_rows
            for tile in range(degrees // 128):
                rows_ref[tile, pl.ds(begin, 2 * group_rows), :] = product[:, tile * 128 : (tile + 1) * 128]
    place = place_ref[pl.ds(first, count)].reshape(count * here, slots)
    copies = []
    for column in range(columns):
        for tile in range(degrees // 128):
            span = slice(tile * 128, (tile + 1) * 128)
            one = rows_ref[tile, pl.ds(column, count * here, stride=columns), :].astype(BF16)
            natural = contract(one.T, place, ((1,), (0,))).astype(BF16)
            where = (column // 2, column % 2, span)
            if last:
                natural = natural + so_far_ref[where]
                natural = jnp.where(alive_ref[span] != 0, natural, jnp.zeros((), BF16))
            natural_ref[where] = natural
        if last:
            where = (column // 2, column % 2)
            copies.append(pltpu.make_async_copy(natural_ref.at[where], out_ref.at[where], refs[-1].at[column]))
            copies[-1].start()
    for copy in copies:
        copy.wait()


def spectra_of(states, roots, places, alive, so_far, first, group):
    state_rows, lanes = states[0].shape
    owners, here, rank, degrees = roots.shape
    slots = places.shape[2]
    columns = state_rows * 2 // here
    last = so_far is not None
    shape = (columns // 2, 2, degrees, slots)
    inputs = ([so_far] if last else []) + [roots, places, alive, *states]
    scratch = [pltpu.VMEM((degrees // 128, len(states) * here * columns, 128), F32)]
    more = {}
    if last:
        scratch += [pltpu.VMEM(shape, BF16), pltpu.SemaphoreType.DMA((columns,))]
        more["out_specs"] = IN_HBM
    return call(
        functools.partial(root_kernel, group, first, last),
        "root",
        jax.ShapeDtypeStruct(shape, BF16),
        whole_blocks(len(inputs)),
        2 * len(states) * here * rank * degrees * columns,
        2 * len(states) * here * rank * degrees,
        scratch,
        mib=24,
        **more,
    )(*inputs)


def per_device(
    fourier, quad_weights, leaf_basis, level_factors, sparsity, root_basis, order_of_slot
):
    slots, columns, lats = fourier.shape
    owners = lax.axis_size("order")
    levels = level_factors.shape[1]
    group = max(2, 16 * owners // columns)
    present = in_hbm(sparsity.transpose(1, 2, 0))
    fourier, leaf_basis, level_factors, root_basis = map(in_hbm, (fourier, leaf_basis, level_factors, root_basis))
    quad_weights = in_hbm(quad_weights.reshape(1, lats))

    def swap(array, axis, bits):
        return lax.ppermute(array, axis, [(i, i ^ bits) for i in range(lax.axis_size(axis))])

    def swap_both(array, order_bits, lat_bits):
        blocks = lax.axis_size("lat")
        pairs = [
            (o * blocks + b, (o ^ order_bits) * blocks + (b ^ lat_bits)) for o in range(owners) for b in range(blocks)
        ]
        return lax.ppermute(array, ("order", "lat"), pairs)

    state = leaf_states(fourier, quad_weights, leaf_basis, owners)
    partner = swap(state, "lat", 1)
    weights = level_weights(level_factors, present, (0,), state)
    states = [next_states(f"level0_{c}", state, partner, weights[0], c) for c in range(2)]
    weights += level_weights(level_factors, present, tuple(range(1, levels)), states[1])
    packed = weights[-2:]
    other_packed = [swap(part, "order", 1) for part in packed]
    for level in range(1, levels - 1):
        partners = [swap(state, "lat", 1 << level) for state in states]
        states = [next_states(f"level{level}_{c}", states[c], partners[c], weights[level]) for c in range(2)]
    top = 1 << levels - 1
    partner = swap(states[0], "lat", top)
    other_partner = swap_both(states[1], 1, top)
    other = swap(states[1], "order", 1)
    roots, places, alive = near_roots(root_basis, order_of_slot, owners, group, states[1])
    both = (
        last_states("last_own", alive, states[0], partner, packed, owners // 2),
        last_states("last_other", alive, other, other_partner, other_packed, owners // 2),
    )
    arrived = [swap(both[k % 2][k // 2], "order", k // 2 * 2) if k > 1 else both[k][0] for k in range(owners)]
    early = 3 * owners // 4
    spectra = spectra_of(arrived[:early], roots, places, alive, None, 0, group)
    return spectra_of(arrived[early:], roots, places, alive, spectra, early, group)


def solution(mesh):
    return jax.shard_map(
        per_device,
        mesh=mesh,
        in_specs=(
            P("order", None, "lat"),
            P("lat"),
            P("order", None, "lat"),
            P("order", None, None, "lat", None, None),
            P("order", None, "lat"),
            P(None, None, "lat"),
            P(),
        ),
        out_specs=P("order", None, "lat", None),
        check_vma=False,
    )
```

```python
import functools

import jax
import jax.numpy as jnp
from jax import lax
from jax.experimental import pallas as pl
from jax.experimental.pallas import tpu as pltpu
from jax.sharding import PartitionSpec as P

DEGREES = 2048
F32, BF16 = jnp.float32, jnp.bfloat16
MIB = 1 << 20
IN_HBM = pl.BlockSpec(memory_space=pltpu.HBM)
IN_SMEM = pl.BlockSpec(memory_space=pltpu.SMEM)
ANYWHERE = pl.BlockSpec(memory_space=pl.ANY)


def contract(lhs, rhs, dims):
    return lax.dot_general(lhs, rhs, (dims, ((), ())), preferred_element_type=F32)


def in_hbm(array):
    return pltpu.with_memory_space_constraint(array, pltpu.HBM)


def call(kernel, name, out_shape, in_specs, flops, size, scratch=(), mib=16, **more):
    return pl.pallas_call(
        kernel,
        out_shape=out_shape,
        in_specs=in_specs,
        scratch_shapes=list(scratch),
        compiler_params=pltpu.CompilerParams(vmem_limit_bytes=mib * MIB),
        cost_estimate=pl.CostEstimate(flops=flops // 1000, bytes_accessed=size // 1000, transcendentals=0),
        name=name,
        **more,
    )


def whole_blocks(count):
    return [pl.BlockSpec()] * count


def leaf_kernel(
    pieces, group, fourier_hbm, weight_hbm, leaf_hbm, state_ref, fourier_ref, weight_ref, leaf_ref, sems
):
    side = lax.axis_index("order") & 1
    slots, columns, lats = fourier_ref.shape
    rank = leaf_ref.shape[1]
    per = slots // pieces
    copies = [pltpu.make_async_copy(weight_hbm, weight_ref, sems.at[0])]
    for piece in range(pieces):
        part = pl.ds(piece * per, per)
        copies.append(pltpu.make_async_copy(fourier_hbm.at[part], fourier_ref.at[part], sems.at[1 + 2 * piece]))
        copies.append(pltpu.make_async_copy(leaf_hbm.at[part], leaf_ref.at[part], sems.at[2 + 2 * piece]))
    for copy in copies:
        copy.start()
    copies[0].wait()
    weight = weight_ref[...]
    mine = lax.broadcasted_iota(jnp.int32, (columns, 2 * rank), 1) < rank
    for pair in range(slots // 2):
        if 2 * pair % per == 0:
            copies[1 + 2 * (2 * pair // per)].wait()
            copies[2 + 2 * (2 * pair // per)].wait()
        both = pl.ds(2 * pair, 2)
        weighted = (fourier_ref[both].astype(F32) * weight[None]).astype(BF16)
        product = contract(
            weighted.reshape(2 * columns, lats), leaf_ref[both].reshape(2 * rank, lats), ((1,), (1,))
        )
        state = jnp.where(mine, product[:columns], product[columns:]).astype(BF16)
        if group % 16:
            state_ref[pair] = state
            continue
        for owner in range(columns // group):
            rows = pl.ds(owner // 2 * group, group)
            state_ref[pair, owner % 2 ^ side, rows] = state[owner * group : (owner + 1) * group]


def leaf_states(fourier, quad_weights, leaf_basis, owners):
    slots, columns, lats = fourier.shape
    rank = leaf_basis.shape[1]
    pairs, half, lanes, group = slots // 2, columns // 2, 2 * rank, columns // owners
    pieces = 2
    state = call(
        functools.partial(leaf_kernel, pieces, group),
        "leaf",
        jax.ShapeDtypeStruct((pairs, columns, lanes) if group % 16 else (pairs, 2, half, lanes), BF16),
        [IN_HBM] * 3,
        2 * slots * columns * rank * lats,
        4 * slots * columns * lats,
        [
            pltpu.VMEM((slots, columns, lats), BF16),
            pltpu.VMEM((1, lats), F32),
            pltpu.VMEM((slots, rank, lats), BF16),
            pltpu.SemaphoreType.DMA((1 + 2 * pieces,)),
        ],
    )(fourier, quad_weights, leaf_basis)
    if group % 16:
        side = lax.axis_index("order") & 1
        state = state.reshape(pairs, owners // 2, 2, group, lanes)
        sides = [lax.dynamic_index_in_dim(state, side ^ i, 2, False).reshape(pairs, half, lanes) for i in range(2)]
        state = jnp.stack(sides, axis=1)
    return state


def factor_kernel(levels, pieces, factor_hbm, present_hbm, after, *refs):
    del after
    weight_refs, (factor_ref, present_ref, sems) = refs[:-3], refs[-3:]
    present_copy = pltpu.make_async_copy(present_hbm, present_ref, sems.at[len(levels) * pieces])
    present_copy.start()
    _, slots, _, rank, _ = factor_ref.shape
    per = slots // pieces
    copies = {}
    for i, level in enumerate(levels):
        for piece in range(pieces):
            part = pl.ds(piece * per, per)
            copies[i, piece] = pltpu.make_async_copy(
                factor_hbm.at[part, level, :, 0], factor_ref.at[i, part], sems.at[i * pieces + piece]
            )
            copies[i, piece].start()
    empty = jnp.zeros((rank, rank), BF16)
    present_copy.wait()
    for i, level in enumerate(levels):
        for pair in range(slots // 2):
            if 2 * pair % per == 0:
                copies[i, 2 * pair // per].wait()
            for half in range(2):
                first, second = (factor_ref[i, slot, half] for slot in (2 * pair, 2 * pair + 1))
                if half:
                    first = jnp.where(present_ref[level, 0, 2 * pair] != 0, first, empty)
                    second = jnp.where(present_ref[level, 0, 2 * pair + 1] != 0, second, empty)
                if weight_refs[i].shape[1] == rank:
                    weight_refs[i + half][pair] = jnp.concatenate([first, second], axis=1)
                    continue
                lanes = pl.ds(half * 2 * rank, 2 * rank)
                weight_refs[i][pair, :rank, lanes] = jnp.concatenate([first, empty], axis=1)
                weight_refs[i][pair, rank:, lanes] = jnp.concatenate([empty, second], axis=1)


def level_weights(level_factors, present, levels, after):
    slots, last, _, _, rank, _ = level_factors.shape
    count, pieces = len(levels), 2
    return call(
        functools.partial(factor_kernel, levels, pieces),
        "factors",
        [
            jax.ShapeDtypeStruct((slots // 2, *((rank, 2 * rank) if level == last - 1 else (2 * rank, 4 * rank))), BF16)
            for level in levels
            for _ in range(1 + (level == last - 1))
        ],
        [IN_HBM, IN_HBM, ANYWHERE],
        slots * rank * rank * 4 * count,
        slots * rank * rank * 16 * count,
        [
            pltpu.VMEM((count, slots, 2, rank, rank), BF16),
            pltpu.SMEM(present.shape, jnp.int32),
            pltpu.SemaphoreType.DMA((count * pieces + 1,)),
        ],
        mib=24,
    )(level_factors, present, after)


def level_kernel(side, state_ref, partner_ref, weight_ref, out_ref):
    for pair in range(out_ref.shape[0]):
        at = pair if side is None else (pair, side)
        both = jnp.concatenate([state_ref[at], partner_ref[at]], axis=1)
        out_ref[pair] = contract(both, weight_ref[pair], ((1,), (1,))).astype(BF16)


def next_states(name, state, partner, weights, side=None):
    pairs, rows, lanes = state.shape[0], *state.shape[-2:]
    return call(
        functools.partial(level_kernel, side),
        name,
        jax.ShapeDtypeStruct((pairs, rows, lanes), BF16),
        whole_blocks(3),
        4 * pairs * rows * lanes * lanes,
        6 * pairs * rows * lanes,
    )(state, partner, weights)


def by_slot(packed):
    first = lax.broadcasted_iota(jnp.int32, packed.shape, 1) < packed.shape[0]
    empty = jnp.zeros(packed.shape, BF16)
    return jnp.concatenate([jnp.where(first, packed, empty), jnp.where(first, empty, packed)], axis=0)


def own_term_kernel(after, state_ref, own_ref, out_ref):
    del after
    for pair in range(state_ref.shape[0]):
        out_ref[pair] = contract(state_ref[pair], by_slot(own_ref[pair]), ((1,), (1,))).astype(BF16)


def own_term(after, state, own):
    pairs, rows, lanes = state.shape
    return call(
        own_term_kernel,
        "own_term",
        jax.ShapeDtypeStruct(state.shape, BF16),
        [ANYWHERE] + whole_blocks(2),
        2 * pairs * rows * lanes * lanes,
        6 * pairs * rows * lanes,
    )(after, state, own)


def last_level_kernel(axis, after, own_ref, partner_ref, cross_ref, *refs):
    del after
    refs = list(refs)
    own_factor_ref = refs.pop(0) if refs[0].shape == cross_ref.shape else None
    out_refs, groups_ref = refs[:-1], refs[-1]
    me = lax.axis_index(axis) // 2
    pairs, owners, group, _ = groups_ref.shape
    for pair in range(pairs):
        cross = by_slot(cross_ref[pair])
        if own_factor_ref is None:
            result = own_ref[pair].astype(F32) + contract(partner_ref[pair], cross, ((1,), (1,)))
        else:
            weight = jnp.concatenate([by_slot(own_factor_ref[pair]), cross], axis=1)
            both = jnp.concatenate([own_ref[pair], partner_ref[pair]], axis=1)
            result = contract(both, weight, ((1,), (1,)))
        result = result.astype(BF16)
        if len(out_refs) == 1:
            out_refs[0][pair] = result
            continue
        for owner in range(owners):
            groups_ref[pair, owner] = result[owner * group : (owner + 1) * group]
    if len(out_refs) > 1:
        for k, out_ref in enumerate(out_refs):
            for pair in range(pairs):
                out_ref[pl.ds(pair * group, group)] = groups_ref[pair, me ^ k]


def last_states(name, after, own, partner, factors, owners):
    pairs, columns, lanes = own.shape
    group = columns // owners
    rows = pairs * group
    by_owner = group % 16 == 0 and owners > 1
    parts = call(
        functools.partial(last_level_kernel, "order"),
        name,
        [jax.ShapeDtypeStruct((rows, lanes), BF16)] * owners if by_owner else [jax.ShapeDtypeStruct(own.shape, BF16)],
        [ANYWHERE] + whole_blocks(2 + len(factors)),
        4 * pairs * columns * lanes * lanes,
        6 * pairs * columns * lanes,
        [pltpu.VMEM((pairs, owners, group, lanes), BF16)],
    )(after, own, partner, *factors)
    if by_owner:
        return parts
    me = lax.axis_index("order") // 2
    parts = [lax.dynamic_slice_in_dim(parts[0], (me ^ k) * group, group, 1) for k in range(owners)]
    return [part.reshape(rows, lanes) for part in parts]


def near_kernel(group, root_hbm, order_ref, after, root_ref, place_ref, alive_ref, rows_ref, sems):
    del after
    owners, here, _, degrees = root_ref.shape
    slots = rows_ref.shape[1]
    me = lax.axis_index("order")
    copies = []
    for k in range(owners):
        copies.append(pltpu.make_async_copy(root_hbm.at[pl.ds((me ^ k) * here, here)], root_ref.at[k], sems.at[k]))
        copies[-1].start()
    lane = lax.broadcasted_iota(jnp.int32, (1, slots), 1)
    for k in range(owners):
        for slot in range(here):
            pair, half = slot // 2, slot % 2
            row = (pair // group * 2 + half) * group + pair % group
            rows_ref[pl.ds(row, 1), :] = (lane == order_ref[(me ^ k) * here + slot]).astype(F32)
        place_ref[k] = rows_ref[...].astype(BF16)
    degree = lax.axis_index("lat") * degrees + lax.broadcasted_iota(jnp.int32, (degrees, slots), 0)
    window = DEGREES // slots * lax.broadcasted_iota(jnp.int32, (degrees, slots), 1)
    alive_ref[...] = (degree >= window).astype(F32).astype(BF16)
    for copy in copies:
        copy.wait()


def near_roots(root_basis, order_of_slot, owners, group, after):
    slots, rank, degrees = root_basis.shape
    here = slots // owners
    return call(
        functools.partial(near_kernel, group),
        "near_roots",
        [
            jax.ShapeDtypeStruct((owners, here, rank, degrees), BF16),
            jax.ShapeDtypeStruct((owners, here, slots), BF16),
            jax.ShapeDtypeStruct((degrees, slots), BF16),
        ],
        [IN_HBM, IN_SMEM, ANYWHERE],
        slots * slots,
        4 * slots * rank * degrees,
        [pltpu.VMEM((here, slots), F32), pltpu.SemaphoreType.DMA((owners,))],
    )(root_basis, order_of_slot, after)


def root_kernel(group, first, last, *refs):
    refs = list(refs)
    so_far_ref = refs.pop(0) if last else None
    root_ref, place_ref, alive_ref = refs[:3]
    count = len(refs) - (7 if last else 5)
    state_refs = refs[3 : 3 + count]
    out_ref, rows_ref = refs[3 + count : 5 + count]
    natural_ref = refs[5 + count] if last else out_ref
    fields, parts, degrees, slots = out_ref.shape
    columns = fields * parts
    rank = root_ref.shape[2]
    group_rows = group * columns
    here = place_ref.shape[1]
    steps = state_refs[0].shape[0] // group_rows
    shape = (group_rows, 2 * rank)
    row_pair = lax.broadcasted_iota(jnp.int32, shape, 0) // columns
    row_half = lax.broadcasted_iota(jnp.int32, shape, 1) // rank
    masks = [[(row_pair == pair) & (row_half == half) for pair in range(group)] for half in range(2)]
    empty = jnp.zeros(shape, BF16)
    for i, state_ref in enumerate(state_refs):
        for step in range(steps):
            state = state_ref[pl.ds(step * group_rows, group_rows)]
            left = jnp.concatenate(
                [jnp.concatenate([jnp.where(m, state, empty) for m in line], axis=1) for line in masks], axis=0
            )
            right = root_ref[first + i, pl.ds(step * group * 2, group * 2)].reshape(group * 2 * rank, degrees)
            product = contract(left, right, ((1,), (0,)))
            begin = (i * steps + step) * 2 * group_rows
            for tile in range(degrees // 128):
                rows_ref[tile, pl.ds(begin, 2 * group_rows), :] = product[:, tile * 128 : (tile + 1) * 128]
    place = place_ref[pl.ds(first, count)].reshape(count * here, slots)
    copies = []
    for column in range(columns):
        for tile in range(degrees // 128):
            span = slice(tile * 128, (tile + 1) * 128)
            one = rows_ref[tile, pl.ds(column, count * here, stride=columns), :].astype(BF16)
            natural = contract(one.T, place, ((1,), (0,))).astype(BF16)
            where = (column // 2, column % 2, span)
            if last:
                natural = natural + so_far_ref[where]
                natural = jnp.where(alive_ref[span] != 0, natural, jnp.zeros((), BF16))
            natural_ref[where] = natural
        if last:
            where = (column // 2, column % 2)
            copies.append(pltpu.make_async_copy(natural_ref.at[where], out_ref.at[where], refs[-1].at[column]))
            copies[-1].start()
    for copy in copies:
        copy.wait()


def spectra_of(states, roots, places, alive, so_far, first, group):
    state_rows, lanes = states[0].shape
    owners, here, rank, degrees = roots.shape
    slots = places.shape[2]
    columns = state_rows * 2 // here
    last = so_far is not None
    shape = (columns // 2, 2, degrees, slots)
    inputs = ([so_far] if last else []) + [roots, places, alive, *states]
    scratch = [pltpu.VMEM((degrees // 128, len(states) * here * columns, 128), F32)]
    more = {}
    if last:
        scratch += [pltpu.VMEM(shape, BF16), pltpu.SemaphoreType.DMA((columns,))]
        more["out_specs"] = IN_HBM
    return call(
        functools.partial(root_kernel, group, first, last),
        "root",
        jax.ShapeDtypeStruct(shape, BF16),
        whole_blocks(len(inputs)),
        2 * len(states) * here * rank * degrees * columns,
        2 * len(states) * here * rank * degrees,
        scratch,
        mib=24,
        **more,
    )(*inputs)


def per_device(
    fourier, quad_weights, leaf_basis, level_factors, sparsity, root_basis, order_of_slot
):
    slots, columns, lats = fourier.shape
    owners = lax.axis_size("order")
    levels = level_factors.shape[1]
    group = max(2, 16 * owners // columns)
    present = in_hbm(sparsity.transpose(1, 2, 0))
    fourier, leaf_basis, level_factors, root_basis = map(in_hbm, (fourier, leaf_basis, level_factors, root_basis))
    quad_weights = in_hbm(quad_weights.reshape(1, lats))

    def swap(array, axis, bits):
        return lax.ppermute(array, axis, [(i, i ^ bits) for i in range(lax.axis_size(axis))])

    def swap_both(array, order_bits, lat_bits):
        blocks = lax.axis_size("lat")
        pairs = [
            (o * blocks + b, (o ^ order_bits) * blocks + (b ^ lat_bits)) for o in range(owners) for b in range(blocks)
        ]
        return lax.ppermute(array, ("order", "lat"), pairs)

    state = leaf_states(fourier, quad_weights, leaf_basis, owners)
    partner = swap(state, "lat", 1)
    weights = level_weights(level_factors, present, (0,), state)
    states = [next_states(f"level0_{c}", state, partner, weights[0], c) for c in range(2)]
    weights += level_weights(level_factors, present, tuple(range(1, levels)), states[1])
    own_factors, cross_factors = weights[-2:]
    other_cross = swap(cross_factors, "order", 1)
    for level in range(1, levels - 1):
        partners = [swap(state, "lat", 1 << level) for state in states]
        states = [next_states(f"level{level}_{c}", states[c], partners[c], weights[level]) for c in range(2)]
    top = 1 << levels - 1
    partner = swap(states[0], "lat", top)
    other_partner = swap_both(states[1], 1, top)
    roots, places, alive = near_roots(root_basis, order_of_slot, owners, group, states[1])
    other_own = swap(own_term(alive, states[1], own_factors), "order", 1)
    both = (
        last_states("last_own", alive, states[0], partner, (cross_factors, own_factors), owners // 2),
        last_states("last_other", alive, other_own, other_partner, (other_cross,), owners // 2),
    )
    arrived = [swap(both[k % 2][k // 2], "order", k // 2 * 2) if k > 1 else both[k][0] for k in range(owners)]
    early = 3 * owners // 4
    spectra = spectra_of(arrived[:early], roots, places, alive, None, 0, group)
    return spectra_of(arrived[early:], roots, places, alive, spectra, early, group)


def solution(mesh):
    return jax.shard_map(
        per_device,
        mesh=mesh,
        in_specs=(
            P("order", None, "lat"),
            P("lat"),
            P("order", None, "lat"),
            P("order", None, None, "lat", None, None),
            P("order", None, "lat"),
            P(None, None, "lat"),
            P(),
        ),
        out_specs=P("order", None, "lat", None),
        check_vma=False,
    )
```

```python
import functools

import jax
import jax.numpy as jnp
from jax import lax
from jax.experimental import pallas as pl
from jax.experimental.pallas import tpu as pltpu
from jax.sharding import PartitionSpec as P

DEGREES = 2048
F32, BF16 = jnp.float32, jnp.bfloat16
MIB = 1 << 20
IN_HBM = pl.BlockSpec(memory_space=pltpu.HBM)
IN_SMEM = pl.BlockSpec(memory_space=pltpu.SMEM)
ANYWHERE = pl.BlockSpec(memory_space=pl.ANY)


def contract(lhs, rhs, dims):
    return lax.dot_general(lhs, rhs, (dims, ((), ())), preferred_element_type=F32)


def in_hbm(array):
    return pltpu.with_memory_space_constraint(array, pltpu.HBM)


def call(kernel, name, out_shape, in_specs, flops, size, scratch=(), mib=16, **more):
    return pl.pallas_call(
        kernel,
        out_shape=out_shape,
        in_specs=in_specs,
        scratch_shapes=list(scratch),
        compiler_params=pltpu.CompilerParams(vmem_limit_bytes=mib * MIB),
        cost_estimate=pl.CostEstimate(flops=flops // 1000, bytes_accessed=size // 1000, transcendentals=0),
        name=name,
        **more,
    )


def whole_blocks(count):
    return [pl.BlockSpec()] * count


def leaf_kernel(
    pieces, group, fourier_hbm, weight_hbm, leaf_hbm, state_ref, fourier_ref, weight_ref, leaf_ref, sems
):
    side = lax.axis_index("order") & 1 ^ 1
    slots, columns, lats = fourier_ref.shape
    rank = leaf_ref.shape[1]
    per = slots // pieces
    copies = [pltpu.make_async_copy(weight_hbm, weight_ref, sems.at[0])]
    for piece in range(pieces):
        part = pl.ds(piece * per, per)
        copies.append(pltpu.make_async_copy(fourier_hbm.at[part], fourier_ref.at[part], sems.at[1 + 2 * piece]))
        copies.append(pltpu.make_async_copy(leaf_hbm.at[part], leaf_ref.at[part], sems.at[2 + 2 * piece]))
    for copy in copies:
        copy.start()
    copies[0].wait()
    weight = weight_ref[...]
    mine = lax.broadcasted_iota(jnp.int32, (columns, 2 * rank), 1) < rank
    for pair in range(slots // 2):
        if 2 * pair % per == 0:
            copies[1 + 2 * (2 * pair // per)].wait()
            copies[2 + 2 * (2 * pair // per)].wait()
        both = pl.ds(2 * pair, 2)
        weighted = (fourier_ref[both].astype(F32) * weight[None]).astype(BF16)
        product = contract(
            weighted.reshape(2 * columns, lats), leaf_ref[both].reshape(2 * rank, lats), ((1,), (1,))
        )
        state = jnp.where(mine, product[:columns], product[columns:]).astype(BF16)
        if group % 16:
            state_ref[pair] = state
            continue
        for owner in range(columns // group):
            rows = pl.ds(owner // 2 * group, group)
            state_ref[pair, owner % 2 ^ side, rows] = state[owner * group : (owner + 1) * group]


def leaf_states(fourier, quad_weights, leaf_basis, owners):
    slots, columns, lats = fourier.shape
    rank = leaf_basis.shape[1]
    pairs, half, lanes, group = slots // 2, columns // 2, 2 * rank, columns // owners
    pieces = 2
    state = call(
        functools.partial(leaf_kernel, pieces, group),
        "leaf",
        jax.ShapeDtypeStruct((pairs, columns, lanes) if group % 16 else (pairs, 2, half, lanes), BF16),
        [IN_HBM] * 3,
        2 * slots * columns * rank * lats,
        4 * slots * columns * lats,
        [
            pltpu.VMEM((slots, columns, lats), BF16),
            pltpu.VMEM((1, lats), F32),
            pltpu.VMEM((slots, rank, lats), BF16),
            pltpu.SemaphoreType.DMA((1 + 2 * pieces,)),
        ],
    )(fourier, quad_weights, leaf_basis)
    if group % 16:
        side = lax.axis_index("order") & 1 ^ 1
        state = state.reshape(pairs, owners // 2, 2, group, lanes)
        sides = [lax.dynamic_index_in_dim(state, side ^ i, 2, False).reshape(pairs, half, lanes) for i in range(2)]
        state = jnp.stack(sides, axis=1)
    return state


def factor_kernel(levels, pieces, factor_hbm, present_hbm, after, *refs):
    del after
    weight_refs, (factor_ref, present_ref, sems) = refs[:-3], refs[-3:]
    present_copy = pltpu.make_async_copy(present_hbm, present_ref, sems.at[len(levels) * pieces])
    present_copy.start()
    _, slots, _, rank, _ = factor_ref.shape
    per = slots // pieces
    copies = {}
    for i, level in enumerate(levels):
        for piece in range(pieces):
            part = pl.ds(piece * per, per)
            copies[i, piece] = pltpu.make_async_copy(
                factor_hbm.at[part, level, :, 0], factor_ref.at[i, part], sems.at[i * pieces + piece]
            )
            copies[i, piece].start()
    empty = jnp.zeros((rank, rank), BF16)
    present_copy.wait()
    for i, level in enumerate(levels):
        for pair in range(slots // 2):
            if 2 * pair % per == 0:
                copies[i, 2 * pair // per].wait()
            for half in range(2):
                first, second = (factor_ref[i, slot, half] for slot in (2 * pair, 2 * pair + 1))
                if half:
                    first = jnp.where(present_ref[level, 0, 2 * pair] != 0, first, empty)
                    second = jnp.where(present_ref[level, 0, 2 * pair + 1] != 0, second, empty)
                if weight_refs[i].shape[1] == rank:
                    weight_refs[i + half][pair] = jnp.concatenate([first, second], axis=1)
                    continue
                lanes = pl.ds(half * 2 * rank, 2 * rank)
                weight_refs[i][pair, :rank, lanes] = jnp.concatenate([first, empty], axis=1)
                weight_refs[i][pair, rank:, lanes] = jnp.concatenate([empty, second], axis=1)


def level_weights(level_factors, present, levels, after):
    slots, last, _, _, rank, _ = level_factors.shape
    count, pieces = len(levels), 2
    return call(
        functools.partial(factor_kernel, levels, pieces),
        "factors",
        [
            jax.ShapeDtypeStruct((slots // 2, *((rank, 2 * rank) if level == last - 1 else (2 * rank, 4 * rank))), BF16)
            for level in levels
            for _ in range(1 + (level == last - 1))
        ],
        [IN_HBM, IN_HBM, ANYWHERE],
        slots * rank * rank * 4 * count,
        slots * rank * rank * 16 * count,
        [
            pltpu.VMEM((count, slots, 2, rank, rank), BF16),
            pltpu.SMEM(present.shape, jnp.int32),
            pltpu.SemaphoreType.DMA((count * pieces + 1,)),
        ],
        mib=24,
    )(level_factors, present, after)


def level_kernel(side, axis, after, state_ref, partner_ref, weight_ref, *refs):
    del after
    out_ref = refs[0]
    me = lax.axis_index(axis) // 2
    for pair in range(weight_ref.shape[0]):
        at = pair if side is None else (pair, side)
        both = jnp.concatenate([state_ref[at], partner_ref[at]], axis=1)
        result = contract(both, weight_ref[pair], ((1,), (1,))).astype(BF16)
        if len(refs) == 1:
            out_ref[pair] = result
            continue
        mine_ref, groups_ref = refs[1:]
        owners, group, _ = groups_ref.shape[1:]
        for owner in range(owners):
            groups_ref[pair, owner] = result[owner * group : (owner + 1) * group]
        mine_ref[pair] = groups_ref[pair, me]
        for k in range(1, owners):
            out_ref[pair, (k - 1) * group : k * group] = groups_ref[pair, me ^ k]


def next_states(name, after, state, partner, weights, side=None, owners=1):
    pairs, rows, lanes = state.shape[0], *state.shape[-2:]
    group = rows // owners
    split = owners > 1 and group % 16 == 0
    shapes = [(pairs, rows - group, lanes), (pairs, group, lanes)] if split else [(pairs, rows, lanes)]
    outs = call(
        functools.partial(level_kernel, side, "order"),
        name,
        [jax.ShapeDtypeStruct(shape, BF16) for shape in shapes],
        [ANYWHERE] + whole_blocks(3),
        4 * pairs * rows * lanes * lanes,
        6 * pairs * rows * lanes,
        [pltpu.VMEM((pairs, owners, group, lanes), BF16)] if split else [],
    )(after, state, partner, weights)
    if owners > 1 and not split:
        me = lax.axis_index("order") // 2
        parts = [lax.dynamic_slice_in_dim(outs[0], (me ^ k) * group, group, 1) for k in range(owners)]
        return [jnp.concatenate(parts[1:], axis=1), parts[0]]
    return outs if split else outs[0]


def by_slot(packed):
    first = lax.broadcasted_iota(jnp.int32, packed.shape, 1) < packed.shape[0]
    empty = jnp.zeros(packed.shape, BF16)
    return jnp.concatenate([jnp.where(first, packed, empty), jnp.where(first, empty, packed)], axis=0)


def own_term_kernel(after, state_ref, own_ref, out_ref):
    del after
    for pair in range(state_ref.shape[0]):
        out_ref[pair] = contract(state_ref[pair], by_slot(own_ref[pair]), ((1,), (1,))).astype(BF16)


def own_term(after, state, own):
    pairs, rows, lanes = state.shape
    return call(
        own_term_kernel,
        "own_term",
        jax.ShapeDtypeStruct(state.shape, BF16),
        [ANYWHERE] + whole_blocks(2),
        2 * pairs * rows * lanes * lanes,
        6 * pairs * rows * lanes,
    )(after, state, own)


def last_level_kernel(turn, axis, after, own_ref, partner_ref, cross_ref, *refs):
    del after
    refs = list(refs)
    own_factor_ref = refs.pop(0) if refs[0].shape == cross_ref.shape else None
    out_refs, groups_ref = refs[:-1], refs[-1]
    me = lax.axis_index(axis) // 2 if turn else 0
    pairs, owners, group, _ = groups_ref.shape
    for pair in range(pairs):
        cross = by_slot(cross_ref[pair])
        if own_factor_ref is None:
            result = own_ref[pair].astype(F32) + contract(partner_ref[pair], cross, ((1,), (1,)))
        else:
            weight = jnp.concatenate([by_slot(own_factor_ref[pair]), cross], axis=1)
            both = jnp.concatenate([own_ref[pair], partner_ref[pair]], axis=1)
            result = contract(both, weight, ((1,), (1,)))
        result = result.astype(BF16)
        if group % 16:
            out_refs[0][pair] = result
            continue
        for owner in range(owners):
            groups_ref[pair, owner] = result[owner * group : (owner + 1) * group]
    if group % 16 == 0:
        for k, out_ref in enumerate(out_refs):
            for pair in range(pairs):
                out_ref[pl.ds(pair * group, group)] = groups_ref[pair, me ^ k]


def last_states(name, after, own, partner, factors, owners, turn):
    pairs, columns, lanes = own.shape
    group = columns // owners
    rows = pairs * group
    aligned = group % 16 == 0
    parts = call(
        functools.partial(last_level_kernel, turn, "order"),
        name,
        [jax.ShapeDtypeStruct((rows, lanes), BF16)] * owners if aligned else [jax.ShapeDtypeStruct(own.shape, BF16)],
        [ANYWHERE] + whole_blocks(2 + len(factors)),
        4 * pairs * columns * lanes * lanes,
        6 * pairs * columns * lanes,
        [pltpu.VMEM((pairs, owners, group, lanes), BF16)],
    )(after, own, partner, *factors)
    if aligned:
        return parts
    me = lax.axis_index("order") // 2 if turn else 0
    parts = [lax.dynamic_slice_in_dim(parts[0], (me ^ k) * group, group, 1) for k in range(owners)]
    return [part.reshape(rows, lanes) for part in parts]


def place_kernel(order, group, slot_ref, after, place_ref, alive_ref, rows_ref):
    del after
    _, here, slots = place_ref.shape
    degrees = alive_ref.shape[0]
    me = lax.axis_index("order")
    lane = lax.broadcasted_iota(jnp.int32, (1, slots), 1)
    for i, k in enumerate(order):
        for slot in range(here):
            pair, half = slot // 2, slot % 2
            row = (pair // group * 2 + half) * group + pair % group
            rows_ref[pl.ds(row, 1), :] = (lane == slot_ref[(me ^ k) * here + slot]).astype(F32)
        place_ref[i] = rows_ref[...].astype(BF16)
    degree = lax.axis_index("lat") * degrees + lax.broadcasted_iota(jnp.int32, (degrees, slots), 0)
    window = DEGREES // slots * lax.broadcasted_iota(jnp.int32, (degrees, slots), 1)
    alive_ref[...] = (degree >= window).astype(F32).astype(BF16)


def places_of(order_of_slot, degrees, order, group, after):
    slots = order_of_slot.shape[0]
    here = slots // len(order)
    return call(
        functools.partial(place_kernel, order, group),
        "places",
        [jax.ShapeDtypeStruct((len(order), here, slots), BF16), jax.ShapeDtypeStruct((degrees, slots), BF16)],
        [IN_SMEM, ANYWHERE],
        slots * slots,
        8 * slots * slots,
        [pltpu.VMEM((here, slots), F32)],
    )(order_of_slot, after)


def root_kernel(group, order, later, *refs):
    last = not later
    refs = list(refs)
    so_far_ref = refs.pop(0) if last else None
    root_ref, place_ref, alive_ref = refs[:3]
    count = len(order)
    state_refs = refs[3 : 3 + count]
    fetches = []
    if last:
        out_ref, rows_ref, natural_ref, sems = refs[3 + count :]
    else:
        out_ref, later_ref, rows_ref, fetched_ref, sems = refs[3 + count :]
        natural_ref = out_ref
        here = fetched_ref.shape[1]
        me = lax.axis_index("order")
        targets = [fetched_ref.at[i] for i in range(count)] + [later_ref.at[i] for i in range(len(later))]
        for i, (k, target) in enumerate(zip(order + later, targets)):
            there = pl.ds((me ^ k) * here, here)
            fetches.append(pltpu.make_async_copy(root_ref.at[there], target, sems.at[i]))
            fetches[-1].start()
        root_ref = fetched_ref
    fields, parts, degrees, slots = out_ref.shape
    columns = fields * parts
    rank = root_ref.shape[2]
    group_rows = group * columns
    here = place_ref.shape[1]
    steps = state_refs[0].shape[0] // group_rows
    shape = (group_rows, 2 * rank)
    row_pair = lax.broadcasted_iota(jnp.int32, shape, 0) // columns
    row_half = lax.broadcasted_iota(jnp.int32, shape, 1) // rank
    masks = [[(row_pair == pair) & (row_half == half) for pair in range(group)] for half in range(2)]
    empty = jnp.zeros(shape, BF16)
    for i, state_ref in enumerate(state_refs):
        if fetches:
            fetches[i].wait()
        for step in range(steps):
            state = state_ref[pl.ds(step * group_rows, group_rows)]
            left = jnp.concatenate(
                [jnp.concatenate([jnp.where(m, state, empty) for m in line], axis=1) for line in masks], axis=0
            )
            right = root_ref[i, pl.ds(step * group * 2, group * 2)].reshape(group * 2 * rank, degrees)
            product = contract(left, right, ((1,), (0,)))
            row = (i * steps + step) * 2 * group_rows
            for tile in range(degrees // 128):
                rows_ref[tile, pl.ds(row, 2 * group_rows), :] = product[:, tile * 128 : (tile + 1) * 128]
    begin = 0 if later else place_ref.shape[0] - count
    place = place_ref[pl.ds(begin, count)].reshape(count * here, slots)
    copies = []
    for column in range(columns):
        for tile in range(degrees // 128):
            span = slice(tile * 128, (tile + 1) * 128)
            one = rows_ref[tile, pl.ds(column, count * here, stride=columns), :].astype(BF16)
            natural = contract(one.T, place, ((1,), (0,))).astype(BF16)
            where = (column // 2, column % 2, span)
            if last:
                natural = natural + so_far_ref[where]
                natural = jnp.where(alive_ref[span] != 0, natural, jnp.zeros((), BF16))
            natural_ref[where] = natural
        if last:
            where = (column // 2, column % 2)
            copies.append(pltpu.make_async_copy(natural_ref.at[where], out_ref.at[where], sems.at[column]))
            copies[-1].start()
    for copy in copies + fetches[count:]:
        copy.wait()


def spectra_of(states, roots, places, alive, so_far, order, later, group):
    state_rows = states[0].shape[0]
    rank, degrees = roots.shape[-2:]
    _, here, slots = places.shape
    columns = state_rows * 2 // here
    count = len(order)
    out = jax.ShapeDtypeStruct((columns // 2, 2, degrees, slots), BF16)
    inputs = [roots, places, alive, *states]
    scratch = [pltpu.VMEM((degrees // 128, count * here * columns, 128), F32)]
    more = {}
    if later:
        in_specs = [IN_HBM] + whole_blocks(len(inputs) - 1)
        out = [out, jax.ShapeDtypeStruct((len(later), here, rank, degrees), BF16)]
        scratch += [pltpu.VMEM((count, here, rank, degrees), BF16), pltpu.SemaphoreType.DMA((count + len(later),))]
    else:
        inputs = [so_far, *inputs]
        in_specs = whole_blocks(len(inputs))
        scratch += [pltpu.VMEM(out.shape, BF16), pltpu.SemaphoreType.DMA((columns,))]
        more["out_specs"] = IN_HBM
    return call(
        functools.partial(root_kernel, group, order, later),
        "root",
        out,
        in_specs,
        2 * count * here * rank * degrees * columns,
        2 * count * here * rank * degrees,
        scratch,
        mib=24,
        **more,
    )(*inputs)


def per_device(
    fourier, quad_weights, leaf_basis, level_factors, sparsity, root_basis, order_of_slot
):
    slots, columns, lats = fourier.shape
    owners = lax.axis_size("order")
    levels = level_factors.shape[1]
    group = max(2, 16 * owners // columns)
    present = in_hbm(sparsity.transpose(1, 2, 0))
    fourier, leaf_basis, level_factors, root_basis = map(in_hbm, (fourier, leaf_basis, level_factors, root_basis))
    quad_weights = in_hbm(quad_weights.reshape(1, lats))

    def swap(array, axis, bits):
        return lax.ppermute(array, axis, [(i, i ^ bits) for i in range(lax.axis_size(axis))])

    def swap_both(array, order_bits, lat_bits):
        blocks = lax.axis_size("lat")
        pairs = [
            (o * blocks + b, (o ^ order_bits) * blocks + (b ^ lat_bits)) for o in range(owners) for b in range(blocks)
        ]
        return lax.ppermute(array, ("order", "lat"), pairs)

    state = leaf_states(fourier, quad_weights, leaf_basis, owners)
    partner = swap(state, "lat", 1)
    weights = list(level_weights(level_factors, present, (0,), state))
    high = owners // 2
    first = next_states("level0_0", state, state, partner, weights[0], 0)
    weights += level_weights(level_factors, present, tuple(range(1, levels)), first)
    own_factors, cross_factors = weights[-2:]
    second = next_states("level0_1", weights[1], state, partner, weights[0], 1)
    other_cross = swap(cross_factors, "order", 1)
    for level in range(1, levels - 1):
        first_partner, second_partner = [swap(state, "lat", 1 << level) for state in (first, second)]
        first = next_states(f"level{level}_0", first, first, first_partner, weights[level])
        parts = high if level == levels - 2 else 1
        second = next_states(f"level{level}_1", second, second, second_partner, weights[level], None, parts)
    top = 1 << levels - 1
    second, mine = second
    first_partner = swap_both(first, 1, top)
    other_own = swap(own_term(first, first, own_factors), "order", 1)
    second_partner = swap(second, "lat", top)
    mine_partner = swap(mine, "lat", top)
    order = tuple(range(1, owners, 2)) + (0,)
    later = tuple(range(2, owners, 2))
    places, alive = places_of(order_of_slot, root_basis.shape[2], order + later, group, mine)
    own = (cross_factors, own_factors)
    pieces = {}
    odd = last_states("last_other", alive, other_own, first_partner, (other_cross,), high, True)
    even = last_states("last_second", alive, second, second_partner, own, high - 1, False)
    (pieces[0],) = last_states("last_mine", alive, mine, mine_partner, own, 1, False)
    for k in range(high):
        pieces[2 * k + 1] = swap(odd[k], "order", 2 * k) if k else odd[k]
        if k:
            pieces[2 * k] = swap(even[k - 1], "order", 2 * k)
    spectra, later_roots = spectra_of([pieces[k] for k in order], root_basis, places, alive, None, order, later, group)
    return spectra_of([pieces[k] for k in later], later_roots, places, alive, spectra, later, (), group)


def solution(mesh):
    return jax.shard_map(
        per_device,
        mesh=mesh,
        in_specs=(
            P("order", None, "lat"),
            P("lat"),
            P("order", None, "lat"),
            P("order", None, None, "lat", None, None),
            P("order", None, "lat"),
            P(None, None, "lat"),
            P(),
        ),
        out_specs=P("order", None, "lat", None),
        check_vma=False,
    )
```

```python
import functools

import jax
import jax.numpy as jnp
from jax import lax
from jax.experimental import pallas as pl
from jax.experimental.pallas import tpu as pltpu
from jax.sharding import PartitionSpec as P

DEGREES = 2048
F32, BF16 = jnp.float32, jnp.bfloat16
MIB = 1 << 20
IN_HBM = pl.BlockSpec(memory_space=pltpu.HBM)
IN_SMEM = pl.BlockSpec(memory_space=pltpu.SMEM)
ANYWHERE = pl.BlockSpec(memory_space=pl.ANY)


def contract(lhs, rhs, dims):
    return lax.dot_general(lhs, rhs, (dims, ((), ())), preferred_element_type=F32)


def in_hbm(array):
    return pltpu.with_memory_space_constraint(array, pltpu.HBM)


def call(kernel, name, out_shape, in_specs, flops, size, scratch=(), mib=16, **more):
    return pl.pallas_call(
        kernel,
        out_shape=out_shape,
        in_specs=in_specs,
        scratch_shapes=list(scratch),
        compiler_params=pltpu.CompilerParams(vmem_limit_bytes=mib * MIB),
        cost_estimate=pl.CostEstimate(flops=flops // 1000, bytes_accessed=size // 1000, transcendentals=0),
        name=name,
        **more,
    )


def whole_blocks(count):
    return [pl.BlockSpec()] * count


def leaf_kernel(
    pieces, group, fourier_hbm, weight_hbm, leaf_hbm, state_ref, fourier_ref, weight_ref, leaf_ref, sems
):
    side = lax.axis_index("order") & 1
    slots, columns, lats = fourier_ref.shape
    rank = leaf_ref.shape[1]
    per = slots // pieces
    copies = [pltpu.make_async_copy(weight_hbm, weight_ref, sems.at[0])]
    for piece in range(pieces):
        part = pl.ds(piece * per, per)
        copies.append(pltpu.make_async_copy(fourier_hbm.at[part], fourier_ref.at[part], sems.at[1 + 2 * piece]))
        copies.append(pltpu.make_async_copy(leaf_hbm.at[part], leaf_ref.at[part], sems.at[2 + 2 * piece]))
    for copy in copies:
        copy.start()
    copies[0].wait()
    weight = weight_ref[...]
    mine = lax.broadcasted_iota(jnp.int32, (columns, 2 * rank), 1) < rank
    for pair in range(slots // 2):
        if 2 * pair % per == 0:
            copies[1 + 2 * (2 * pair // per)].wait()
            copies[2 + 2 * (2 * pair // per)].wait()
        both = pl.ds(2 * pair, 2)
        weighted = (fourier_ref[both].astype(F32) * weight[None]).astype(BF16)
        product = contract(
            weighted.reshape(2 * columns, lats), leaf_ref[both].reshape(2 * rank, lats), ((1,), (1,))
        )
        state = jnp.where(mine, product[:columns], product[columns:]).astype(BF16)
        if group % 16:
            state_ref[pair] = state
            continue
        for owner in range(columns // group):
            rows = pl.ds(owner // 2 * group, group)
            state_ref[pair, owner % 2 ^ side, rows] = state[owner * group : (owner + 1) * group]


def leaf_states(fourier, quad_weights, leaf_basis, owners):
    slots, columns, lats = fourier.shape
    rank = leaf_basis.shape[1]
    pairs, half, lanes, group = slots // 2, columns // 2, 2 * rank, columns // owners
    pieces = 2
    state = call(
        functools.partial(leaf_kernel, pieces, group),
        "leaf",
        jax.ShapeDtypeStruct((pairs, columns, lanes) if group % 16 else (pairs, 2, half, lanes), BF16),
        [IN_HBM] * 3,
        2 * slots * columns * rank * lats,
        4 * slots * columns * lats,
        [
            pltpu.VMEM((slots, columns, lats), BF16),
            pltpu.VMEM((1, lats), F32),
            pltpu.VMEM((slots, rank, lats), BF16),
            pltpu.SemaphoreType.DMA((1 + 2 * pieces,)),
        ],
    )(fourier, quad_weights, leaf_basis)
    if group % 16:
        side = lax.axis_index("order") & 1
        state = state.reshape(pairs, owners // 2, 2, group, lanes)
        sides = [lax.dynamic_index_in_dim(state, side ^ i, 2, False).reshape(pairs, half, lanes) for i in range(2)]
        state = jnp.stack(sides, axis=1)
    return state


def factor_kernel(levels, pieces, factor_hbm, present_hbm, after, *refs):
    del after
    weight_refs, (factor_ref, present_ref, sems) = refs[:-3], refs[-3:]
    present_copy = pltpu.make_async_copy(present_hbm, present_ref, sems.at[len(levels) * pieces])
    present_copy.start()
    _, slots, _, rank, _ = factor_ref.shape
    per = slots // pieces
    copies = {}
    for i, level in enumerate(levels):
        for piece in range(pieces):
            part = pl.ds(piece * per, per)
            copies[i, piece] = pltpu.make_async_copy(
                factor_hbm.at[part, level, :, 0], factor_ref.at[i, part], sems.at[i * pieces + piece]
            )
            copies[i, piece].start()
    empty = jnp.zeros((rank, rank), BF16)
    present_copy.wait()
    for i, level in enumerate(levels):
        for pair in range(slots // 2):
            if 2 * pair % per == 0:
                copies[i, 2 * pair // per].wait()
            for half in range(2):
                first, second = (factor_ref[i, slot, half] for slot in (2 * pair, 2 * pair + 1))
                if half:
                    first = jnp.where(present_ref[level, 0, 2 * pair] != 0, first, empty)
                    second = jnp.where(present_ref[level, 0, 2 * pair + 1] != 0, second, empty)
                if weight_refs[i].shape[1] == rank:
                    weight_refs[i + half][pair] = jnp.concatenate([first, second], axis=1)
                    continue
                lanes = pl.ds(half * 2 * rank, 2 * rank)
                weight_refs[i][pair, :rank, lanes] = jnp.concatenate([first, empty], axis=1)
                weight_refs[i][pair, rank:, lanes] = jnp.concatenate([empty, second], axis=1)


def level_weights(level_factors, present, levels, after):
    slots, last, _, _, rank, _ = level_factors.shape
    count, pieces = len(levels), 2
    return call(
        functools.partial(factor_kernel, levels, pieces),
        "factors",
        [
            jax.ShapeDtypeStruct((slots // 2, *((rank, 2 * rank) if level == last - 1 else (2 * rank, 4 * rank))), BF16)
            for level in levels
            for _ in range(1 + (level == last - 1))
        ],
        [IN_HBM, IN_HBM, ANYWHERE],
        slots * rank * rank * 4 * count,
        slots * rank * rank * 16 * count,
        [
            pltpu.VMEM((count, slots, 2, rank, rank), BF16),
            pltpu.SMEM(present.shape, jnp.int32),
            pltpu.SemaphoreType.DMA((count * pieces + 1,)),
        ],
        mib=24,
    )(level_factors, present, after)


def level_kernel(side, state_ref, partner_ref, weight_ref, out_ref):
    for pair in range(out_ref.shape[0]):
        at = pair if side is None else (pair, side)
        both = jnp.concatenate([state_ref[at], partner_ref[at]], axis=1)
        out_ref[pair] = contract(both, weight_ref[pair], ((1,), (1,))).astype(BF16)


def next_states(name, state, partner, weights, side=None):
    pairs, rows, lanes = state.shape[0], *state.shape[-2:]
    return call(
        functools.partial(level_kernel, side),
        name,
        jax.ShapeDtypeStruct((pairs, rows, lanes), BF16),
        whole_blocks(3),
        4 * pairs * rows * lanes * lanes,
        6 * pairs * rows * lanes,
    )(state, partner, weights)


def by_slot(packed):
    first = lax.broadcasted_iota(jnp.int32, packed.shape, 1) < packed.shape[0]
    empty = jnp.zeros(packed.shape, BF16)
    return jnp.concatenate([jnp.where(first, packed, empty), jnp.where(first, empty, packed)], axis=0)


def own_term_kernel(after, state_ref, own_ref, out_ref):
    del after
    for pair in range(state_ref.shape[0]):
        out_ref[pair] = contract(state_ref[pair], by_slot(own_ref[pair]), ((1,), (1,))).astype(BF16)


def own_term(after, state, own):
    pairs, rows, lanes = state.shape
    return call(
        own_term_kernel,
        "own_term",
        jax.ShapeDtypeStruct(state.shape, BF16),
        [ANYWHERE] + whole_blocks(2),
        2 * pairs * rows * lanes * lanes,
        6 * pairs * rows * lanes,
    )(after, state, own)


def last_level_kernel(axis, after, own_ref, partner_ref, cross_ref, *refs):
    del after
    refs = list(refs)
    own_factor_ref = refs.pop(0) if refs[0].shape == cross_ref.shape else None
    out_refs, groups_ref = refs[:-1], refs[-1]
    me = lax.axis_index(axis) // 2
    pairs, owners, group, _ = groups_ref.shape
    for pair in range(pairs):
        cross = by_slot(cross_ref[pair])
        if own_factor_ref is None:
            result = own_ref[pair].astype(F32) + contract(partner_ref[pair], cross, ((1,), (1,)))
        else:
            weight = jnp.concatenate([by_slot(own_factor_ref[pair]), cross], axis=1)
            both = jnp.concatenate([own_ref[pair], partner_ref[pair]], axis=1)
            result = contract(both, weight, ((1,), (1,)))
        result = result.astype(BF16)
        if len(out_refs) == 1:
            out_refs[0][pair] = result
            continue
        for owner in range(owners):
            groups_ref[pair, owner] = result[owner * group : (owner + 1) * group]
    if len(out_refs) > 1:
        for k, out_ref in enumerate(out_refs):
            for pair in range(pairs):
                out_ref[pl.ds(pair * group, group)] = groups_ref[pair, me ^ k]


def last_states(name, after, own, partner, factors, owners):
    pairs, columns, lanes = own.shape
    group = columns // owners
    rows = pairs * group
    by_owner = group % 16 == 0 and owners > 1
    parts = call(
        functools.partial(last_level_kernel, "order"),
        name,
        [jax.ShapeDtypeStruct((rows, lanes), BF16)] * owners if by_owner else [jax.ShapeDtypeStruct(own.shape, BF16)],
        [ANYWHERE] + whole_blocks(2 + len(factors)),
        4 * pairs * columns * lanes * lanes,
        6 * pairs * columns * lanes,
        [pltpu.VMEM((pairs, owners, group, lanes), BF16)],
    )(after, own, partner, *factors)
    if by_owner:
        return parts
    me = lax.axis_index("order") // 2
    parts = [lax.dynamic_slice_in_dim(parts[0], (me ^ k) * group, group, 1) for k in range(owners)]
    return [part.reshape(rows, lanes) for part in parts]


def near_kernel(group, root_hbm, order_ref, after, root_ref, place_ref, alive_ref, rows_ref, sems):
    del after
    owners, here, _, degrees = root_ref.shape
    slots = rows_ref.shape[1]
    me = lax.axis_index("order")
    copies = []
    for k in range(owners):
        copies.append(pltpu.make_async_copy(root_hbm.at[pl.ds((me ^ k) * here, here)], root_ref.at[k], sems.at[k]))
        copies[-1].start()
    lane = lax.broadcasted_iota(jnp.int32, (1, slots), 1)
    for k in range(owners):
        for slot in range(here):
            pair, half = slot // 2, slot % 2
            row = (pair // group * 2 + half) * group + pair % group
            rows_ref[pl.ds(row, 1), :] = (lane == order_ref[(me ^ k) * here + slot]).astype(F32)
        place_ref[k] = rows_ref[...].astype(BF16)
    degree = lax.axis_index("lat") * degrees + lax.broadcasted_iota(jnp.int32, (degrees, slots), 0)
    window = DEGREES // slots * lax.broadcasted_iota(jnp.int32, (degrees, slots), 1)
    alive_ref[...] = (degree >= window).astype(F32).astype(BF16)
    for copy in copies:
        copy.wait()


def near_roots(root_basis, order_of_slot, owners, group, after):
    slots, rank, degrees = root_basis.shape
    here = slots // owners
    return call(
        functools.partial(near_kernel, group),
        "near_roots",
        [
            jax.ShapeDtypeStruct((owners, here, rank, degrees), BF16),
            jax.ShapeDtypeStruct((owners, here, slots), BF16),
            jax.ShapeDtypeStruct((degrees, slots), BF16),
        ],
        [IN_HBM, IN_SMEM, ANYWHERE],
        slots * slots,
        4 * slots * rank * degrees,
        [pltpu.VMEM((here, slots), F32), pltpu.SemaphoreType.DMA((owners,))],
    )(root_basis, order_of_slot, after)


def root_kernel(group, first, last, *refs):
    refs = list(refs)
    so_far_ref = refs.pop(0) if last else None
    root_ref, place_ref, alive_ref = refs[:3]
    count = len(refs) - (7 if last else 5)
    state_refs = refs[3 : 3 + count]
    out_ref, rows_ref = refs[3 + count : 5 + count]
    natural_ref = refs[5 + count] if last else out_ref
    fields, parts, degrees, slots = out_ref.shape
    columns = fields * parts
    rank = root_ref.shape[2]
    group_rows = group * columns
    here = place_ref.shape[1]
    steps = state_refs[0].shape[0] // group_rows
    shape = (group_rows, 2 * rank)
    row_pair = lax.broadcasted_iota(jnp.int32, shape, 0) // columns
    row_half = lax.broadcasted_iota(jnp.int32, shape, 1) // rank
    masks = [[(row_pair == pair) & (row_half == half) for pair in range(group)] for half in range(2)]
    empty = jnp.zeros(shape, BF16)
    for i, state_ref in enumerate(state_refs):
        for step in range(steps):
            state = state_ref[pl.ds(step * group_rows, group_rows)]
            left = jnp.concatenate(
                [jnp.concatenate([jnp.where(m, state, empty) for m in line], axis=1) for line in masks], axis=0
            )
            right = root_ref[first + i, pl.ds(step * group * 2, group * 2)].reshape(group * 2 * rank, degrees)
            product = contract(left, right, ((1,), (0,)))
            begin = (i * steps + step) * 2 * group_rows
            for tile in range(degrees // 128):
                rows_ref[tile, pl.ds(begin, 2 * group_rows), :] = product[:, tile * 128 : (tile + 1) * 128]
    place = place_ref[pl.ds(first, count)].reshape(count * here, slots)
    copies = []
    for column in range(columns):
        for tile in range(degrees // 128):
            span = slice(tile * 128, (tile + 1) * 128)
            one = rows_ref[tile, pl.ds(column, count * here, stride=columns), :].astype(BF16)
            natural = contract(one.T, place, ((1,), (0,))).astype(BF16)
            where = (column // 2, column % 2, span)
            if last:
                natural = natural + so_far_ref[where]
                natural = jnp.where(alive_ref[span] != 0, natural, jnp.zeros((), BF16))
            natural_ref[where] = natural
        if last:
            where = (column // 2, column % 2)
            copies.append(pltpu.make_async_copy(natural_ref.at[where], out_ref.at[where], refs[-1].at[column]))
            copies[-1].start()
    for copy in copies:
        copy.wait()


def spectra_of(states, roots, places, alive, so_far, first, group):
    state_rows, lanes = states[0].shape
    owners, here, rank, degrees = roots.shape
    slots = places.shape[2]
    columns = state_rows * 2 // here
    last = so_far is not None
    shape = (columns // 2, 2, degrees, slots)
    inputs = ([so_far] if last else []) + [roots, places, alive, *states]
    scratch = [pltpu.VMEM((degrees // 128, len(states) * here * columns, 128), F32)]
    more = {}
    if last:
        scratch += [pltpu.VMEM(shape, BF16), pltpu.SemaphoreType.DMA((columns,))]
        more["out_specs"] = IN_HBM
    return call(
        functools.partial(root_kernel, group, first, last),
        "root",
        jax.ShapeDtypeStruct(shape, BF16),
        whole_blocks(len(inputs)),
        2 * len(states) * here * rank * degrees * columns,
        2 * len(states) * here * rank * degrees,
        scratch,
        mib=24,
        **more,
    )(*inputs)


def per_device(
    fourier, quad_weights, leaf_basis, level_factors, sparsity, root_basis, order_of_slot
):
    slots, columns, lats = fourier.shape
    owners = lax.axis_size("order")
    levels = level_factors.shape[1]
    group = max(2, 16 * owners // columns)
    present = in_hbm(sparsity.transpose(1, 2, 0))
    fourier, leaf_basis, level_factors, root_basis = map(in_hbm, (fourier, leaf_basis, level_factors, root_basis))
    quad_weights = in_hbm(quad_weights.reshape(1, lats))

    def swap(array, axis, bits):
        return lax.ppermute(array, axis, [(i, i ^ bits) for i in range(lax.axis_size(axis))])

    def swap_both(array, order_bits, lat_bits):
        blocks = lax.axis_size("lat")
        pairs = [
            (o * blocks + b, (o ^ order_bits) * blocks + (b ^ lat_bits)) for o in range(owners) for b in range(blocks)
        ]
        return lax.ppermute(array, ("order", "lat"), pairs)

    state = leaf_states(fourier, quad_weights, leaf_basis, owners)
    partner = swap(state, "lat", 1)
    weights = level_weights(level_factors, present, (0,), state)
    states = [next_states(f"level0_{c}", state, partner, weights[0], c) for c in range(2)]
    weights += level_weights(level_factors, present, tuple(range(1, levels)), states[1])
    own_factors, cross_factors = weights[-2:]
    other_cross = swap(cross_factors, "order", 1)
    for level in range(1, levels - 1):
        partners = [swap(state, "lat", 1 << level) for state in states]
        states = [next_states(f"level{level}_{c}", states[c], partners[c], weights[level]) for c in range(2)]
    top = 1 << levels - 1
    partner = swap(states[0], "lat", top)
    other_partner = swap_both(states[1], 1, top)
    other_own = swap(own_term(states[1], states[1], own_factors), "order", 1)
    roots, places, alive = near_roots(root_basis, order_of_slot, owners, group, states[1])
    both = (
        last_states("last_own", alive, states[0], partner, (cross_factors, own_factors), owners // 2),
        last_states("last_other", alive, other_own, other_partner, (other_cross,), owners // 2),
    )
    arrived = [swap(both[k % 2][k // 2], "order", k // 2 * 2) if k > 1 else both[k][0] for k in range(owners)]
    early = 3 * owners // 4
    spectra = spectra_of(arrived[:early], roots, places, alive, None, 0, group)
    return spectra_of(arrived[early:], roots, places, alive, spectra, early, group)


def solution(mesh):
    return jax.shard_map(
        per_device,
        mesh=mesh,
        in_specs=(
            P("order", None, "lat"),
            P("lat"),
            P("order", None, "lat"),
            P("order", None, None, "lat", None, None),
            P("order", None, "lat"),
            P(None, None, "lat"),
            P(),
        ),
        out_specs=P("order", None, "lat", None),
        check_vma=False,
    )
```

```python
import functools

import jax
import jax.numpy as jnp
from jax import lax
from jax.experimental import pallas as pl
from jax.experimental.pallas import tpu as pltpu
from jax.sharding import PartitionSpec as P

DEGREES = 2048
F32, BF16 = jnp.float32, jnp.bfloat16
MIB = 1 << 20
IN_HBM = pl.BlockSpec(memory_space=pltpu.HBM)
IN_SMEM = pl.BlockSpec(memory_space=pltpu.SMEM)
ANYWHERE = pl.BlockSpec(memory_space=pl.ANY)


def contract(lhs, rhs, dims):
    return lax.dot_general(lhs, rhs, (dims, ((), ())), preferred_element_type=F32)


def in_hbm(array):
    return pltpu.with_memory_space_constraint(array, pltpu.HBM)


def call(kernel, name, out_shape, in_specs, flops, size, scratch=(), mib=16, **more):
    return pl.pallas_call(
        kernel,
        out_shape=out_shape,
        in_specs=in_specs,
        scratch_shapes=list(scratch),
        compiler_params=pltpu.CompilerParams(vmem_limit_bytes=mib * MIB),
        cost_estimate=pl.CostEstimate(flops=flops // 1000, bytes_accessed=size // 1000, transcendentals=0),
        name=name,
        **more,
    )


def whole_blocks(count):
    return [pl.BlockSpec()] * count


def leaf_kernel(
    pieces, group, fourier_hbm, weight_hbm, leaf_hbm, state_ref, fourier_ref, weight_ref, leaf_ref, sems
):
    side = lax.axis_index("order") & 1
    slots, columns, lats = fourier_ref.shape
    rank = leaf_ref.shape[1]
    per = slots // pieces
    copies = [pltpu.make_async_copy(weight_hbm, weight_ref, sems.at[0])]
    for piece in range(pieces):
        part = pl.ds(piece * per, per)
        copies.append(pltpu.make_async_copy(fourier_hbm.at[part], fourier_ref.at[part], sems.at[1 + 2 * piece]))
        copies.append(pltpu.make_async_copy(leaf_hbm.at[part], leaf_ref.at[part], sems.at[2 + 2 * piece]))
    for copy in copies:
        copy.start()
    copies[0].wait()
    weight = weight_ref[...]
    mine = lax.broadcasted_iota(jnp.int32, (columns, 2 * rank), 1) < rank
    for pair in range(slots // 2):
        if 2 * pair % per == 0:
            copies[1 + 2 * (2 * pair // per)].wait()
            copies[2 + 2 * (2 * pair // per)].wait()
        both = pl.ds(2 * pair, 2)
        weighted = (fourier_ref[both].astype(F32) * weight[None]).astype(BF16)
        product = contract(
            weighted.reshape(2 * columns, lats), leaf_ref[both].reshape(2 * rank, lats), ((1,), (1,))
        )
        state = jnp.where(mine, product[:columns], product[columns:]).astype(BF16)
        if group % 16:
            state_ref[pair] = state
            continue
        for owner in range(columns // group):
            rows = pl.ds(owner // 2 * group, group)
            state_ref[pair, owner % 2 ^ side, rows] = state[owner * group : (owner + 1) * group]


def leaf_states(fourier, quad_weights, leaf_basis, owners):
    slots, columns, lats = fourier.shape
    rank = leaf_basis.shape[1]
    pairs, half, lanes, group = slots // 2, columns // 2, 2 * rank, columns // owners
    pieces = 2
    state = call(
        functools.partial(leaf_kernel, pieces, group),
        "leaf",
        jax.ShapeDtypeStruct((pairs, columns, lanes) if group % 16 else (pairs, 2, half, lanes), BF16),
        [IN_HBM] * 3,
        2 * slots * columns * rank * lats,
        4 * slots * columns * lats,
        [
            pltpu.VMEM((slots, columns, lats), BF16),
            pltpu.VMEM((1, lats), F32),
            pltpu.VMEM((slots, rank, lats), BF16),
            pltpu.SemaphoreType.DMA((1 + 2 * pieces,)),
        ],
    )(fourier, quad_weights, leaf_basis)
    if group % 16:
        side = lax.axis_index("order") & 1
        state = state.reshape(pairs, owners // 2, 2, group, lanes)
        sides = [lax.dynamic_index_in_dim(state, side ^ i, 2, False).reshape(pairs, half, lanes) for i in range(2)]
        state = jnp.stack(sides, axis=1)
    return state


def factor_kernel(levels, pieces, factor_hbm, present_hbm, after, *refs):
    del after
    weight_refs, (factor_ref, present_ref, sems) = refs[:-3], refs[-3:]
    present_copy = pltpu.make_async_copy(present_hbm, present_ref, sems.at[len(levels) * pieces])
    present_copy.start()
    _, slots, _, rank, _ = factor_ref.shape
    per = slots // pieces
    copies = {}
    for i, level in enumerate(levels):
        for piece in range(pieces):
            part = pl.ds(piece * per, per)
            copies[i, piece] = pltpu.make_async_copy(
                factor_hbm.at[part, level, :, 0], factor_ref.at[i, part], sems.at[i * pieces + piece]
            )
            copies[i, piece].start()
    empty = jnp.zeros((rank, rank), BF16)
    present_copy.wait()
    for i, level in enumerate(levels):
        for pair in range(slots // 2):
            if 2 * pair % per == 0:
                copies[i, 2 * pair // per].wait()
            for half in range(2):
                first, second = (factor_ref[i, slot, half] for slot in (2 * pair, 2 * pair + 1))
                if half:
                    first = jnp.where(present_ref[level, 0, 2 * pair] != 0, first, empty)
                    second = jnp.where(present_ref[level, 0, 2 * pair + 1] != 0, second, empty)
                if weight_refs[i].shape[1] == rank:
                    weight_refs[i + half][pair] = jnp.concatenate([first, second], axis=1)
                    continue
                lanes = pl.ds(half * 2 * rank, 2 * rank)
                weight_refs[i][pair, :rank, lanes] = jnp.concatenate([first, empty], axis=1)
                weight_refs[i][pair, rank:, lanes] = jnp.concatenate([empty, second], axis=1)


def level_weights(level_factors, present, levels, after):
    slots, last, _, _, rank, _ = level_factors.shape
    count, pieces = len(levels), 2
    return call(
        functools.partial(factor_kernel, levels, pieces),
        "factors",
        [
            jax.ShapeDtypeStruct((slots // 2, *((rank, 2 * rank) if level == last - 1 else (2 * rank, 4 * rank))), BF16)
            for level in levels
            for _ in range(1 + (level == last - 1))
        ],
        [IN_HBM, IN_HBM, ANYWHERE],
        slots * rank * rank * 4 * count,
        slots * rank * rank * 16 * count,
        [
            pltpu.VMEM((count, slots, 2, rank, rank), BF16),
            pltpu.SMEM(present.shape, jnp.int32),
            pltpu.SemaphoreType.DMA((count * pieces + 1,)),
        ],
        mib=24,
    )(level_factors, present, after)


def level_kernel(side, axis, state_ref, partner_ref, weight_ref, *refs):
    out_ref = refs[0]
    me = lax.axis_index(axis) // 2
    for pair in range(weight_ref.shape[0]):
        at = pair if side is None else (pair, side)
        both = jnp.concatenate([state_ref[at], partner_ref[at]], axis=1)
        result = contract(both, weight_ref[pair], ((1,), (1,))).astype(BF16)
        if len(refs) == 1:
            out_ref[pair] = result
            continue
        early_ref, groups_ref = refs[1:]
        owners, group, _ = groups_ref.shape[1:]
        for owner in range(owners):
            groups_ref[pair, owner] = result[owner * group : (owner + 1) * group]
        for k in range(owners):
            rows = pl.ds((k - 1) % owners * group, group)
            part = groups_ref[pair, me ^ k]
            out_ref[pair, rows] = part
            if k:
                early_ref[pair, rows] = part


def next_states(name, state, partner, weights, side=None, owners=1):
    pairs, rows, lanes = state.shape[0], *state.shape[-2:]
    group = rows // owners
    split = owners > 1 and group % 16 == 0
    shapes = [(pairs, rows, lanes)] + [(pairs, rows - group, lanes)] * split
    outs = call(
        functools.partial(level_kernel, side, "order"),
        name,
        [jax.ShapeDtypeStruct(shape, BF16) for shape in shapes],
        whole_blocks(3),
        4 * pairs * rows * lanes * lanes,
        6 * pairs * rows * lanes,
        [pltpu.VMEM((pairs, owners, group, lanes), BF16)] if split else [],
    )(state, partner, weights)
    if owners > 1 and not split:
        me = lax.axis_index("order") // 2
        parts = [lax.dynamic_slice_in_dim(outs[0], (me ^ k) * group, group, 1) for k in range(owners)]
        early = jnp.concatenate(parts[1:], axis=1)
        return [jnp.concatenate([early, parts[0]], axis=1), early]
    return outs if split else outs[0]


def late_kernel(after, state_ref, out_ref):
    del after
    rows = out_ref.shape[1]
    for pair in range(state_ref.shape[0]):
        out_ref[pair] = state_ref[pair, state_ref.shape[1] - rows :]


def late_columns(after, state, rows):
    pairs, columns, lanes = state.shape
    if rows % 16:
        return state[:, columns - rows :]
    return call(
        late_kernel,
        "late_columns",
        jax.ShapeDtypeStruct((pairs, rows, lanes), BF16),
        [ANYWHERE] + whole_blocks(1),
        1,
        4 * pairs * rows * lanes,
    )(after, state)


def by_slot(packed):
    first = lax.broadcasted_iota(jnp.int32, packed.shape, 1) < packed.shape[0]
    empty = jnp.zeros(packed.shape, BF16)
    return jnp.concatenate([jnp.where(first, packed, empty), jnp.where(first, empty, packed)], axis=0)


def own_term_kernel(after, state_ref, own_ref, out_ref):
    del after
    for pair in range(state_ref.shape[0]):
        out_ref[pair] = contract(state_ref[pair], by_slot(own_ref[pair]), ((1,), (1,))).astype(BF16)


def own_term(after, state, own):
    pairs, rows, lanes = state.shape
    return call(
        own_term_kernel,
        "own_term",
        jax.ShapeDtypeStruct(state.shape, BF16),
        [ANYWHERE] + whole_blocks(2),
        2 * pairs * rows * lanes * lanes,
        6 * pairs * rows * lanes,
    )(after, state, own)


def last_level_kernel(turn, begin, axis, after, own_ref, partner_ref, cross_ref, *refs):
    del after
    refs = list(refs)
    own_factor_ref = refs.pop(0) if refs[0].shape == cross_ref.shape else None
    out_refs, groups_ref = refs[:-1], refs[-1]
    me = lax.axis_index(axis) // 2 if turn else 0
    pairs, owners, group, _ = groups_ref.shape
    for pair in range(pairs):
        cross = by_slot(cross_ref[pair])
        own = own_ref[pair, begin : begin + owners * group]
        if own_factor_ref is None:
            result = own.astype(F32) + contract(partner_ref[pair], cross, ((1,), (1,)))
        else:
            weight = jnp.concatenate([by_slot(own_factor_ref[pair]), cross], axis=1)
            both = jnp.concatenate([own, partner_ref[pair]], axis=1)
            result = contract(both, weight, ((1,), (1,)))
        result = result.astype(BF16)
        if group % 16:
            out_refs[0][pair] = result
            continue
        for owner in range(owners):
            groups_ref[pair, owner] = result[owner * group : (owner + 1) * group]
    if group % 16 == 0:
        for k, out_ref in enumerate(out_refs):
            for pair in range(pairs):
                out_ref[pl.ds(pair * group, group)] = groups_ref[pair, me ^ k]


def last_states(name, after, own, partner, factors, owners, turn, begin=0):
    pairs, columns, lanes = partner.shape
    group = columns // owners
    rows = pairs * group
    aligned = group % 16 == 0
    if not aligned:
        own = own[:, begin : begin + columns]
        begin = 0
    parts = call(
        functools.partial(last_level_kernel, turn, begin, "order"),
        name,
        [jax.ShapeDtypeStruct((rows, lanes), BF16)] * owners if aligned else [jax.ShapeDtypeStruct(own.shape, BF16)],
        [ANYWHERE] + whole_blocks(2 + len(factors)),
        4 * pairs * columns * lanes * lanes,
        6 * pairs * columns * lanes,
        [pltpu.VMEM((pairs, owners, group, lanes), BF16)],
    )(after, own, partner, *factors)
    if aligned:
        return parts
    me = lax.axis_index("order") // 2 if turn else 0
    parts = [lax.dynamic_slice_in_dim(parts[0], (me ^ k) * group, group, 1) for k in range(owners)]
    return [part.reshape(rows, lanes) for part in parts]


def near_kernel(group, root_hbm, order_ref, after, root_ref, place_ref, alive_ref, rows_ref, sems):
    del after
    owners, here, _, degrees = root_ref.shape
    slots = rows_ref.shape[1]
    me = lax.axis_index("order")
    copies = []
    for k in range(owners):
        copies.append(pltpu.make_async_copy(root_hbm.at[pl.ds((me ^ k) * here, here)], root_ref.at[k], sems.at[k]))
        copies[-1].start()
    lane = lax.broadcasted_iota(jnp.int32, (1, slots), 1)
    for k in range(owners):
        for slot in range(here):
            pair, half = slot // 2, slot % 2
            row = (pair // group * 2 + half) * group + pair % group
            rows_ref[pl.ds(row, 1), :] = (lane == order_ref[(me ^ k) * here + slot]).astype(F32)
        place_ref[k] = rows_ref[...].astype(BF16)
    degree = lax.axis_index("lat") * degrees + lax.broadcasted_iota(jnp.int32, (degrees, slots), 0)
    window = DEGREES // slots * lax.broadcasted_iota(jnp.int32, (degrees, slots), 1)
    alive_ref[...] = (degree >= window).astype(F32).astype(BF16)
    for copy in copies:
        copy.wait()


def near_roots(root_basis, order_of_slot, owners, group, after):
    slots, rank, degrees = root_basis.shape
    here = slots // owners
    return call(
        functools.partial(near_kernel, group),
        "near_roots",
        [
            jax.ShapeDtypeStruct((owners, here, rank, degrees), BF16),
            jax.ShapeDtypeStruct((owners, here, slots), BF16),
            jax.ShapeDtypeStruct((degrees, slots), BF16),
        ],
        [IN_HBM, IN_SMEM, ANYWHERE],
        slots * slots,
        4 * slots * rank * degrees,
        [pltpu.VMEM((here, slots), F32), pltpu.SemaphoreType.DMA((owners,))],
    )(root_basis, order_of_slot, after)


def root_kernel(group, first, last, *refs):
    refs = list(refs)
    so_far_ref = refs.pop(0) if last else None
    root_ref, place_ref, alive_ref = refs[:3]
    count = len(refs) - (7 if last else 5)
    state_refs = refs[3 : 3 + count]
    out_ref, rows_ref = refs[3 + count : 5 + count]
    natural_ref = refs[5 + count] if last else out_ref
    fields, parts, degrees, slots = out_ref.shape
    columns = fields * parts
    rank = root_ref.shape[2]
    group_rows = group * columns
    here = place_ref.shape[1]
    steps = state_refs[0].shape[0] // group_rows
    shape = (group_rows, 2 * rank)
    row_pair = lax.broadcasted_iota(jnp.int32, shape, 0) // columns
    row_half = lax.broadcasted_iota(jnp.int32, shape, 1) // rank
    masks = [[(row_pair == pair) & (row_half == half) for pair in range(group)] for half in range(2)]
    empty = jnp.zeros(shape, BF16)
    for i, state_ref in enumerate(state_refs):
        for step in range(steps):
            state = state_ref[pl.ds(step * group_rows, group_rows)]
            left = jnp.concatenate(
                [jnp.concatenate([jnp.where(m, state, empty) for m in line], axis=1) for line in masks], axis=0
            )
            right = root_ref[first + i, pl.ds(step * group * 2, group * 2)].reshape(group * 2 * rank, degrees)
            product = contract(left, right, ((1,), (0,)))
            begin = (i * steps + step) * 2 * group_rows
            for tile in range(degrees // 128):
                rows_ref[tile, pl.ds(begin, 2 * group_rows), :] = product[:, tile * 128 : (tile + 1) * 128]
    place = place_ref[pl.ds(first, count)].reshape(count * here, slots)
    copies = []
    for column in range(columns):
        for tile in range(degrees // 128):
            span = slice(tile * 128, (tile + 1) * 128)
            one = rows_ref[tile, pl.ds(column, count * here, stride=columns), :].astype(BF16)
            natural = contract(one.T, place, ((1,), (0,))).astype(BF16)
            where = (column // 2, column % 2, span)
            if last:
                natural = natural + so_far_ref[where]
                natural = jnp.where(alive_ref[span] != 0, natural, jnp.zeros((), BF16))
            natural_ref[where] = natural
        if last:
            where = (column // 2, column % 2)
            copies.append(pltpu.make_async_copy(natural_ref.at[where], out_ref.at[where], refs[-1].at[column]))
            copies[-1].start()
    for copy in copies:
        copy.wait()


def spectra_of(states, roots, places, alive, so_far, first, group):
    state_rows, lanes = states[0].shape
    owners, here, rank, degrees = roots.shape
    slots = places.shape[2]
    columns = state_rows * 2 // here
    last = so_far is not None
    shape = (columns // 2, 2, degrees, slots)
    inputs = ([so_far] if last else []) + [roots, places, alive, *states]
    scratch = [pltpu.VMEM((degrees // 128, len(states) * here * columns, 128), F32)]
    more = {}
    if last:
        scratch += [pltpu.VMEM(shape, BF16), pltpu.SemaphoreType.DMA((columns,))]
        more["out_specs"] = IN_HBM
    return call(
        functools.partial(root_kernel, group, first, last),
        "root",
        jax.ShapeDtypeStruct(shape, BF16),
        whole_blocks(len(inputs)),
        2 * len(states) * here * rank * degrees * columns,
        2 * len(states) * here * rank * degrees,
        scratch,
        mib=24,
        **more,
    )(*inputs)


def per_device(
    fourier, quad_weights, leaf_basis, level_factors, sparsity, root_basis, order_of_slot
):
    slots, columns, lats = fourier.shape
    owners = lax.axis_size("order")
    levels = level_factors.shape[1]
    group = max(2, 16 * owners // columns)
    present = in_hbm(sparsity.transpose(1, 2, 0))
    fourier, leaf_basis, level_factors, root_basis = map(in_hbm, (fourier, leaf_basis, level_factors, root_basis))
    quad_weights = in_hbm(quad_weights.reshape(1, lats))

    def swap(array, axis, bits):
        return lax.ppermute(array, axis, [(i, i ^ bits) for i in range(lax.axis_size(axis))])

    def swap_both(array, order_bits, lat_bits):
        blocks = lax.axis_size("lat")
        pairs = [
            (o * blocks + b, (o ^ order_bits) * blocks + (b ^ lat_bits)) for o in range(owners) for b in range(blocks)
        ]
        return lax.ppermute(array, ("order", "lat"), pairs)

    state = leaf_states(fourier, quad_weights, leaf_basis, owners)
    partner = swap(state, "lat", 1)
    weights = level_weights(level_factors, present, (0,), state)
    states = [next_states(f"level0_{c}", state, partner, weights[0], c) for c in range(2)]
    weights += level_weights(level_factors, present, tuple(range(1, levels)), states[1])
    own_factors, cross_factors = weights[-2:]
    other_cross = swap(cross_factors, "order", 1)
    high = owners // 2
    own_columns = columns // owners
    for level in range(1, levels - 1):
        partners = [swap(state, "lat", 1 << level) for state in states]
        parts = high if level == levels - 2 else 1
        states = [
            next_states(f"level{level}_{c}", states[c], partners[c], weights[level], None, parts if c else 1)
            for c in range(2)
        ]
    top = 1 << levels - 1
    mine, (other, early) = states
    mine_partner = swap(mine, "lat", top)
    early_partner = swap_both(early, 1, top)
    other_own = swap(own_term(other, other, own_factors), "order", 1)
    roots, places, alive = near_roots(root_basis, order_of_slot, owners, group, other)
    late_partner = swap_both(late_columns(alive, other, own_columns), 1, top)
    even = last_states("last_own", alive, mine, mine_partner, (cross_factors, own_factors), high, True)
    begin = columns // 2 - own_columns
    odd = last_states("last_early", alive, other_own, early_partner, (other_cross,), high - 1, False)
    odd = [*last_states("last_late", alive, other_own, late_partner, (other_cross,), 1, False, begin), *odd]
    arrived = [swap((odd if k % 2 else even)[k // 2], "order", k // 2 * 2) if k > 1 else (even, odd)[k][0] for k in range(owners)]
    early = 3 * owners // 4
    spectra = spectra_of(arrived[:early], roots, places, alive, None, 0, group)
    return spectra_of(arrived[early:], roots, places, alive, spectra, early, group)


def solution(mesh):
    return jax.shard_map(
        per_device,
        mesh=mesh,
        in_specs=(
            P("order", None, "lat"),
            P("lat"),
            P("order", None, "lat"),
            P("order", None, None, "lat", None, None),
            P("order", None, "lat"),
            P(None, None, "lat"),
            P(),
        ),
        out_specs=P("order", None, "lat", None),
        check_vma=False,
    )
```

```python
import functools

import jax
import jax.numpy as jnp
from jax import lax
from jax.experimental import pallas as pl
from jax.experimental.pallas import tpu as pltpu
from jax.sharding import PartitionSpec as P

DEGREES = 2048
F32, BF16 = jnp.float32, jnp.bfloat16
MIB = 1 << 20
IN_HBM = pl.BlockSpec(memory_space=pltpu.HBM)
IN_SMEM = pl.BlockSpec(memory_space=pltpu.SMEM)
ANYWHERE = pl.BlockSpec(memory_space=pl.ANY)


def contract(lhs, rhs, dims):
    return lax.dot_general(lhs, rhs, (dims, ((), ())), preferred_element_type=F32)


def in_hbm(array):
    return pltpu.with_memory_space_constraint(array, pltpu.HBM)


def call(kernel, name, out_shape, in_specs, flops, size, scratch=(), mib=16, **more):
    return pl.pallas_call(
        kernel,
        out_shape=out_shape,
        in_specs=in_specs,
        scratch_shapes=list(scratch),
        compiler_params=pltpu.CompilerParams(vmem_limit_bytes=mib * MIB),
        cost_estimate=pl.CostEstimate(flops=flops // 1000, bytes_accessed=size // 1000, transcendentals=0),
        name=name,
        **more,
    )


def whole_blocks(count):
    return [pl.BlockSpec()] * count


def leaf_kernel(
    pieces, group, fourier_hbm, weight_hbm, leaf_hbm, state_ref, fourier_ref, weight_ref, leaf_ref, sems
):
    side = lax.axis_index("order") & 1
    slots, columns, lats = fourier_ref.shape
    rank = leaf_ref.shape[1]
    per = slots // pieces
    copies = [pltpu.make_async_copy(weight_hbm, weight_ref, sems.at[0])]
    for piece in range(pieces):
        part = pl.ds(piece * per, per)
        copies.append(pltpu.make_async_copy(fourier_hbm.at[part], fourier_ref.at[part], sems.at[1 + 2 * piece]))
        copies.append(pltpu.make_async_copy(leaf_hbm.at[part], leaf_ref.at[part], sems.at[2 + 2 * piece]))
    for copy in copies:
        copy.start()
    copies[0].wait()
    weight = weight_ref[...]
    mine = lax.broadcasted_iota(jnp.int32, (columns, 2 * rank), 1) < rank
    for pair in range(slots // 2):
        if 2 * pair % per == 0:
            copies[1 + 2 * (2 * pair // per)].wait()
            copies[2 + 2 * (2 * pair // per)].wait()
        both = pl.ds(2 * pair, 2)
        weighted = (fourier_ref[both].astype(F32) * weight[None]).astype(BF16)
        product = contract(
            weighted.reshape(2 * columns, lats), leaf_ref[both].reshape(2 * rank, lats), ((1,), (1,))
        )
        state = jnp.where(mine, product[:columns], product[columns:]).astype(BF16)
        if group % 16:
            state_ref[pair] = state
            continue
        for owner in range(columns // group):
            rows = pl.ds(owner // 2 * group, group)
            state_ref[pair, owner % 2 ^ side, rows] = state[owner * group : (owner + 1) * group]


def leaf_states(fourier, quad_weights, leaf_basis, owners):
    slots, columns, lats = fourier.shape
    rank = leaf_basis.shape[1]
    pairs, half, lanes, group = slots // 2, columns // 2, 2 * rank, columns // owners
    pieces = 2
    state = call(
        functools.partial(leaf_kernel, pieces, group),
        "leaf",
        jax.ShapeDtypeStruct((pairs, columns, lanes) if group % 16 else (pairs, 2, half, lanes), BF16),
        [IN_HBM] * 3,
        2 * slots * columns * rank * lats,
        4 * slots * columns * lats,
        [
            pltpu.VMEM((slots, columns, lats), BF16),
            pltpu.VMEM((1, lats), F32),
            pltpu.VMEM((slots, rank, lats), BF16),
            pltpu.SemaphoreType.DMA((1 + 2 * pieces,)),
        ],
    )(fourier, quad_weights, leaf_basis)
    if group % 16:
        side = lax.axis_index("order") & 1
        state = state.reshape(pairs, owners // 2, 2, group, lanes)
        sides = [lax.dynamic_index_in_dim(state, side ^ i, 2, False).reshape(pairs, half, lanes) for i in range(2)]
        state = jnp.stack(sides, axis=1)
    return state


def factor_kernel(levels, pieces, factor_hbm, present_hbm, after, *refs):
    del after
    weight_refs, (factor_ref, present_ref, sems) = refs[:-3], refs[-3:]
    present_copy = pltpu.make_async_copy(present_hbm, present_ref, sems.at[len(levels) * pieces])
    present_copy.start()
    _, slots, _, rank, _ = factor_ref.shape
    per = slots // pieces
    copies = {}
    for i, level in enumerate(levels):
        for piece in range(pieces):
            part = pl.ds(piece * per, per)
            copies[i, piece] = pltpu.make_async_copy(
                factor_hbm.at[part, level, :, 0], factor_ref.at[i, part], sems.at[i * pieces + piece]
            )
            copies[i, piece].start()
    empty = jnp.zeros((rank, rank), BF16)
    present_copy.wait()
    for i, level in enumerate(levels):
        for pair in range(slots // 2):
            if 2 * pair % per == 0:
                copies[i, 2 * pair // per].wait()
            for half in range(2):
                first, second = (factor_ref[i, slot, half] for slot in (2 * pair, 2 * pair + 1))
                if half:
                    first = jnp.where(present_ref[level, 0, 2 * pair] != 0, first, empty)
                    second = jnp.where(present_ref[level, 0, 2 * pair + 1] != 0, second, empty)
                if weight_refs[i].shape[1] == rank:
                    weight_refs[i + half][pair] = jnp.concatenate([first, second], axis=1)
                    continue
                lanes = pl.ds(half * 2 * rank, 2 * rank)
                weight_refs[i][pair, :rank, lanes] = jnp.concatenate([first, empty], axis=1)
                weight_refs[i][pair, rank:, lanes] = jnp.concatenate([empty, second], axis=1)


def level_weights(level_factors, present, levels, after):
    slots, last, _, _, rank, _ = level_factors.shape
    count, pieces = len(levels), 2
    return call(
        functools.partial(factor_kernel, levels, pieces),
        "factors",
        [
            jax.ShapeDtypeStruct((slots // 2, *((rank, 2 * rank) if level == last - 1 else (2 * rank, 4 * rank))), BF16)
            for level in levels
            for _ in range(1 + (level == last - 1))
        ],
        [IN_HBM, IN_HBM, ANYWHERE],
        slots * rank * rank * 4 * count,
        slots * rank * rank * 16 * count,
        [
            pltpu.VMEM((count, slots, 2, rank, rank), BF16),
            pltpu.SMEM(present.shape, jnp.int32),
            pltpu.SemaphoreType.DMA((count * pieces + 1,)),
        ],
        mib=24,
    )(level_factors, present, after)


def level_kernel(side, axis, state_ref, partner_ref, weight_ref, *refs):
    out_ref = refs[0]
    me = lax.axis_index(axis) // 2
    for pair in range(weight_ref.shape[0]):
        at = pair if side is None else (pair, side)
        both = jnp.concatenate([state_ref[at], partner_ref[at]], axis=1)
        result = contract(both, weight_ref[pair], ((1,), (1,))).astype(BF16)
        if len(refs) == 1:
            out_ref[pair] = result
            continue
        early_ref, groups_ref = refs[1:]
        owners, group, _ = groups_ref.shape[1:]
        for owner in range(owners):
            groups_ref[pair, owner] = result[owner * group : (owner + 1) * group]
        for k in range(owners):
            rows = pl.ds((k - 1) % owners * group, group)
            part = groups_ref[pair, me ^ k]
            out_ref[pair, rows] = part
            if k:
                early_ref[pair, rows] = part


def next_states(name, state, partner, weights, side=None, owners=1):
    pairs, rows, lanes = state.shape[0], *state.shape[-2:]
    group = rows // owners
    split = owners > 1 and group % 16 == 0
    shapes = [(pairs, rows, lanes)] + [(pairs, rows - group, lanes)] * split
    outs = call(
        functools.partial(level_kernel, side, "order"),
        name,
        [jax.ShapeDtypeStruct(shape, BF16) for shape in shapes],
        whole_blocks(3),
        4 * pairs * rows * lanes * lanes,
        6 * pairs * rows * lanes,
        [pltpu.VMEM((pairs, owners, group, lanes), BF16)] if split else [],
    )(state, partner, weights)
    if owners > 1 and not split:
        me = lax.axis_index("order") // 2
        parts = [lax.dynamic_slice_in_dim(outs[0], (me ^ k) * group, group, 1) for k in range(owners)]
        early = jnp.concatenate(parts[1:], axis=1)
        return [jnp.concatenate([early, parts[0]], axis=1), early]
    return outs if split else outs[0]


def late_kernel(after, state_ref, out_ref):
    del after
    rows = out_ref.shape[1]
    for pair in range(state_ref.shape[0]):
        out_ref[pair] = state_ref[pair, state_ref.shape[1] - rows :]


def late_columns(after, state, rows):
    pairs, columns, lanes = state.shape
    if rows % 16:
        return state[:, columns - rows :]
    return call(
        late_kernel,
        "late_columns",
        jax.ShapeDtypeStruct((pairs, rows, lanes), BF16),
        [ANYWHERE] + whole_blocks(1),
        1,
        4 * pairs * rows * lanes,
    )(after, state)


def by_slot(packed):
    first = lax.broadcasted_iota(jnp.int32, packed.shape, 1) < packed.shape[0]
    empty = jnp.zeros(packed.shape, BF16)
    return jnp.concatenate([jnp.where(first, packed, empty), jnp.where(first, empty, packed)], axis=0)


def own_term_kernel(after, state_ref, own_ref, out_ref):
    del after
    for pair in range(state_ref.shape[0]):
        out_ref[pair] = contract(state_ref[pair], by_slot(own_ref[pair]), ((1,), (1,))).astype(BF16)


def own_term(after, state, own):
    pairs, rows, lanes = state.shape
    return call(
        own_term_kernel,
        "own_term",
        jax.ShapeDtypeStruct(state.shape, BF16),
        [ANYWHERE] + whole_blocks(2),
        2 * pairs * rows * lanes * lanes,
        6 * pairs * rows * lanes,
    )(after, state, own)


def last_level_kernel(turn, begin, axis, after, own_ref, partner_ref, cross_ref, *refs):
    del after
    refs = list(refs)
    own_factor_ref = refs.pop(0) if refs[0].shape == cross_ref.shape else None
    out_refs, groups_ref = refs[:-1], refs[-1]
    me = lax.axis_index(axis) // 2 if turn else 0
    pairs, owners, group, _ = groups_ref.shape
    for pair in range(pairs):
        cross = by_slot(cross_ref[pair])
        own = own_ref[pair, begin : begin + owners * group]
        if own_factor_ref is None:
            result = own.astype(F32) + contract(partner_ref[pair], cross, ((1,), (1,)))
        else:
            weight = jnp.concatenate([by_slot(own_factor_ref[pair]), cross], axis=1)
            both = jnp.concatenate([own, partner_ref[pair]], axis=1)
            result = contract(both, weight, ((1,), (1,)))
        result = result.astype(BF16)
        if group % 16:
            out_refs[0][pair] = result
            continue
        for owner in range(owners):
            groups_ref[pair, owner] = result[owner * group : (owner + 1) * group]
    if group % 16 == 0:
        for k, out_ref in enumerate(out_refs):
            for pair in range(pairs):
                out_ref[pl.ds(pair * group, group)] = groups_ref[pair, me ^ k]


def last_states(name, after, own, partner, factors, owners, turn, begin=0):
    pairs, columns, lanes = partner.shape
    group = columns // owners
    rows = pairs * group
    aligned = group % 16 == 0
    if not aligned:
        own = own[:, begin : begin + columns]
        begin = 0
    parts = call(
        functools.partial(last_level_kernel, turn, begin, "order"),
        name,
        [jax.ShapeDtypeStruct((rows, lanes), BF16)] * owners if aligned else [jax.ShapeDtypeStruct(own.shape, BF16)],
        [ANYWHERE] + whole_blocks(2 + len(factors)),
        4 * pairs * columns * lanes * lanes,
        6 * pairs * columns * lanes,
        [pltpu.VMEM((pairs, owners, group, lanes), BF16)],
    )(after, own, partner, *factors)
    if aligned:
        return parts
    me = lax.axis_index("order") // 2 if turn else 0
    parts = [lax.dynamic_slice_in_dim(parts[0], (me ^ k) * group, group, 1) for k in range(owners)]
    return [part.reshape(rows, lanes) for part in parts]


def near_kernel(group, root_hbm, order_ref, after, root_ref, place_ref, alive_ref, rows_ref, sems):
    del after
    early, here, _, degrees = root_ref.shape
    owners, _, slots = place_ref.shape
    me = lax.axis_index("order")
    copies = []
    for k in range(early):
        copies.append(pltpu.make_async_copy(root_hbm.at[pl.ds((me ^ k) * here, here)], root_ref.at[k], sems.at[k]))
        copies[-1].start()
    lane = lax.broadcasted_iota(jnp.int32, (1, slots), 1)
    for k in range(owners):
        for slot in range(here):
            pair, half = slot // 2, slot % 2
            row = (pair // group * 2 + half) * group + pair % group
            rows_ref[pl.ds(row, 1), :] = (lane == order_ref[(me ^ k) * here + slot]).astype(F32)
        place_ref[k] = rows_ref[...].astype(BF16)
    degree = lax.axis_index("lat") * degrees + lax.broadcasted_iota(jnp.int32, (degrees, slots), 0)
    window = DEGREES // slots * lax.broadcasted_iota(jnp.int32, (degrees, slots), 1)
    alive_ref[...] = (degree >= window).astype(F32).astype(BF16)
    for copy in copies:
        copy.wait()


def near_roots(root_basis, order_of_slot, owners, early, group, after):
    slots, rank, degrees = root_basis.shape
    here = slots // owners
    return call(
        functools.partial(near_kernel, group),
        "near_roots",
        [
            jax.ShapeDtypeStruct((early, here, rank, degrees), BF16),
            jax.ShapeDtypeStruct((owners, here, slots), BF16),
            jax.ShapeDtypeStruct((degrees, slots), BF16),
        ],
        [IN_HBM, IN_SMEM, ANYWHERE],
        slots * slots,
        4 * slots * rank * degrees,
        [pltpu.VMEM((here, slots), F32), pltpu.SemaphoreType.DMA((early,))],
    )(root_basis, order_of_slot, after)


def root_kernel(group, first, last, *refs):
    refs = list(refs)
    so_far_ref = refs.pop(0) if last else None
    root_ref, place_ref, alive_ref = refs[:3]
    count = root_ref.shape[0]
    state_refs, refs = refs[3 : 3 + count], refs[3 + count :]
    copies = []
    if last:
        out_ref, rows_ref, natural_ref, sems = refs
    else:
        root_hbm, out_ref, later_ref, rows_ref, sems = refs
        natural_ref = out_ref
        later, here = later_ref.shape[:2]
        for i in range(later):
            there = pl.ds((lax.axis_index("order") ^ (count + i)) * here, here)
            copies.append(pltpu.make_async_copy(root_hbm.at[there], later_ref.at[i], sems.at[i]))
            copies[-1].start()
    fields, parts, degrees, slots = out_ref.shape
    columns = fields * parts
    rank = root_ref.shape[2]
    group_rows = group * columns
    here = place_ref.shape[1]
    steps = state_refs[0].shape[0] // group_rows
    shape = (group_rows, 2 * rank)
    row_pair = lax.broadcasted_iota(jnp.int32, shape, 0) // columns
    row_half = lax.broadcasted_iota(jnp.int32, shape, 1) // rank
    masks = [[(row_pair == pair) & (row_half == half) for pair in range(group)] for half in range(2)]
    empty = jnp.zeros(shape, BF16)
    for i, state_ref in enumerate(state_refs):
        for step in range(steps):
            state = state_ref[pl.ds(step * group_rows, group_rows)]
            left = jnp.concatenate(
                [jnp.concatenate([jnp.where(m, state, empty) for m in line], axis=1) for line in masks], axis=0
            )
            right = root_ref[i, pl.ds(step * group * 2, group * 2)].reshape(group * 2 * rank, degrees)
            product = contract(left, right, ((1,), (0,)))
            begin = (i * steps + step) * 2 * group_rows
            for tile in range(degrees // 128):
                rows_ref[tile, pl.ds(begin, 2 * group_rows), :] = product[:, tile * 128 : (tile + 1) * 128]
    place = place_ref[pl.ds(first, count)].reshape(count * here, slots)
    per = max(1, fields // 4)
    for column in range(columns):
        for tile in range(degrees // 128):
            span = slice(tile * 128, (tile + 1) * 128)
            one = rows_ref[tile, pl.ds(column, count * here, stride=columns), :].astype(BF16)
            natural = contract(one.T, place, ((1,), (0,))).astype(BF16)
            where = (column // 2, column % 2, span)
            if last:
                natural = natural + so_far_ref[where]
                natural = jnp.where(alive_ref[span] != 0, natural, jnp.zeros((), BF16))
            natural_ref[where] = natural
        if last and (column + 1) % (2 * per) == 0:
            done = column // (2 * per)
            where = pl.ds(done * per, per)
            copies.append(pltpu.make_async_copy(natural_ref.at[where], out_ref.at[where], sems.at[done]))
            copies[-1].start()
    for copy in copies:
        copy.wait()


def spectra_of(states, roots, places, alive, so_far, first, group):
    state_rows = states[0].shape[0]
    count, here, rank, degrees = roots[0].shape
    owners, _, slots = places.shape
    columns = state_rows * 2 // here
    last = so_far is not None
    out = jax.ShapeDtypeStruct((columns // 2, 2, degrees, slots), BF16)
    inputs = [roots[0], places, alive, *states]
    in_specs = whole_blocks(len(inputs))
    scratch = [pltpu.VMEM((degrees // 128, count * here * columns, 128), F32)]
    more = {}
    if last:
        inputs = [so_far, *inputs]
        in_specs = whole_blocks(len(inputs))
        scratch += [pltpu.VMEM(out.shape, BF16), pltpu.SemaphoreType.DMA((columns // 2,))]
        more["out_specs"] = IN_HBM
    else:
        inputs.append(roots[1])
        in_specs.append(IN_HBM)
        out = [out, jax.ShapeDtypeStruct((owners - count, here, rank, degrees), BF16)]
        scratch.append(pltpu.SemaphoreType.DMA((owners - count,)))
    return call(
        functools.partial(root_kernel, group, first, last),
        "root",
        out,
        in_specs,
        2 * count * here * rank * degrees * columns,
        2 * count * here * rank * degrees,
        scratch,
        mib=24,
        **more,
    )(*inputs)


def per_device(
    fourier, quad_weights, leaf_basis, level_factors, sparsity, root_basis, order_of_slot
):
    slots, columns, lats = fourier.shape
    owners = lax.axis_size("order")
    levels = level_factors.shape[1]
    group = max(2, 16 * owners // columns)
    present = in_hbm(sparsity.transpose(1, 2, 0))
    fourier, leaf_basis, level_factors, root_basis = map(in_hbm, (fourier, leaf_basis, level_factors, root_basis))
    quad_weights = in_hbm(quad_weights.reshape(1, lats))

    def swap(array, axis, bits):
        return lax.ppermute(array, axis, [(i, i ^ bits) for i in range(lax.axis_size(axis))])

    def swap_both(array, order_bits, lat_bits):
        blocks = lax.axis_size("lat")
        pairs = [
            (o * blocks + b, (o ^ order_bits) * blocks + (b ^ lat_bits)) for o in range(owners) for b in range(blocks)
        ]
        return lax.ppermute(array, ("order", "lat"), pairs)

    state = leaf_states(fourier, quad_weights, leaf_basis, owners)
    partner = swap(state, "lat", 1)
    weights = level_weights(level_factors, present, (0,), state)
    states = [next_states(f"level0_{c}", state, partner, weights[0], c) for c in range(2)]
    weights += level_weights(level_factors, present, tuple(range(1, levels)), states[1])
    own_factors, cross_factors = weights[-2:]
    other_cross = swap(cross_factors, "order", 1)
    early_pieces = 3 * owners // 4
    high = owners // 2
    own_columns = columns // owners
    for level in range(1, levels - 1):
        partners = [swap(state, "lat", 1 << level) for state in states]
        parts = high if level == levels - 2 else 1
        states = [
            next_states(f"level{level}_{c}", states[c], partners[c], weights[level], None, parts if c else 1)
            for c in range(2)
        ]
    top = 1 << levels - 1
    mine, (other, early) = states
    mine_partner = swap(mine, "lat", top)
    early_partner = swap_both(early, 1, top)
    other_own = swap(own_term(other, other, own_factors), "order", 1)
    roots, places, alive = near_roots(root_basis, order_of_slot, owners, early_pieces, group, other)
    late_partner = swap_both(late_columns(alive, other, own_columns), 1, top)
    even = last_states("last_own", alive, mine, mine_partner, (cross_factors, own_factors), high, True)
    begin = columns // 2 - own_columns
    odd = last_states("last_early", alive, other_own, early_partner, (other_cross,), high - 1, False)
    odd = [*last_states("last_late", alive, other_own, late_partner, (other_cross,), 1, False, begin), *odd]
    arrived = [swap((odd if k % 2 else even)[k // 2], "order", k // 2 * 2) if k > 1 else (even, odd)[k][0] for k in range(owners)]
    roots = [roots, root_basis]
    spectra, later_roots = spectra_of(arrived[:early_pieces], roots, places, alive, None, 0, group)
    return spectra_of(arrived[early_pieces:], [later_roots], places, alive, spectra, early_pieces, group)


def solution(mesh):
    return jax.shard_map(
        per_device,
        mesh=mesh,
        in_specs=(
            P("order", None, "lat"),
            P("lat"),
            P("order", None, "lat"),
            P("order", None, None, "lat", None, None),
            P("order", None, "lat"),
            P(None, None, "lat"),
            P(),
        ),
        out_specs=P("order", None, "lat", None),
        check_vma=False,
    )
```

```python
import functools

import jax
import jax.numpy as jnp
from jax import lax
from jax.experimental import pallas as pl
from jax.experimental.pallas import tpu as pltpu
from jax.sharding import PartitionSpec as P

DEGREES = 2048
F32, BF16 = jnp.float32, jnp.bfloat16
MIB = 1 << 20
IN_HBM = pl.BlockSpec(memory_space=pltpu.HBM)
IN_SMEM = pl.BlockSpec(memory_space=pltpu.SMEM)
ANYWHERE = pl.BlockSpec(memory_space=pl.ANY)


def contract(lhs, rhs, dims):
    return lax.dot_general(lhs, rhs, (dims, ((), ())), preferred_element_type=F32)


def in_hbm(array):
    return pltpu.with_memory_space_constraint(array, pltpu.HBM)


def call(kernel, name, out_shape, in_specs, flops, size, scratch=(), mib=16, **more):
    return pl.pallas_call(
        kernel,
        out_shape=out_shape,
        in_specs=in_specs,
        scratch_shapes=list(scratch),
        compiler_params=pltpu.CompilerParams(vmem_limit_bytes=mib * MIB),
        cost_estimate=pl.CostEstimate(flops=flops // 1000, bytes_accessed=size // 1000, transcendentals=0),
        name=name,
        **more,
    )


def whole_blocks(count):
    return [pl.BlockSpec()] * count


def fetch_roots(k, root_hbm, root_ref, sem):
    here = root_ref.shape[0]
    me = lax.axis_index("order")
    return pltpu.make_async_copy(root_hbm.at[pl.ds((me ^ k) * here, here)], root_ref, sem)


def leaf_kernel(
    pieces, group, fourier_hbm, weight_hbm, leaf_hbm, root_hbm, state_ref, root_ref, fourier_ref, weight_ref, leaf_ref, sems
):
    side = lax.axis_index("order") & 1
    slots, columns, lats = fourier_ref.shape
    rank = leaf_ref.shape[1]
    per = slots // pieces
    copies = [pltpu.make_async_copy(weight_hbm, weight_ref, sems.at[0])]
    for piece in range(pieces):
        part = pl.ds(piece * per, per)
        copies.append(pltpu.make_async_copy(fourier_hbm.at[part], fourier_ref.at[part], sems.at[1 + 2 * piece]))
        copies.append(pltpu.make_async_copy(leaf_hbm.at[part], leaf_ref.at[part], sems.at[2 + 2 * piece]))
    copies.append(fetch_roots(0, root_hbm, root_ref, sems.at[1 + 2 * pieces]))
    for copy in copies:
        copy.start()
    copies[0].wait()
    weight = weight_ref[...]
    mine = lax.broadcasted_iota(jnp.int32, (columns, 2 * rank), 1) < rank
    for pair in range(slots // 2):
        if 2 * pair % per == 0:
            copies[1 + 2 * (2 * pair // per)].wait()
            copies[2 + 2 * (2 * pair // per)].wait()
        both = pl.ds(2 * pair, 2)
        weighted = (fourier_ref[both].astype(F32) * weight[None]).astype(BF16)
        product = contract(
            weighted.reshape(2 * columns, lats), leaf_ref[both].reshape(2 * rank, lats), ((1,), (1,))
        )
        state = jnp.where(mine, product[:columns], product[columns:]).astype(BF16)
        if group % 16:
            state_ref[pair] = state
            continue
        for owner in range(columns // group):
            rows = pl.ds(owner // 2 * group, group)
            state_ref[pair, owner % 2 ^ side, rows] = state[owner * group : (owner + 1) * group]
    copies[-1].wait()


def leaf_states(fourier, quad_weights, leaf_basis, root_basis, owners):
    slots, columns, lats = fourier.shape
    rank = leaf_basis.shape[1]
    pairs, half, lanes, group = slots // 2, columns // 2, 2 * rank, columns // owners
    pieces = 2
    shape = (pairs, columns, lanes) if group % 16 else (pairs, 2, half, lanes)
    state, root = call(
        functools.partial(leaf_kernel, pieces, group),
        "leaf",
        [
            jax.ShapeDtypeStruct(shape, BF16),
            jax.ShapeDtypeStruct((root_basis.shape[0] // owners, *root_basis.shape[1:]), BF16),
        ],
        [IN_HBM] * 4,
        2 * slots * columns * rank * lats,
        4 * slots * columns * lats,
        [
            pltpu.VMEM((slots, columns, lats), BF16),
            pltpu.VMEM((1, lats), F32),
            pltpu.VMEM((slots, rank, lats), BF16),
            pltpu.SemaphoreType.DMA((2 + 2 * pieces,)),
        ],
    )(fourier, quad_weights, leaf_basis, root_basis)
    if group % 16:
        side = lax.axis_index("order") & 1
        state = state.reshape(pairs, owners // 2, 2, group, lanes)
        sides = [lax.dynamic_index_in_dim(state, side ^ i, 2, False).reshape(pairs, half, lanes) for i in range(2)]
        state = jnp.stack(sides, axis=1)
    return state, root


def factor_kernel(levels, pieces, roots, factor_hbm, present_hbm, after, *refs):
    del after
    weight_refs, (factor_ref, present_ref, sems) = list(refs[:-3]), refs[-3:]
    fetches = []
    if roots:
        root_hbm, root_ref = weight_refs.pop(0), weight_refs.pop()
        fetches.append(fetch_roots(1, root_hbm, root_ref, sems.at[len(levels) * pieces + 1]))
    present_copy = pltpu.make_async_copy(present_hbm, present_ref, sems.at[len(levels) * pieces])
    present_copy.start()
    _, slots, _, rank, _ = factor_ref.shape
    per = slots // pieces
    copies = {}
    for i, level in enumerate(levels):
        for piece in range(pieces):
            part = pl.ds(piece * per, per)
            copies[i, piece] = pltpu.make_async_copy(
                factor_hbm.at[part, level, :, 0], factor_ref.at[i, part], sems.at[i * pieces + piece]
            )
            copies[i, piece].start()
    for fetch in fetches:
        fetch.start()
    empty = jnp.zeros((rank, rank), BF16)
    present_copy.wait()
    for i, level in enumerate(levels):
        for pair in range(slots // 2):
            if 2 * pair % per == 0:
                copies[i, 2 * pair // per].wait()
            for half in range(2):
                first, second = (factor_ref[i, slot, half] for slot in (2 * pair, 2 * pair + 1))
                if half:
                    first = jnp.where(present_ref[level, 0, 2 * pair] != 0, first, empty)
                    second = jnp.where(present_ref[level, 0, 2 * pair + 1] != 0, second, empty)
                if weight_refs[i].shape[1] == rank:
                    weight_refs[i + half][pair] = jnp.concatenate([first, second], axis=1)
                    continue
                lanes = pl.ds(half * 2 * rank, 2 * rank)
                weight_refs[i][pair, :rank, lanes] = jnp.concatenate([first, empty], axis=1)
                weight_refs[i][pair, rank:, lanes] = jnp.concatenate([empty, second], axis=1)
    for fetch in fetches:
        fetch.wait()


def level_weights(level_factors, present, levels, after, root_basis=None):
    slots, last, _, _, rank, _ = level_factors.shape
    count, pieces = len(levels), 2
    roots = []
    if root_basis is not None:
        roots = [jax.ShapeDtypeStruct((root_basis.shape[0] // lax.axis_size("order"), *root_basis.shape[1:]), BF16)]
    return call(
        functools.partial(factor_kernel, levels, pieces, root_basis is not None),
        "factors",
        [
            jax.ShapeDtypeStruct((slots // 2, *((rank, 2 * rank) if level == last - 1 else (2 * rank, 4 * rank))), BF16)
            for level in levels
            for _ in range(1 + (level == last - 1))
        ]
        + roots,
        [IN_HBM, IN_HBM, ANYWHERE] + [IN_HBM] * len(roots),
        slots * rank * rank * 4 * count,
        slots * rank * rank * 16 * count,
        [
            pltpu.VMEM((count, slots, 2, rank, rank), BF16),
            pltpu.SMEM(present.shape, jnp.int32),
            pltpu.SemaphoreType.DMA((count * pieces + 1 + len(roots),)),
        ],
        mib=24,
    )(level_factors, present, after, *([root_basis] if roots else []))


def level_kernel(side, axis, state_ref, partner_ref, weight_ref, *refs):
    if len(refs) > 1:
        own_ref, *refs = refs
    out_ref = refs[0]
    me = lax.axis_index(axis) // 2
    for pair in range(weight_ref.shape[0]):
        at = pair if side is None else (pair, side)
        both = jnp.concatenate([state_ref[at], partner_ref[at]], axis=1)
        result = contract(both, weight_ref[pair], ((1,), (1,))).astype(BF16)
        if len(refs) == 1:
            out_ref[pair] = result
            continue
        early_ref, term_ref, groups_ref = refs[1:]
        owners, group, _ = groups_ref.shape[1:]
        for owner in range(owners):
            groups_ref[pair, owner] = result[owner * group : (owner + 1) * group]
        for k in range(owners):
            rows = pl.ds((k - 1) % owners * group, group)
            part = groups_ref[pair, me ^ k]
            out_ref[pair, rows] = part
            if k:
                early_ref[pair, rows] = part
        term_ref[pair] = contract(out_ref[pair], by_slot(own_ref[pair]), ((1,), (1,))).astype(BF16)


def next_states(name, state, partner, weights, side=None, owners=1, own=None):
    pairs, rows, lanes = state.shape[0], *state.shape[-2:]
    group = rows // owners
    split = owners > 1 and group % 16 == 0
    shapes = [(pairs, rows, lanes)] + [(pairs, rows - group, lanes), (pairs, rows, lanes)] * split
    outs = call(
        functools.partial(level_kernel, side, "order"),
        name,
        [jax.ShapeDtypeStruct(shape, BF16) for shape in shapes],
        whole_blocks(3 + split),
        4 * pairs * rows * lanes * lanes,
        6 * pairs * rows * lanes,
        [pltpu.VMEM((pairs, owners, group, lanes), BF16)] if split else [],
    )(state, partner, weights, *([own] if split else []))
    if owners > 1 and not split:
        me = lax.axis_index("order") // 2
        parts = [lax.dynamic_slice_in_dim(outs[0], (me ^ k) * group, group, 1) for k in range(owners)]
        early = jnp.concatenate(parts[1:], axis=1)
        state = jnp.concatenate([early, parts[0]], axis=1)
        return [state, early, own_term(state, own)]
    return outs if split else outs[0]


def late_kernel(after, state_ref, out_ref):
    del after
    rows = out_ref.shape[1]
    for pair in range(state_ref.shape[0]):
        out_ref[pair] = state_ref[pair, state_ref.shape[1] - rows :]


def late_columns(after, state, rows):
    pairs, columns, lanes = state.shape
    if rows % 16:
        return state[:, columns - rows :]
    return call(
        late_kernel,
        "late_columns",
        jax.ShapeDtypeStruct((pairs, rows, lanes), BF16),
        [ANYWHERE] + whole_blocks(1),
        1,
        4 * pairs * rows * lanes,
    )(after, state)


def by_slot(packed):
    first = lax.broadcasted_iota(jnp.int32, packed.shape, 1) < packed.shape[0]
    empty = jnp.zeros(packed.shape, BF16)
    return jnp.concatenate([jnp.where(first, packed, empty), jnp.where(first, empty, packed)], axis=0)


def own_term_kernel(state_ref, own_ref, out_ref):
    for pair in range(state_ref.shape[0]):
        out_ref[pair] = contract(state_ref[pair], by_slot(own_ref[pair]), ((1,), (1,))).astype(BF16)


def own_term(state, own):
    pairs, rows, lanes = state.shape
    return call(
        own_term_kernel,
        "own_term",
        jax.ShapeDtypeStruct(state.shape, BF16),
        whole_blocks(2),
        2 * pairs * rows * lanes * lanes,
        6 * pairs * rows * lanes,
    )(state, own)


def last_level_kernel(turn, begin, axis, after, own_ref, partner_ref, cross_ref, *refs):
    del after
    refs = list(refs)
    own_factor_ref = refs.pop(0) if refs[0].shape == cross_ref.shape else None
    out_refs, groups_ref = refs[:-1], refs[-1]
    me = lax.axis_index(axis) // 2 if turn else 0
    pairs, owners, group, _ = groups_ref.shape
    for pair in range(pairs):
        cross = by_slot(cross_ref[pair])
        own = own_ref[pair, begin : begin + owners * group]
        if own_factor_ref is None:
            result = own.astype(F32) + contract(partner_ref[pair], cross, ((1,), (1,)))
        else:
            weight = jnp.concatenate([by_slot(own_factor_ref[pair]), cross], axis=1)
            both = jnp.concatenate([own, partner_ref[pair]], axis=1)
            result = contract(both, weight, ((1,), (1,)))
        result = result.astype(BF16)
        if group % 16:
            out_refs[0][pair] = result
            continue
        for owner in range(owners):
            groups_ref[pair, owner] = result[owner * group : (owner + 1) * group]
    if group % 16 == 0:
        for k, out_ref in enumerate(out_refs):
            for pair in range(pairs):
                out_ref[pl.ds(pair * group, group)] = groups_ref[pair, me ^ k]


def last_states(name, after, own, partner, factors, owners, turn, begin=0):
    pairs, columns, lanes = partner.shape
    group = columns // owners
    rows = pairs * group
    aligned = group % 16 == 0
    if not aligned:
        own = own[:, begin : begin + columns]
        begin = 0
    parts = call(
        functools.partial(last_level_kernel, turn, begin, "order"),
        name,
        [jax.ShapeDtypeStruct((rows, lanes), BF16)] * owners if aligned else [jax.ShapeDtypeStruct(own.shape, BF16)],
        [ANYWHERE] + whole_blocks(2 + len(factors)),
        4 * pairs * columns * lanes * lanes,
        6 * pairs * columns * lanes,
        [pltpu.VMEM((pairs, owners, group, lanes), BF16)],
    )(after, own, partner, *factors)
    if aligned:
        return parts
    me = lax.axis_index("order") // 2 if turn else 0
    parts = [lax.dynamic_slice_in_dim(parts[0], (me ^ k) * group, group, 1) for k in range(owners)]
    return [part.reshape(rows, lanes) for part in parts]


def near_kernel(group, root_hbm, order_ref, after, root_ref, place_ref, alive_ref, rows_ref, sems):
    del after
    early = root_ref.shape[0]
    owners, here, slots = place_ref.shape
    degrees = alive_ref.shape[0]
    me = lax.axis_index("order")
    copies = []
    for k in range(early):
        copies.append(fetch_roots(2 + k, root_hbm, root_ref.at[k], sems.at[k]))
        copies[-1].start()
    lane = lax.broadcasted_iota(jnp.int32, (1, slots), 1)
    for k in range(owners):
        for slot in range(here):
            pair, half = slot // 2, slot % 2
            row = (pair // group * 2 + half) * group + pair % group
            rows_ref[pl.ds(row, 1), :] = (lane == order_ref[(me ^ k) * here + slot]).astype(F32)
        place_ref[k] = rows_ref[...].astype(BF16)
    degree = lax.axis_index("lat") * degrees + lax.broadcasted_iota(jnp.int32, (degrees, slots), 0)
    window = DEGREES // slots * lax.broadcasted_iota(jnp.int32, (degrees, slots), 1)
    alive_ref[...] = (degree >= window).astype(F32).astype(BF16)
    for copy in copies:
        copy.wait()


def near_roots(root_basis, order_of_slot, owners, early, group, after):
    slots, rank, degrees = root_basis.shape
    here = slots // owners
    return call(
        functools.partial(near_kernel, group),
        "near_roots",
        [
            jax.ShapeDtypeStruct((early, here, rank, degrees), BF16),
            jax.ShapeDtypeStruct((owners, here, slots), BF16),
            jax.ShapeDtypeStruct((degrees, slots), BF16),
        ],
        [IN_HBM, IN_SMEM, ANYWHERE],
        slots * slots,
        4 * slots * rank * degrees,
        [pltpu.VMEM((here, slots), F32), pltpu.SemaphoreType.DMA((early,))],
    )(root_basis, order_of_slot, after)


def root_kernel(group, first, last, *refs):
    refs = list(refs)
    so_far_ref = refs.pop(0) if last else None
    place_ref, alive_ref = refs.pop(0), refs.pop(0)
    count = place_ref.shape[0] - first if last else first
    first = first if last else 0
    root_refs = refs[:count]
    if last:
        root_refs = [refs[0].at[i] for i in range(count)]
    elif count > 2:
        root_refs = refs[:2] + [refs[2].at[i] for i in range(count - 2)]
    refs = refs[1:] if last else refs[3:]
    state_refs, refs = refs[:count], refs[count:]
    copies = []
    if last:
        out_ref, rows_ref, natural_ref, sems = refs
    else:
        root_hbm, out_ref, later_ref, rows_ref, sems = refs
        natural_ref = out_ref
        for i in range(later_ref.shape[0]):
            copies.append(fetch_roots(count + i, root_hbm, later_ref.at[i], sems.at[i]))
            copies[-1].start()
    fields, parts, degrees, slots = out_ref.shape
    columns = fields * parts
    rank = root_refs[0].shape[1]
    group_rows = group * columns
    here = place_ref.shape[1]
    steps = state_refs[0].shape[0] // group_rows
    shape = (group_rows, 2 * rank)
    row_pair = lax.broadcasted_iota(jnp.int32, shape, 0) // columns
    row_half = lax.broadcasted_iota(jnp.int32, shape, 1) // rank
    masks = [[(row_pair == pair) & (row_half == half) for pair in range(group)] for half in range(2)]
    empty = jnp.zeros(shape, BF16)
    for i, state_ref in enumerate(state_refs):
        for step in range(steps):
            state = state_ref[pl.ds(step * group_rows, group_rows)]
            left = jnp.concatenate(
                [jnp.concatenate([jnp.where(m, state, empty) for m in line], axis=1) for line in masks], axis=0
            )
            right = root_refs[i][pl.ds(step * group * 2, group * 2)].reshape(group * 2 * rank, degrees)
            product = contract(left, right, ((1,), (0,)))
            begin = (i * steps + step) * 2 * group_rows
            for tile in range(degrees // 128):
                rows_ref[tile, pl.ds(begin, 2 * group_rows), :] = product[:, tile * 128 : (tile + 1) * 128]
    place = place_ref[pl.ds(first, count)].reshape(count * here, slots)
    per = max(1, fields // 4)
    for column in range(columns):
        for tile in range(degrees // 128):
            span = slice(tile * 128, (tile + 1) * 128)
            one = rows_ref[tile, pl.ds(column, count * here, stride=columns), :].astype(BF16)
            natural = contract(one.T, place, ((1,), (0,))).astype(BF16)
            where = (column // 2, column % 2, span)
            if last:
                natural = natural + so_far_ref[where]
                natural = jnp.where(alive_ref[span] != 0, natural, jnp.zeros((), BF16))
            natural_ref[where] = natural
        if last and (column + 1) % (2 * per) == 0:
            done = column // (2 * per)
            where = pl.ds(done * per, per)
            copies.append(pltpu.make_async_copy(natural_ref.at[where], out_ref.at[where], sems.at[done]))
            copies[-1].start()
    for copy in copies:
        copy.wait()


def spectra_of(states, roots, places, alive, so_far, first, group):
    state_rows = states[0].shape[0]
    rank, degrees = roots[0].shape[-2:]
    owners, here, slots = places.shape
    count = len(states)
    columns = state_rows * 2 // here
    last = so_far is not None
    out = jax.ShapeDtypeStruct((columns // 2, 2, degrees, slots), BF16)
    root_basis = roots[-1]
    inputs = [places, alive, *(roots if so_far is not None else roots[:-1]), *states]
    in_specs = whole_blocks(len(inputs))
    scratch = [pltpu.VMEM((degrees // 128, count * here * columns, 128), F32)]
    more = {}
    if last:
        inputs = [so_far, *inputs]
        in_specs = whole_blocks(len(inputs))
        scratch += [pltpu.VMEM(out.shape, BF16), pltpu.SemaphoreType.DMA((columns // 2,))]
        more["out_specs"] = IN_HBM
    else:
        inputs.append(root_basis)
        in_specs.append(IN_HBM)
        out = [out, jax.ShapeDtypeStruct((owners - count, here, rank, degrees), BF16)]
        scratch.append(pltpu.SemaphoreType.DMA((owners - count,)))
    return call(
        functools.partial(root_kernel, group, first, last),
        "root",
        out,
        in_specs,
        2 * count * here * rank * degrees * columns,
        2 * count * here * rank * degrees,
        scratch,
        mib=24,
        **more,
    )(*inputs)


def per_device(
    fourier, quad_weights, leaf_basis, level_factors, sparsity, root_basis, order_of_slot
):
    slots, columns, lats = fourier.shape
    owners = lax.axis_size("order")
    levels = level_factors.shape[1]
    group = max(2, 16 * owners // columns)
    present = in_hbm(sparsity.transpose(1, 2, 0))
    fourier, leaf_basis, level_factors, root_basis = map(in_hbm, (fourier, leaf_basis, level_factors, root_basis))
    quad_weights = in_hbm(quad_weights.reshape(1, lats))

    def swap(array, axis, bits):
        return lax.ppermute(array, axis, [(i, i ^ bits) for i in range(lax.axis_size(axis))])

    def swap_both(array, order_bits, lat_bits):
        blocks = lax.axis_size("lat")
        pairs = [
            (o * blocks + b, (o ^ order_bits) * blocks + (b ^ lat_bits)) for o in range(owners) for b in range(blocks)
        ]
        return lax.ppermute(array, ("order", "lat"), pairs)

    state, root_0 = leaf_states(fourier, quad_weights, leaf_basis, root_basis, owners)
    partner = swap(state, "lat", 1)
    weights = level_weights(level_factors, present, (0,), state)
    states = [next_states(f"level0_{c}", state, partner, weights[0], c) for c in range(2)]
    weights += level_weights(level_factors, present, tuple(range(1, levels)), states[1], root_basis)
    own_factors, cross_factors, root_1 = weights[-3:]
    other_cross = swap(cross_factors, "order", 1)
    early_pieces = 3 * owners // 4
    high = owners // 2
    own_columns = columns // owners
    for level in range(1, levels - 1):
        partners = [swap(state, "lat", 1 << level) for state in states]
        parts = high if level == levels - 2 else 1
        states = [
            next_states(f"level{level}_{c}", states[c], partners[c], weights[level], None, parts if c else 1, own_factors)
            for c in range(2)
        ]
    top = 1 << levels - 1
    mine, (other, early, term) = states
    mine_partner = swap(mine, "lat", top)
    early_partner = swap_both(early, 1, top)
    other_own = swap(term, "order", 1)
    roots, places, alive = near_roots(root_basis, order_of_slot, owners, early_pieces - 2, group, other)
    late_partner = swap_both(late_columns(alive, other, own_columns), 1, top)
    even = last_states("last_own", alive, mine, mine_partner, (cross_factors, own_factors), high, True)
    begin = columns // 2 - own_columns
    odd = last_states("last_early", alive, other_own, early_partner, (other_cross,), high - 1, False)
    odd = [*last_states("last_late", alive, other_own, late_partner, (other_cross,), 1, False, begin), *odd]
    arrived = [swap((odd if k % 2 else even)[k // 2], "order", k // 2 * 2) if k > 1 else (even, odd)[k][0] for k in range(owners)]
    roots = [root_0, root_1, roots, root_basis]
    spectra, later_roots = spectra_of(arrived[:early_pieces], roots, places, alive, None, early_pieces, group)
    return spectra_of(arrived[early_pieces:], [later_roots], places, alive, spectra, early_pieces, group)


def solution(mesh):
    return jax.shard_map(
        per_device,
        mesh=mesh,
        in_specs=(
            P("order", None, "lat"),
            P("lat"),
            P("order", None, "lat"),
            P("order", None, None, "lat", None, None),
            P("order", None, "lat"),
            P(None, None, "lat"),
            P(),
        ),
        out_specs=P("order", None, "lat", None),
        check_vma=False,
    )
```

```python
import functools

import jax
import jax.numpy as jnp
from jax import lax
from jax.experimental import pallas as pl
from jax.experimental.pallas import tpu as pltpu
from jax.sharding import PartitionSpec as P

DEGREES = 2048
F32, BF16 = jnp.float32, jnp.bfloat16
MIB = 1 << 20
IN_HBM = pl.BlockSpec(memory_space=pltpu.HBM)
IN_SMEM = pl.BlockSpec(memory_space=pltpu.SMEM)
ANYWHERE = pl.BlockSpec(memory_space=pl.ANY)


def contract(lhs, rhs, dims):
    return lax.dot_general(lhs, rhs, (dims, ((), ())), preferred_element_type=F32)


def in_hbm(array):
    return pltpu.with_memory_space_constraint(array, pltpu.HBM)


def call(kernel, name, out_shape, in_specs, flops, size, scratch=(), mib=16, **more):
    return pl.pallas_call(
        kernel,
        out_shape=out_shape,
        in_specs=in_specs,
        scratch_shapes=list(scratch),
        compiler_params=pltpu.CompilerParams(vmem_limit_bytes=mib * MIB),
        cost_estimate=pl.CostEstimate(flops=flops // 1000, bytes_accessed=size // 1000, transcendentals=0),
        name=name,
        **more,
    )


def whole_blocks(count):
    return [pl.BlockSpec()] * count


def fetch_roots(k, root_hbm, root_ref, sem):
    here = root_ref.shape[0]
    me = lax.axis_index("order")
    return pltpu.make_async_copy(root_hbm.at[pl.ds((me ^ k) * here, here)], root_ref, sem)


def leaf_kernel(
    pieces, group, fourier_hbm, weight_hbm, leaf_hbm, root_hbm, state_ref, root_ref, fourier_ref, weight_ref, leaf_ref, sems
):
    side = lax.axis_index("order") & 1
    slots, columns, lats = fourier_ref.shape
    rank = leaf_ref.shape[1]
    per = slots // pieces
    copies = [pltpu.make_async_copy(weight_hbm, weight_ref, sems.at[0])]
    for piece in range(pieces):
        part = pl.ds(piece * per, per)
        copies.append(pltpu.make_async_copy(fourier_hbm.at[part], fourier_ref.at[part], sems.at[1 + 2 * piece]))
        copies.append(pltpu.make_async_copy(leaf_hbm.at[part], leaf_ref.at[part], sems.at[2 + 2 * piece]))
    copies.append(fetch_roots(0, root_hbm, root_ref, sems.at[1 + 2 * pieces]))
    for copy in copies:
        copy.start()
    copies[0].wait()
    weight = weight_ref[...]
    mine = lax.broadcasted_iota(jnp.int32, (columns, 2 * rank), 1) < rank
    for pair in range(slots // 2):
        if 2 * pair % per == 0:
            copies[1 + 2 * (2 * pair // per)].wait()
            copies[2 + 2 * (2 * pair // per)].wait()
        both = pl.ds(2 * pair, 2)
        weighted = (fourier_ref[both].astype(F32) * weight[None]).astype(BF16)
        product = contract(
            weighted.reshape(2 * columns, lats), leaf_ref[both].reshape(2 * rank, lats), ((1,), (1,))
        )
        state = jnp.where(mine, product[:columns], product[columns:]).astype(BF16)
        if group % 16:
            state_ref[pair] = state
            continue
        for owner in range(columns // group):
            rows = pl.ds(owner // 2 * group, group)
            state_ref[pair, owner % 2 ^ side, rows] = state[owner * group : (owner + 1) * group]
    copies[-1].wait()


def leaf_states(fourier, quad_weights, leaf_basis, root_basis, owners):
    slots, columns, lats = fourier.shape
    rank = leaf_basis.shape[1]
    pairs, half, lanes, group = slots // 2, columns // 2, 2 * rank, columns // owners
    pieces = 2
    shape = (pairs, columns, lanes) if group % 16 else (pairs, 2, half, lanes)
    state, root = call(
        functools.partial(leaf_kernel, pieces, group),
        "leaf",
        [
            jax.ShapeDtypeStruct(shape, BF16),
            jax.ShapeDtypeStruct((root_basis.shape[0] // owners, *root_basis.shape[1:]), BF16),
        ],
        [IN_HBM] * 4,
        2 * slots * columns * rank * lats,
        4 * slots * columns * lats,
        [
            pltpu.VMEM((slots, columns, lats), BF16),
            pltpu.VMEM((1, lats), F32),
            pltpu.VMEM((slots, rank, lats), BF16),
            pltpu.SemaphoreType.DMA((2 + 2 * pieces,)),
        ],
    )(fourier, quad_weights, leaf_basis, root_basis)
    if group % 16:
        side = lax.axis_index("order") & 1
        state = state.reshape(pairs, owners // 2, 2, group, lanes)
        sides = [lax.dynamic_index_in_dim(state, side ^ i, 2, False).reshape(pairs, half, lanes) for i in range(2)]
        state = jnp.stack(sides, axis=1)
    return state, root


def factor_kernel(levels, pieces, roots, factor_hbm, present_hbm, after, *refs):
    del after
    weight_refs, (factor_ref, present_ref, sems) = list(refs[:-3]), refs[-3:]
    fetches = []
    if roots:
        root_hbm, root_ref = weight_refs.pop(0), weight_refs.pop()
        for i in range(root_ref.shape[0]):
            fetches.append(fetch_roots(1 + i, root_hbm, root_ref.at[i], sems.at[len(levels) * pieces + 1 + i]))
    present_copy = pltpu.make_async_copy(present_hbm, present_ref, sems.at[len(levels) * pieces])
    present_copy.start()
    _, slots, _, rank, _ = factor_ref.shape
    per = slots // pieces
    copies = {}
    for i, level in enumerate(levels):
        for piece in range(pieces):
            part = pl.ds(piece * per, per)
            copies[i, piece] = pltpu.make_async_copy(
                factor_hbm.at[part, level, :, 0], factor_ref.at[i, part], sems.at[i * pieces + piece]
            )
            copies[i, piece].start()
    for fetch in fetches:
        fetch.start()
    empty = jnp.zeros((rank, rank), BF16)
    present_copy.wait()
    for i, level in enumerate(levels):
        for pair in range(slots // 2):
            if 2 * pair % per == 0:
                copies[i, 2 * pair // per].wait()
            for half in range(2):
                first, second = (factor_ref[i, slot, half] for slot in (2 * pair, 2 * pair + 1))
                if half:
                    first = jnp.where(present_ref[level, 0, 2 * pair] != 0, first, empty)
                    second = jnp.where(present_ref[level, 0, 2 * pair + 1] != 0, second, empty)
                if weight_refs[i].shape[1] == rank:
                    weight_refs[i + half][pair] = jnp.concatenate([first, second], axis=1)
                    continue
                lanes = pl.ds(half * 2 * rank, 2 * rank)
                weight_refs[i][pair, :rank, lanes] = jnp.concatenate([first, empty], axis=1)
                weight_refs[i][pair, rank:, lanes] = jnp.concatenate([empty, second], axis=1)
    for fetch in fetches:
        fetch.wait()


def level_weights(level_factors, present, levels, after, root_basis=None, root_pieces=0):
    slots, last, _, _, rank, _ = level_factors.shape
    count, pieces = len(levels), 2
    roots = []
    if root_pieces:
        here = root_basis.shape[0] // lax.axis_size("order")
        roots = [jax.ShapeDtypeStruct((root_pieces, here, *root_basis.shape[1:]), BF16)]
    return call(
        functools.partial(factor_kernel, levels, pieces, root_pieces),
        "factors",
        [
            jax.ShapeDtypeStruct((slots // 2, *((rank, 2 * rank) if level == last - 1 else (2 * rank, 4 * rank))), BF16)
            for level in levels
            for _ in range(1 + (level == last - 1))
        ]
        + roots,
        [IN_HBM, IN_HBM, ANYWHERE] + [IN_HBM] * len(roots),
        slots * rank * rank * 4 * count,
        slots * rank * rank * 16 * count,
        [
            pltpu.VMEM((count, slots, 2, rank, rank), BF16),
            pltpu.SMEM(present.shape, jnp.int32),
            pltpu.SemaphoreType.DMA((count * pieces + 1 + root_pieces,)),
        ],
        mib=24,
    )(level_factors, present, after, *([root_basis] if roots else []))


def level_kernel(side, axis, state_ref, partner_ref, weight_ref, *refs):
    if len(refs) > 1:
        own_ref, *refs = refs
    out_ref = refs[0]
    me = lax.axis_index(axis) // 2
    for pair in range(weight_ref.shape[0]):
        at = pair if side is None else (pair, side)
        both = jnp.concatenate([state_ref[at], partner_ref[at]], axis=1)
        result = contract(both, weight_ref[pair], ((1,), (1,))).astype(BF16)
        if len(refs) == 1:
            out_ref[pair] = result
            continue
        early_ref, term_ref, groups_ref = refs[1:]
        owners, group, _ = groups_ref.shape[1:]
        for owner in range(owners):
            groups_ref[pair, owner] = result[owner * group : (owner + 1) * group]
        for k in range(owners):
            rows = pl.ds((k - 1) % owners * group, group)
            part = groups_ref[pair, me ^ k]
            out_ref[pair, rows] = part
            if k:
                early_ref[pair, rows] = part
        term_ref[pair] = contract(out_ref[pair], by_slot(own_ref[pair]), ((1,), (1,))).astype(BF16)


def next_states(name, state, partner, weights, side=None, owners=1, own=None):
    pairs, rows, lanes = state.shape[0], *state.shape[-2:]
    group = rows // owners
    split = owners > 1 and group % 16 == 0
    shapes = [(pairs, rows, lanes)] + [(pairs, rows - group, lanes), (pairs, rows, lanes)] * split
    outs = call(
        functools.partial(level_kernel, side, "order"),
        name,
        [jax.ShapeDtypeStruct(shape, BF16) for shape in shapes],
        whole_blocks(3 + split),
        4 * pairs * rows * lanes * lanes,
        6 * pairs * rows * lanes,
        [pltpu.VMEM((pairs, owners, group, lanes), BF16)] if split else [],
    )(state, partner, weights, *([own] if split else []))
    if owners > 1 and not split:
        me = lax.axis_index("order") // 2
        parts = [lax.dynamic_slice_in_dim(outs[0], (me ^ k) * group, group, 1) for k in range(owners)]
        early = jnp.concatenate(parts[1:], axis=1)
        state = jnp.concatenate([early, parts[0]], axis=1)
        return [state, early, own_term(state, own)]
    return outs if split else outs[0]


def late_kernel(after, state_ref, out_ref):
    del after
    rows = out_ref.shape[1]
    for pair in range(state_ref.shape[0]):
        out_ref[pair] = state_ref[pair, state_ref.shape[1] - rows :]


def late_columns(after, state, rows):
    pairs, columns, lanes = state.shape
    if rows % 16:
        return state[:, columns - rows :]
    return call(
        late_kernel,
        "late_columns",
        jax.ShapeDtypeStruct((pairs, rows, lanes), BF16),
        [ANYWHERE] + whole_blocks(1),
        1,
        4 * pairs * rows * lanes,
    )(after, state)


def by_slot(packed):
    first = lax.broadcasted_iota(jnp.int32, packed.shape, 1) < packed.shape[0]
    empty = jnp.zeros(packed.shape, BF16)
    return jnp.concatenate([jnp.where(first, packed, empty), jnp.where(first, empty, packed)], axis=0)


def own_term_kernel(state_ref, own_ref, out_ref):
    for pair in range(state_ref.shape[0]):
        out_ref[pair] = contract(state_ref[pair], by_slot(own_ref[pair]), ((1,), (1,))).astype(BF16)


def own_term(state, own):
    pairs, rows, lanes = state.shape
    return call(
        own_term_kernel,
        "own_term",
        jax.ShapeDtypeStruct(state.shape, BF16),
        whole_blocks(2),
        2 * pairs * rows * lanes * lanes,
        6 * pairs * rows * lanes,
    )(state, own)


def last_level_kernel(turn, begin, axis, after, own_ref, partner_ref, cross_ref, *refs):
    del after
    refs = list(refs)
    own_factor_ref = refs.pop(0) if refs[0].shape == cross_ref.shape else None
    out_refs, groups_ref = refs[:-1], refs[-1]
    me = lax.axis_index(axis) // 2 if turn else 0
    pairs, owners, group, _ = groups_ref.shape
    for pair in range(pairs):
        cross = by_slot(cross_ref[pair])
        own = own_ref[pair, begin : begin + owners * group]
        if own_factor_ref is None:
            result = own.astype(F32) + contract(partner_ref[pair], cross, ((1,), (1,)))
        else:
            weight = jnp.concatenate([by_slot(own_factor_ref[pair]), cross], axis=1)
            both = jnp.concatenate([own, partner_ref[pair]], axis=1)
            result = contract(both, weight, ((1,), (1,)))
        result = result.astype(BF16)
        if group % 16:
            out_refs[0][pair] = result
            continue
        for owner in range(owners):
            groups_ref[pair, owner] = result[owner * group : (owner + 1) * group]
    if group % 16 == 0:
        for k, out_ref in enumerate(out_refs):
            for pair in range(pairs):
                out_ref[pl.ds(pair * group, group)] = groups_ref[pair, me ^ k]


def last_states(name, after, own, partner, factors, owners, turn, begin=0):
    pairs, columns, lanes = partner.shape
    group = columns // owners
    rows = pairs * group
    aligned = group % 16 == 0
    if not aligned:
        own = own[:, begin : begin + columns]
        begin = 0
    parts = call(
        functools.partial(last_level_kernel, turn, begin, "order"),
        name,
        [jax.ShapeDtypeStruct((rows, lanes), BF16)] * owners if aligned else [jax.ShapeDtypeStruct(own.shape, BF16)],
        [ANYWHERE] + whole_blocks(2 + len(factors)),
        4 * pairs * columns * lanes * lanes,
        6 * pairs * columns * lanes,
        [pltpu.VMEM((pairs, owners, group, lanes), BF16)],
    )(after, own, partner, *factors)
    if aligned:
        return parts
    me = lax.axis_index("order") // 2 if turn else 0
    parts = [lax.dynamic_slice_in_dim(parts[0], (me ^ k) * group, group, 1) for k in range(owners)]
    return [part.reshape(rows, lanes) for part in parts]


def place_kernel(group, order_ref, after, place_ref, alive_ref, rows_ref):
    del after
    owners, here, slots = place_ref.shape
    degrees = alive_ref.shape[0]
    me = lax.axis_index("order")
    lane = lax.broadcasted_iota(jnp.int32, (1, slots), 1)
    for k in range(owners):
        for slot in range(here):
            pair, half = slot // 2, slot % 2
            row = (pair // group * 2 + half) * group + pair % group
            rows_ref[pl.ds(row, 1), :] = (lane == order_ref[(me ^ k) * here + slot]).astype(F32)
        place_ref[k] = rows_ref[...].astype(BF16)
    degree = lax.axis_index("lat") * degrees + lax.broadcasted_iota(jnp.int32, (degrees, slots), 0)
    window = DEGREES // slots * lax.broadcasted_iota(jnp.int32, (degrees, slots), 1)
    alive_ref[...] = (degree >= window).astype(F32).astype(BF16)


def places_of(order_of_slot, degrees, owners, group, after):
    slots = order_of_slot.shape[0]
    here = slots // owners
    return call(
        functools.partial(place_kernel, group),
        "places",
        [jax.ShapeDtypeStruct((owners, here, slots), BF16), jax.ShapeDtypeStruct((degrees, slots), BF16)],
        [IN_SMEM, ANYWHERE],
        slots * slots,
        8 * slots * slots,
        [pltpu.VMEM((here, slots), F32)],
    )(order_of_slot, after)


def root_kernel(group, first, last, *refs):
    refs = list(refs)
    so_far_ref = refs.pop(0) if last else None
    place_ref, alive_ref = refs.pop(0), refs.pop(0)
    count = place_ref.shape[0] - first if last else first
    first = first if last else 0
    if last:
        root_refs = [refs[0].at[i] for i in range(count)]
    else:
        root_refs = refs[:1] + [refs[1].at[i] for i in range(count - 1)]
    refs = refs[1:] if last else refs[2:]
    state_refs, refs = refs[:count], refs[count:]
    copies = []
    if last:
        out_ref, rows_ref, natural_ref, sems = refs
    else:
        root_hbm, out_ref, later_ref, rows_ref, sems = refs
        natural_ref = out_ref
        for i in range(later_ref.shape[0]):
            copies.append(fetch_roots(count + i, root_hbm, later_ref.at[i], sems.at[i]))
            copies[-1].start()
    fields, parts, degrees, slots = out_ref.shape
    columns = fields * parts
    rank = root_refs[0].shape[1]
    group_rows = group * columns
    here = place_ref.shape[1]
    steps = state_refs[0].shape[0] // group_rows
    shape = (group_rows, 2 * rank)
    row_pair = lax.broadcasted_iota(jnp.int32, shape, 0) // columns
    row_half = lax.broadcasted_iota(jnp.int32, shape, 1) // rank
    masks = [[(row_pair == pair) & (row_half == half) for pair in range(group)] for half in range(2)]
    empty = jnp.zeros(shape, BF16)
    for i, state_ref in enumerate(state_refs):
        for step in range(steps):
            state = state_ref[pl.ds(step * group_rows, group_rows)]
            left = jnp.concatenate(
                [jnp.concatenate([jnp.where(m, state, empty) for m in line], axis=1) for line in masks], axis=0
            )
            right = root_refs[i][pl.ds(step * group * 2, group * 2)].reshape(group * 2 * rank, degrees)
            product = contract(left, right, ((1,), (0,)))
            begin = (i * steps + step) * 2 * group_rows
            for tile in range(degrees // 128):
                rows_ref[tile, pl.ds(begin, 2 * group_rows), :] = product[:, tile * 128 : (tile + 1) * 128]
    place = place_ref[pl.ds(first, count)].reshape(count * here, slots)
    per = max(1, fields // 4)
    for column in range(columns):
        for tile in range(degrees // 128):
            span = slice(tile * 128, (tile + 1) * 128)
            one = rows_ref[tile, pl.ds(column, count * here, stride=columns), :].astype(BF16)
            natural = contract(one.T, place, ((1,), (0,))).astype(BF16)
            where = (column // 2, column % 2, span)
            if last:
                natural = natural + so_far_ref[where]
                natural = jnp.where(alive_ref[span] != 0, natural, jnp.zeros((), BF16))
            natural_ref[where] = natural
        if last and (column + 1) % (2 * per) == 0:
            done = column // (2 * per)
            where = pl.ds(done * per, per)
            copies.append(pltpu.make_async_copy(natural_ref.at[where], out_ref.at[where], sems.at[done]))
            copies[-1].start()
    for copy in copies:
        copy.wait()


def spectra_of(states, roots, places, alive, so_far, first, group):
    state_rows = states[0].shape[0]
    rank, degrees = roots[0].shape[-2:]
    owners, here, slots = places.shape
    count = len(states)
    columns = state_rows * 2 // here
    last = so_far is not None
    out = jax.ShapeDtypeStruct((columns // 2, 2, degrees, slots), BF16)
    root_basis = roots[-1]
    inputs = [places, alive, *(roots if so_far is not None else roots[:-1]), *states]
    in_specs = whole_blocks(len(inputs))
    scratch = [pltpu.VMEM((degrees // 128, count * here * columns, 128), F32)]
    more = {}
    if last:
        inputs = [so_far, *inputs]
        in_specs = whole_blocks(len(inputs))
        scratch += [pltpu.VMEM(out.shape, BF16), pltpu.SemaphoreType.DMA((columns // 2,))]
        more["out_specs"] = IN_HBM
    else:
        inputs.append(root_basis)
        in_specs.append(IN_HBM)
        out = [out, jax.ShapeDtypeStruct((owners - count, here, rank, degrees), BF16)]
        scratch.append(pltpu.SemaphoreType.DMA((owners - count,)))
    return call(
        functools.partial(root_kernel, group, first, last),
        "root",
        out,
        in_specs,
        2 * count * here * rank * degrees * columns,
        2 * count * here * rank * degrees,
        scratch,
        mib=24,
        **more,
    )(*inputs)


def per_device(
    fourier, quad_weights, leaf_basis, level_factors, sparsity, root_basis, order_of_slot
):
    slots, columns, lats = fourier.shape
    owners = lax.axis_size("order")
    levels = level_factors.shape[1]
    group = max(2, 16 * owners // columns)
    present = in_hbm(sparsity.transpose(1, 2, 0))
    fourier, leaf_basis, level_factors, root_basis = map(in_hbm, (fourier, leaf_basis, level_factors, root_basis))
    quad_weights = in_hbm(quad_weights.reshape(1, lats))

    def swap(array, axis, bits):
        return lax.ppermute(array, axis, [(i, i ^ bits) for i in range(lax.axis_size(axis))])

    def swap_both(array, order_bits, lat_bits):
        blocks = lax.axis_size("lat")
        pairs = [
            (o * blocks + b, (o ^ order_bits) * blocks + (b ^ lat_bits)) for o in range(owners) for b in range(blocks)
        ]
        return lax.ppermute(array, ("order", "lat"), pairs)

    early_pieces = 3 * owners // 4
    state, root_0 = leaf_states(fourier, quad_weights, leaf_basis, root_basis, owners)
    partner = swap(state, "lat", 1)
    weights = level_weights(level_factors, present, (0,), state)
    states = [next_states(f"level0_{c}", state, partner, weights[0], c) for c in range(2)]
    weights += level_weights(level_factors, present, tuple(range(1, levels)), states[1], root_basis, early_pieces - 1)
    own_factors, cross_factors, early_roots = weights[-3:]
    other_cross = swap(cross_factors, "order", 1)
    high = owners // 2
    own_columns = columns // owners
    for level in range(1, levels - 1):
        partners = [swap(state, "lat", 1 << level) for state in states]
        parts = high if level == levels - 2 else 1
        states = [
            next_states(f"level{level}_{c}", states[c], partners[c], weights[level], None, parts if c else 1, own_factors)
            for c in range(2)
        ]
    top = 1 << levels - 1
    mine, (other, early, term) = states
    mine_partner = swap(mine, "lat", top)
    early_partner = swap_both(early, 1, top)
    other_own = swap(term, "order", 1)
    places, alive = places_of(order_of_slot, root_basis.shape[2], owners, group, other)
    late_partner = swap_both(late_columns(alive, other, own_columns), 1, top)
    even = last_states("last_own", alive, mine, mine_partner, (cross_factors, own_factors), high, True)
    begin = columns // 2 - own_columns
    odd = last_states("last_early", alive, other_own, early_partner, (other_cross,), high - 1, False)
    odd = [*last_states("last_late", alive, other_own, late_partner, (other_cross,), 1, False, begin), *odd]
    arrived = [swap((odd if k % 2 else even)[k // 2], "order", k // 2 * 2) if k > 1 else (even, odd)[k][0] for k in range(owners)]
    roots = [root_0, early_roots, root_basis]
    spectra, later_roots = spectra_of(arrived[:early_pieces], roots, places, alive, None, early_pieces, group)
    return spectra_of(arrived[early_pieces:], [later_roots], places, alive, spectra, early_pieces, group)


def solution(mesh):
    return jax.shard_map(
        per_device,
        mesh=mesh,
        in_specs=(
            P("order", None, "lat"),
            P("lat"),
            P("order", None, "lat"),
            P("order", None, None, "lat", None, None),
            P("order", None, "lat"),
            P(None, None, "lat"),
            P(),
        ),
        out_specs=P("order", None, "lat", None),
        check_vma=False,
    )
```

```python
import functools

import jax
import jax.numpy as jnp
from jax import lax
from jax.experimental import pallas as pl
from jax.experimental.pallas import tpu as pltpu
from jax.sharding import PartitionSpec as P

DEGREES = 2048
F32, BF16 = jnp.float32, jnp.bfloat16
MIB = 1 << 20
IN_HBM = pl.BlockSpec(memory_space=pltpu.HBM)
IN_SMEM = pl.BlockSpec(memory_space=pltpu.SMEM)
ANYWHERE = pl.BlockSpec(memory_space=pl.ANY)


def contract(lhs, rhs, dims):
    return lax.dot_general(lhs, rhs, (dims, ((), ())), preferred_element_type=F32)


def in_hbm(array):
    return pltpu.with_memory_space_constraint(array, pltpu.HBM)


def call(kernel, name, out_shape, in_specs, flops, size, scratch=(), mib=16, **more):
    return pl.pallas_call(
        kernel,
        out_shape=out_shape,
        in_specs=in_specs,
        scratch_shapes=list(scratch),
        compiler_params=pltpu.CompilerParams(vmem_limit_bytes=mib * MIB),
        cost_estimate=pl.CostEstimate(flops=flops // 1000, bytes_accessed=size // 1000, transcendentals=0),
        name=name,
        **more,
    )


def whole_blocks(count):
    return [pl.BlockSpec()] * count


def fetch_roots(k, root_hbm, root_ref, sem):
    here = root_ref.shape[0]
    me = lax.axis_index("order")
    return pltpu.make_async_copy(root_hbm.at[pl.ds((me ^ k) * here, here)], root_ref, sem)


def leaf_kernel(
    pieces, group, fourier_hbm, weight_hbm, leaf_hbm, root_hbm, state_ref, root_ref, fourier_ref, weight_ref, leaf_ref, sems
):
    side = lax.axis_index("order") & 1
    slots, columns, lats = fourier_ref.shape
    rank = leaf_ref.shape[1]
    per = slots // pieces
    copies = [pltpu.make_async_copy(weight_hbm, weight_ref, sems.at[0])]
    for piece in range(pieces):
        part = pl.ds(piece * per, per)
        copies.append(pltpu.make_async_copy(fourier_hbm.at[part], fourier_ref.at[part], sems.at[1 + 2 * piece]))
        copies.append(pltpu.make_async_copy(leaf_hbm.at[part], leaf_ref.at[part], sems.at[2 + 2 * piece]))
    copies.append(fetch_roots(0, root_hbm, root_ref, sems.at[1 + 2 * pieces]))
    for copy in copies:
        copy.start()
    copies[0].wait()
    weight = weight_ref[...]
    mine = lax.broadcasted_iota(jnp.int32, (columns, 2 * rank), 1) < rank
    for pair in range(slots // 2):
        if 2 * pair % per == 0:
            copies[1 + 2 * (2 * pair // per)].wait()
            copies[2 + 2 * (2 * pair // per)].wait()
        both = pl.ds(2 * pair, 2)
        weighted = (fourier_ref[both].astype(F32) * weight[None]).astype(BF16)
        product = contract(
            weighted.reshape(2 * columns, lats), leaf_ref[both].reshape(2 * rank, lats), ((1,), (1,))
        )
        state = jnp.where(mine, product[:columns], product[columns:]).astype(BF16)
        if group % 16:
            state_ref[pair] = state
            continue
        for owner in range(columns // group):
            rows = pl.ds(owner // 2 * group, group)
            state_ref[pair, owner % 2 ^ side, rows] = state[owner * group : (owner + 1) * group]
    copies[-1].wait()


def leaf_states(fourier, quad_weights, leaf_basis, root_basis, owners):
    slots, columns, lats = fourier.shape
    rank = leaf_basis.shape[1]
    pairs, half, lanes, group = slots // 2, columns // 2, 2 * rank, columns // owners
    pieces = 2
    shape = (pairs, columns, lanes) if group % 16 else (pairs, 2, half, lanes)
    state, root = call(
        functools.partial(leaf_kernel, pieces, group),
        "leaf",
        [
            jax.ShapeDtypeStruct(shape, BF16),
            jax.ShapeDtypeStruct((root_basis.shape[0] // owners, *root_basis.shape[1:]), BF16),
        ],
        [IN_HBM] * 4,
        2 * slots * columns * rank * lats,
        4 * slots * columns * lats,
        [
            pltpu.VMEM((slots, columns, lats), BF16),
            pltpu.VMEM((1, lats), F32),
            pltpu.VMEM((slots, rank, lats), BF16),
            pltpu.SemaphoreType.DMA((2 + 2 * pieces,)),
        ],
    )(fourier, quad_weights, leaf_basis, root_basis)
    if group % 16:
        side = lax.axis_index("order") & 1
        state = state.reshape(pairs, owners // 2, 2, group, lanes)
        sides = [lax.dynamic_index_in_dim(state, side ^ i, 2, False).reshape(pairs, half, lanes) for i in range(2)]
        state = jnp.stack(sides, axis=1)
    return state, root


def factor_kernel(levels, pieces, roots, factor_hbm, present_hbm, after, *refs):
    del after
    weight_refs, (factor_ref, present_ref, sems) = list(refs[:-3]), refs[-3:]
    fetches = []
    if roots:
        root_hbm, root_ref = weight_refs.pop(0), weight_refs.pop()
        for i in range(root_ref.shape[0]):
            fetches.append(fetch_roots(1 + i, root_hbm, root_ref.at[i], sems.at[len(levels) * pieces + 1 + i]))
    present_copy = pltpu.make_async_copy(present_hbm, present_ref, sems.at[len(levels) * pieces])
    present_copy.start()
    _, slots, _, rank, _ = factor_ref.shape
    per = slots // pieces
    copies = {}
    for i, level in enumerate(levels):
        for piece in range(pieces):
            part = pl.ds(piece * per, per)
            copies[i, piece] = pltpu.make_async_copy(
                factor_hbm.at[part, level, :, 0], factor_ref.at[i, part], sems.at[i * pieces + piece]
            )
            copies[i, piece].start()
    for fetch in fetches:
        fetch.start()
    empty = jnp.zeros((rank, rank), BF16)
    present_copy.wait()
    for i, level in enumerate(levels):
        for pair in range(slots // 2):
            if 2 * pair % per == 0:
                copies[i, 2 * pair // per].wait()
            for half in range(2):
                first, second = (factor_ref[i, slot, half] for slot in (2 * pair, 2 * pair + 1))
                if half:
                    first = jnp.where(present_ref[level, 0, 2 * pair] != 0, first, empty)
                    second = jnp.where(present_ref[level, 0, 2 * pair + 1] != 0, second, empty)
                if weight_refs[i].shape[1] == rank:
                    weight_refs[i + half][pair] = jnp.concatenate([first, second], axis=1)
                    continue
                lanes = pl.ds(half * 2 * rank, 2 * rank)
                weight_refs[i][pair, :rank, lanes] = jnp.concatenate([first, empty], axis=1)
                weight_refs[i][pair, rank:, lanes] = jnp.concatenate([empty, second], axis=1)
    for fetch in fetches:
        fetch.wait()


def level_weights(level_factors, present, levels, after, root_basis=None, root_pieces=0):
    slots, last, _, _, rank, _ = level_factors.shape
    count, pieces = len(levels), 2
    roots = []
    if root_pieces:
        here = root_basis.shape[0] // lax.axis_size("order")
        roots = [jax.ShapeDtypeStruct((root_pieces, here, *root_basis.shape[1:]), BF16)]
    return call(
        functools.partial(factor_kernel, levels, pieces, root_pieces),
        "factors",
        [
            jax.ShapeDtypeStruct((slots // 2, *((rank, 2 * rank) if level == last - 1 else (2 * rank, 4 * rank))), BF16)
            for level in levels
            for _ in range(1 + (level == last - 1))
        ]
        + roots,
        [IN_HBM, IN_HBM, ANYWHERE] + [IN_HBM] * len(roots),
        slots * rank * rank * 4 * count,
        slots * rank * rank * 16 * count,
        [
            pltpu.VMEM((count, slots, 2, rank, rank), BF16),
            pltpu.SMEM(present.shape, jnp.int32),
            pltpu.SemaphoreType.DMA((count * pieces + 1 + root_pieces,)),
        ],
        mib=24,
    )(level_factors, present, after, *([root_basis] if roots else []))


def level_kernel(side, axis, state_ref, partner_ref, weight_ref, *refs):
    if len(refs) > 1:
        own_ref, *refs = refs
    out_ref = refs[0]
    me = lax.axis_index(axis) // 2
    for pair in range(weight_ref.shape[0]):
        at = pair if side is None else (pair, side)
        both = jnp.concatenate([state_ref[at], partner_ref[at]], axis=1)
        result = contract(both, weight_ref[pair], ((1,), (1,))).astype(BF16)
        if len(refs) == 1:
            out_ref[pair] = result
            continue
        early_ref, term_ref, groups_ref = refs[1:]
        owners, group, _ = groups_ref.shape[1:]
        for owner in range(owners):
            groups_ref[pair, owner] = result[owner * group : (owner + 1) * group]
        for k in range(owners):
            rows = pl.ds((k - 1) % owners * group, group)
            part = groups_ref[pair, me ^ k]
            out_ref[pair, rows] = part
            if k:
                early_ref[pair, rows] = part
        term_ref[pair] = contract(out_ref[pair], by_slot(own_ref[pair]), ((1,), (1,))).astype(BF16)


def next_states(name, state, partner, weights, side=None, owners=1, own=None):
    pairs, rows, lanes = state.shape[0], *state.shape[-2:]
    group = rows // owners
    split = owners > 1 and group % 16 == 0
    shapes = [(pairs, rows, lanes)] + [(pairs, rows - group, lanes), (pairs, rows, lanes)] * split
    outs = call(
        functools.partial(level_kernel, side, "order"),
        name,
        [jax.ShapeDtypeStruct(shape, BF16) for shape in shapes],
        whole_blocks(3 + split),
        4 * pairs * rows * lanes * lanes,
        6 * pairs * rows * lanes,
        [pltpu.VMEM((pairs, owners, group, lanes), BF16)] if split else [],
    )(state, partner, weights, *([own] if split else []))
    if owners > 1 and not split:
        me = lax.axis_index("order") // 2
        parts = [lax.dynamic_slice_in_dim(outs[0], (me ^ k) * group, group, 1) for k in range(owners)]
        early = jnp.concatenate(parts[1:], axis=1)
        state = jnp.concatenate([early, parts[0]], axis=1)
        return [state, early, own_term(state, own)]
    return outs if split else outs[0]


def late_kernel(after, state_ref, out_ref):
    del after
    rows = out_ref.shape[1]
    for pair in range(state_ref.shape[0]):
        out_ref[pair] = state_ref[pair, state_ref.shape[1] - rows :]


def late_columns(after, state, rows):
    pairs, columns, lanes = state.shape
    if rows % 16:
        return state[:, columns - rows :]
    return call(
        late_kernel,
        "late_columns",
        jax.ShapeDtypeStruct((pairs, rows, lanes), BF16),
        [ANYWHERE] + whole_blocks(1),
        1,
        4 * pairs * rows * lanes,
    )(after, state)


def by_slot(packed):
    first = lax.broadcasted_iota(jnp.int32, packed.shape, 1) < packed.shape[0]
    empty = jnp.zeros(packed.shape, BF16)
    return jnp.concatenate([jnp.where(first, packed, empty), jnp.where(first, empty, packed)], axis=0)


def own_term_kernel(state_ref, own_ref, out_ref):
    for pair in range(state_ref.shape[0]):
        out_ref[pair] = contract(state_ref[pair], by_slot(own_ref[pair]), ((1,), (1,))).astype(BF16)


def own_term(state, own):
    pairs, rows, lanes = state.shape
    return call(
        own_term_kernel,
        "own_term",
        jax.ShapeDtypeStruct(state.shape, BF16),
        whole_blocks(2),
        2 * pairs * rows * lanes * lanes,
        6 * pairs * rows * lanes,
    )(state, own)


def last_level_kernel(turn, begin, axis, after, own_ref, partner_ref, cross_ref, *refs):
    del after
    refs = list(refs)
    own_factor_ref = refs.pop(0) if refs[0].shape == cross_ref.shape else None
    out_refs, groups_ref = refs[:-1], refs[-1]
    me = lax.axis_index(axis) // 2 if turn else 0
    pairs, owners, group, _ = groups_ref.shape
    for pair in range(pairs):
        cross = by_slot(cross_ref[pair])
        own = own_ref[pair, begin : begin + owners * group]
        if own_factor_ref is None:
            result = own.astype(F32) + contract(partner_ref[pair], cross, ((1,), (1,)))
        else:
            weight = jnp.concatenate([by_slot(own_factor_ref[pair]), cross], axis=1)
            both = jnp.concatenate([own, partner_ref[pair]], axis=1)
            result = contract(both, weight, ((1,), (1,)))
        result = result.astype(BF16)
        if group % 16:
            out_refs[0][pair] = result
            continue
        for owner in range(owners):
            groups_ref[pair, owner] = result[owner * group : (owner + 1) * group]
    if group % 16 == 0:
        for k, out_ref in enumerate(out_refs):
            for pair in range(pairs):
                out_ref[pl.ds(pair * group, group)] = groups_ref[pair, me ^ k]


def last_states(name, after, own, partner, factors, owners, turn, begin=0):
    pairs, columns, lanes = partner.shape
    group = columns // owners
    rows = pairs * group
    aligned = group % 16 == 0
    if not aligned:
        own = own[:, begin : begin + columns]
        begin = 0
    parts = call(
        functools.partial(last_level_kernel, turn, begin, "order"),
        name,
        [jax.ShapeDtypeStruct((rows, lanes), BF16)] * owners if aligned else [jax.ShapeDtypeStruct(own.shape, BF16)],
        [ANYWHERE] + whole_blocks(2 + len(factors)),
        4 * pairs * columns * lanes * lanes,
        6 * pairs * columns * lanes,
        [pltpu.VMEM((pairs, owners, group, lanes), BF16)],
    )(after, own, partner, *factors)
    if aligned:
        return parts
    me = lax.axis_index("order") // 2 if turn else 0
    parts = [lax.dynamic_slice_in_dim(parts[0], (me ^ k) * group, group, 1) for k in range(owners)]
    return [part.reshape(rows, lanes) for part in parts]


def place_kernel(group, order_ref, after, root_hbm, place_ref, alive_ref, later_ref, rows_ref, sems):
    del after
    owners, here, slots = place_ref.shape
    degrees = alive_ref.shape[0]
    me = lax.axis_index("order")
    later = later_ref.shape[0]
    fetches = [fetch_roots(owners - later + i, root_hbm, later_ref.at[i], sems.at[i]) for i in range(later)]
    for fetch in fetches:
        fetch.start()
    lane = lax.broadcasted_iota(jnp.int32, (1, slots), 1)
    for k in range(owners):
        for slot in range(here):
            pair, half = slot // 2, slot % 2
            row = (pair // group * 2 + half) * group + pair % group
            rows_ref[pl.ds(row, 1), :] = (lane == order_ref[(me ^ k) * here + slot]).astype(F32)
        place_ref[k] = rows_ref[...].astype(BF16)
    degree = lax.axis_index("lat") * degrees + lax.broadcasted_iota(jnp.int32, (degrees, slots), 0)
    window = DEGREES // slots * lax.broadcasted_iota(jnp.int32, (degrees, slots), 1)
    alive_ref[...] = (degree >= window).astype(F32).astype(BF16)
    for fetch in fetches:
        fetch.wait()


def places_of(order_of_slot, root_basis, owners, later, group, after):
    slots, rank, degrees = root_basis.shape
    here = slots // owners
    return call(
        functools.partial(place_kernel, group),
        "places",
        [
            jax.ShapeDtypeStruct((owners, here, slots), BF16),
            jax.ShapeDtypeStruct((degrees, slots), BF16),
            jax.ShapeDtypeStruct((later, here, rank, degrees), BF16),
        ],
        [IN_SMEM, ANYWHERE, IN_HBM],
        slots * slots,
        8 * slots * slots,
        [pltpu.VMEM((here, slots), F32), pltpu.SemaphoreType.DMA((later,))],
    )(order_of_slot, after, root_basis)


def root_kernel(group, first, last, *refs):
    refs = list(refs)
    so_far_ref = refs.pop(0) if last else None
    place_ref, alive_ref = refs.pop(0), refs.pop(0)
    count = place_ref.shape[0] - first if last else first
    first = first if last else 0
    if last:
        root_refs = [refs[0].at[i] for i in range(count)]
    else:
        root_refs = refs[:1] + [refs[1].at[i] for i in range(count - 1)]
    refs = refs[1:] if last else refs[2:]
    state_refs, refs = refs[:count], refs[count:]
    copies = []
    if last:
        out_ref, rows_ref, natural_ref, sems = refs
    else:
        out_ref, rows_ref = refs
        natural_ref = out_ref
    fields, parts, degrees, slots = out_ref.shape
    columns = fields * parts
    rank = root_refs[0].shape[1]
    group_rows = group * columns
    here = place_ref.shape[1]
    steps = state_refs[0].shape[0] // group_rows
    shape = (group_rows, 2 * rank)
    row_pair = lax.broadcasted_iota(jnp.int32, shape, 0) // columns
    row_half = lax.broadcasted_iota(jnp.int32, shape, 1) // rank
    masks = [[(row_pair == pair) & (row_half == half) for pair in range(group)] for half in range(2)]
    empty = jnp.zeros(shape, BF16)
    for i, state_ref in enumerate(state_refs):
        for step in range(steps):
            state = state_ref[pl.ds(step * group_rows, group_rows)]
            left = jnp.concatenate(
                [jnp.concatenate([jnp.where(m, state, empty) for m in line], axis=1) for line in masks], axis=0
            )
            right = root_refs[i][pl.ds(step * group * 2, group * 2)].reshape(group * 2 * rank, degrees)
            product = contract(left, right, ((1,), (0,)))
            begin = (i * steps + step) * 2 * group_rows
            for tile in range(degrees // 128):
                rows_ref[tile, pl.ds(begin, 2 * group_rows), :] = product[:, tile * 128 : (tile + 1) * 128]
    place = place_ref[pl.ds(first, count)].reshape(count * here, slots)
    per = max(1, fields // 4)
    for column in range(columns):
        for tile in range(degrees // 128):
            span = slice(tile * 128, (tile + 1) * 128)
            one = rows_ref[tile, pl.ds(column, count * here, stride=columns), :].astype(BF16)
            natural = contract(one.T, place, ((1,), (0,))).astype(BF16)
            where = (column // 2, column % 2, span)
            if last:
                natural = natural + so_far_ref[where]
                natural = jnp.where(alive_ref[span] != 0, natural, jnp.zeros((), BF16))
            natural_ref[where] = natural
        if last and (column + 1) % (2 * per) == 0:
            done = column // (2 * per)
            where = pl.ds(done * per, per)
            copies.append(pltpu.make_async_copy(natural_ref.at[where], out_ref.at[where], sems.at[done]))
            copies[-1].start()
    for copy in copies:
        copy.wait()


def spectra_of(states, roots, places, alive, so_far, first, group):
    state_rows = states[0].shape[0]
    rank, degrees = roots[0].shape[-2:]
    owners, here, slots = places.shape
    count = len(states)
    columns = state_rows * 2 // here
    last = so_far is not None
    out = jax.ShapeDtypeStruct((columns // 2, 2, degrees, slots), BF16)
    inputs = [places, alive, *roots, *states]
    in_specs = whole_blocks(len(inputs))
    scratch = [pltpu.VMEM((degrees // 128, count * here * columns, 128), F32)]
    more = {}
    if last:
        inputs = [so_far, *inputs]
        in_specs = whole_blocks(len(inputs))
        scratch += [pltpu.VMEM(out.shape, BF16), pltpu.SemaphoreType.DMA((columns // 2,))]
        more["out_specs"] = IN_HBM
    return call(
        functools.partial(root_kernel, group, first, last),
        "root",
        out,
        in_specs,
        2 * count * here * rank * degrees * columns,
        2 * count * here * rank * degrees,
        scratch,
        mib=24,
        **more,
    )(*inputs)


def per_device(
    fourier, quad_weights, leaf_basis, level_factors, sparsity, root_basis, order_of_slot
):
    slots, columns, lats = fourier.shape
    owners = lax.axis_size("order")
    levels = level_factors.shape[1]
    group = max(2, 16 * owners // columns)
    present = in_hbm(sparsity.transpose(1, 2, 0))
    fourier, leaf_basis, level_factors, root_basis = map(in_hbm, (fourier, leaf_basis, level_factors, root_basis))
    quad_weights = in_hbm(quad_weights.reshape(1, lats))

    def swap(array, axis, bits):
        return lax.ppermute(array, axis, [(i, i ^ bits) for i in range(lax.axis_size(axis))])

    def swap_both(array, order_bits, lat_bits):
        blocks = lax.axis_size("lat")
        pairs = [
            (o * blocks + b, (o ^ order_bits) * blocks + (b ^ lat_bits)) for o in range(owners) for b in range(blocks)
        ]
        return lax.ppermute(array, ("order", "lat"), pairs)

    early_pieces = 3 * owners // 4
    state, root_0 = leaf_states(fourier, quad_weights, leaf_basis, root_basis, owners)
    partner = swap(state, "lat", 1)
    weights = level_weights(level_factors, present, (0,), state)
    states = [next_states(f"level0_{c}", state, partner, weights[0], c) for c in range(2)]
    weights += level_weights(level_factors, present, tuple(range(1, levels)), states[1], root_basis, early_pieces - 1)
    own_factors, cross_factors, early_roots = weights[-3:]
    other_cross = swap(cross_factors, "order", 1)
    high = owners // 2
    own_columns = columns // owners
    for level in range(1, levels - 1):
        partners = [swap(state, "lat", 1 << level) for state in states]
        parts = high if level == levels - 2 else 1
        states = [
            next_states(f"level{level}_{c}", states[c], partners[c], weights[level], None, parts if c else 1, own_factors)
            for c in range(2)
        ]
    top = 1 << levels - 1
    mine, (other, early, term) = states
    mine_partner = swap(mine, "lat", top)
    early_partner = swap_both(early, 1, top)
    other_own = swap(term, "order", 1)
    places, alive, later_roots = places_of(
        order_of_slot, root_basis, owners, owners - early_pieces, group, other
    )
    late_partner = swap_both(late_columns(alive, other, own_columns), 1, top)
    even = last_states("last_own", alive, mine, mine_partner, (cross_factors, own_factors), high, True)
    begin = columns // 2 - own_columns
    odd = last_states("last_early", alive, other_own, early_partner, (other_cross,), high - 1, False)
    odd = [*last_states("last_late", alive, other_own, late_partner, (other_cross,), 1, False, begin), *odd]
    arrived = [swap((odd if k % 2 else even)[k // 2], "order", k // 2 * 2) if k > 1 else (even, odd)[k][0] for k in range(owners)]
    roots = [root_0, early_roots]
    spectra = spectra_of(arrived[:early_pieces], roots, places, alive, None, early_pieces, group)
    return spectra_of(arrived[early_pieces:], [later_roots], places, alive, spectra, early_pieces, group)


def solution(mesh):
    return jax.shard_map(
        per_device,
        mesh=mesh,
        in_specs=(
            P("order", None, "lat"),
            P("lat"),
            P("order", None, "lat"),
            P("order", None, None, "lat", None, None),
            P("order", None, "lat"),
            P(None, None, "lat"),
            P(),
        ),
        out_specs=P("order", None, "lat", None),
        check_vma=False,
    )
```

```python
import functools

import jax
import jax.numpy as jnp
from jax import lax
from jax.experimental import pallas as pl
from jax.experimental.pallas import tpu as pltpu
from jax.sharding import PartitionSpec as P

DEGREES = 2048
F32, BF16 = jnp.float32, jnp.bfloat16
MIB = 1 << 20
IN_HBM = pl.BlockSpec(memory_space=pltpu.HBM)
IN_SMEM = pl.BlockSpec(memory_space=pltpu.SMEM)
ANYWHERE = pl.BlockSpec(memory_space=pl.ANY)


def contract(lhs, rhs, dims):
    return lax.dot_general(lhs, rhs, (dims, ((), ())), preferred_element_type=F32)


def in_hbm(array):
    return pltpu.with_memory_space_constraint(array, pltpu.HBM)


def call(kernel, name, out_shape, in_specs, flops, size, scratch=(), mib=16, **more):
    return pl.pallas_call(
        kernel,
        out_shape=out_shape,
        in_specs=in_specs,
        scratch_shapes=list(scratch),
        compiler_params=pltpu.CompilerParams(vmem_limit_bytes=mib * MIB),
        cost_estimate=pl.CostEstimate(flops=flops // 1000, bytes_accessed=size // 1000, transcendentals=0),
        name=name,
        **more,
    )


def whole_blocks(count):
    return [pl.BlockSpec()] * count


def fetch_roots(k, root_hbm, root_ref, sem):
    here = root_ref.shape[0]
    me = lax.axis_index("order")
    return pltpu.make_async_copy(root_hbm.at[pl.ds((me ^ k) * here, here)], root_ref, sem)


def leaf_kernel(
    pieces, group, fourier_hbm, weight_hbm, leaf_hbm, root_hbm, state_ref, root_ref, fourier_ref, weight_ref, leaf_ref, sems
):
    side = lax.axis_index("order") & 1
    slots, columns, lats = fourier_ref.shape
    rank = leaf_ref.shape[1]
    per = slots // pieces
    copies = [pltpu.make_async_copy(weight_hbm, weight_ref, sems.at[0])]
    for piece in range(pieces):
        part = pl.ds(piece * per, per)
        copies.append(pltpu.make_async_copy(fourier_hbm.at[part], fourier_ref.at[part], sems.at[1 + 2 * piece]))
        copies.append(pltpu.make_async_copy(leaf_hbm.at[part], leaf_ref.at[part], sems.at[2 + 2 * piece]))
    copies.append(fetch_roots(0, root_hbm, root_ref, sems.at[1 + 2 * pieces]))
    for copy in copies:
        copy.start()
    copies[0].wait()
    weight = weight_ref[...]
    mine = lax.broadcasted_iota(jnp.int32, (columns, 2 * rank), 1) < rank
    for pair in range(slots // 2):
        if 2 * pair % per == 0:
            copies[1 + 2 * (2 * pair // per)].wait()
            copies[2 + 2 * (2 * pair // per)].wait()
        both = pl.ds(2 * pair, 2)
        weighted = (fourier_ref[both].astype(F32) * weight[None]).astype(BF16)
        product = contract(
            weighted.reshape(2 * columns, lats), leaf_ref[both].reshape(2 * rank, lats), ((1,), (1,))
        )
        state = jnp.where(mine, product[:columns], product[columns:]).astype(BF16)
        if group % 16:
            state_ref[pair] = state
            continue
        for owner in range(columns // group):
            rows = pl.ds(owner // 2 * group, group)
            state_ref[pair, owner % 2 ^ side, rows] = state[owner * group : (owner + 1) * group]
    copies[-1].wait()


def leaf_states(fourier, quad_weights, leaf_basis, root_basis, owners):
    slots, columns, lats = fourier.shape
    rank = leaf_basis.shape[1]
    pairs, half, lanes, group = slots // 2, columns // 2, 2 * rank, columns // owners
    pieces = 2
    shape = (pairs, columns, lanes) if group % 16 else (pairs, 2, half, lanes)
    state, root = call(
        functools.partial(leaf_kernel, pieces, group),
        "leaf",
        [
            jax.ShapeDtypeStruct(shape, BF16),
            jax.ShapeDtypeStruct((root_basis.shape[0] // owners, *root_basis.shape[1:]), BF16),
        ],
        [IN_HBM] * 4,
        2 * slots * columns * rank * lats,
        4 * slots * columns * lats,
        [
            pltpu.VMEM((slots, columns, lats), BF16),
            pltpu.VMEM((1, lats), F32),
            pltpu.VMEM((slots, rank, lats), BF16),
            pltpu.SemaphoreType.DMA((2 + 2 * pieces,)),
        ],
    )(fourier, quad_weights, leaf_basis, root_basis)
    if group % 16:
        side = lax.axis_index("order") & 1
        state = state.reshape(pairs, owners // 2, 2, group, lanes)
        sides = [lax.dynamic_index_in_dim(state, side ^ i, 2, False).reshape(pairs, half, lanes) for i in range(2)]
        state = jnp.stack(sides, axis=1)
    return state, root


def factor_kernel(levels, pieces, roots, factor_hbm, present_hbm, after, *refs):
    del after
    weight_refs, (factor_ref, present_ref, sems) = list(refs[:-3]), refs[-3:]
    fetches = []
    if roots:
        root_hbm, root_ref = weight_refs.pop(0), weight_refs.pop()
        for i in range(root_ref.shape[0]):
            fetches.append(fetch_roots(1 + i, root_hbm, root_ref.at[i], sems.at[len(levels) * pieces + 1 + i]))
    present_copy = pltpu.make_async_copy(present_hbm, present_ref, sems.at[len(levels) * pieces])
    present_copy.start()
    _, slots, _, rank, _ = factor_ref.shape
    per = slots // pieces
    copies = {}
    for i, level in enumerate(levels):
        for piece in range(pieces):
            part = pl.ds(piece * per, per)
            copies[i, piece] = pltpu.make_async_copy(
                factor_hbm.at[part, level, :, 0], factor_ref.at[i, part], sems.at[i * pieces + piece]
            )
            copies[i, piece].start()
    for fetch in fetches:
        fetch.start()
    empty = jnp.zeros((rank, rank), BF16)
    present_copy.wait()
    for i, level in enumerate(levels):
        for pair in range(slots // 2):
            if 2 * pair % per == 0:
                copies[i, 2 * pair // per].wait()
            for half in range(2):
                first, second = (factor_ref[i, slot, half] for slot in (2 * pair, 2 * pair + 1))
                if half:
                    first = jnp.where(present_ref[level, 0, 2 * pair] != 0, first, empty)
                    second = jnp.where(present_ref[level, 0, 2 * pair + 1] != 0, second, empty)
                if weight_refs[i].shape[1] == rank:
                    weight_refs[i + half][pair] = jnp.concatenate([first, second], axis=1)
                    continue
                lanes = pl.ds(half * 2 * rank, 2 * rank)
                weight_refs[i][pair, :rank, lanes] = jnp.concatenate([first, empty], axis=1)
                weight_refs[i][pair, rank:, lanes] = jnp.concatenate([empty, second], axis=1)
    for fetch in fetches:
        fetch.wait()


def level_weights(level_factors, present, levels, after, root_basis=None, root_pieces=0):
    slots, last, _, _, rank, _ = level_factors.shape
    count, pieces = len(levels), 2
    roots = []
    if root_pieces:
        here = root_basis.shape[0] // lax.axis_size("order")
        roots = [jax.ShapeDtypeStruct((root_pieces, here, *root_basis.shape[1:]), BF16)]
    return call(
        functools.partial(factor_kernel, levels, pieces, root_pieces),
        "factors",
        [
            jax.ShapeDtypeStruct((slots // 2, *((rank, 2 * rank) if level == last - 1 else (2 * rank, 4 * rank))), BF16)
            for level in levels
            for _ in range(1 + (level == last - 1))
        ]
        + roots,
        [IN_HBM, IN_HBM, ANYWHERE] + [IN_HBM] * len(roots),
        slots * rank * rank * 4 * count,
        slots * rank * rank * 16 * count,
        [
            pltpu.VMEM((count, slots, 2, rank, rank), BF16),
            pltpu.SMEM(present.shape, jnp.int32),
            pltpu.SemaphoreType.DMA((count * pieces + 1 + root_pieces,)),
        ],
        mib=24,
    )(level_factors, present, after, *([root_basis] if roots else []))


def level_kernel(side, axis, state_ref, partner_ref, weight_ref, *refs):
    if len(refs) > 1:
        own_ref, *refs = refs
    out_ref = refs[0]
    me = lax.axis_index(axis) // 2
    for pair in range(weight_ref.shape[0]):
        at = pair if side is None else (pair, side)
        both = jnp.concatenate([state_ref[at], partner_ref[at]], axis=1)
        result = contract(both, weight_ref[pair], ((1,), (1,))).astype(BF16)
        if len(refs) == 1:
            out_ref[pair] = result
            continue
        early_ref, term_ref, groups_ref = refs[1:]
        owners, group, _ = groups_ref.shape[1:]
        for owner in range(owners):
            groups_ref[pair, owner] = result[owner * group : (owner + 1) * group]
        for k in range(owners):
            rows = pl.ds((k - 1) % owners * group, group)
            part = groups_ref[pair, me ^ k]
            out_ref[pair, rows] = part
            if k:
                early_ref[pair, rows] = part
        term_ref[pair] = contract(out_ref[pair], by_slot(own_ref[pair]), ((1,), (1,))).astype(BF16)


def next_states(name, state, partner, weights, side=None, owners=1, own=None):
    pairs, rows, lanes = state.shape[0], *state.shape[-2:]
    group = rows // owners
    split = owners > 1 and group % 16 == 0
    shapes = [(pairs, rows, lanes)] + [(pairs, rows - group, lanes), (pairs, rows, lanes)] * split
    outs = call(
        functools.partial(level_kernel, side, "order"),
        name,
        [jax.ShapeDtypeStruct(shape, BF16) for shape in shapes],
        whole_blocks(3 + split),
        4 * pairs * rows * lanes * lanes,
        6 * pairs * rows * lanes,
        [pltpu.VMEM((pairs, owners, group, lanes), BF16)] if split else [],
    )(state, partner, weights, *([own] if split else []))
    if owners > 1 and not split:
        me = lax.axis_index("order") // 2
        parts = [lax.dynamic_slice_in_dim(outs[0], (me ^ k) * group, group, 1) for k in range(owners)]
        early = jnp.concatenate(parts[1:], axis=1)
        state = jnp.concatenate([early, parts[0]], axis=1)
        return [state, early, own_term(state, own)]
    return outs if split else outs[0]


def late_kernel(after, state_ref, out_ref):
    del after
    rows = out_ref.shape[1]
    for pair in range(state_ref.shape[0]):
        out_ref[pair] = state_ref[pair, state_ref.shape[1] - rows :]


def late_columns(after, state, rows):
    pairs, columns, lanes = state.shape
    if rows % 16:
        return state[:, columns - rows :]
    return call(
        late_kernel,
        "late_columns",
        jax.ShapeDtypeStruct((pairs, rows, lanes), BF16),
        [ANYWHERE] + whole_blocks(1),
        1,
        4 * pairs * rows * lanes,
    )(after, state)


def by_slot(packed):
    first = lax.broadcasted_iota(jnp.int32, packed.shape, 1) < packed.shape[0]
    empty = jnp.zeros(packed.shape, BF16)
    return jnp.concatenate([jnp.where(first, packed, empty), jnp.where(first, empty, packed)], axis=0)


def own_term_kernel(state_ref, own_ref, out_ref):
    for pair in range(state_ref.shape[0]):
        out_ref[pair] = contract(state_ref[pair], by_slot(own_ref[pair]), ((1,), (1,))).astype(BF16)


def own_term(state, own):
    pairs, rows, lanes = state.shape
    return call(
        own_term_kernel,
        "own_term",
        jax.ShapeDtypeStruct(state.shape, BF16),
        whole_blocks(2),
        2 * pairs * rows * lanes * lanes,
        6 * pairs * rows * lanes,
    )(state, own)


def last_level_kernel(turn, begin, axis, after, own_ref, partner_ref, cross_ref, *refs):
    del after
    refs = list(refs)
    own_factor_ref = refs.pop(0) if refs[0].shape == cross_ref.shape else None
    out_refs, groups_ref = refs[:-1], refs[-1]
    me = lax.axis_index(axis) // 2 if turn else 0
    pairs, owners, group, _ = groups_ref.shape
    for pair in range(pairs):
        cross = by_slot(cross_ref[pair])
        own = own_ref[pair, begin : begin + owners * group]
        if own_factor_ref is None:
            result = own.astype(F32) + contract(partner_ref[pair], cross, ((1,), (1,)))
        else:
            weight = jnp.concatenate([by_slot(own_factor_ref[pair]), cross], axis=1)
            both = jnp.concatenate([own, partner_ref[pair]], axis=1)
            result = contract(both, weight, ((1,), (1,)))
        result = result.astype(BF16)
        if group % 16:
            out_refs[0][pair] = result
            continue
        for owner in range(owners):
            groups_ref[pair, owner] = result[owner * group : (owner + 1) * group]
    if group % 16 == 0:
        for k, out_ref in enumerate(out_refs):
            for pair in range(pairs):
                out_ref[pl.ds(pair * group, group)] = groups_ref[pair, me ^ k]


def last_states(name, after, own, partner, factors, owners, turn, begin=0):
    pairs, columns, lanes = partner.shape
    group = columns // owners
    rows = pairs * group
    aligned = group % 16 == 0
    if not aligned:
        own = own[:, begin : begin + columns]
        begin = 0
    parts = call(
        functools.partial(last_level_kernel, turn, begin, "order"),
        name,
        [jax.ShapeDtypeStruct((rows, lanes), BF16)] * owners if aligned else [jax.ShapeDtypeStruct(own.shape, BF16)],
        [ANYWHERE] + whole_blocks(2 + len(factors)),
        4 * pairs * columns * lanes * lanes,
        6 * pairs * columns * lanes,
        [pltpu.VMEM((pairs, owners, group, lanes), BF16)],
    )(after, own, partner, *factors)
    if aligned:
        return parts
    me = lax.axis_index("order") // 2 if turn else 0
    parts = [lax.dynamic_slice_in_dim(parts[0], (me ^ k) * group, group, 1) for k in range(owners)]
    return [part.reshape(rows, lanes) for part in parts]


def place_kernel(group, order_ref, after, root_hbm, place_ref, alive_ref, later_ref, rows_ref, sems):
    del after
    owners, here, slots = place_ref.shape
    degrees = alive_ref.shape[0]
    me = lax.axis_index("order")
    later = later_ref.shape[0]
    fetches = [fetch_roots(owners - later + i, root_hbm, later_ref.at[i], sems.at[i]) for i in range(later)]
    for fetch in fetches:
        fetch.start()
    lane = lax.broadcasted_iota(jnp.int32, (1, slots), 1)
    for k in range(owners):
        for slot in range(here):
            pair, half = slot // 2, slot % 2
            row = (pair // group * 2 + half) * group + pair % group
            rows_ref[pl.ds(row, 1), :] = (lane == order_ref[(me ^ k) * here + slot]).astype(F32)
        place_ref[k] = rows_ref[...].astype(BF16)
    degree = lax.axis_index("lat") * degrees + lax.broadcasted_iota(jnp.int32, (degrees, slots), 0)
    window = DEGREES // slots * lax.broadcasted_iota(jnp.int32, (degrees, slots), 1)
    alive_ref[...] = (degree >= window).astype(F32).astype(BF16)
    for fetch in fetches:
        fetch.wait()


def places_of(order_of_slot, root_basis, owners, later, group, after):
    slots, rank, degrees = root_basis.shape
    here = slots // owners
    return call(
        functools.partial(place_kernel, group),
        "places",
        [
            jax.ShapeDtypeStruct((owners, here, slots), BF16),
            jax.ShapeDtypeStruct((degrees, slots), BF16),
            jax.ShapeDtypeStruct((later, here, rank, degrees), BF16),
        ],
        [IN_SMEM, ANYWHERE, IN_HBM],
        slots * slots,
        8 * slots * slots,
        [pltpu.VMEM((here, slots), F32), pltpu.SemaphoreType.DMA((later,))],
    )(order_of_slot, after, root_basis)


def root_kernel(group, first, last, *refs):
    refs = list(refs)
    so_far_ref = refs.pop(0) if last else None
    place_ref, alive_ref = refs.pop(0), refs.pop(0)
    count = place_ref.shape[0] - first if last else first
    first = first if last else 0
    if last:
        root_refs = [refs[0].at[i] for i in range(count)]
    else:
        root_refs = refs[:1] + [refs[1].at[i] for i in range(count - 1)]
    refs = refs[1:] if last else refs[2:]
    state_refs, refs = refs[:count], refs[count:]
    copies = []
    if last:
        out_ref, rows_ref, natural_ref, sems = refs
    else:
        out_ref, rows_ref = refs
        natural_ref = out_ref
    fields, parts, degrees, slots = out_ref.shape
    columns = fields * parts
    rank = root_refs[0].shape[1]
    group_rows = group * columns
    here = place_ref.shape[1]
    steps = state_refs[0].shape[0] // group_rows
    shape = (group_rows, 2 * rank)
    row_pair = lax.broadcasted_iota(jnp.int32, shape, 0) // columns
    row_half = lax.broadcasted_iota(jnp.int32, shape, 1) // rank
    masks = [[(row_pair == pair) & (row_half == half) for pair in range(group)] for half in range(2)]
    empty = jnp.zeros(shape, BF16)
    for i, state_ref in enumerate(state_refs):
        for step in range(steps):
            state = state_ref[pl.ds(step * group_rows, group_rows)]
            left = jnp.concatenate(
                [jnp.concatenate([jnp.where(m, state, empty) for m in line], axis=1) for line in masks], axis=0
            )
            right = root_refs[i][pl.ds(step * group * 2, group * 2)].reshape(group * 2 * rank, degrees)
            product = contract(left, right, ((1,), (0,)))
            begin = (i * steps + step) * 2 * group_rows
            for tile in range(degrees // 128):
                rows_ref[tile, pl.ds(begin, 2 * group_rows), :] = product[:, tile * 128 : (tile + 1) * 128]
    place = place_ref[pl.ds(first, count)].reshape(count * here, slots)
    per = max(1, fields // 4)
    for column in range(columns):
        tiles = [
            rows_ref[tile, pl.ds(column, count * here, stride=columns), :].astype(BF16) for tile in range(degrees // 128)
        ]
        natural = contract(jnp.concatenate(tiles, axis=1).T, place, ((1,), (0,))).astype(BF16)
        where = (column // 2, column % 2)
        if last:
            natural = natural + so_far_ref[where]
            natural = jnp.where(alive_ref[...] != 0, natural, jnp.zeros((), BF16))
        natural_ref[where] = natural
        if last and (column + 1) % (2 * per) == 0:
            done = column // (2 * per)
            where = pl.ds(done * per, per)
            copies.append(pltpu.make_async_copy(natural_ref.at[where], out_ref.at[where], sems.at[done]))
            copies[-1].start()
    for copy in copies:
        copy.wait()


def spectra_of(states, roots, places, alive, so_far, first, group):
    state_rows = states[0].shape[0]
    rank, degrees = roots[0].shape[-2:]
    owners, here, slots = places.shape
    count = len(states)
    columns = state_rows * 2 // here
    last = so_far is not None
    out = jax.ShapeDtypeStruct((columns // 2, 2, degrees, slots), BF16)
    inputs = [places, alive, *roots, *states]
    in_specs = whole_blocks(len(inputs))
    scratch = [pltpu.VMEM((degrees // 128, count * here * columns, 128), F32)]
    more = {}
    if last:
        inputs = [so_far, *inputs]
        in_specs = whole_blocks(len(inputs))
        scratch += [pltpu.VMEM(out.shape, BF16), pltpu.SemaphoreType.DMA((columns // 2,))]
        more["out_specs"] = IN_HBM
    return call(
        functools.partial(root_kernel, group, first, last),
        "root",
        out,
        in_specs,
        2 * count * here * rank * degrees * columns,
        2 * count * here * rank * degrees,
        scratch,
        mib=24,
        **more,
    )(*inputs)


def per_device(
    fourier, quad_weights, leaf_basis, level_factors, sparsity, root_basis, order_of_slot
):
    slots, columns, lats = fourier.shape
    owners = lax.axis_size("order")
    levels = level_factors.shape[1]
    group = max(2, 16 * owners // columns)
    present = in_hbm(sparsity.transpose(1, 2, 0))
    fourier, leaf_basis, level_factors, root_basis = map(in_hbm, (fourier, leaf_basis, level_factors, root_basis))
    quad_weights = in_hbm(quad_weights.reshape(1, lats))

    def swap(array, axis, bits):
        return lax.ppermute(array, axis, [(i, i ^ bits) for i in range(lax.axis_size(axis))])

    def swap_both(array, order_bits, lat_bits):
        blocks = lax.axis_size("lat")
        pairs = [
            (o * blocks + b, (o ^ order_bits) * blocks + (b ^ lat_bits)) for o in range(owners) for b in range(blocks)
        ]
        return lax.ppermute(array, ("order", "lat"), pairs)

    early_pieces = 3 * owners // 4
    state, root_0 = leaf_states(fourier, quad_weights, leaf_basis, root_basis, owners)
    partner = swap(state, "lat", 1)
    weights = level_weights(level_factors, present, (0,), state)
    states = [next_states(f"level0_{c}", state, partner, weights[0], c) for c in range(2)]
    weights += level_weights(level_factors, present, tuple(range(1, levels)), states[1], root_basis, early_pieces - 1)
    own_factors, cross_factors, early_roots = weights[-3:]
    other_cross = swap(cross_factors, "order", 1)
    high = owners // 2
    own_columns = columns // owners
    for level in range(1, levels - 1):
        partners = [swap(state, "lat", 1 << level) for state in states]
        parts = high if level == levels - 2 else 1
        states = [
            next_states(f"level{level}_{c}", states[c], partners[c], weights[level], None, parts if c else 1, own_factors)
            for c in range(2)
        ]
    top = 1 << levels - 1
    mine, (other, early, term) = states
    mine_partner = swap(mine, "lat", top)
    early_partner = swap_both(early, 1, top)
    other_own = swap(term, "order", 1)
    places, alive, later_roots = places_of(
        order_of_slot, root_basis, owners, owners - early_pieces, group, other
    )
    late_partner = swap_both(late_columns(alive, other, own_columns), 1, top)
    even = last_states("last_own", alive, mine, mine_partner, (cross_factors, own_factors), high, True)
    begin = columns // 2 - own_columns
    odd = last_states("last_early", alive, other_own, early_partner, (other_cross,), high - 1, False)
    odd = [*last_states("last_late", alive, other_own, late_partner, (other_cross,), 1, False, begin), *odd]
    arrived = [swap((odd if k % 2 else even)[k // 2], "order", k // 2 * 2) if k > 1 else (even, odd)[k][0] for k in range(owners)]
    roots = [root_0, early_roots]
    spectra = spectra_of(arrived[:early_pieces], roots, places, alive, None, early_pieces, group)
    return spectra_of(arrived[early_pieces:], [later_roots], places, alive, spectra, early_pieces, group)


def solution(mesh):
    return jax.shard_map(
        per_device,
        mesh=mesh,
        in_specs=(
            P("order", None, "lat"),
            P("lat"),
            P("order", None, "lat"),
            P("order", None, None, "lat", None, None),
            P("order", None, "lat"),
            P(None, None, "lat"),
            P(),
        ),
        out_specs=P("order", None, "lat", None),
        check_vma=False,
    )
```

```python
import functools

import jax
import jax.numpy as jnp
from jax import lax
from jax.experimental import pallas as pl
from jax.experimental.pallas import tpu as pltpu
from jax.sharding import PartitionSpec as P

DEGREES = 2048
F32, BF16 = jnp.float32, jnp.bfloat16
MIB = 1 << 20
IN_HBM = pl.BlockSpec(memory_space=pltpu.HBM)
IN_SMEM = pl.BlockSpec(memory_space=pltpu.SMEM)
ANYWHERE = pl.BlockSpec(memory_space=pl.ANY)


def contract(lhs, rhs, dims):
    return lax.dot_general(lhs, rhs, (dims, ((), ())), preferred_element_type=F32)


def in_hbm(array):
    return pltpu.with_memory_space_constraint(array, pltpu.HBM)


def call(kernel, name, out_shape, in_specs, flops, size, scratch=(), mib=16, **more):
    return pl.pallas_call(
        kernel,
        out_shape=out_shape,
        in_specs=in_specs,
        scratch_shapes=list(scratch),
        compiler_params=pltpu.CompilerParams(vmem_limit_bytes=mib * MIB),
        cost_estimate=pl.CostEstimate(flops=flops // 1000, bytes_accessed=size // 1000, transcendentals=0),
        name=name,
        **more,
    )


def whole_blocks(count):
    return [pl.BlockSpec()] * count


def fetch_roots(k, root_hbm, root_ref, sem):
    here = root_ref.shape[0]
    me = lax.axis_index("order")
    return pltpu.make_async_copy(root_hbm.at[pl.ds((me ^ k) * here, here)], root_ref, sem)


def leaf_kernel(
    pieces, group, fourier_hbm, weight_hbm, leaf_hbm, root_hbm, state_ref, root_ref, fourier_ref, weight_ref, leaf_ref, sems
):
    side = lax.axis_index("order") & 1
    slots, columns, lats = fourier_ref.shape
    rank = leaf_ref.shape[1]
    per = slots // pieces
    copies = [pltpu.make_async_copy(weight_hbm, weight_ref, sems.at[0])]
    for piece in range(pieces):
        part = pl.ds(piece * per, per)
        copies.append(pltpu.make_async_copy(fourier_hbm.at[part], fourier_ref.at[part], sems.at[1 + 2 * piece]))
        copies.append(pltpu.make_async_copy(leaf_hbm.at[part], leaf_ref.at[part], sems.at[2 + 2 * piece]))
    copies.append(fetch_roots(0, root_hbm, root_ref, sems.at[1 + 2 * pieces]))
    for copy in copies:
        copy.start()
    copies[0].wait()
    weight = weight_ref[...]
    mine = lax.broadcasted_iota(jnp.int32, (columns, 2 * rank), 1) < rank
    for pair in range(slots // 2):
        if 2 * pair % per == 0:
            copies[1 + 2 * (2 * pair // per)].wait()
            copies[2 + 2 * (2 * pair // per)].wait()
        both = pl.ds(2 * pair, 2)
        weighted = (fourier_ref[both].astype(F32) * weight[None]).astype(BF16)
        product = contract(
            weighted.reshape(2 * columns, lats), leaf_ref[both].reshape(2 * rank, lats), ((1,), (1,))
        )
        state = jnp.where(mine, product[:columns], product[columns:]).astype(BF16)
        if group % 16:
            state_ref[pair] = state
            continue
        for owner in range(columns // group):
            rows = pl.ds(owner // 2 * group, group)
            state_ref[pair, owner % 2 ^ side, rows] = state[owner * group : (owner + 1) * group]
    copies[-1].wait()


def leaf_states(fourier, quad_weights, leaf_basis, root_basis, owners):
    slots, columns, lats = fourier.shape
    rank = leaf_basis.shape[1]
    pairs, half, lanes, group = slots // 2, columns // 2, 2 * rank, columns // owners
    pieces = 2
    shape = (pairs, columns, lanes) if group % 16 else (pairs, 2, half, lanes)
    state, root = call(
        functools.partial(leaf_kernel, pieces, group),
        "leaf",
        [
            jax.ShapeDtypeStruct(shape, BF16),
            jax.ShapeDtypeStruct((root_basis.shape[0] // owners, *root_basis.shape[1:]), BF16),
        ],
        [IN_HBM] * 4,
        2 * slots * columns * rank * lats,
        4 * slots * columns * lats,
        [
            pltpu.VMEM((slots, columns, lats), BF16),
            pltpu.VMEM((1, lats), F32),
            pltpu.VMEM((slots, rank, lats), BF16),
            pltpu.SemaphoreType.DMA((2 + 2 * pieces,)),
        ],
    )(fourier, quad_weights, leaf_basis, root_basis)
    if group % 16:
        side = lax.axis_index("order") & 1
        state = state.reshape(pairs, owners // 2, 2, group, lanes)
        sides = [lax.dynamic_index_in_dim(state, side ^ i, 2, False).reshape(pairs, half, lanes) for i in range(2)]
        state = jnp.stack(sides, axis=1)
    return state, root


def factor_kernel(levels, pieces, roots, factor_hbm, present_hbm, after, *refs):
    del after
    weight_refs, (factor_ref, present_ref, sems) = list(refs[:-3]), refs[-3:]
    fetches = []
    if roots:
        root_hbm, root_ref = weight_refs.pop(0), weight_refs.pop()
        for i in range(root_ref.shape[0]):
            fetches.append(fetch_roots(1 + i, root_hbm, root_ref.at[i], sems.at[len(levels) * pieces + 1 + i]))
    present_copy = pltpu.make_async_copy(present_hbm, present_ref, sems.at[len(levels) * pieces])
    present_copy.start()
    _, slots, _, rank, _ = factor_ref.shape
    per = slots // pieces
    copies = {}
    for i, level in enumerate(levels):
        for piece in range(pieces):
            part = pl.ds(piece * per, per)
            copies[i, piece] = pltpu.make_async_copy(
                factor_hbm.at[part, level, :, 0], factor_ref.at[i, part], sems.at[i * pieces + piece]
            )
            copies[i, piece].start()
    for fetch in fetches:
        fetch.start()
    empty = jnp.zeros((rank, rank), BF16)
    present_copy.wait()
    for i, level in enumerate(levels):
        for pair in range(slots // 2):
            if 2 * pair % per == 0:
                copies[i, 2 * pair // per].wait()
            for half in range(2):
                first, second = (factor_ref[i, slot, half] for slot in (2 * pair, 2 * pair + 1))
                if half:
                    first = jnp.where(present_ref[level, 0, 2 * pair] != 0, first, empty)
                    second = jnp.where(present_ref[level, 0, 2 * pair + 1] != 0, second, empty)
                if weight_refs[i].shape[1] == rank:
                    weight_refs[i + half][pair] = jnp.concatenate([first, second], axis=1)
                    continue
                lanes = pl.ds(half * 2 * rank, 2 * rank)
                weight_refs[i][pair, :rank, lanes] = jnp.concatenate([first, empty], axis=1)
                weight_refs[i][pair, rank:, lanes] = jnp.concatenate([empty, second], axis=1)
    for fetch in fetches:
        fetch.wait()


def level_weights(level_factors, present, levels, after, root_basis=None, root_pieces=0):
    slots, last, _, _, rank, _ = level_factors.shape
    count, pieces = len(levels), 2
    roots = []
    if root_pieces:
        here = root_basis.shape[0] // lax.axis_size("order")
        roots = [jax.ShapeDtypeStruct((root_pieces, here, *root_basis.shape[1:]), BF16)]
    return call(
        functools.partial(factor_kernel, levels, pieces, root_pieces),
        "factors",
        [
            jax.ShapeDtypeStruct((slots // 2, *((rank, 2 * rank) if level == last - 1 else (2 * rank, 4 * rank))), BF16)
            for level in levels
            for _ in range(1 + (level == last - 1))
        ]
        + roots,
        [IN_HBM, IN_HBM, ANYWHERE] + [IN_HBM] * len(roots),
        slots * rank * rank * 4 * count,
        slots * rank * rank * 16 * count,
        [
            pltpu.VMEM((count, slots, 2, rank, rank), BF16),
            pltpu.SMEM(present.shape, jnp.int32),
            pltpu.SemaphoreType.DMA((count * pieces + 1 + root_pieces,)),
        ],
        mib=24,
    )(level_factors, present, after, *([root_basis] if roots else []))


def first_level_kernel(state_ref, partner_ref, weight_ref, *out_refs):
    pairs, sides, rows, lanes = state_ref.shape
    for pair in range(pairs):
        both = [ref[pair].reshape(sides * rows, lanes) for ref in (state_ref, partner_ref)]
        result = contract(jnp.concatenate(both, axis=1), weight_ref[pair], ((1,), (1,))).astype(BF16)
        for side, out_ref in enumerate(out_refs):
            out_ref[pair] = result[side * rows : (side + 1) * rows]


def first_states(state, partner, weights):
    pairs, sides, rows, lanes = state.shape
    return call(
        first_level_kernel,
        "level0",
        [jax.ShapeDtypeStruct((pairs, rows, lanes), BF16)] * sides,
        whole_blocks(3),
        4 * pairs * sides * rows * lanes * lanes,
        6 * pairs * sides * rows * lanes,
    )(state, partner, weights)


def level_kernel(side, axis, state_ref, partner_ref, weight_ref, *refs):
    if len(refs) > 1:
        own_ref, *refs = refs
    out_ref = refs[0]
    me = lax.axis_index(axis) // 2
    for pair in range(weight_ref.shape[0]):
        at = pair if side is None else (pair, side)
        both = jnp.concatenate([state_ref[at], partner_ref[at]], axis=1)
        result = contract(both, weight_ref[pair], ((1,), (1,))).astype(BF16)
        if len(refs) == 1:
            out_ref[pair] = result
            continue
        early_ref, term_ref, groups_ref = refs[1:]
        owners, group, _ = groups_ref.shape[1:]
        for owner in range(owners):
            groups_ref[pair, owner] = result[owner * group : (owner + 1) * group]
        for k in range(owners):
            rows = pl.ds((k - 1) % owners * group, group)
            part = groups_ref[pair, me ^ k]
            out_ref[pair, rows] = part
            if k:
                early_ref[pair, rows] = part
        term_ref[pair] = contract(out_ref[pair], by_slot(own_ref[pair]), ((1,), (1,))).astype(BF16)


def next_states(name, state, partner, weights, side=None, owners=1, own=None):
    pairs, rows, lanes = state.shape[0], *state.shape[-2:]
    group = rows // owners
    split = owners > 1 and group % 16 == 0
    shapes = [(pairs, rows, lanes)] + [(pairs, rows - group, lanes), (pairs, rows, lanes)] * split
    outs = call(
        functools.partial(level_kernel, side, "order"),
        name,
        [jax.ShapeDtypeStruct(shape, BF16) for shape in shapes],
        whole_blocks(3 + split),
        4 * pairs * rows * lanes * lanes,
        6 * pairs * rows * lanes,
        [pltpu.VMEM((pairs, owners, group, lanes), BF16)] if split else [],
    )(state, partner, weights, *([own] if split else []))
    if owners > 1 and not split:
        me = lax.axis_index("order") // 2
        parts = [lax.dynamic_slice_in_dim(outs[0], (me ^ k) * group, group, 1) for k in range(owners)]
        early = jnp.concatenate(parts[1:], axis=1)
        state = jnp.concatenate([early, parts[0]], axis=1)
        return [state, early, own_term(state, own)]
    return outs if split else outs[0]


def late_kernel(after, state_ref, out_ref):
    del after
    rows = out_ref.shape[1]
    for pair in range(state_ref.shape[0]):
        out_ref[pair] = state_ref[pair, state_ref.shape[1] - rows :]


def late_columns(after, state, rows):
    pairs, columns, lanes = state.shape
    if rows % 16:
        return state[:, columns - rows :]
    return call(
        late_kernel,
        "late_columns",
        jax.ShapeDtypeStruct((pairs, rows, lanes), BF16),
        [ANYWHERE] + whole_blocks(1),
        1,
        4 * pairs * rows * lanes,
    )(after, state)


def by_slot(packed):
    first = lax.broadcasted_iota(jnp.int32, packed.shape, 1) < packed.shape[0]
    empty = jnp.zeros(packed.shape, BF16)
    return jnp.concatenate([jnp.where(first, packed, empty), jnp.where(first, empty, packed)], axis=0)


def own_term_kernel(state_ref, own_ref, out_ref):
    for pair in range(state_ref.shape[0]):
        out_ref[pair] = contract(state_ref[pair], by_slot(own_ref[pair]), ((1,), (1,))).astype(BF16)


def own_term(state, own):
    pairs, rows, lanes = state.shape
    return call(
        own_term_kernel,
        "own_term",
        jax.ShapeDtypeStruct(state.shape, BF16),
        whole_blocks(2),
        2 * pairs * rows * lanes * lanes,
        6 * pairs * rows * lanes,
    )(state, own)


def last_level_kernel(turn, begin, axis, after, own_ref, partner_ref, cross_ref, *refs):
    del after
    refs = list(refs)
    own_factor_ref = refs.pop(0) if refs[0].shape == cross_ref.shape else None
    out_refs, groups_ref = refs[:-1], refs[-1]
    me = lax.axis_index(axis) // 2 if turn else 0
    pairs, owners, group, _ = groups_ref.shape
    for pair in range(pairs):
        cross = by_slot(cross_ref[pair])
        own = own_ref[pair, begin : begin + owners * group]
        if own_factor_ref is None:
            result = own.astype(F32) + contract(partner_ref[pair], cross, ((1,), (1,)))
        else:
            weight = jnp.concatenate([by_slot(own_factor_ref[pair]), cross], axis=1)
            both = jnp.concatenate([own, partner_ref[pair]], axis=1)
            result = contract(both, weight, ((1,), (1,)))
        result = result.astype(BF16)
        if group % 16:
            out_refs[0][pair] = result
            continue
        for owner in range(owners):
            groups_ref[pair, owner] = result[owner * group : (owner + 1) * group]
    if group % 16 == 0:
        for k, out_ref in enumerate(out_refs):
            for pair in range(pairs):
                out_ref[pl.ds(pair * group, group)] = groups_ref[pair, me ^ k]


def last_states(name, after, own, partner, factors, owners, turn, begin=0):
    pairs, columns, lanes = partner.shape
    group = columns // owners
    rows = pairs * group
    aligned = group % 16 == 0
    if not aligned:
        own = own[:, begin : begin + columns]
        begin = 0
    parts = call(
        functools.partial(last_level_kernel, turn, begin, "order"),
        name,
        [jax.ShapeDtypeStruct((rows, lanes), BF16)] * owners if aligned else [jax.ShapeDtypeStruct(own.shape, BF16)],
        [ANYWHERE] + whole_blocks(2 + len(factors)),
        4 * pairs * columns * lanes * lanes,
        6 * pairs * columns * lanes,
        [pltpu.VMEM((pairs, owners, group, lanes), BF16)],
    )(after, own, partner, *factors)
    if aligned:
        return parts
    me = lax.axis_index("order") // 2 if turn else 0
    parts = [lax.dynamic_slice_in_dim(parts[0], (me ^ k) * group, group, 1) for k in range(owners)]
    return [part.reshape(rows, lanes) for part in parts]


def place_kernel(group, order_ref, after, root_hbm, place_ref, alive_ref, later_ref, rows_ref, sems):
    del after
    owners, here, slots = place_ref.shape
    degrees = alive_ref.shape[0]
    me = lax.axis_index("order")
    later = later_ref.shape[0]
    fetches = [fetch_roots(owners - later + i, root_hbm, later_ref.at[i], sems.at[i]) for i in range(later)]
    for fetch in fetches:
        fetch.start()
    lane = lax.broadcasted_iota(jnp.int32, (1, slots), 1)
    for k in range(owners):
        for slot in range(here):
            pair, half = slot // 2, slot % 2
            row = (pair // group * 2 + half) * group + pair % group
            rows_ref[pl.ds(row, 1), :] = (lane == order_ref[(me ^ k) * here + slot]).astype(F32)
        place_ref[k] = rows_ref[...].astype(BF16)
    degree = lax.axis_index("lat") * degrees + lax.broadcasted_iota(jnp.int32, (degrees, slots), 0)
    window = DEGREES // slots * lax.broadcasted_iota(jnp.int32, (degrees, slots), 1)
    alive_ref[...] = (degree >= window).astype(F32).astype(BF16)
    for fetch in fetches:
        fetch.wait()


def places_of(order_of_slot, root_basis, owners, later, group, after):
    slots, rank, degrees = root_basis.shape
    here = slots // owners
    return call(
        functools.partial(place_kernel, group),
        "places",
        [
            jax.ShapeDtypeStruct((owners, here, slots), BF16),
            jax.ShapeDtypeStruct((degrees, slots), BF16),
            jax.ShapeDtypeStruct((later, here, rank, degrees), BF16),
        ],
        [IN_SMEM, ANYWHERE, IN_HBM],
        slots * slots,
        8 * slots * slots,
        [pltpu.VMEM((here, slots), F32), pltpu.SemaphoreType.DMA((later,))],
    )(order_of_slot, after, root_basis)


def root_kernel(group, first, last, *refs):
    refs = list(refs)
    so_far_ref = refs.pop(0) if last else None
    place_ref, alive_ref = refs.pop(0), refs.pop(0)
    count = place_ref.shape[0] - first if last else first
    first = first if last else 0
    if last:
        root_refs = [refs[0].at[i] for i in range(count)]
    else:
        root_refs = refs[:1] + [refs[1].at[i] for i in range(count - 1)]
    refs = refs[1:] if last else refs[2:]
    state_refs, refs = refs[:count], refs[count:]
    copies = []
    if last:
        out_ref, rows_ref, natural_ref, sems = refs
    else:
        out_ref, rows_ref = refs
        natural_ref = out_ref
    fields, parts, degrees, slots = out_ref.shape
    columns = fields * parts
    rank = root_refs[0].shape[1]
    group_rows = group * columns
    here = place_ref.shape[1]
    steps = state_refs[0].shape[0] // group_rows
    shape = (group_rows, 2 * rank)
    row_pair = lax.broadcasted_iota(jnp.int32, shape, 0) // columns
    row_half = lax.broadcasted_iota(jnp.int32, shape, 1) // rank
    masks = [[(row_pair == pair) & (row_half == half) for pair in range(group)] for half in range(2)]
    empty = jnp.zeros(shape, BF16)
    for i, state_ref in enumerate(state_refs):
        for step in range(steps):
            state = state_ref[pl.ds(step * group_rows, group_rows)]
            left = jnp.concatenate(
                [jnp.concatenate([jnp.where(m, state, empty) for m in line], axis=1) for line in masks], axis=0
            )
            right = root_refs[i][pl.ds(step * group * 2, group * 2)].reshape(group * 2 * rank, degrees)
            product = contract(left, right, ((1,), (0,)))
            begin = (i * steps + step) * 2 * group_rows
            for tile in range(degrees // 128):
                rows_ref[tile, pl.ds(begin, 2 * group_rows), :] = product[:, tile * 128 : (tile + 1) * 128]
    place = place_ref[pl.ds(first, count)].reshape(count * here, slots)
    per = max(1, fields // 4)
    for column in range(columns):
        tiles = [
            rows_ref[tile, pl.ds(column, count * here, stride=columns), :].astype(BF16) for tile in range(degrees // 128)
        ]
        natural = contract(jnp.concatenate(tiles, axis=1).T, place, ((1,), (0,))).astype(BF16)
        where = (column // 2, column % 2)
        if last:
            natural = natural + so_far_ref[where]
            natural = jnp.where(alive_ref[...] != 0, natural, jnp.zeros((), BF16))
        natural_ref[where] = natural
        if last and (column + 1) % (2 * per) == 0:
            done = column // (2 * per)
            where = pl.ds(done * per, per)
            copies.append(pltpu.make_async_copy(natural_ref.at[where], out_ref.at[where], sems.at[done]))
            copies[-1].start()
    for copy in copies:
        copy.wait()


def spectra_of(states, roots, places, alive, so_far, first, group):
    state_rows = states[0].shape[0]
    rank, degrees = roots[0].shape[-2:]
    owners, here, slots = places.shape
    count = len(states)
    columns = state_rows * 2 // here
    last = so_far is not None
    out = jax.ShapeDtypeStruct((columns // 2, 2, degrees, slots), BF16)
    inputs = [places, alive, *roots, *states]
    in_specs = whole_blocks(len(inputs))
    scratch = [pltpu.VMEM((degrees // 128, count * here * columns, 128), F32)]
    more = {}
    if last:
        inputs = [so_far, *inputs]
        in_specs = whole_blocks(len(inputs))
        scratch += [pltpu.VMEM(out.shape, BF16), pltpu.SemaphoreType.DMA((columns // 2,))]
        more["out_specs"] = IN_HBM
    return call(
        functools.partial(root_kernel, group, first, last),
        "root",
        out,
        in_specs,
        2 * count * here * rank * degrees * columns,
        2 * count * here * rank * degrees,
        scratch,
        mib=24,
        **more,
    )(*inputs)


def per_device(
    fourier, quad_weights, leaf_basis, level_factors, sparsity, root_basis, order_of_slot
):
    slots, columns, lats = fourier.shape
    owners = lax.axis_size("order")
    levels = level_factors.shape[1]
    group = max(2, 16 * owners // columns)
    present = in_hbm(sparsity.transpose(1, 2, 0))
    fourier, leaf_basis, level_factors, root_basis = map(in_hbm, (fourier, leaf_basis, level_factors, root_basis))
    quad_weights = in_hbm(quad_weights.reshape(1, lats))

    def swap(array, axis, bits):
        return lax.ppermute(array, axis, [(i, i ^ bits) for i in range(lax.axis_size(axis))])

    def swap_both(array, order_bits, lat_bits):
        blocks = lax.axis_size("lat")
        pairs = [
            (o * blocks + b, (o ^ order_bits) * blocks + (b ^ lat_bits)) for o in range(owners) for b in range(blocks)
        ]
        return lax.ppermute(array, ("order", "lat"), pairs)

    early_pieces = 3 * owners // 4
    state, root_0 = leaf_states(fourier, quad_weights, leaf_basis, root_basis, owners)
    partner = swap(state, "lat", 1)
    weights = level_weights(level_factors, present, (0,), state)
    states = first_states(state, partner, weights[0])
    weights += level_weights(level_factors, present, tuple(range(1, levels)), states[1], root_basis, early_pieces - 1)
    own_factors, cross_factors, early_roots = weights[-3:]
    other_cross = swap(cross_factors, "order", 1)
    high = owners // 2
    own_columns = columns // owners
    for level in range(1, levels - 1):
        partners = [swap(state, "lat", 1 << level) for state in states]
        parts = high if level == levels - 2 else 1
        states = [
            next_states(f"level{level}_{c}", states[c], partners[c], weights[level], None, parts if c else 1, own_factors)
            for c in range(2)
        ]
    top = 1 << levels - 1
    mine, (other, early, term) = states
    mine_partner = swap(mine, "lat", top)
    early_partner = swap_both(early, 1, top)
    other_own = swap(term, "order", 1)
    places, alive, later_roots = places_of(
        order_of_slot, root_basis, owners, owners - early_pieces, group, other
    )
    late_partner = swap_both(late_columns(alive, other, own_columns), 1, top)
    even = last_states("last_own", alive, mine, mine_partner, (cross_factors, own_factors), high, True)
    begin = columns // 2 - own_columns
    odd = last_states("last_early", alive, other_own, early_partner, (other_cross,), high - 1, False)
    odd = [*last_states("last_late", alive, other_own, late_partner, (other_cross,), 1, False, begin), *odd]
    arrived = [swap((odd if k % 2 else even)[k // 2], "order", k // 2 * 2) if k > 1 else (even, odd)[k][0] for k in range(owners)]
    roots = [root_0, early_roots]
    spectra = spectra_of(arrived[:early_pieces], roots, places, alive, None, early_pieces, group)
    return spectra_of(arrived[early_pieces:], [later_roots], places, alive, spectra, early_pieces, group)


def solution(mesh):
    return jax.shard_map(
        per_device,
        mesh=mesh,
        in_specs=(
            P("order", None, "lat"),
            P("lat"),
            P("order", None, "lat"),
            P("order", None, None, "lat", None, None),
            P("order", None, "lat"),
            P(None, None, "lat"),
            P(),
        ),
        out_specs=P("order", None, "lat", None),
        check_vma=False,
    )
```

```python
import functools

import jax
import jax.numpy as jnp
from jax import lax
from jax.experimental import pallas as pl
from jax.experimental.pallas import tpu as pltpu
from jax.sharding import PartitionSpec as P

DEGREES = 2048
F32, BF16 = jnp.float32, jnp.bfloat16
MIB = 1 << 20
IN_HBM = pl.BlockSpec(memory_space=pltpu.HBM)
IN_SMEM = pl.BlockSpec(memory_space=pltpu.SMEM)
ANYWHERE = pl.BlockSpec(memory_space=pl.ANY)


def contract(lhs, rhs, dims):
    return lax.dot_general(lhs, rhs, (dims, ((), ())), preferred_element_type=F32)


def in_hbm(array):
    return pltpu.with_memory_space_constraint(array, pltpu.HBM)


def call(kernel, name, out_shape, in_specs, flops, size, scratch=(), mib=16, **more):
    return pl.pallas_call(
        kernel,
        out_shape=out_shape,
        in_specs=in_specs,
        scratch_shapes=list(scratch),
        compiler_params=pltpu.CompilerParams(vmem_limit_bytes=mib * MIB),
        cost_estimate=pl.CostEstimate(flops=flops // 1000, bytes_accessed=size // 1000, transcendentals=0),
        name=name,
        **more,
    )


def whole_blocks(count):
    return [pl.BlockSpec()] * count


def fetch_roots(k, root_hbm, root_ref, sem, here=None, begin=0):
    size = root_ref.shape[0]
    here = here or size
    me = lax.axis_index("order")
    return pltpu.make_async_copy(root_hbm.at[pl.ds((me ^ k) * here + begin, size)], root_ref, sem)


def leaf_kernel(
    pieces, group, fourier_hbm, weight_hbm, leaf_hbm, root_hbm, state_ref, root_ref, fourier_ref, weight_ref, leaf_ref, sems
):
    side = lax.axis_index("order") & 1
    slots, columns, lats = fourier_ref.shape
    rank = leaf_ref.shape[1]
    per = slots // pieces
    copies = [pltpu.make_async_copy(weight_hbm, weight_ref, sems.at[0])]
    for piece in range(pieces):
        part = pl.ds(piece * per, per)
        copies.append(pltpu.make_async_copy(fourier_hbm.at[part], fourier_ref.at[part], sems.at[1 + 2 * piece]))
        copies.append(pltpu.make_async_copy(leaf_hbm.at[part], leaf_ref.at[part], sems.at[2 + 2 * piece]))
    copies.append(fetch_roots(0, root_hbm, root_ref, sems.at[1 + 2 * pieces]))
    for copy in copies:
        copy.start()
    copies[0].wait()
    weight = weight_ref[...]
    mine = lax.broadcasted_iota(jnp.int32, (columns, 2 * rank), 1) < rank
    for pair in range(slots // 2):
        if 2 * pair % per == 0:
            copies[1 + 2 * (2 * pair // per)].wait()
            copies[2 + 2 * (2 * pair // per)].wait()
        both = pl.ds(2 * pair, 2)
        weighted = (fourier_ref[both].astype(F32) * weight[None]).astype(BF16)
        product = contract(
            weighted.reshape(2 * columns, lats), leaf_ref[both].reshape(2 * rank, lats), ((1,), (1,))
        )
        state = jnp.where(mine, product[:columns], product[columns:]).astype(BF16)
        if group % 16:
            state_ref[pair] = state
            continue
        for owner in range(columns // group):
            rows = pl.ds(owner // 2 * group, group)
            state_ref[pair, owner % 2 ^ side, rows] = state[owner * group : (owner + 1) * group]
    copies[-1].wait()


def leaf_states(fourier, quad_weights, leaf_basis, root_basis, owners):
    slots, columns, lats = fourier.shape
    rank = leaf_basis.shape[1]
    pairs, half, lanes, group = slots // 2, columns // 2, 2 * rank, columns // owners
    pieces = 2
    shape = (pairs, columns, lanes) if group % 16 else (pairs, 2, half, lanes)
    state, root = call(
        functools.partial(leaf_kernel, pieces, group),
        "leaf",
        [
            jax.ShapeDtypeStruct(shape, BF16),
            jax.ShapeDtypeStruct((root_basis.shape[0] // owners, *root_basis.shape[1:]), BF16),
        ],
        [IN_HBM] * 4,
        2 * slots * columns * rank * lats,
        4 * slots * columns * lats,
        [
            pltpu.VMEM((slots, columns, lats), BF16),
            pltpu.VMEM((1, lats), F32),
            pltpu.VMEM((slots, rank, lats), BF16),
            pltpu.SemaphoreType.DMA((2 + 2 * pieces,)),
        ],
    )(fourier, quad_weights, leaf_basis, root_basis)
    if group % 16:
        side = lax.axis_index("order") & 1
        state = state.reshape(pairs, owners // 2, 2, group, lanes)
        sides = [lax.dynamic_index_in_dim(state, side ^ i, 2, False).reshape(pairs, half, lanes) for i in range(2)]
        state = jnp.stack(sides, axis=1)
    return state, root


def factor_kernel(levels, pieces, roots, factor_hbm, present_hbm, after, *refs):
    del after
    weight_refs, (factor_ref, present_ref, sems) = list(refs[:-3]), refs[-3:]
    fetches = []
    if roots:
        root_hbm, root_ref = weight_refs.pop(0), weight_refs.pop()
        for i in range(root_ref.shape[0]):
            fetches.append(fetch_roots(1 + i, root_hbm, root_ref.at[i], sems.at[len(levels) * pieces + 1 + i]))
    present_copy = pltpu.make_async_copy(present_hbm, present_ref, sems.at[len(levels) * pieces])
    present_copy.start()
    _, slots, _, rank, _ = factor_ref.shape
    per = slots // pieces
    copies = {}
    for i, level in enumerate(levels):
        for piece in range(pieces):
            part = pl.ds(piece * per, per)
            copies[i, piece] = pltpu.make_async_copy(
                factor_hbm.at[part, level, :, 0], factor_ref.at[i, part], sems.at[i * pieces + piece]
            )
            copies[i, piece].start()
    for fetch in fetches:
        fetch.start()
    empty = jnp.zeros((rank, rank), BF16)
    present_copy.wait()
    for i, level in enumerate(levels):
        for pair in range(slots // 2):
            if 2 * pair % per == 0:
                copies[i, 2 * pair // per].wait()
            for half in range(2):
                first, second = (factor_ref[i, slot, half] for slot in (2 * pair, 2 * pair + 1))
                if half:
                    first = jnp.where(present_ref[level, 0, 2 * pair] != 0, first, empty)
                    second = jnp.where(present_ref[level, 0, 2 * pair + 1] != 0, second, empty)
                if weight_refs[i].shape[1] == rank:
                    weight_refs[i + half][pair] = jnp.concatenate([first, second], axis=1)
                    continue
                lanes = pl.ds(half * 2 * rank, 2 * rank)
                weight_refs[i][pair, :rank, lanes] = jnp.concatenate([first, empty], axis=1)
                weight_refs[i][pair, rank:, lanes] = jnp.concatenate([empty, second], axis=1)
    for fetch in fetches:
        fetch.wait()


def level_weights(level_factors, present, levels, after, root_basis=None, root_pieces=0):
    slots, last, _, _, rank, _ = level_factors.shape
    count, pieces = len(levels), 2
    roots = []
    if root_pieces:
        here = root_basis.shape[0] // lax.axis_size("order")
        roots = [jax.ShapeDtypeStruct((root_pieces, here, *root_basis.shape[1:]), BF16)]
    return call(
        functools.partial(factor_kernel, levels, pieces, root_pieces),
        "factors",
        [
            jax.ShapeDtypeStruct((slots // 2, *((rank, 2 * rank) if level == last - 1 else (2 * rank, 4 * rank))), BF16)
            for level in levels
            for _ in range(1 + (level == last - 1))
        ]
        + roots,
        [IN_HBM, IN_HBM, ANYWHERE] + [IN_HBM] * len(roots),
        slots * rank * rank * 4 * count,
        slots * rank * rank * 16 * count,
        [
            pltpu.VMEM((count, slots, 2, rank, rank), BF16),
            pltpu.SMEM(present.shape, jnp.int32),
            pltpu.SemaphoreType.DMA((count * pieces + 1 + root_pieces,)),
        ],
        mib=24,
    )(level_factors, present, after, *([root_basis] if roots else []))


def first_level_kernel(state_ref, partner_ref, weight_ref, *out_refs):
    pairs, sides, rows, lanes = state_ref.shape
    for pair in range(pairs):
        both = [ref[pair].reshape(sides * rows, lanes) for ref in (state_ref, partner_ref)]
        result = contract(jnp.concatenate(both, axis=1), weight_ref[pair], ((1,), (1,))).astype(BF16)
        for side, out_ref in enumerate(out_refs):
            out_ref[pair] = result[side * rows : (side + 1) * rows]


def first_states(state, partner, weights):
    pairs, sides, rows, lanes = state.shape
    return call(
        first_level_kernel,
        "level0",
        [jax.ShapeDtypeStruct((pairs, rows, lanes), BF16)] * sides,
        whole_blocks(3),
        4 * pairs * sides * rows * lanes * lanes,
        6 * pairs * sides * rows * lanes,
    )(state, partner, weights)


def level_kernel(side, axis, state_ref, partner_ref, weight_ref, *refs):
    if len(refs) > 1:
        own_ref, *refs = refs
    out_ref = refs[0]
    me = lax.axis_index(axis) // 2
    for pair in range(weight_ref.shape[0]):
        at = pair if side is None else (pair, side)
        both = jnp.concatenate([state_ref[at], partner_ref[at]], axis=1)
        result = contract(both, weight_ref[pair], ((1,), (1,))).astype(BF16)
        if len(refs) == 1:
            out_ref[pair] = result
            continue
        early_ref, term_ref, groups_ref = refs[1:]
        owners, group, _ = groups_ref.shape[1:]
        for owner in range(owners):
            groups_ref[pair, owner] = result[owner * group : (owner + 1) * group]
        for k in range(owners):
            rows = pl.ds((k - 1) % owners * group, group)
            part = groups_ref[pair, me ^ k]
            out_ref[pair, rows] = part
            if k:
                early_ref[pair, rows] = part
        term_ref[pair] = contract(out_ref[pair], by_slot(own_ref[pair]), ((1,), (1,))).astype(BF16)


def next_states(name, state, partner, weights, side=None, owners=1, own=None):
    pairs, rows, lanes = state.shape[0], *state.shape[-2:]
    group = rows // owners
    split = owners > 1 and group % 16 == 0
    shapes = [(pairs, rows, lanes)] + [(pairs, rows - group, lanes), (pairs, rows, lanes)] * split
    outs = call(
        functools.partial(level_kernel, side, "order"),
        name,
        [jax.ShapeDtypeStruct(shape, BF16) for shape in shapes],
        whole_blocks(3 + split),
        4 * pairs * rows * lanes * lanes,
        6 * pairs * rows * lanes,
        [pltpu.VMEM((pairs, owners, group, lanes), BF16)] if split else [],
    )(state, partner, weights, *([own] if split else []))
    if owners > 1 and not split:
        me = lax.axis_index("order") // 2
        parts = [lax.dynamic_slice_in_dim(outs[0], (me ^ k) * group, group, 1) for k in range(owners)]
        early = jnp.concatenate(parts[1:], axis=1)
        state = jnp.concatenate([early, parts[0]], axis=1)
        return [state, early, own_term(state, own)]
    return outs if split else outs[0]


def late_kernel(after, state_ref, out_ref):
    del after
    rows = out_ref.shape[1]
    for pair in range(state_ref.shape[0]):
        out_ref[pair] = state_ref[pair, state_ref.shape[1] - rows :]


def late_columns(after, state, rows):
    pairs, columns, lanes = state.shape
    if rows % 16:
        return state[:, columns - rows :]
    return call(
        late_kernel,
        "late_columns",
        jax.ShapeDtypeStruct((pairs, rows, lanes), BF16),
        [ANYWHERE] + whole_blocks(1),
        1,
        4 * pairs * rows * lanes,
    )(after, state)


def by_slot(packed):
    first = lax.broadcasted_iota(jnp.int32, packed.shape, 1) < packed.shape[0]
    empty = jnp.zeros(packed.shape, BF16)
    return jnp.concatenate([jnp.where(first, packed, empty), jnp.where(first, empty, packed)], axis=0)


def own_term_kernel(state_ref, own_ref, out_ref):
    for pair in range(state_ref.shape[0]):
        out_ref[pair] = contract(state_ref[pair], by_slot(own_ref[pair]), ((1,), (1,))).astype(BF16)


def own_term(state, own):
    pairs, rows, lanes = state.shape
    return call(
        own_term_kernel,
        "own_term",
        jax.ShapeDtypeStruct(state.shape, BF16),
        whole_blocks(2),
        2 * pairs * rows * lanes * lanes,
        6 * pairs * rows * lanes,
    )(state, own)


def last_level_kernel(turn, begin, axis, after, own_ref, partner_ref, cross_ref, *refs):
    del after
    refs = list(refs)
    own_factor_ref = refs.pop(0) if refs[0].shape == cross_ref.shape else None
    out_refs, groups_ref = refs[:-1], refs[-1]
    me = lax.axis_index(axis) // 2 if turn else 0
    pairs, owners, group, _ = groups_ref.shape
    for pair in range(pairs):
        cross = by_slot(cross_ref[pair])
        own = own_ref[pair, begin : begin + owners * group]
        if own_factor_ref is None:
            result = own.astype(F32) + contract(partner_ref[pair], cross, ((1,), (1,)))
        else:
            weight = jnp.concatenate([by_slot(own_factor_ref[pair]), cross], axis=1)
            both = jnp.concatenate([own, partner_ref[pair]], axis=1)
            result = contract(both, weight, ((1,), (1,)))
        result = result.astype(BF16)
        if group % 16:
            out_refs[0][pair] = result
            continue
        for owner in range(owners):
            groups_ref[pair, owner] = result[owner * group : (owner + 1) * group]
    if group % 16 == 0:
        for k, out_ref in enumerate(out_refs):
            for pair in range(pairs):
                out_ref[pl.ds(pair * group, group)] = groups_ref[pair, me ^ k]


def last_states(name, after, own, partner, factors, owners, turn, begin=0):
    pairs, columns, lanes = partner.shape
    group = columns // owners
    rows = pairs * group
    aligned = group % 16 == 0
    if not aligned:
        own = own[:, begin : begin + columns]
        begin = 0
    parts = call(
        functools.partial(last_level_kernel, turn, begin, "order"),
        name,
        [jax.ShapeDtypeStruct((rows, lanes), BF16)] * owners if aligned else [jax.ShapeDtypeStruct(own.shape, BF16)],
        [ANYWHERE] + whole_blocks(2 + len(factors)),
        4 * pairs * columns * lanes * lanes,
        6 * pairs * columns * lanes,
        [pltpu.VMEM((pairs, owners, group, lanes), BF16)],
    )(after, own, partner, *factors)
    if aligned:
        return parts
    me = lax.axis_index("order") // 2 if turn else 0
    parts = [lax.dynamic_slice_in_dim(parts[0], (me ^ k) * group, group, 1) for k in range(owners)]
    return [part.reshape(rows, lanes) for part in parts]


def place_kernel(group, order_ref, after, root_hbm, place_ref, alive_ref, later_ref, rows_ref, sems):
    del after
    owners, here, slots = place_ref.shape
    degrees = alive_ref.shape[0]
    me = lax.axis_index("order")
    later = later_ref.shape[0]
    fetches = [fetch_roots(owners - later + i, root_hbm, later_ref.at[i], sems.at[i], here) for i in range(later)]
    for fetch in fetches:
        fetch.start()
    lane = lax.broadcasted_iota(jnp.int32, (1, slots), 1)
    for k in range(owners):
        for slot in range(here):
            pair, half = slot // 2, slot % 2
            row = (pair // group * 2 + half) * group + pair % group
            rows_ref[pl.ds(row, 1), :] = (lane == order_ref[(me ^ k) * here + slot]).astype(F32)
        place_ref[k] = rows_ref[...].astype(BF16)
    degree = lax.axis_index("lat") * degrees + lax.broadcasted_iota(jnp.int32, (degrees, slots), 0)
    window = DEGREES // slots * lax.broadcasted_iota(jnp.int32, (degrees, slots), 1)
    alive_ref[...] = (degree >= window).astype(F32).astype(BF16)
    for fetch in fetches:
        fetch.wait()


def places_of(order_of_slot, root_basis, owners, later, group, after):
    slots, rank, degrees = root_basis.shape
    here = slots // owners
    return call(
        functools.partial(place_kernel, group),
        "places",
        [
            jax.ShapeDtypeStruct((owners, here, slots), BF16),
            jax.ShapeDtypeStruct((degrees, slots), BF16),
            jax.ShapeDtypeStruct((later, here // 2, rank, degrees), BF16),
        ],
        [IN_SMEM, ANYWHERE, IN_HBM],
        slots * slots,
        8 * slots * slots,
        [pltpu.VMEM((here, slots), F32), pltpu.SemaphoreType.DMA((later,))],
    )(order_of_slot, after, root_basis)


def root_kernel(group, first, last, *refs):
    refs = list(refs)
    so_far_ref = refs.pop(0) if last else None
    place_ref, alive_ref = refs.pop(0), refs.pop(0)
    count = place_ref.shape[0] - first if last else first
    first = first if last else 0
    if last:
        root_refs = [(refs[0].at[i], refs[1].at[i]) for i in range(count)]
    else:
        root_refs = [(ref,) for ref in refs[:1] + [refs[1].at[i] for i in range(count - 1)]]
    refs = refs[2:]
    state_refs, refs = refs[:count], refs[count:]
    copies = []
    if last:
        out_ref, rows_ref, natural_ref, sems = refs
    else:
        root_hbm, out_ref, later_ref, rows_ref, sems = refs
        natural_ref = out_ref
        half = later_ref.shape[1]
        for i in range(later_ref.shape[0]):
            copies.append(fetch_roots(count + i, root_hbm, later_ref.at[i], sems.at[i], 2 * half, half))
            copies[-1].start()
    fields, parts, degrees, slots = out_ref.shape
    columns = fields * parts
    rank = root_refs[0][0].shape[1]
    group_rows = group * columns
    here = place_ref.shape[1]
    steps = state_refs[0].shape[0] // group_rows
    shape = (group_rows, 2 * rank)
    row_pair = lax.broadcasted_iota(jnp.int32, shape, 0) // columns
    row_half = lax.broadcasted_iota(jnp.int32, shape, 1) // rank
    masks = [[(row_pair == pair) & (row_half == half) for pair in range(group)] for half in range(2)]
    empty = jnp.zeros(shape, BF16)
    for i, state_ref in enumerate(state_refs):
        for step in range(steps):
            state = state_ref[pl.ds(step * group_rows, group_rows)]
            left = jnp.concatenate(
                [jnp.concatenate([jnp.where(m, state, empty) for m in line], axis=1) for line in masks], axis=0
            )
            halves = len(root_refs[i])
            part, at = divmod(step, steps // halves)
            right = root_refs[i][part][pl.ds(at * group * 2, group * 2)].reshape(group * 2 * rank, degrees)
            product = contract(left, right, ((1,), (0,)))
            begin = (i * steps + step) * 2 * group_rows
            for tile in range(degrees // 128):
                rows_ref[tile, pl.ds(begin, 2 * group_rows), :] = product[:, tile * 128 : (tile + 1) * 128]
    place = place_ref[pl.ds(first, count)].reshape(count * here, slots)
    per = max(1, fields // 4)
    for column in range(columns):
        tiles = [
            rows_ref[tile, pl.ds(column, count * here, stride=columns), :].astype(BF16) for tile in range(degrees // 128)
        ]
        natural = contract(jnp.concatenate(tiles, axis=1).T, place, ((1,), (0,))).astype(BF16)
        where = (column // 2, column % 2)
        if last:
            natural = natural + so_far_ref[where]
            natural = jnp.where(alive_ref[...] != 0, natural, jnp.zeros((), BF16))
        natural_ref[where] = natural
        if last and (column + 1) % (2 * per) == 0:
            done = column // (2 * per)
            where = pl.ds(done * per, per)
            copies.append(pltpu.make_async_copy(natural_ref.at[where], out_ref.at[where], sems.at[done]))
            copies[-1].start()
    for copy in copies:
        copy.wait()


def spectra_of(states, roots, places, alive, so_far, first, group, root_basis=None):
    state_rows = states[0].shape[0]
    rank, degrees = roots[0].shape[-2:]
    owners, here, slots = places.shape
    count = len(states)
    columns = state_rows * 2 // here
    last = so_far is not None
    out = jax.ShapeDtypeStruct((columns // 2, 2, degrees, slots), BF16)
    inputs = [places, alive, *roots, *states]
    in_specs = whole_blocks(len(inputs))
    scratch = [pltpu.VMEM((degrees // 128, count * here * columns, 128), F32)]
    more = {}
    if last:
        inputs = [so_far, *inputs]
        in_specs = whole_blocks(len(inputs))
        scratch += [pltpu.VMEM(out.shape, BF16), pltpu.SemaphoreType.DMA((columns // 2,))]
        more["out_specs"] = IN_HBM
    else:
        inputs.append(root_basis)
        in_specs.append(IN_HBM)
        out = [out, jax.ShapeDtypeStruct((owners - count, here // 2, rank, degrees), BF16)]
        scratch.append(pltpu.SemaphoreType.DMA((owners - count,)))
    return call(
        functools.partial(root_kernel, group, first, last),
        "root",
        out,
        in_specs,
        2 * count * here * rank * degrees * columns,
        2 * count * here * rank * degrees,
        scratch,
        mib=24,
        **more,
    )(*inputs)


def per_device(
    fourier, quad_weights, leaf_basis, level_factors, sparsity, root_basis, order_of_slot
):
    slots, columns, lats = fourier.shape
    owners = lax.axis_size("order")
    levels = level_factors.shape[1]
    group = max(2, 16 * owners // columns)
    present = in_hbm(sparsity.transpose(1, 2, 0))
    fourier, leaf_basis, level_factors, root_basis = map(in_hbm, (fourier, leaf_basis, level_factors, root_basis))
    quad_weights = in_hbm(quad_weights.reshape(1, lats))

    def swap(array, axis, bits):
        return lax.ppermute(array, axis, [(i, i ^ bits) for i in range(lax.axis_size(axis))])

    def swap_both(array, order_bits, lat_bits):
        blocks = lax.axis_size("lat")
        pairs = [
            (o * blocks + b, (o ^ order_bits) * blocks + (b ^ lat_bits)) for o in range(owners) for b in range(blocks)
        ]
        return lax.ppermute(array, ("order", "lat"), pairs)

    early_pieces = 3 * owners // 4
    state, root_0 = leaf_states(fourier, quad_weights, leaf_basis, root_basis, owners)
    partner = swap(state, "lat", 1)
    weights = level_weights(level_factors, present, (0,), state)
    states = first_states(state, partner, weights[0])
    weights += level_weights(level_factors, present, tuple(range(1, levels)), states[1], root_basis, early_pieces - 1)
    own_factors, cross_factors, early_roots = weights[-3:]
    other_cross = swap(cross_factors, "order", 1)
    high = owners // 2
    own_columns = columns // owners
    for level in range(1, levels - 1):
        partners = [swap(state, "lat", 1 << level) for state in states]
        parts = high if level == levels - 2 else 1
        states = [
            next_states(f"level{level}_{c}", states[c], partners[c], weights[level], None, parts if c else 1, own_factors)
            for c in range(2)
        ]
    top = 1 << levels - 1
    mine, (other, early, term) = states
    mine_partner = swap(mine, "lat", top)
    early_partner = swap_both(early, 1, top)
    other_own = swap(term, "order", 1)
    places, alive, later_roots = places_of(
        order_of_slot, root_basis, owners, owners - early_pieces, group, other
    )
    late_partner = swap_both(late_columns(alive, other, own_columns), 1, top)
    even = last_states("last_own", alive, mine, mine_partner, (cross_factors, own_factors), high, True)
    begin = columns // 2 - own_columns
    odd = last_states("last_early", alive, other_own, early_partner, (other_cross,), high - 1, False)
    odd = [*last_states("last_late", alive, other_own, late_partner, (other_cross,), 1, False, begin), *odd]
    arrived = [swap((odd if k % 2 else even)[k // 2], "order", k // 2 * 2) if k > 1 else (even, odd)[k][0] for k in range(owners)]
    roots = [root_0, early_roots]
    spectra, more_roots = spectra_of(arrived[:early_pieces], roots, places, alive, None, early_pieces, group, root_basis)
    return spectra_of(arrived[early_pieces:], [later_roots, more_roots], places, alive, spectra, early_pieces, group)


def solution(mesh):
    return jax.shard_map(
        per_device,
        mesh=mesh,
        in_specs=(
            P("order", None, "lat"),
            P("lat"),
            P("order", None, "lat"),
            P("order", None, None, "lat", None, None),
            P("order", None, "lat"),
            P(None, None, "lat"),
            P(),
        ),
        out_specs=P("order", None, "lat", None),
        check_vma=False,
    )
```

```python
import functools

import jax
import jax.numpy as jnp
from jax import lax
from jax.experimental import pallas as pl
from jax.experimental.pallas import tpu as pltpu
from jax.sharding import PartitionSpec as P

DEGREES = 2048
F32, BF16 = jnp.float32, jnp.bfloat16
MIB = 1 << 20
IN_HBM = pl.BlockSpec(memory_space=pltpu.HBM)
IN_SMEM = pl.BlockSpec(memory_space=pltpu.SMEM)
ANYWHERE = pl.BlockSpec(memory_space=pl.ANY)


def contract(lhs, rhs, dims):
    return lax.dot_general(lhs, rhs, (dims, ((), ())), preferred_element_type=F32)


def in_hbm(array):
    return pltpu.with_memory_space_constraint(array, pltpu.HBM)


def call(kernel, name, out_shape, in_specs, flops, size, scratch=(), mib=16, **more):
    return pl.pallas_call(
        kernel,
        out_shape=out_shape,
        in_specs=in_specs,
        scratch_shapes=list(scratch),
        compiler_params=pltpu.CompilerParams(vmem_limit_bytes=mib * MIB),
        cost_estimate=pl.CostEstimate(flops=flops // 1000, bytes_accessed=size // 1000, transcendentals=0),
        name=name,
        **more,
    )


def whole_blocks(count):
    return [pl.BlockSpec()] * count


def fetch_roots(k, root_hbm, root_ref, sem):
    here = root_ref.shape[0]
    me = lax.axis_index("order")
    return pltpu.make_async_copy(root_hbm.at[pl.ds((me ^ k) * here, here)], root_ref, sem)


def leaf_kernel(
    pieces, group, fourier_hbm, weight_hbm, leaf_hbm, root_hbm, state_ref, root_ref, fourier_ref, weight_ref, leaf_ref, sems
):
    side = lax.axis_index("order") & 1
    slots, columns, lats = fourier_ref.shape
    rank = leaf_ref.shape[1]
    per = slots // pieces
    copies = [pltpu.make_async_copy(weight_hbm, weight_ref, sems.at[0])]
    for piece in range(pieces):
        part = pl.ds(piece * per, per)
        copies.append(pltpu.make_async_copy(fourier_hbm.at[part], fourier_ref.at[part], sems.at[1 + 2 * piece]))
        copies.append(pltpu.make_async_copy(leaf_hbm.at[part], leaf_ref.at[part], sems.at[2 + 2 * piece]))
    copies.append(fetch_roots(0, root_hbm, root_ref, sems.at[1 + 2 * pieces]))
    for copy in copies:
        copy.start()
    copies[0].wait()
    weight = weight_ref[...]
    mine = lax.broadcasted_iota(jnp.int32, (columns, 2 * rank), 1) < rank
    for pair in range(slots // 2):
        if 2 * pair % per == 0:
            copies[1 + 2 * (2 * pair // per)].wait()
            copies[2 + 2 * (2 * pair // per)].wait()
        both = pl.ds(2 * pair, 2)
        weighted = (fourier_ref[both].astype(F32) * weight[None]).astype(BF16)
        product = contract(
            weighted.reshape(2 * columns, lats), leaf_ref[both].reshape(2 * rank, lats), ((1,), (1,))
        )
        state = jnp.where(mine, product[:columns], product[columns:]).astype(BF16)
        if group % 16:
            state_ref[pair] = state
            continue
        for owner in range(columns // group):
            rows = pl.ds(owner // 2 * group, group)
            state_ref[pair, owner % 2 ^ side, rows] = state[owner * group : (owner + 1) * group]
    copies[-1].wait()


def leaf_states(fourier, quad_weights, leaf_basis, root_basis, owners):
    slots, columns, lats = fourier.shape
    rank = leaf_basis.shape[1]
    pairs, half, lanes, group = slots // 2, columns // 2, 2 * rank, columns // owners
    pieces = 2
    shape = (pairs, columns, lanes) if group % 16 else (pairs, 2, half, lanes)
    state, root = call(
        functools.partial(leaf_kernel, pieces, group),
        "leaf",
        [
            jax.ShapeDtypeStruct(shape, BF16),
            jax.ShapeDtypeStruct((root_basis.shape[0] // owners, *root_basis.shape[1:]), BF16),
        ],
        [IN_HBM] * 4,
        2 * slots * columns * rank * lats,
        4 * slots * columns * lats,
        [
            pltpu.VMEM((slots, columns, lats), BF16),
            pltpu.VMEM((1, lats), F32),
            pltpu.VMEM((slots, rank, lats), BF16),
            pltpu.SemaphoreType.DMA((2 + 2 * pieces,)),
        ],
    )(fourier, quad_weights, leaf_basis, root_basis)
    if group % 16:
        side = lax.axis_index("order") & 1
        state = state.reshape(pairs, owners // 2, 2, group, lanes)
        sides = [lax.dynamic_index_in_dim(state, side ^ i, 2, False).reshape(pairs, half, lanes) for i in range(2)]
        state = jnp.stack(sides, axis=1)
    return state, root


def factor_kernel(levels, pieces, roots, factor_hbm, present_hbm, after, *refs):
    del after
    weight_refs, (factor_ref, present_ref, sems) = list(refs[:-3]), refs[-3:]
    fetches = []
    if roots:
        root_hbm, root_ref = weight_refs.pop(0), weight_refs.pop()
        for i in range(root_ref.shape[0]):
            fetches.append(fetch_roots(1 + i, root_hbm, root_ref.at[i], sems.at[len(levels) * pieces + 1 + i]))
    present_copy = pltpu.make_async_copy(present_hbm, present_ref, sems.at[len(levels) * pieces])
    present_copy.start()
    _, slots, _, rank, _ = factor_ref.shape
    per = slots // pieces
    copies = {}
    for i, level in enumerate(levels):
        for piece in range(pieces):
            part = pl.ds(piece * per, per)
            copies[i, piece] = pltpu.make_async_copy(
                factor_hbm.at[part, level, :, 0], factor_ref.at[i, part], sems.at[i * pieces + piece]
            )
            copies[i, piece].start()
    for fetch in fetches:
        fetch.start()
    empty = jnp.zeros((rank, rank), BF16)
    present_copy.wait()
    for i, level in enumerate(levels):
        for pair in range(slots // 2):
            if 2 * pair % per == 0:
                copies[i, 2 * pair // per].wait()
            for half in range(2):
                first, second = (factor_ref[i, slot, half] for slot in (2 * pair, 2 * pair + 1))
                if half:
                    first = jnp.where(present_ref[level, 0, 2 * pair] != 0, first, empty)
                    second = jnp.where(present_ref[level, 0, 2 * pair + 1] != 0, second, empty)
                if weight_refs[i].shape[1] == rank:
                    weight_refs[i + half][pair] = jnp.concatenate([first, second], axis=1)
                    continue
                lanes = pl.ds(half * 2 * rank, 2 * rank)
                weight_refs[i][pair, :rank, lanes] = jnp.concatenate([first, empty], axis=1)
                weight_refs[i][pair, rank:, lanes] = jnp.concatenate([empty, second], axis=1)
    for fetch in fetches:
        fetch.wait()


def level_weights(level_factors, present, levels, after, root_basis=None, root_pieces=0):
    slots, last, _, _, rank, _ = level_factors.shape
    count, pieces = len(levels), 2
    roots = []
    if root_pieces:
        here = root_basis.shape[0] // lax.axis_size("order")
        roots = [jax.ShapeDtypeStruct((root_pieces, here, *root_basis.shape[1:]), BF16)]
    return call(
        functools.partial(factor_kernel, levels, pieces, root_pieces),
        "factors",
        [
            jax.ShapeDtypeStruct((slots // 2, *((rank, 2 * rank) if level == last - 1 else (2 * rank, 4 * rank))), BF16)
            for level in levels
            for _ in range(1 + (level == last - 1))
        ]
        + roots,
        [IN_HBM, IN_HBM, ANYWHERE] + [IN_HBM] * len(roots),
        slots * rank * rank * 4 * count,
        slots * rank * rank * 16 * count,
        [
            pltpu.VMEM((count, slots, 2, rank, rank), BF16),
            pltpu.SMEM(present.shape, jnp.int32),
            pltpu.SemaphoreType.DMA((count * pieces + 1 + root_pieces,)),
        ],
        mib=24,
    )(level_factors, present, after, *([root_basis] if roots else []))


def first_level_kernel(state_ref, partner_ref, weight_ref, *out_refs):
    pairs, sides, rows, lanes = state_ref.shape
    for pair in range(pairs):
        both = [ref[pair].reshape(sides * rows, lanes) for ref in (state_ref, partner_ref)]
        result = contract(jnp.concatenate(both, axis=1), weight_ref[pair], ((1,), (1,))).astype(BF16)
        for side, out_ref in enumerate(out_refs):
            out_ref[pair] = result[side * rows : (side + 1) * rows]


def first_states(state, partner, weights):
    pairs, sides, rows, lanes = state.shape
    return call(
        first_level_kernel,
        "level0",
        [jax.ShapeDtypeStruct((pairs, rows, lanes), BF16)] * sides,
        whole_blocks(3),
        4 * pairs * sides * rows * lanes * lanes,
        6 * pairs * sides * rows * lanes,
    )(state, partner, weights)


def level_kernel(side, axis, state_ref, partner_ref, weight_ref, *refs):
    if len(refs) > 1:
        own_ref, *refs = refs
    out_ref = refs[0]
    me = lax.axis_index(axis) // 2
    for pair in range(weight_ref.shape[0]):
        at = pair if side is None else (pair, side)
        both = jnp.concatenate([state_ref[at], partner_ref[at]], axis=1)
        result = contract(both, weight_ref[pair], ((1,), (1,))).astype(BF16)
        if len(refs) == 1:
            out_ref[pair] = result
            continue
        early_ref, term_ref, groups_ref = refs[1:]
        owners, group, _ = groups_ref.shape[1:]
        for owner in range(owners):
            groups_ref[pair, owner] = result[owner * group : (owner + 1) * group]
        for k in range(owners):
            rows = pl.ds((k - 1) % owners * group, group)
            part = groups_ref[pair, me ^ k]
            out_ref[pair, rows] = part
            if k:
                early_ref[pair, rows] = part
        term_ref[pair] = contract(out_ref[pair], by_slot(own_ref[pair]), ((1,), (1,))).astype(BF16)


def next_states(name, state, partner, weights, side=None, owners=1, own=None):
    pairs, rows, lanes = state.shape[0], *state.shape[-2:]
    group = rows // owners
    split = owners > 1 and group % 16 == 0
    shapes = [(pairs, rows, lanes)] + [(pairs, rows - group, lanes), (pairs, rows, lanes)] * split
    outs = call(
        functools.partial(level_kernel, side, "order"),
        name,
        [jax.ShapeDtypeStruct(shape, BF16) for shape in shapes],
        whole_blocks(3 + split),
        4 * pairs * rows * lanes * lanes,
        6 * pairs * rows * lanes,
        [pltpu.VMEM((pairs, owners, group, lanes), BF16)] if split else [],
    )(state, partner, weights, *([own] if split else []))
    if owners > 1 and not split:
        me = lax.axis_index("order") // 2
        parts = [lax.dynamic_slice_in_dim(outs[0], (me ^ k) * group, group, 1) for k in range(owners)]
        early = jnp.concatenate(parts[1:], axis=1)
        state = jnp.concatenate([early, parts[0]], axis=1)
        return [state, early, own_term(state, own)]
    return outs if split else outs[0]


def late_kernel(after, state_ref, out_ref):
    del after
    rows = out_ref.shape[1]
    for pair in range(state_ref.shape[0]):
        out_ref[pair] = state_ref[pair, state_ref.shape[1] - rows :]


def late_columns(after, state, rows):
    pairs, columns, lanes = state.shape
    if rows % 16:
        return state[:, columns - rows :]
    return call(
        late_kernel,
        "late_columns",
        jax.ShapeDtypeStruct((pairs, rows, lanes), BF16),
        [ANYWHERE] + whole_blocks(1),
        1,
        4 * pairs * rows * lanes,
    )(after, state)


def by_slot(packed):
    first = lax.broadcasted_iota(jnp.int32, packed.shape, 1) < packed.shape[0]
    empty = jnp.zeros(packed.shape, BF16)
    return jnp.concatenate([jnp.where(first, packed, empty), jnp.where(first, empty, packed)], axis=0)


def own_term_kernel(state_ref, own_ref, out_ref):
    for pair in range(state_ref.shape[0]):
        out_ref[pair] = contract(state_ref[pair], by_slot(own_ref[pair]), ((1,), (1,))).astype(BF16)


def own_term(state, own):
    pairs, rows, lanes = state.shape
    return call(
        own_term_kernel,
        "own_term",
        jax.ShapeDtypeStruct(state.shape, BF16),
        whole_blocks(2),
        2 * pairs * rows * lanes * lanes,
        6 * pairs * rows * lanes,
    )(state, own)


def last_level_kernel(turn, begin, axis, after, own_ref, partner_ref, cross_ref, *refs):
    del after
    refs = list(refs)
    own_factor_ref = refs.pop(0) if refs[0].shape == cross_ref.shape else None
    out_refs, groups_ref = refs[:-1], refs[-1]
    me = lax.axis_index(axis) // 2 if turn else 0
    pairs, owners, group, _ = groups_ref.shape
    for pair in range(pairs):
        cross = by_slot(cross_ref[pair])
        own = own_ref[pair, begin : begin + owners * group]
        if own_factor_ref is None:
            result = own.astype(F32) + contract(partner_ref[pair], cross, ((1,), (1,)))
        else:
            weight = jnp.concatenate([by_slot(own_factor_ref[pair]), cross], axis=1)
            both = jnp.concatenate([own, partner_ref[pair]], axis=1)
            result = contract(both, weight, ((1,), (1,)))
        result = result.astype(BF16)
        if group % 16:
            out_refs[0][pair] = result
            continue
        for owner in range(owners):
            groups_ref[pair, owner] = result[owner * group : (owner + 1) * group]
    if group % 16 == 0:
        for k, out_ref in enumerate(out_refs):
            for pair in range(pairs):
                out_ref[pl.ds(pair * group, group)] = groups_ref[pair, me ^ k]


def last_states(name, after, own, partner, factors, owners, turn, begin=0):
    pairs, columns, lanes = partner.shape
    group = columns // owners
    rows = pairs * group
    aligned = group % 16 == 0
    if not aligned:
        own = own[:, begin : begin + columns]
        begin = 0
    parts = call(
        functools.partial(last_level_kernel, turn, begin, "order"),
        name,
        [jax.ShapeDtypeStruct((rows, lanes), BF16)] * owners if aligned else [jax.ShapeDtypeStruct(own.shape, BF16)],
        [ANYWHERE] + whole_blocks(2 + len(factors)),
        4 * pairs * columns * lanes * lanes,
        6 * pairs * columns * lanes,
        [pltpu.VMEM((pairs, owners, group, lanes), BF16)],
    )(after, own, partner, *factors)
    if aligned:
        return parts
    me = lax.axis_index("order") // 2 if turn else 0
    parts = [lax.dynamic_slice_in_dim(parts[0], (me ^ k) * group, group, 1) for k in range(owners)]
    return [part.reshape(rows, lanes) for part in parts]


def place_kernel(group, order_ref, after, root_hbm, place_ref, alive_ref, later_ref, rows_ref, sems):
    del after
    owners, here, slots = place_ref.shape
    degrees = alive_ref.shape[0]
    me = lax.axis_index("order")
    later = later_ref.shape[0]
    fetches = [fetch_roots(owners - later + i, root_hbm, later_ref.at[i], sems.at[i]) for i in range(later)]
    for fetch in fetches:
        fetch.start()
    lane = lax.broadcasted_iota(jnp.int32, (1, slots), 1)
    for k in range(owners):
        for slot in range(here):
            pair, half = slot // 2, slot % 2
            row = (pair // group * 2 + half) * group + pair % group
            rows_ref[pl.ds(row, 1), :] = (lane == order_ref[(me ^ k) * here + slot]).astype(F32)
        place_ref[k] = rows_ref[...].astype(BF16)
    degree = lax.axis_index("lat") * degrees + lax.broadcasted_iota(jnp.int32, (degrees, slots), 0)
    window = DEGREES // slots * lax.broadcasted_iota(jnp.int32, (degrees, slots), 1)
    alive_ref[...] = (degree >= window).astype(F32).astype(BF16)
    for fetch in fetches:
        fetch.wait()


def places_of(order_of_slot, root_basis, owners, later, group, after):
    slots, rank, degrees = root_basis.shape
    here = slots // owners
    return call(
        functools.partial(place_kernel, group),
        "places",
        [
            jax.ShapeDtypeStruct((owners, here, slots), BF16),
            jax.ShapeDtypeStruct((degrees, slots), BF16),
            jax.ShapeDtypeStruct((later, here, rank, degrees), BF16),
        ],
        [IN_SMEM, ANYWHERE, IN_HBM],
        slots * slots,
        8 * slots * slots,
        [pltpu.VMEM((here, slots), F32), pltpu.SemaphoreType.DMA((later,))],
    )(order_of_slot, after, root_basis)


def root_kernel(group, first, last, *refs):
    refs = list(refs)
    so_far_ref = refs.pop(0) if last else None
    place_ref, alive_ref = refs.pop(0), refs.pop(0)
    count = place_ref.shape[0] - first if last else first
    first = first if last else 0
    if last:
        root_refs = [refs[0].at[i] for i in range(count)]
    else:
        root_refs = refs[:1] + [refs[1].at[i] for i in range(count - 1)]
    refs = refs[1:] if last else refs[2:]
    state_refs, refs = refs[:count], refs[count:]
    copies = []
    if last:
        out_ref, rows_ref, natural_ref, sems = refs
    else:
        out_ref, rows_ref = refs
        natural_ref = out_ref
    fields, parts, degrees, slots = out_ref.shape
    columns = fields * parts
    rank = root_refs[0].shape[1]
    group_rows = group * columns
    here = place_ref.shape[1]
    steps = state_refs[0].shape[0] // group_rows
    shape = (group_rows, 2 * rank)
    row_pair = lax.broadcasted_iota(jnp.int32, shape, 0) // columns
    row_half = lax.broadcasted_iota(jnp.int32, shape, 1) // rank
    masks = [[(row_pair == pair) & (row_half == half) for pair in range(group)] for half in range(2)]
    empty = jnp.zeros(shape, BF16)
    for i, state_ref in enumerate(state_refs):
        for step in range(steps):
            state = state_ref[pl.ds(step * group_rows, group_rows)]
            left = jnp.concatenate(
                [jnp.concatenate([jnp.where(m, state, empty) for m in line], axis=1) for line in masks], axis=0
            )
            right = root_refs[i][pl.ds(step * group * 2, group * 2)].reshape(group * 2 * rank, degrees)
            product = contract(left, right, ((1,), (0,)))
            begin = (i * steps + step) * 2 * group_rows
            for tile in range(degrees // 128):
                rows_ref[tile, pl.ds(begin, 2 * group_rows), :] = product[:, tile * 128 : (tile + 1) * 128]
    place = place_ref[pl.ds(first, count)].reshape(count * here, slots)
    for column in range(columns):
        tiles = [
            rows_ref[tile, pl.ds(column, count * here, stride=columns), :].astype(BF16) for tile in range(degrees // 128)
        ]
        natural = contract(jnp.concatenate(tiles, axis=1).T, place, ((1,), (0,))).astype(BF16)
        where = (column // 2, column % 2)
        if last:
            natural = natural + so_far_ref[where]
            natural = jnp.where(alive_ref[...] != 0, natural, jnp.zeros((), BF16))
        natural_ref[where] = natural
        if last:
            copies.append(pltpu.make_async_copy(natural_ref.at[where], out_ref.at[where], sems.at[column]))
            copies[-1].start()
    for copy in copies:
        copy.wait()


def spectra_of(states, roots, places, alive, so_far, first, group):
    state_rows = states[0].shape[0]
    rank, degrees = roots[0].shape[-2:]
    owners, here, slots = places.shape
    count = len(states)
    columns = state_rows * 2 // here
    last = so_far is not None
    out = jax.ShapeDtypeStruct((columns // 2, 2, degrees, slots), BF16)
    inputs = [places, alive, *roots, *states]
    in_specs = whole_blocks(len(inputs))
    scratch = [pltpu.VMEM((degrees // 128, count * here * columns, 128), F32)]
    more = {}
    if last:
        inputs = [so_far, *inputs]
        in_specs = whole_blocks(len(inputs))
        scratch += [pltpu.VMEM(out.shape, BF16), pltpu.SemaphoreType.DMA((columns,))]
        more["out_specs"] = IN_HBM
    return call(
        functools.partial(root_kernel, group, first, last),
        "root",
        out,
        in_specs,
        2 * count * here * rank * degrees * columns,
        2 * count * here * rank * degrees,
        scratch,
        mib=24,
        **more,
    )(*inputs)


def per_device(
    fourier, quad_weights, leaf_basis, level_factors, sparsity, root_basis, order_of_slot
):
    slots, columns, lats = fourier.shape
    owners = lax.axis_size("order")
    levels = level_factors.shape[1]
    group = max(2, 16 * owners // columns)
    present = in_hbm(sparsity.transpose(1, 2, 0))
    fourier, leaf_basis, level_factors, root_basis = map(in_hbm, (fourier, leaf_basis, level_factors, root_basis))
    quad_weights = in_hbm(quad_weights.reshape(1, lats))

    def swap(array, axis, bits):
        return lax.ppermute(array, axis, [(i, i ^ bits) for i in range(lax.axis_size(axis))])

    def swap_both(array, order_bits, lat_bits):
        blocks = lax.axis_size("lat")
        pairs = [
            (o * blocks + b, (o ^ order_bits) * blocks + (b ^ lat_bits)) for o in range(owners) for b in range(blocks)
        ]
        return lax.ppermute(array, ("order", "lat"), pairs)

    early_pieces = 3 * owners // 4
    state, root_0 = leaf_states(fourier, quad_weights, leaf_basis, root_basis, owners)
    partner = swap(state, "lat", 1)
    weights = level_weights(level_factors, present, (0,), state)
    states = first_states(state, partner, weights[0])
    weights += level_weights(level_factors, present, tuple(range(1, levels)), states[1], root_basis, early_pieces - 1)
    own_factors, cross_factors, early_roots = weights[-3:]
    other_cross = swap(cross_factors, "order", 1)
    high = owners // 2
    own_columns = columns // owners
    for level in range(1, levels - 1):
        partners = [swap(state, "lat", 1 << level) for state in states]
        parts = high if level == levels - 2 else 1
        states = [
            next_states(f"level{level}_{c}", states[c], partners[c], weights[level], None, parts if c else 1, own_factors)
            for c in range(2)
        ]
    top = 1 << levels - 1
    mine, (other, early, term) = states
    mine_partner = swap(mine, "lat", top)
    early_partner = swap_both(early, 1, top)
    other_own = swap(term, "order", 1)
    places, alive, later_roots = places_of(
        order_of_slot, root_basis, owners, owners - early_pieces, group, other
    )
    late_partner = swap_both(late_columns(alive, other, own_columns), 1, top)
    even = last_states("last_own", alive, mine, mine_partner, (cross_factors, own_factors), high, True)
    begin = columns // 2 - own_columns
    odd = last_states("last_early", alive, other_own, early_partner, (other_cross,), high - 1, False)
    odd = [*last_states("last_late", alive, other_own, late_partner, (other_cross,), 1, False, begin), *odd]
    arrived = [swap((odd if k % 2 else even)[k // 2], "order", k // 2 * 2) if k > 1 else (even, odd)[k][0] for k in range(owners)]
    roots = [root_0, early_roots]
    spectra = spectra_of(arrived[:early_pieces], roots, places, alive, None, early_pieces, group)
    return spectra_of(arrived[early_pieces:], [later_roots], places, alive, spectra, early_pieces, group)


def solution(mesh):
    return jax.shard_map(
        per_device,
        mesh=mesh,
        in_specs=(
            P("order", None, "lat"),
            P("lat"),
            P("order", None, "lat"),
            P("order", None, None, "lat", None, None),
            P("order", None, "lat"),
            P(None, None, "lat"),
            P(),
        ),
        out_specs=P("order", None, "lat", None),
        check_vma=False,
    )
```

```python
import functools

import jax
import jax.numpy as jnp
from jax import lax
from jax.experimental import pallas as pl
from jax.experimental.pallas import tpu as pltpu
from jax.sharding import PartitionSpec as P

DEGREES = 2048
F32, BF16 = jnp.float32, jnp.bfloat16
MIB = 1 << 20
IN_HBM = pl.BlockSpec(memory_space=pltpu.HBM)
IN_SMEM = pl.BlockSpec(memory_space=pltpu.SMEM)
ANYWHERE = pl.BlockSpec(memory_space=pl.ANY)


def contract(lhs, rhs, dims):
    return lax.dot_general(lhs, rhs, (dims, ((), ())), preferred_element_type=F32)


def in_hbm(array):
    return pltpu.with_memory_space_constraint(array, pltpu.HBM)


def call(kernel, name, out_shape, in_specs, flops, size, scratch=(), mib=16, **more):
    return pl.pallas_call(
        kernel,
        out_shape=out_shape,
        in_specs=in_specs,
        scratch_shapes=list(scratch),
        compiler_params=pltpu.CompilerParams(vmem_limit_bytes=mib * MIB),
        cost_estimate=pl.CostEstimate(flops=flops // 1000, bytes_accessed=size // 1000, transcendentals=0),
        name=name,
        **more,
    )


def whole_blocks(count):
    return [pl.BlockSpec()] * count


def fetch_roots(k, root_hbm, root_ref, sem):
    here = root_ref.shape[0]
    me = lax.axis_index("order")
    return pltpu.make_async_copy(root_hbm.at[pl.ds((me ^ k) * here, here)], root_ref, sem)


def leaf_kernel(
    pieces, group, fourier_hbm, weight_hbm, leaf_hbm, root_hbm, state_ref, root_ref, fourier_ref, weight_ref, leaf_ref, sems
):
    side = lax.axis_index("order") & 1
    slots, columns, lats = fourier_ref.shape
    rank = leaf_ref.shape[1]
    per = slots // pieces
    copies = [pltpu.make_async_copy(weight_hbm, weight_ref, sems.at[0])]
    for piece in range(pieces):
        part = pl.ds(piece * per, per)
        copies.append(pltpu.make_async_copy(fourier_hbm.at[part], fourier_ref.at[part], sems.at[1 + 2 * piece]))
        copies.append(pltpu.make_async_copy(leaf_hbm.at[part], leaf_ref.at[part], sems.at[2 + 2 * piece]))
    copies.append(fetch_roots(0, root_hbm, root_ref, sems.at[1 + 2 * pieces]))
    for copy in copies:
        copy.start()
    copies[0].wait()
    weight = weight_ref[...]
    mine = lax.broadcasted_iota(jnp.int32, (columns, 2 * rank), 1) < rank
    for pair in range(slots // 2):
        if 2 * pair % per == 0:
            copies[1 + 2 * (2 * pair // per)].wait()
            copies[2 + 2 * (2 * pair // per)].wait()
        both = pl.ds(2 * pair, 2)
        weighted = (fourier_ref[both].astype(F32) * weight[None]).astype(BF16)
        product = contract(
            weighted.reshape(2 * columns, lats), leaf_ref[both].reshape(2 * rank, lats), ((1,), (1,))
        )
        state = jnp.where(mine, product[:columns], product[columns:]).astype(BF16)
        if group % 16:
            state_ref[pair] = state
            continue
        for owner in range(columns // group):
            rows = pl.ds(owner // 2 * group, group)
            state_ref[pair, owner % 2 ^ side, rows] = state[owner * group : (owner + 1) * group]
    copies[-1].wait()


def leaf_states(fourier, quad_weights, leaf_basis, root_basis, owners):
    slots, columns, lats = fourier.shape
    rank = leaf_basis.shape[1]
    pairs, half, lanes, group = slots // 2, columns // 2, 2 * rank, columns // owners
    pieces = 2
    shape = (pairs, columns, lanes) if group % 16 else (pairs, 2, half, lanes)
    state, root = call(
        functools.partial(leaf_kernel, pieces, group),
        "leaf",
        [
            jax.ShapeDtypeStruct(shape, BF16),
            jax.ShapeDtypeStruct((root_basis.shape[0] // owners, *root_basis.shape[1:]), BF16),
        ],
        [IN_HBM] * 4,
        2 * slots * columns * rank * lats,
        4 * slots * columns * lats,
        [
            pltpu.VMEM((slots, columns, lats), BF16),
            pltpu.VMEM((1, lats), F32),
            pltpu.VMEM((slots, rank, lats), BF16),
            pltpu.SemaphoreType.DMA((2 + 2 * pieces,)),
        ],
    )(fourier, quad_weights, leaf_basis, root_basis)
    if group % 16:
        side = lax.axis_index("order") & 1
        state = state.reshape(pairs, owners // 2, 2, group, lanes)
        sides = [lax.dynamic_index_in_dim(state, side ^ i, 2, False).reshape(pairs, half, lanes) for i in range(2)]
        state = jnp.stack(sides, axis=1)
    return state, root


def factor_kernel(levels, pieces, roots, factor_hbm, present_hbm, after, *refs):
    del after
    weight_refs, (factor_ref, present_ref, sems) = list(refs[:-3]), refs[-3:]
    fetches = []
    if roots:
        root_hbm, root_ref = weight_refs.pop(0), weight_refs.pop()
        for i in range(root_ref.shape[0]):
            fetches.append(fetch_roots(1 + i, root_hbm, root_ref.at[i], sems.at[len(levels) * pieces + 1 + i]))
    present_copy = pltpu.make_async_copy(present_hbm, present_ref, sems.at[len(levels) * pieces])
    present_copy.start()
    _, slots, _, rank, _ = factor_ref.shape
    per = slots // pieces
    copies = {}
    for i, level in enumerate(levels):
        for piece in range(pieces):
            part = pl.ds(piece * per, per)
            copies[i, piece] = pltpu.make_async_copy(
                factor_hbm.at[part, level, :, 0], factor_ref.at[i, part], sems.at[i * pieces + piece]
            )
            copies[i, piece].start()
    for fetch in fetches:
        fetch.start()
    empty = jnp.zeros((rank, rank), BF16)
    present_copy.wait()
    for i, level in enumerate(levels):
        for pair in range(slots // 2):
            if 2 * pair % per == 0:
                copies[i, 2 * pair // per].wait()
            for half in range(2):
                first, second = (factor_ref[i, slot, half] for slot in (2 * pair, 2 * pair + 1))
                if half:
                    first = jnp.where(present_ref[level, 0, 2 * pair] != 0, first, empty)
                    second = jnp.where(present_ref[level, 0, 2 * pair + 1] != 0, second, empty)
                if weight_refs[i].shape[1] == rank:
                    weight_refs[i + half][pair] = jnp.concatenate([first, second], axis=1)
                    continue
                lanes = pl.ds(half * 2 * rank, 2 * rank)
                weight_refs[i][pair, :rank, lanes] = jnp.concatenate([first, empty], axis=1)
                weight_refs[i][pair, rank:, lanes] = jnp.concatenate([empty, second], axis=1)
    for fetch in fetches:
        fetch.wait()


def level_weights(level_factors, present, levels, after, root_basis=None, root_pieces=0):
    slots, last, _, _, rank, _ = level_factors.shape
    count = len(levels)
    pieces = 2 if count == 1 else 1
    roots = []
    if root_pieces:
        here = root_basis.shape[0] // lax.axis_size("order")
        roots = [jax.ShapeDtypeStruct((root_pieces, here, *root_basis.shape[1:]), BF16)]
    return call(
        functools.partial(factor_kernel, levels, pieces, root_pieces),
        "factors",
        [
            jax.ShapeDtypeStruct((slots // 2, *((rank, 2 * rank) if level == last - 1 else (2 * rank, 4 * rank))), BF16)
            for level in levels
            for _ in range(1 + (level == last - 1))
        ]
        + roots,
        [IN_HBM, IN_HBM, ANYWHERE] + [IN_HBM] * len(roots),
        slots * rank * rank * 4 * count,
        slots * rank * rank * 16 * count,
        [
            pltpu.VMEM((count, slots, 2, rank, rank), BF16),
            pltpu.SMEM(present.shape, jnp.int32),
            pltpu.SemaphoreType.DMA((count * pieces + 1 + root_pieces,)),
        ],
        mib=24,
    )(level_factors, present, after, *([root_basis] if roots else []))


def level_kernel(side, axis, state_ref, partner_ref, weight_ref, *refs):
    if len(refs) > 1:
        own_ref, *refs = refs
    out_ref = refs[0]
    me = lax.axis_index(axis) // 2
    for pair in range(weight_ref.shape[0]):
        at = pair if side is None else (pair, side)
        both = jnp.concatenate([state_ref[at], partner_ref[at]], axis=1)
        result = contract(both, weight_ref[pair], ((1,), (1,))).astype(BF16)
        if len(refs) == 1:
            out_ref[pair] = result
            continue
        early_ref, term_ref, groups_ref = refs[1:]
        owners, group, _ = groups_ref.shape[1:]
        for owner in range(owners):
            groups_ref[pair, owner] = result[owner * group : (owner + 1) * group]
        for k in range(owners):
            rows = pl.ds((k - 1) % owners * group, group)
            part = groups_ref[pair, me ^ k]
            out_ref[pair, rows] = part
            if k:
                early_ref[pair, rows] = part
        term_ref[pair] = contract(out_ref[pair], by_slot(own_ref[pair]), ((1,), (1,))).astype(BF16)


def next_states(name, state, partner, weights, side=None, owners=1, own=None):
    pairs, rows, lanes = state.shape[0], *state.shape[-2:]
    group = rows // owners
    split = owners > 1 and group % 16 == 0
    shapes = [(pairs, rows, lanes)] + [(pairs, rows - group, lanes), (pairs, rows, lanes)] * split
    outs = call(
        functools.partial(level_kernel, side, "order"),
        name,
        [jax.ShapeDtypeStruct(shape, BF16) for shape in shapes],
        whole_blocks(3 + split),
        4 * pairs * rows * lanes * lanes,
        6 * pairs * rows * lanes,
        [pltpu.VMEM((pairs, owners, group, lanes), BF16)] if split else [],
    )(state, partner, weights, *([own] if split else []))
    if owners > 1 and not split:
        me = lax.axis_index("order") // 2
        parts = [lax.dynamic_slice_in_dim(outs[0], (me ^ k) * group, group, 1) for k in range(owners)]
        early = jnp.concatenate(parts[1:], axis=1)
        state = jnp.concatenate([early, parts[0]], axis=1)
        return [state, early, own_term(state, own)]
    return outs if split else outs[0]


def late_kernel(after, state_ref, out_ref):
    del after
    rows = out_ref.shape[1]
    for pair in range(state_ref.shape[0]):
        out_ref[pair] = state_ref[pair, state_ref.shape[1] - rows :]


def late_columns(after, state, rows):
    pairs, columns, lanes = state.shape
    if rows % 16:
        return state[:, columns - rows :]
    return call(
        late_kernel,
        "late_columns",
        jax.ShapeDtypeStruct((pairs, rows, lanes), BF16),
        [ANYWHERE] + whole_blocks(1),
        1,
        4 * pairs * rows * lanes,
    )(after, state)


def by_slot(packed):
    first = lax.broadcasted_iota(jnp.int32, packed.shape, 1) < packed.shape[0]
    empty = jnp.zeros(packed.shape, BF16)
    return jnp.concatenate([jnp.where(first, packed, empty), jnp.where(first, empty, packed)], axis=0)


def own_term_kernel(state_ref, own_ref, out_ref):
    for pair in range(state_ref.shape[0]):
        out_ref[pair] = contract(state_ref[pair], by_slot(own_ref[pair]), ((1,), (1,))).astype(BF16)


def own_term(state, own):
    pairs, rows, lanes = state.shape
    return call(
        own_term_kernel,
        "own_term",
        jax.ShapeDtypeStruct(state.shape, BF16),
        whole_blocks(2),
        2 * pairs * rows * lanes * lanes,
        6 * pairs * rows * lanes,
    )(state, own)


def last_level_kernel(turn, begin, axis, after, own_ref, partner_ref, cross_ref, *refs):
    del after
    refs = list(refs)
    own_factor_ref = refs.pop(0) if refs[0].shape == cross_ref.shape else None
    out_refs, groups_ref = refs[:-1], refs[-1]
    me = lax.axis_index(axis) // 2 if turn else 0
    pairs, owners, group, _ = groups_ref.shape
    for pair in range(pairs):
        cross = by_slot(cross_ref[pair])
        own = own_ref[pair, begin : begin + owners * group]
        if own_factor_ref is None:
            result = own.astype(F32) + contract(partner_ref[pair], cross, ((1,), (1,)))
        else:
            weight = jnp.concatenate([by_slot(own_factor_ref[pair]), cross], axis=1)
            both = jnp.concatenate([own, partner_ref[pair]], axis=1)
            result = contract(both, weight, ((1,), (1,)))
        result = result.astype(BF16)
        if group % 16:
            out_refs[0][pair] = result
            continue
        for owner in range(owners):
            groups_ref[pair, owner] = result[owner * group : (owner + 1) * group]
    if group % 16 == 0:
        for k, out_ref in enumerate(out_refs):
            for pair in range(pairs):
                out_ref[pl.ds(pair * group, group)] = groups_ref[pair, me ^ k]


def last_states(name, after, own, partner, factors, owners, turn, begin=0):
    pairs, columns, lanes = partner.shape
    group = columns // owners
    rows = pairs * group
    aligned = group % 16 == 0
    if not aligned:
        own = own[:, begin : begin + columns]
        begin = 0
    parts = call(
        functools.partial(last_level_kernel, turn, begin, "order"),
        name,
        [jax.ShapeDtypeStruct((rows, lanes), BF16)] * owners if aligned else [jax.ShapeDtypeStruct(own.shape, BF16)],
        [ANYWHERE] + whole_blocks(2 + len(factors)),
        4 * pairs * columns * lanes * lanes,
        6 * pairs * columns * lanes,
        [pltpu.VMEM((pairs, owners, group, lanes), BF16)],
    )(after, own, partner, *factors)
    if aligned:
        return parts
    me = lax.axis_index("order") // 2 if turn else 0
    parts = [lax.dynamic_slice_in_dim(parts[0], (me ^ k) * group, group, 1) for k in range(owners)]
    return [part.reshape(rows, lanes) for part in parts]


def place_kernel(group, order_ref, after, root_hbm, place_ref, alive_ref, later_ref, rows_ref, sems):
    del after
    owners, here, slots = place_ref.shape
    degrees = alive_ref.shape[0]
    me = lax.axis_index("order")
    later = later_ref.shape[0]
    fetches = [fetch_roots(owners - later + i, root_hbm, later_ref.at[i], sems.at[i]) for i in range(later)]
    for fetch in fetches:
        fetch.start()
    lane = lax.broadcasted_iota(jnp.int32, (1, slots), 1)
    for k in range(owners):
        for slot in range(here):
            pair, half = slot // 2, slot % 2
            row = (pair // group * 2 + half) * group + pair % group
            rows_ref[pl.ds(row, 1), :] = (lane == order_ref[(me ^ k) * here + slot]).astype(F32)
        place_ref[k] = rows_ref[...].astype(BF16)
    degree = lax.axis_index("lat") * degrees + lax.broadcasted_iota(jnp.int32, (degrees, slots), 0)
    window = DEGREES // slots * lax.broadcasted_iota(jnp.int32, (degrees, slots), 1)
    alive_ref[...] = (degree >= window).astype(F32).astype(BF16)
    for fetch in fetches:
        fetch.wait()


def places_of(order_of_slot, root_basis, owners, later, group, after):
    slots, rank, degrees = root_basis.shape
    here = slots // owners
    return call(
        functools.partial(place_kernel, group),
        "places",
        [
            jax.ShapeDtypeStruct((owners, here, slots), BF16),
            jax.ShapeDtypeStruct((degrees, slots), BF16),
            jax.ShapeDtypeStruct((later, here, rank, degrees), BF16),
        ],
        [IN_SMEM, ANYWHERE, IN_HBM],
        slots * slots,
        8 * slots * slots,
        [pltpu.VMEM((here, slots), F32), pltpu.SemaphoreType.DMA((later,))],
    )(order_of_slot, after, root_basis)


def root_kernel(group, first, last, *refs):
    refs = list(refs)
    so_far_ref = refs.pop(0) if last else None
    place_ref, alive_ref = refs.pop(0), refs.pop(0)
    count = place_ref.shape[0] - first if last else first
    first = first if last else 0
    if last:
        root_refs = [refs[0].at[i] for i in range(count)]
    else:
        root_refs = refs[:1] + [refs[1].at[i] for i in range(count - 1)]
    refs = refs[1:] if last else refs[2:]
    state_refs, refs = refs[:count], refs[count:]
    copies = []
    if last:
        out_ref, rows_ref, natural_ref, sems = refs
    else:
        out_ref, rows_ref = refs
        natural_ref = out_ref
    fields, parts, degrees, slots = out_ref.shape
    columns = fields * parts
    rank = root_refs[0].shape[1]
    group_rows = group * columns
    here = place_ref.shape[1]
    steps = state_refs[0].shape[0] // group_rows
    shape = (group_rows, 2 * rank)
    row_pair = lax.broadcasted_iota(jnp.int32, shape, 0) // columns
    row_half = lax.broadcasted_iota(jnp.int32, shape, 1) // rank
    masks = [[(row_pair == pair) & (row_half == half) for pair in range(group)] for half in range(2)]
    empty = jnp.zeros(shape, BF16)
    for i, state_ref in enumerate(state_refs):
        for step in range(steps):
            state = state_ref[pl.ds(step * group_rows, group_rows)]
            left = jnp.concatenate(
                [jnp.concatenate([jnp.where(m, state, empty) for m in line], axis=1) for line in masks], axis=0
            )
            right = root_refs[i][pl.ds(step * group * 2, group * 2)].reshape(group * 2 * rank, degrees)
            product = contract(left, right, ((1,), (0,)))
            begin = (i * steps + step) * 2 * group_rows
            for tile in range(degrees // 128):
                rows_ref[tile, pl.ds(begin, 2 * group_rows), :] = product[:, tile * 128 : (tile + 1) * 128]
    place = place_ref[pl.ds(first, count)].reshape(count * here, slots)
    per = max(1, fields // 4)
    for column in range(columns):
        for tile in range(degrees // 128):
            span = slice(tile * 128, (tile + 1) * 128)
            one = rows_ref[tile, pl.ds(column, count * here, stride=columns), :].astype(BF16)
            natural = contract(one.T, place, ((1,), (0,))).astype(BF16)
            where = (column // 2, column % 2, span)
            if last:
                natural = natural + so_far_ref[where]
                natural = jnp.where(alive_ref[span] != 0, natural, jnp.zeros((), BF16))
            natural_ref[where] = natural
        if last and (column + 1) % (2 * per) == 0:
            done = column // (2 * per)
            where = pl.ds(done * per, per)
            copies.append(pltpu.make_async_copy(natural_ref.at[where], out_ref.at[where], sems.at[done]))
            copies[-1].start()
    for copy in copies:
        copy.wait()


def spectra_of(states, roots, places, alive, so_far, first, group):
    state_rows = states[0].shape[0]
    rank, degrees = roots[0].shape[-2:]
    owners, here, slots = places.shape
    count = len(states)
    columns = state_rows * 2 // here
    last = so_far is not None
    out = jax.ShapeDtypeStruct((columns // 2, 2, degrees, slots), BF16)
    inputs = [places, alive, *roots, *states]
    in_specs = whole_blocks(len(inputs))
    scratch = [pltpu.VMEM((degrees // 128, count * here * columns, 128), F32)]
    more = {}
    if last:
        inputs = [so_far, *inputs]
        in_specs = whole_blocks(len(inputs))
        scratch += [pltpu.VMEM(out.shape, BF16), pltpu.SemaphoreType.DMA((columns // 2,))]
        more["out_specs"] = IN_HBM
    return call(
        functools.partial(root_kernel, group, first, last),
        "root",
        out,
        in_specs,
        2 * count * here * rank * degrees * columns,
        2 * count * here * rank * degrees,
        scratch,
        mib=24,
        **more,
    )(*inputs)


def per_device(
    fourier, quad_weights, leaf_basis, level_factors, sparsity, root_basis, order_of_slot
):
    slots, columns, lats = fourier.shape
    owners = lax.axis_size("order")
    levels = level_factors.shape[1]
    group = max(2, 16 * owners // columns)
    present = in_hbm(sparsity.transpose(1, 2, 0))
    fourier, leaf_basis, level_factors, root_basis = map(in_hbm, (fourier, leaf_basis, level_factors, root_basis))
    quad_weights = in_hbm(quad_weights.reshape(1, lats))

    def swap(array, axis, bits):
        return lax.ppermute(array, axis, [(i, i ^ bits) for i in range(lax.axis_size(axis))])

    def swap_both(array, order_bits, lat_bits):
        blocks = lax.axis_size("lat")
        pairs = [
            (o * blocks + b, (o ^ order_bits) * blocks + (b ^ lat_bits)) for o in range(owners) for b in range(blocks)
        ]
        return lax.ppermute(array, ("order", "lat"), pairs)

    early_pieces = 3 * owners // 4
    state, root_0 = leaf_states(fourier, quad_weights, leaf_basis, root_basis, owners)
    partner = swap(state, "lat", 1)
    weights = level_weights(level_factors, present, (0,), state)
    states = [next_states(f"level0_{c}", state, partner, weights[0], c) for c in range(2)]
    weights += level_weights(level_factors, present, tuple(range(1, levels)), states[1], root_basis, early_pieces - 1)
    own_factors, cross_factors, early_roots = weights[-3:]
    other_cross = swap(cross_factors, "order", 1)
    high = owners // 2
    own_columns = columns // owners
    for level in range(1, levels - 1):
        partners = [swap(state, "lat", 1 << level) for state in states]
        parts = high if level == levels - 2 else 1
        states = [
            next_states(f"level{level}_{c}", states[c], partners[c], weights[level], None, parts if c else 1, own_factors)
            for c in range(2)
        ]
    top = 1 << levels - 1
    mine, (other, early, term) = states
    mine_partner = swap(mine, "lat", top)
    early_partner = swap_both(early, 1, top)
    other_own = swap(term, "order", 1)
    places, alive, later_roots = places_of(
        order_of_slot, root_basis, owners, owners - early_pieces, group, other
    )
    late_partner = swap_both(late_columns(alive, other, own_columns), 1, top)
    even = last_states("last_own", alive, mine, mine_partner, (cross_factors, own_factors), high, True)
    begin = columns // 2 - own_columns
    odd = last_states("last_early", alive, other_own, early_partner, (other_cross,), high - 1, False)
    odd = [*last_states("last_late", alive, other_own, late_partner, (other_cross,), 1, False, begin), *odd]
    arrived = [swap((odd if k % 2 else even)[k // 2], "order", k // 2 * 2) if k > 1 else (even, odd)[k][0] for k in range(owners)]
    roots = [root_0, early_roots]
    spectra = spectra_of(arrived[:early_pieces], roots, places, alive, None, early_pieces, group)
    return spectra_of(arrived[early_pieces:], [later_roots], places, alive, spectra, early_pieces, group)


def solution(mesh):
    return jax.shard_map(
        per_device,
        mesh=mesh,
        in_specs=(
            P("order", None, "lat"),
            P("lat"),
            P("order", None, "lat"),
            P("order", None, None, "lat", None, None),
            P("order", None, "lat"),
            P(None, None, "lat"),
            P(),
        ),
        out_specs=P("order", None, "lat", None),
        check_vma=False,
    )
```
